32 devices in a mesh: dp: 8 (over z, y), row: 2 (over core), col: 2 (over x).
Axes of the slice: x: 2, y: 2, z: 4, core: 2. Of those that a mesh axis runs over, the one named last changes fastest.
Arguments:
- block_in: bfloat16 [8192, 1024], P(('dp', 'col'), 'row'), may hold values from -6 to 6
- w_query: bfloat16 [1024, 1024], P('row', 'col'), may hold values from -2 to 2
- w_key: bfloat16 [1024, 1024], P('row', 'col'), may hold values from -2 to 2
- w_value: bfloat16 [1024, 1024], P('row', 'col'), may hold values from -0.1875 to 0.1875
- w_output: bfloat16 [1024, 1024], P('col', 'row'), may hold values from -2 to 2
- w_gate: bfloat16 [1024, 2816], P('row', 'col'), may hold values from -0.1875 to 0.1875
- w_up: bfloat16 [1024, 2816], P('row', 'col'), may hold values from -0.1875 to 0.1875
- w_down: bfloat16 [2816, 1024], P('col', 'row'), may hold values from -2 to 2
- qnorm_gain: float32 [1024], P('col'), may hold values from 0.5 to 2.5
- knorm_gain: float32 [1024], P('col'), may hold values from 0.5 to 2.5
- attn_gain: float32 [1024], P('row'), may hold values from 0.4 to 1.6
- mlp_gain: float32 [1024], P('row'), may hold values from 0.4 to 1.6
- cotangent: bfloat16 [8192, 1024], P(('dp', 'col'), 'row'), may hold values from -6 to 6
Outputs:
- block_out: float32 [8192, 1024], P(('dp', 'col'), 'row')
- grad_input: float32 [8192, 1024], P(('dp', 'col'), 'row')
- grad_query: float32 [1024, 1024], P('row', 'col')
- grad_key: float32 [1024, 1024], P('row', 'col')
- grad_value: float32 [1024, 1024], P('row', 'col')
- grad_output: float32 [1024, 1024], P('col', 'row')
- grad_gate: float32 [1024, 2816], P('row', 'col')
- grad_up: float32 [1024, 2816], P('row', 'col')
- grad_down: float32 [2816, 1024], P('col', 'row')
- grad_qgain: float32 [1024], P('col')
- grad_kgain: float32 [1024], P('col')
- grad_attngain: float32 [1024], P('row')
- grad_mlpgain: float32 [1024], P('row')
The draws below stay inside these ranges and needn't reach their ends.
All inputs are finite; a program needn't handle non-finite values.
Results may differ from the reference program's by a relative error of at most 0.015.
The reference program's roundings to bfloat16 on the way count: a program that leaves them out, or rounds other values in their place, can miss the bound.
Values may be sent and summed in bfloat16 or wider, within the bound.
No kernel may reach another device: no remote copies, remote signals or barrier semaphores. Data moves between devices by JAX's collectives and lax.ppermute only.
A program may use at most 128 MiB of HBM per device.

```python
import math
import jax
import jax.numpy as jnp
from jax import lax

D = 1024
HEADS = 16
HEAD = 64
FF = 2816
SEQ = 512
TOKENS = 8192
N_DP = 8


def rising_columns(key, base_draw, columns, fan_in):
    ramp_factor = 3.0 ** (jnp.arange(columns, dtype=jnp.float32) / columns)
    jitter = jnp.exp(jax.random.uniform(key, (columns,), jnp.float32, -0.35, 0.35))
    return base_draw * (0.6 * ramp_factor * jitter / math.sqrt(fan_in))[None, :]


def draw_w_query(key, part):
    key = jax.random.fold_in(key, 11)
    base_key, col_key = jax.random.split(key)
    base_draw = jnp.clip(jax.random.normal(base_key, (D, D), jnp.float32), -4.0, 4.0)
    return rising_columns(col_key, base_draw, D, D).astype(jnp.bfloat16)


def draw_w_key(key, part):
    key = jax.random.fold_in(key, 23)
    base_key, col_key = jax.random.split(key)
    base_draw = jnp.clip(jax.random.normal(base_key, (D, D), jnp.float32), -4.0, 4.0)
    return rising_columns(col_key, base_draw, D, D).astype(jnp.bfloat16)


def draw_w_output(key, part):
    key = jax.random.fold_in(key, 37)
    base_key, col_key = jax.random.split(key)
    base_draw = jnp.clip(jax.random.normal(base_key, (D, D), jnp.float32), -4.0, 4.0)
    return rising_columns(col_key, base_draw, D, D).astype(jnp.bfloat16)


def draw_w_down(key, part):
    key = jax.random.fold_in(key, 41)
    base_key, col_key = jax.random.split(key)
    base_draw = jnp.clip(jax.random.normal(base_key, (FF, D), jnp.float32), -4.0, 4.0)
    return rising_columns(col_key, base_draw, D, FF).astype(jnp.bfloat16)


def block_levels(stream_key, shape, cuts, smallest, largest):
    level, own = 1.0, jax.random.fold_in(stream_key, 6)
    for dim, blocks in cuts:
        draws = jnp.exp(jax.random.uniform(jax.random.fold_in(own, dim), (blocks,), jnp.float32, smallest / len(cuts), largest / len(cuts)))
        level = level * jnp.repeat(draws, shape[dim] // blocks).reshape([-1 if axis == dim else 1 for axis in range(len(shape))])
    return level


def centred(key, extent, scale, most, cuts=(), kind=jnp.bfloat16):
    values = jax.random.normal(key, extent, jnp.float32) * scale
    if len(cuts) > 0:
        values = block_levels(key, extent, cuts, -0.22, 0.18) * values
    return jnp.clip(values, min=-most, max=most).astype(kind)


def setup_inputs(seed: int = 0) -> dict:
    key_of = jax.random.split(jax.random.key(seed), 14)
    return {
        "block_in": centred(key_of[0], (TOKENS, D), 1.0, 6.0, ((0, 16), (1, 2))),
        "w_query": draw_w_query(jax.random.fold_in(key_of[13], 71), 0),
        "w_key": draw_w_key(jax.random.fold_in(key_of[13], 71), 0),
        "w_value": centred(key_of[3], (D, D), D ** -0.5, 0.1875, ((0, 2), (1, 2))),
        "w_output": draw_w_output(jax.random.fold_in(key_of[13], 71), 0),
        "w_gate": centred(key_of[5], (D, FF), D ** -0.5, 0.1875, ((0, 2), (1, 2))),
        "w_up": centred(key_of[6], (D, FF), D ** -0.5, 0.1875, ((0, 2), (1, 2))),
        "w_down": draw_w_down(jax.random.fold_in(key_of[13], 71), 0),
        "qnorm_gain": jnp.clip(0.5 + 2.0 * jax.random.uniform(key_of[8], (D,), jnp.float32) ** block_levels(key_of[8], (D,), ((0, 2),), -0.2, 0.2), 0.5, 2.5),
        "knorm_gain": jnp.clip(0.5 + 2.0 * jax.random.uniform(key_of[9], (D,), jnp.float32) ** block_levels(key_of[9], (D,), ((0, 2),), -0.2, 0.2), 0.5, 2.5),
        "attn_gain": jnp.clip(1.0 + 0.12 * jax.random.normal(key_of[10], (D,), jnp.float32), 0.4, 1.6),
        "mlp_gain": jnp.clip(1.0 + 0.12 * jax.random.normal(key_of[11], (D,), jnp.float32), 0.4, 1.6),
        "cotangent": centred(key_of[12], (TOKENS, D), 1.0, 6.0, ((0, 16), (1, 2))),
    }


EPSILON = 1e-06
ROPE_BASE = 500000.0
MASKED = -1e+30

@jax.custom_vjp
def low(v):
    return lax.optimization_barrier(v.astype(jnp.bfloat16)).astype(jnp.float32)

@jax.custom_vjp
def low_back(v):
    return v

def low_keep(v):
    return (low(v), None)

def low_pass(kept, grad):
    return (grad,)

def back_keep(v):
    return (v, None)

def back_low(kept, grad):
    return (low(grad),)
low.defvjp(low_keep, low_pass)
low_back.defvjp(back_keep, back_low)

def product(left, right):
    return jnp.dot(left, right, precision=lax.Precision.HIGHEST, preferred_element_type=jnp.float32)

def rms_norm(values, gain_vec):
    return values * lax.rsqrt(lax.optimization_barrier(jnp.mean(values * values, axis=-1, keepdims=True)) + EPSILON) * gain_vec

def rotate(values, positions):
    half_width = HEAD // 2
    frequency = jnp.exp(jnp.arange(half_width, dtype=jnp.float32) * (-2.0 * math.log(ROPE_BASE) / HEAD))
    angles = positions[:, None] * frequency[None, :]
    cosine = jnp.cos(angles)[:, None, :]
    sine_part = jnp.sin(angles)[:, None, :]
    shaped = values.reshape(values.shape[0], HEADS, 2, half_width)
    first_half = shaped[:, :, 0]
    second_half = shaped[:, :, 1]
    turned = jnp.stack([first_half * cosine - second_half * sine_part, second_half * cosine + first_half * sine_part], axis=2)
    return turned.reshape(values.shape[0], D)

def attend(operands):
    query_rows, key_rows, value_rows = operands
    query_heads = query_rows.reshape(SEQ, HEADS, HEAD)
    key_heads = key_rows.reshape(SEQ, HEADS, HEAD)
    value_heads = value_rows.reshape(SEQ, HEADS, HEAD)
    scores = jnp.einsum('qhd,khd->hqk', query_heads, key_heads, precision=lax.Precision.HIGHEST, preferred_element_type=jnp.float32) * (1.0 / math.sqrt(HEAD))
    scores = low_back(scores)
    causal = jnp.arange(SEQ)[:, None] >= jnp.arange(SEQ)[None, :]
    scores = jnp.where(causal[None], scores, MASKED)
    attention = jax.nn.softmax(scores, axis=-1)
    mixed_rows = jnp.einsum('hqk,khd->qhd', low(attention), value_heads, precision=lax.Precision.HIGHEST, preferred_element_type=jnp.float32)
    return mixed_rows.reshape(SEQ, D)

def layer(rows_in, w_query, w_key, w_value, w_output, w_gate, w_up, w_down, qnorm_gain, knorm_gain, attn_gain, mlp_gain):
    row_count = rows_in.shape[0]
    positions = (jnp.arange(row_count) % SEQ).astype(jnp.float32)
    queries = low_back(product(rows_in, w_query))
    keys_all = low_back(product(rows_in, w_key))
    values = low(low_back(product(rows_in, w_value)))
    rot_query = low(rotate(rms_norm(queries, qnorm_gain), positions))
    rot_key = low(rotate(rms_norm(keys_all, knorm_gain), positions))
    seq_count = row_count // SEQ
    mixed_all = lax.map(jax.checkpoint(attend), (rot_query.reshape(seq_count, SEQ, D), rot_key.reshape(seq_count, SEQ, D), values.reshape(seq_count, SEQ, D)))
    mixed_all = low(low_back(mixed_all.reshape(row_count, D)))
    branch_attn = low_back(product(mixed_all, w_output))
    hidden_in = rows_in + rms_norm(branch_attn, attn_gain)
    hidden_low = low(hidden_in)
    gate_act = low_back(product(hidden_low, w_gate))
    up_act = low_back(product(hidden_low, w_up))
    activated = low(jax.nn.silu(gate_act) * up_act)
    branch_ff = low_back(product(activated, w_down))
    return hidden_in + rms_norm(branch_ff, mlp_gain)

def reference(block_in, w_query, w_key, w_value, w_output, w_gate, w_up, w_down, qnorm_gain, knorm_gain, attn_gain, mlp_gain, cotangent):
    params = tuple((item.astype(jnp.float32) for item in (w_query, w_key, w_value, w_output, w_gate, w_up, w_down, qnorm_gain, knorm_gain, attn_gain, mlp_gain)))
    group_rows = TOKENS // N_DP
    inputs_grouped = block_in.astype(jnp.float32).reshape(N_DP, group_rows, D)
    cot_grouped = cotangent.astype(jnp.float32).reshape(N_DP, group_rows, D)

    def group_step(running, operands):
        rows_in, rows_cot = operands
        result, pullback = jax.vjp(layer, rows_in, *params)
        gradients = pullback(rows_cot)
        running = jax.tree.map(jnp.add, running, tuple(gradients[1:]))
        return (running, (result, gradients[0]))
    initial = tuple((jnp.zeros(item.shape, jnp.float32) for item in params))
    totals, (outputs, grad_rows) = lax.scan(group_step, initial, (inputs_grouped, cot_grouped))
    return (outputs.reshape(TOKENS, D), grad_rows.reshape(TOKENS, D), totals[0], totals[1], totals[2], totals[3], totals[4], totals[5], totals[6], totals[7], totals[8], totals[9], totals[10])
```

```python
import math

import jax
import jax.numpy as jnp
from jax import lax
from jax.sharding import PartitionSpec as P

D = 1024
HEAD = 64
SEQ = 512
EPSILON = 1e-06
ROPE_BASE = 500000.0
MASKED = -1e30
CHUNKS = 2

F32 = jnp.float32
BF16 = jnp.bfloat16


def swap(values, axis):
    return lax.ppermute(values, axis, [(0, 1), (1, 0)])


def dot(left, right):
    return jnp.dot(left, right, preferred_element_type=F32)


def dot_t(left, right):
    return lax.dot_general(left, right, (((1,), (1,)), ((), ())), preferred_element_type=F32)


def t_dot(left, right):
    return lax.dot_general(left, right, (((0,), (0,)), ((), ())), preferred_element_type=F32)


def rope_tables(row_count):
    half_width = HEAD // 2
    frequency = jnp.exp(jnp.arange(half_width, dtype=F32) * (-2.0 * math.log(ROPE_BASE) / HEAD))
    positions = (jnp.arange(row_count) % SEQ).astype(F32)
    angles = positions[:, None] * frequency[None, :]
    return (jnp.cos(angles)[:, None, :], jnp.sin(angles)[:, None, :])


def rotate(values, cosine, sine_part):
    row_count = values.shape[0]
    shaped = values.reshape(row_count, -1, 2, HEAD // 2)
    first_half = shaped[:, :, 0]
    second_half = shaped[:, :, 1]
    turned = jnp.stack(
        [
            first_half * cosine - second_half * sine_part,
            second_half * cosine + first_half * sine_part,
        ],
        axis=2,
    )
    return turned.reshape(row_count, -1)


def dp_bit(bit):
    return (lax.axis_index("dp") >> bit) & 1


def dp_exchange(values, bit):
    size = lax.axis_size("dp")
    return lax.ppermute(values, "dp", [(i, i ^ (1 << bit)) for i in range(size)])


def dp_bits():
    return range(lax.axis_size("dp").bit_length() - 1)


def dp_total(grad):
    current = grad
    for bit in dp_bits():
        half = current.shape[0] // 2
        mine = dp_bit(bit)
        keep = lax.dynamic_slice_in_dim(current, mine * half, half, 0)
        give = lax.dynamic_slice_in_dim(current, (1 - mine) * half, half, 0)
        received = dp_exchange(give.astype(BF16), bit)
        current = keep.astype(F32) + received.astype(F32)
    current = current.astype(BF16)
    for bit in reversed(dp_bits()):
        received = dp_exchange(current, bit)
        lower = dp_bit(bit) == 0
        current = jnp.concatenate(
            [jnp.where(lower, current, received), jnp.where(lower, received, current)], axis=0
        )
    return current.astype(F32)


def dp_total_small(values):
    for bit in dp_bits():
        values = values + dp_exchange(values, bit)
    return values


def norm_back(branch, scale, gain_vec, grad_out):
    weighted = grad_out * gain_vec
    inner = jnp.sum(weighted * branch, axis=1, keepdims=True)
    grad_branch = scale * weighted - branch * (scale * scale * scale * inner / D)
    grad_gain = jnp.sum(grad_out * branch * scale, axis=0)
    return (grad_branch.astype(BF16), grad_gain)


def col_total(partial):
    low = partial.astype(BF16)
    return low.astype(F32) + swap(low, "col").astype(F32)


def on_device(
    block_in,
    w_query,
    w_key,
    w_value,
    w_output,
    w_gate,
    w_up,
    w_down,
    qnorm_gain,
    knorm_gain,
    attn_gain,
    mlp_gain,
    cotangent,
):
    rows, half = block_in.shape
    col_width = w_query.shape[1]
    ff_width = w_gate.shape[1]
    head_count = col_width // HEAD
    factor = 1.0 / math.sqrt(HEAD)
    row_position = lax.axis_index("row")
    col_position = lax.axis_index("col")
    same = row_position == col_position

    in_swapped = swap(block_in, "col")
    in_mine = jnp.where(same, block_in, in_swapped)
    in_give = jnp.where(same, in_swapped, block_in)
    wqkv_mine = jnp.concatenate([w_query, w_key, w_value], axis=1)
    wqkv_theirs = swap(wqkv_mine, "row")
    in_theirs = swap(in_give, "row")
    gains = jnp.stack([attn_gain, mlp_gain])
    gains = jnp.concatenate([gains, swap(gains, "row")], axis=1)
    attn_gain_full, mlp_gain_full = gains[0], gains[1]
    wo_theirs = swap(w_output, "row")
    wgu_mine = jnp.concatenate([w_gate, w_up], axis=1)
    wgu_theirs = swap(wgu_mine, "row")
    wd_theirs = swap(w_down, "row")

    projected = dot(in_mine, wqkv_mine) + dot(in_theirs, wqkv_theirs)
    queries = projected[:, :col_width]
    keys_raw = projected[:, col_width : 2 * col_width]
    value_low = projected[:, 2 * col_width :].astype(BF16)
    totals = jnp.stack([jnp.sum(queries * queries, axis=1), jnp.sum(keys_raw * keys_raw, axis=1)])
    totals = totals + swap(totals, "col")
    scales = lax.rsqrt(totals / D + EPSILON)
    query_scale = scales[0][:, None]
    key_scale = scales[1][:, None]
    cosine, sine_part = rope_tables(rows)
    query_rot = rotate(queries * query_scale * qnorm_gain, cosine, sine_part).astype(BF16)
    key_rot = rotate(keys_raw * key_scale * knorm_gain, cosine, sine_part).astype(BF16)
    query_heads = query_rot.reshape(rows, head_count, HEAD)
    key_heads = key_rot.reshape(rows, head_count, HEAD)
    value_heads = value_low.reshape(rows, head_count, HEAD)
    causal = (jnp.arange(SEQ)[:, None] >= jnp.arange(SEQ)[None, :])[None]

    def masked_scores():
        raw = jnp.einsum("qhd,khd->hqk", query_heads, key_heads, preferred_element_type=F32)
        return jnp.where(causal, raw * factor, MASKED)

    scores = masked_scores()
    peak_score = jnp.max(scores, axis=-1, keepdims=True)
    exponent = jnp.exp(scores - peak_score)
    exp_total = jnp.sum(exponent, axis=-1, keepdims=True)
    attention = exponent / exp_total
    log_total = peak_score + jnp.log(exp_total)
    mixed = jnp.einsum(
        "hqk,khd->qhd", attention.astype(BF16), value_heads, preferred_element_type=F32
    )
    mixed_low = mixed.reshape(rows, col_width).astype(BF16)
    mixed_theirs = swap(mixed_low, "row")

    cot_swapped = swap(cotangent, "col")
    cot_mine = jnp.where(same, cotangent, cot_swapped)
    cot_theirs = swap(jnp.where(same, cot_swapped, cotangent), "row")

    def pieces(values, index):
        size = rows // CHUNKS
        return values[index * size : (index + 1) * size]

    chunk = range(CHUNKS)
    in_full = jnp.concatenate([in_mine, in_theirs], axis=1)
    cot_full = jnp.concatenate([cot_mine, cot_theirs], axis=1)

    attn_partial = []
    for i in chunk:
        part = pieces(mixed_low, i)
        attn_partial.append(
            jnp.concatenate([dot(part, w_output), dot(part, wo_theirs)], axis=1)
        )
    branch_attn = [col_total(p) for p in attn_partial]
    attn_scale = []
    hidden_in = []
    hidden_low = []
    for i in chunk:
        branch = branch_attn[i]
        scale = lax.rsqrt(jnp.mean(branch * branch, axis=1, keepdims=True) + EPSILON)
        attn_scale.append(scale)
        hidden_in.append(pieces(in_full, i).astype(F32) + branch * scale * attn_gain_full)
        hidden_low.append(hidden_in[i].astype(BF16))

    gate_act, up_act, sigmoid_gate, activated = [], [], [], []
    branch_ff = []
    for i in chunk:
        low = hidden_low[i]
        gate_up = dot(low[:, :half], wgu_mine) + dot(low[:, half:], wgu_theirs)
        gate_act.append(gate_up[:, :ff_width])
        up_act.append(gate_up[:, ff_width:])
        sigmoid_gate.append(jax.nn.sigmoid(gate_act[i]))
        activated.append((gate_act[i] * sigmoid_gate[i] * up_act[i]).astype(BF16))
        partial = jnp.concatenate([dot(activated[i], w_down), dot(activated[i], wd_theirs)], axis=1)
        branch_ff.append(col_total(partial))
    hidden_all = jnp.concatenate(hidden_low, axis=0)
    hidden_theirs = swap(hidden_all[:, half:], "row")
    act_all = jnp.concatenate(activated, axis=0)
    act_theirs = swap(act_all, "row")

    block_out, grad_ffbranch = [], []
    mlpgain_part = 0.0
    for i in chunk:
        branch = branch_ff[i]
        scale = lax.rsqrt(jnp.mean(branch * branch, axis=1, keepdims=True) + EPSILON)
        block_out.append(hidden_in[i] + branch * scale * mlp_gain_full)
        upstream = pieces(cot_full, i).astype(F32)
        grad_branch, grad_gain = norm_back(branch, scale, mlp_gain_full, upstream)
        grad_ffbranch.append(grad_branch)
        mlpgain_part = mlpgain_part + grad_gain
    gff_all = jnp.concatenate(grad_ffbranch, axis=0)
    gff_theirs = swap(gff_all[:, half:], "row")
    grad_down = dp_total(t_dot(act_all, gff_all[:, :half]) + t_dot(act_theirs, gff_theirs))

    grad_gateup, grad_hidden = [], []
    for i in chunk:
        gff = grad_ffbranch[i]
        grad_act = dot_t(gff[:, :half], w_down) + dot_t(gff[:, half:], wd_theirs)
        sg = sigmoid_gate[i]
        grad_gate_act = grad_act * up_act[i] * sg * (1.0 + gate_act[i] * (1.0 - sg))
        grad_up_act = grad_act * gate_act[i] * sg
        grad_gateup.append(jnp.concatenate([grad_gate_act, grad_up_act], axis=1).astype(BF16))
        partial = jnp.concatenate(
            [dot_t(grad_gateup[i], wgu_mine), dot_t(grad_gateup[i], wgu_theirs)], axis=1
        )
        grad_hidden.append(pieces(cot_full, i).astype(F32) + col_total(partial))
    ggu_all = jnp.concatenate(grad_gateup, axis=0)
    ggu_theirs = swap(ggu_all, "row")
    grad_gu = t_dot(hidden_all[:, :half], ggu_all) + t_dot(hidden_theirs, ggu_theirs)
    grad_gate = dp_total(grad_gu[:, :ff_width])
    grad_up = dp_total(grad_gu[:, ff_width:])

    grad_attnbranch, grad_mixed = [], []
    attngain_part = 0.0
    for i in chunk:
        grad_branch, grad_gain = norm_back(
            branch_attn[i], attn_scale[i], attn_gain_full, grad_hidden[i]
        )
        grad_attnbranch.append(grad_branch)
        attngain_part = attngain_part + grad_gain
        grad_mixed.append(
            (dot_t(grad_branch[:, :half], w_output) + dot_t(grad_branch[:, half:], wo_theirs)).astype(
                BF16
            )
        )
    gattn_all = jnp.concatenate(grad_attnbranch, axis=0)
    gattn_theirs = swap(gattn_all[:, half:], "row")
    grad_outw = dp_total(t_dot(mixed_low, gattn_all[:, :half]) + t_dot(mixed_theirs, gattn_theirs))

    grad_mix_heads = jnp.concatenate(grad_mixed, axis=0).reshape(rows, head_count, HEAD)
    attention_back = jnp.exp(masked_scores() - log_total)
    grad_attention = jnp.einsum(
        "qhd,khd->hqk", grad_mix_heads, value_heads, preferred_element_type=F32
    )
    grad_values = jnp.einsum(
        "hqk,qhd->khd", attention_back.astype(BF16), grad_mix_heads, preferred_element_type=F32
    )
    inner_attn = jnp.sum(attention_back * grad_attention, axis=-1, keepdims=True)
    grad_scores = (attention_back * (grad_attention - inner_attn)).astype(BF16)
    grad_qrot = (
        jnp.einsum("hqk,khd->qhd", grad_scores, key_heads, preferred_element_type=F32) * factor
    )
    grad_krot = (
        jnp.einsum("hqk,qhd->khd", grad_scores, query_heads, preferred_element_type=F32) * factor
    )
    grad_qnormed = rotate(grad_qrot.reshape(rows, col_width), cosine, -sine_part)
    grad_knormed = rotate(grad_krot.reshape(rows, col_width), cosine, -sine_part)
    weighted_q = grad_qnormed * qnorm_gain
    weighted_k = grad_knormed * knorm_gain
    inner = jnp.stack(
        [jnp.sum(weighted_q * queries, axis=1), jnp.sum(weighted_k * keys_raw, axis=1)]
    )
    inner = inner + swap(inner, "col")
    grad_queries = query_scale * weighted_q - queries * (
        query_scale * query_scale * query_scale * inner[0][:, None] / D
    )
    grad_keys = key_scale * weighted_k - keys_raw * (
        key_scale * key_scale * key_scale * inner[1][:, None] / D
    )
    qgain_part = jnp.sum(grad_qnormed * queries * query_scale, axis=0)
    kgain_part = jnp.sum(grad_knormed * keys_raw * key_scale, axis=0)
    grad_qkv = jnp.concatenate(
        [grad_queries, grad_keys, grad_values.reshape(rows, col_width)], axis=1
    ).astype(BF16)
    gqkv_theirs = swap(grad_qkv, "row")
    grad_qkvw = dp_total(t_dot(in_mine, grad_qkv) + t_dot(in_give, gqkv_theirs))

    gain_mine = jnp.concatenate([mlpgain_part[:half], attngain_part[:half], qgain_part, kgain_part])
    gain_give = jnp.concatenate([mlpgain_part[half:], attngain_part[half:], qgain_part, kgain_part])
    gain_total = dp_total_small(gain_mine + swap(gain_give, "row"))
    grad_mlpgain, grad_attngain, grad_qgain, grad_kgain = jnp.split(
        gain_total, [half, 2 * half, 2 * half + col_width]
    )

    grad_in_mine = dot_t(grad_qkv, wqkv_mine)
    grad_in_theirs = dot_t(grad_qkv, wqkv_theirs)
    hidden_grad = jnp.concatenate(grad_hidden, axis=0)
    pair = ("row", "col")
    stays = grad_in_mine + hidden_grad[:, :half]
    moves = grad_in_theirs + hidden_grad[:, half:]
    across = lax.ppermute(grad_in_mine.astype(BF16), pair, [(1, 0), (2, 3)])
    corner = lax.ppermute(grad_in_theirs.astype(BF16), pair, [(1, 2), (2, 1)])
    beside = lax.ppermute(moves, pair, [(0, 2), (3, 1)])
    grad_input = jnp.where(same, stays, beside) + jnp.where(same, across, corner).astype(F32)
    out_full = jnp.concatenate(block_out, axis=0)
    out_beside = lax.ppermute(out_full[:, half:], pair, [(0, 2), (3, 1)])
    out_final = jnp.where(same, out_full[:, :half], out_beside)
    return (
        out_final,
        grad_input,
        grad_qkvw[:, :col_width],
        grad_qkvw[:, col_width : 2 * col_width],
        grad_qkvw[:, 2 * col_width :],
        grad_outw,
        grad_gate,
        grad_up,
        grad_down,
        grad_qgain,
        grad_kgain,
        grad_attngain,
        grad_mlpgain,
    )


def solution(mesh):
    tokens = P(("dp", "col"), "row")
    in_specs = (
        tokens,
        P("row", "col"),
        P("row", "col"),
        P("row", "col"),
        P("col", "row"),
        P("row", "col"),
        P("row", "col"),
        P("col", "row"),
        P("col"),
        P("col"),
        P("row"),
        P("row"),
        tokens,
    )
    out_specs = (
        tokens,
        tokens,
        P("row", "col"),
        P("row", "col"),
        P("row", "col"),
        P("col", "row"),
        P("row", "col"),
        P("row", "col"),
        P("col", "row"),
        P("col"),
        P("col"),
        P("row"),
        P("row"),
    )
    return jax.shard_map(
        on_device, mesh=mesh, in_specs=in_specs, out_specs=out_specs, check_vma=False
    )
```

```python
import math

import jax
import jax.numpy as jnp
from jax import lax
from jax.sharding import PartitionSpec as P

D = 1024
HEAD = 64
SEQ = 512
EPSILON = 1e-06
ROPE_BASE = 500000.0
MASKED = -1e30
CHUNKS = 2

F32 = jnp.float32
BF16 = jnp.bfloat16


def swap(values, axis):
    return lax.ppermute(values, axis, [(0, 1), (1, 0)])


def dot(left, right):
    return jnp.dot(left, right, preferred_element_type=F32)


def dot_t(left, right):
    return lax.dot_general(left, right, (((1,), (1,)), ((), ())), preferred_element_type=F32)


def t_dot(left, right):
    return lax.dot_general(left, right, (((0,), (0,)), ((), ())), preferred_element_type=F32)


def rope_tables(row_count):
    half_width = HEAD // 2
    frequency = jnp.exp(jnp.arange(half_width, dtype=F32) * (-2.0 * math.log(ROPE_BASE) / HEAD))
    positions = (jnp.arange(row_count) % SEQ).astype(F32)
    angles = positions[:, None] * frequency[None, :]
    return (jnp.cos(angles)[:, None, :], jnp.sin(angles)[:, None, :])


def rotate(values, cosine, sine_part):
    row_count = values.shape[0]
    shaped = values.reshape(row_count, -1, 2, HEAD // 2)
    first_half = shaped[:, :, 0]
    second_half = shaped[:, :, 1]
    turned = jnp.stack(
        [
            first_half * cosine - second_half * sine_part,
            second_half * cosine + first_half * sine_part,
        ],
        axis=2,
    )
    return turned.reshape(row_count, -1)


def dp_bit(bit):
    return (lax.axis_index("dp") >> bit) & 1


def dp_exchange(values, bit):
    size = lax.axis_size("dp")
    return lax.ppermute(values, "dp", [(i, i ^ (1 << bit)) for i in range(size)])


def dp_bits():
    return range(lax.axis_size("dp").bit_length() - 1)


def dp_total(grad):
    return lax.psum(grad.astype(BF16), "dp").astype(F32)


def dp_total_small(values):
    for bit in dp_bits():
        values = values + dp_exchange(values, bit)
    return values


def norm_back(branch, scale, gain_vec, grad_out):
    weighted = grad_out * gain_vec
    inner = jnp.sum(weighted * branch, axis=1, keepdims=True)
    grad_branch = scale * weighted - branch * (scale * scale * scale * inner / D)
    grad_gain = jnp.sum(grad_out * branch * scale, axis=0)
    return (grad_branch.astype(BF16), grad_gain)


def col_total(partial):
    low = partial.astype(BF16)
    return low.astype(F32) + swap(low, "col").astype(F32)


def on_device(
    block_in,
    w_query,
    w_key,
    w_value,
    w_output,
    w_gate,
    w_up,
    w_down,
    qnorm_gain,
    knorm_gain,
    attn_gain,
    mlp_gain,
    cotangent,
):
    rows, half = block_in.shape
    col_width = w_query.shape[1]
    ff_width = w_gate.shape[1]
    head_count = col_width // HEAD
    factor = 1.0 / math.sqrt(HEAD)
    row_position = lax.axis_index("row")
    col_position = lax.axis_index("col")
    same = row_position == col_position

    in_swapped = swap(block_in, "col")
    in_mine = jnp.where(same, block_in, in_swapped)
    in_give = jnp.where(same, in_swapped, block_in)
    wqkv_mine = jnp.concatenate([w_query, w_key, w_value], axis=1)
    wqkv_theirs = swap(wqkv_mine, "row")
    in_theirs = swap(in_give, "row")
    gains = jnp.stack([attn_gain, mlp_gain])
    gains = jnp.concatenate([gains, swap(gains, "row")], axis=1)
    attn_gain_full, mlp_gain_full = gains[0], gains[1]
    wo_theirs = swap(w_output, "row")
    wgu_mine = jnp.concatenate([w_gate, w_up], axis=1)
    wgu_theirs = swap(wgu_mine, "row")
    wd_theirs = swap(w_down, "row")

    projected = dot(in_mine, wqkv_mine) + dot(in_theirs, wqkv_theirs)
    queries = projected[:, :col_width]
    keys_raw = projected[:, col_width : 2 * col_width]
    value_low = projected[:, 2 * col_width :].astype(BF16)
    totals = jnp.stack([jnp.sum(queries * queries, axis=1), jnp.sum(keys_raw * keys_raw, axis=1)])
    totals = totals + swap(totals, "col")
    scales = lax.rsqrt(totals / D + EPSILON)
    query_scale = scales[0][:, None]
    key_scale = scales[1][:, None]
    cosine, sine_part = rope_tables(rows)
    query_rot = rotate(queries * query_scale * qnorm_gain, cosine, sine_part).astype(BF16)
    key_rot = rotate(keys_raw * key_scale * knorm_gain, cosine, sine_part).astype(BF16)
    query_heads = query_rot.reshape(rows, head_count, HEAD)
    key_heads = key_rot.reshape(rows, head_count, HEAD)
    value_heads = value_low.reshape(rows, head_count, HEAD)
    causal = (jnp.arange(SEQ)[:, None] >= jnp.arange(SEQ)[None, :])[None]

    def masked_scores():
        raw = jnp.einsum("qhd,khd->hqk", query_heads, key_heads, preferred_element_type=F32)
        return jnp.where(causal, raw * factor, MASKED)

    scores = masked_scores()
    peak_score = jnp.max(scores, axis=-1, keepdims=True)
    exponent = jnp.exp(scores - peak_score)
    exp_total = jnp.sum(exponent, axis=-1, keepdims=True)
    attention = exponent / exp_total
    log_total = peak_score + jnp.log(exp_total)
    mixed = jnp.einsum(
        "hqk,khd->qhd", attention.astype(BF16), value_heads, preferred_element_type=F32
    )
    mixed_low = mixed.reshape(rows, col_width).astype(BF16)
    mixed_theirs = swap(mixed_low, "row")

    cot_swapped = swap(cotangent, "col")
    cot_mine = jnp.where(same, cotangent, cot_swapped)
    cot_theirs = swap(jnp.where(same, cot_swapped, cotangent), "row")

    def pieces(values, index):
        size = rows // CHUNKS
        return values[index * size : (index + 1) * size]

    chunk = range(CHUNKS)
    in_full = jnp.concatenate([in_mine, in_theirs], axis=1)
    cot_full = jnp.concatenate([cot_mine, cot_theirs], axis=1)

    attn_partial = []
    for i in chunk:
        part = pieces(mixed_low, i)
        attn_partial.append(
            jnp.concatenate([dot(part, w_output), dot(part, wo_theirs)], axis=1)
        )
    branch_attn = [col_total(p) for p in attn_partial]
    attn_scale = []
    hidden_in = []
    hidden_low = []
    for i in chunk:
        branch = branch_attn[i]
        scale = lax.rsqrt(jnp.mean(branch * branch, axis=1, keepdims=True) + EPSILON)
        attn_scale.append(scale)
        hidden_in.append(pieces(in_full, i).astype(F32) + branch * scale * attn_gain_full)
        hidden_low.append(hidden_in[i].astype(BF16))

    gate_act, up_act, sigmoid_gate, activated = [], [], [], []
    branch_ff = []
    for i in chunk:
        low = hidden_low[i]
        gate_up = dot(low[:, :half], wgu_mine) + dot(low[:, half:], wgu_theirs)
        gate_act.append(gate_up[:, :ff_width])
        up_act.append(gate_up[:, ff_width:])
        sigmoid_gate.append(jax.nn.sigmoid(gate_act[i]))
        activated.append((gate_act[i] * sigmoid_gate[i] * up_act[i]).astype(BF16))
        partial = jnp.concatenate([dot(activated[i], w_down), dot(activated[i], wd_theirs)], axis=1)
        branch_ff.append(col_total(partial))
    hidden_all = jnp.concatenate(hidden_low, axis=0)
    hidden_theirs = swap(hidden_all[:, half:], "row")
    act_all = jnp.concatenate(activated, axis=0)
    act_theirs = swap(act_all, "row")

    block_out, grad_ffbranch = [], []
    mlpgain_part = 0.0
    for i in chunk:
        branch = branch_ff[i]
        scale = lax.rsqrt(jnp.mean(branch * branch, axis=1, keepdims=True) + EPSILON)
        block_out.append(hidden_in[i] + branch * scale * mlp_gain_full)
        upstream = pieces(cot_full, i).astype(F32)
        grad_branch, grad_gain = norm_back(branch, scale, mlp_gain_full, upstream)
        grad_ffbranch.append(grad_branch)
        mlpgain_part = mlpgain_part + grad_gain
    gff_all = jnp.concatenate(grad_ffbranch, axis=0)
    gff_theirs = swap(gff_all[:, half:], "row")
    grad_down = dp_total(t_dot(act_all, gff_all[:, :half]) + t_dot(act_theirs, gff_theirs))

    grad_gateup, grad_hidden = [], []
    for i in chunk:
        gff = grad_ffbranch[i]
        grad_act = dot_t(gff[:, :half], w_down) + dot_t(gff[:, half:], wd_theirs)
        sg = sigmoid_gate[i]
        grad_gate_act = grad_act * up_act[i] * sg * (1.0 + gate_act[i] * (1.0 - sg))
        grad_up_act = grad_act * gate_act[i] * sg
        grad_gateup.append(jnp.concatenate([grad_gate_act, grad_up_act], axis=1).astype(BF16))
        partial = jnp.concatenate(
            [dot_t(grad_gateup[i], wgu_mine), dot_t(grad_gateup[i], wgu_theirs)], axis=1
        )
        grad_hidden.append(pieces(cot_full, i).astype(F32) + col_total(partial))
    ggu_all = jnp.concatenate(grad_gateup, axis=0)
    ggu_theirs = swap(ggu_all, "row")
    grad_gu = t_dot(hidden_all[:, :half], ggu_all) + t_dot(hidden_theirs, ggu_theirs)
    grad_gate = dp_total(grad_gu[:, :ff_width])
    grad_up = dp_total(grad_gu[:, ff_width:])

    grad_attnbranch, grad_mixed = [], []
    attngain_part = 0.0
    for i in chunk:
        grad_branch, grad_gain = norm_back(
            branch_attn[i], attn_scale[i], attn_gain_full, grad_hidden[i]
        )
        grad_attnbranch.append(grad_branch)
        attngain_part = attngain_part + grad_gain
        grad_mixed.append(
            (dot_t(grad_branch[:, :half], w_output) + dot_t(grad_branch[:, half:], wo_theirs)).astype(
                BF16
            )
        )
    gattn_all = jnp.concatenate(grad_attnbranch, axis=0)
    gattn_theirs = swap(gattn_all[:, half:], "row")
    grad_outw = dp_total(t_dot(mixed_low, gattn_all[:, :half]) + t_dot(mixed_theirs, gattn_theirs))

    grad_mix_heads = jnp.concatenate(grad_mixed, axis=0).reshape(rows, head_count, HEAD)
    attention_back = jnp.exp(masked_scores() - log_total)
    grad_attention = jnp.einsum(
        "qhd,khd->hqk", grad_mix_heads, value_heads, preferred_element_type=F32
    )
    grad_values = jnp.einsum(
        "hqk,qhd->khd", attention_back.astype(BF16), grad_mix_heads, preferred_element_type=F32
    )
    inner_attn = jnp.sum(attention_back * grad_attention, axis=-1, keepdims=True)
    grad_scores = (attention_back * (grad_attention - inner_attn)).astype(BF16)
    grad_qrot = (
        jnp.einsum("hqk,khd->qhd", grad_scores, key_heads, preferred_element_type=F32) * factor
    )
    grad_krot = (
        jnp.einsum("hqk,qhd->khd", grad_scores, query_heads, preferred_element_type=F32) * factor
    )
    grad_qnormed = rotate(grad_qrot.reshape(rows, col_width), cosine, -sine_part)
    grad_knormed = rotate(grad_krot.reshape(rows, col_width), cosine, -sine_part)
    weighted_q = grad_qnormed * qnorm_gain
    weighted_k = grad_knormed * knorm_gain
    inner = jnp.stack(
        [jnp.sum(weighted_q * queries, axis=1), jnp.sum(weighted_k * keys_raw, axis=1)]
    )
    inner = inner + swap(inner, "col")
    grad_queries = query_scale * weighted_q - queries * (
        query_scale * query_scale * query_scale * inner[0][:, None] / D
    )
    grad_keys = key_scale * weighted_k - keys_raw * (
        key_scale * key_scale * key_scale * inner[1][:, None] / D
    )
    qgain_part = jnp.sum(grad_qnormed * queries * query_scale, axis=0)
    kgain_part = jnp.sum(grad_knormed * keys_raw * key_scale, axis=0)
    grad_qkv = jnp.concatenate(
        [grad_queries, grad_keys, grad_values.reshape(rows, col_width)], axis=1
    ).astype(BF16)
    gqkv_theirs = swap(grad_qkv, "row")
    grad_qkvw = dp_total(t_dot(in_mine, grad_qkv) + t_dot(in_give, gqkv_theirs))

    gain_mine = jnp.concatenate([mlpgain_part[:half], attngain_part[:half], qgain_part, kgain_part])
    gain_give = jnp.concatenate([mlpgain_part[half:], attngain_part[half:], qgain_part, kgain_part])
    gain_total = dp_total_small(gain_mine + swap(gain_give, "row"))
    grad_mlpgain, grad_attngain, grad_qgain, grad_kgain = jnp.split(
        gain_total, [half, 2 * half, 2 * half + col_width]
    )

    grad_in_mine = dot_t(grad_qkv, wqkv_mine)
    grad_in_theirs = dot_t(grad_qkv, wqkv_theirs)
    hidden_grad = jnp.concatenate(grad_hidden, axis=0)
    pair = ("row", "col")
    stays = grad_in_mine + hidden_grad[:, :half]
    moves = grad_in_theirs + hidden_grad[:, half:]
    across = lax.ppermute(grad_in_mine.astype(BF16), pair, [(1, 0), (2, 3)])
    corner = lax.ppermute(grad_in_theirs.astype(BF16), pair, [(1, 2), (2, 1)])
    beside = lax.ppermute(moves, pair, [(0, 2), (3, 1)])
    grad_input = jnp.where(same, stays, beside) + jnp.where(same, across, corner).astype(F32)
    out_full = jnp.concatenate(block_out, axis=0)
    out_beside = lax.ppermute(out_full[:, half:], pair, [(0, 2), (3, 1)])
    out_final = jnp.where(same, out_full[:, :half], out_beside)
    return (
        out_final,
        grad_input,
        grad_qkvw[:, :col_width],
        grad_qkvw[:, col_width : 2 * col_width],
        grad_qkvw[:, 2 * col_width :],
        grad_outw,
        grad_gate,
        grad_up,
        grad_down,
        grad_qgain,
        grad_kgain,
        grad_attngain,
        grad_mlpgain,
    )


def solution(mesh):
    tokens = P(("dp", "col"), "row")
    in_specs = (
        tokens,
        P("row", "col"),
        P("row", "col"),
        P("row", "col"),
        P("col", "row"),
        P("row", "col"),
        P("row", "col"),
        P("col", "row"),
        P("col"),
        P("col"),
        P("row"),
        P("row"),
        tokens,
    )
    out_specs = (
        tokens,
        tokens,
        P("row", "col"),
        P("row", "col"),
        P("row", "col"),
        P("col", "row"),
        P("row", "col"),
        P("row", "col"),
        P("col", "row"),
        P("col"),
        P("col"),
        P("row"),
        P("row"),
    )
    return jax.shard_map(
        on_device, mesh=mesh, in_specs=in_specs, out_specs=out_specs, check_vma=False
    )
```

```python
import functools
import math

import jax
import jax.numpy as jnp
from jax import lax
from jax.experimental import pallas as pl
from jax.experimental.pallas import tpu as pltpu
from jax.sharding import PartitionSpec as P

D = 1024
HEAD = 64
SEQ = 512
EPSILON = 1e-06
ROPE_BASE = 500000.0
MASKED = -1e30
CHUNK = 256
TILE = 256
LANES = 128
FACTOR = 1.0 / math.sqrt(HEAD)

F32 = jnp.float32
BF16 = jnp.bfloat16


def swap(values, axis):
    return lax.ppermute(values, axis, [(0, 1), (1, 0)])


def dot(left, right):
    return jnp.dot(left, right, preferred_element_type=F32)


def dot_t(left, right):
    return lax.dot_general(left, right, (((1,), (1,)), ((), ())), preferred_element_type=F32)


def t_dot(left, right):
    return lax.dot_general(left, right, (((0,), (0,)), ((), ())), preferred_element_type=F32)


def shape(dims, kind=BF16):
    return jax.ShapeDtypeStruct(dims, kind)


def call(kernel, outs, args, flops, name, scalars=0, after=()):
    count = len(args)
    skip = len(after)
    vmem = pl.BlockSpec(memory_space=pltpu.VMEM)
    smem = pl.BlockSpec(memory_space=pltpu.SMEM)
    moved = sum(math.prod(o.shape) * o.dtype.itemsize for o in outs)
    moved += sum(math.prod(a.shape) * a.dtype.itemsize for a in args)

    def body(*refs):
        kernel(*refs[:count], *refs[count + skip :])

    return pl.pallas_call(
        body,
        out_shape=tuple(outs),
        in_specs=[smem] * scalars
        + [vmem] * (count - scalars)
        + [pl.BlockSpec(memory_space=pl.ANY)] * skip,
        out_specs=tuple([vmem] * len(outs)),
        compiler_params=pltpu.CompilerParams(
            vmem_limit_bytes=24 << 20, fuse_transposed_lhs_in_matmul=True
        ),
        cost_estimate=pl.CostEstimate(
            flops=int(flops), bytes_accessed=int(moved), transcendentals=0
        ),
        name=name,
    )(*args, *after)


def tiles(extent, size=TILE):
    return [slice(at, min(at + size, extent)) for at in range(0, extent, size)]


def row_sum(values):
    return jnp.sum(values, axis=1, keepdims=True)


def columns_to_rows(columns):
    count = columns[0].shape[0]
    lane = lax.broadcasted_iota(jnp.int32, (count, LANES), 1)
    packed = jnp.zeros((count, LANES), F32)
    for index, column in enumerate(columns):
        packed = jnp.where(lane == index, column, packed)
    return packed.T[:8]


def rows_to_columns(rows, count):
    turned = jnp.concatenate([rows] * (LANES // 8), axis=0).T
    return [turned[:, i : i + 1] for i in range(count)]


def rms_scale(total):
    return lax.rsqrt(total / D + EPSILON)


def turn(values, cosine, sine_part):
    lane = lax.broadcasted_iota(jnp.int32, cosine.shape, 1)
    first = (lane % HEAD) < HEAD // 2
    out = []
    for tile in tiles(values.shape[1], LANES):
        part = values[:, tile]
        other = jnp.where(
            first, pltpu.roll(part, LANES - HEAD // 2, 1), pltpu.roll(part, HEAD // 2, 1)
        )
        out.append(part * cosine + other * sine_part)
    return jnp.concatenate(out, axis=1)


def rope_tables(count):
    half = HEAD // 2
    frequency = jnp.exp(jnp.arange(half, dtype=F32) * (-2.0 * math.log(ROPE_BASE) / HEAD))
    angles = jnp.arange(count).astype(F32)[:, None] * frequency[None, :]
    cosine, sine_part = jnp.cos(angles), jnp.sin(angles)
    repeats = LANES // HEAD
    return (
        jnp.concatenate([cosine, cosine] * repeats, axis=1),
        jnp.concatenate([-sine_part, sine_part] * repeats, axis=1),
    )


def lower_triangle():
    rows = lax.broadcasted_iota(jnp.int32, (CHUNK, CHUNK), 0)
    cols = lax.broadcasted_iota(jnp.int32, (CHUNK, CHUNK), 1)
    return rows >= cols


def keep_rows(pairs):
    for before, out in pairs:
        out[:CHUNK] = before[:CHUNK]


def head_mask(count, index):
    lane = lax.broadcasted_iota(jnp.int32, (count, LANES), 1)
    return (lane < HEAD) if index == 0 else (lane >= HEAD)


def only(mask, values):
    return jnp.where(mask, values, jnp.zeros_like(values))


def branch_of(mine, theirs):
    branch = mine[...].astype(F32) + theirs[...].astype(F32)
    return branch, rms_scale(row_sum(branch * branch))


def norm_back(branch, scale, gain_vec, grad_out):
    weighted = grad_out * gain_vec
    inner = row_sum(weighted * branch)
    grad_branch = scale * weighted - branch * (scale * scale * scale * inner / D)
    grad_gain = jnp.sum(grad_out * branch * scale, axis=0, keepdims=True)
    return grad_branch, grad_gain


def query_key_kernel(
    flags, block, over, beside, corner, wq, wqt, wk, wkt, q_out, k_out, total_out, mine, theirs
):
    same = flags[0] == 1
    mine[...] = jnp.where(same, block[...], over[...])
    theirs[...] = jnp.where(same, beside[...], corner[...])
    query_sum = 0.0
    key_sum = 0.0
    for tile in tiles(wq.shape[1]):
        query = dot(mine[...], wq[:, tile]) + dot(theirs[...], wqt[:, tile])
        q_out[:, tile] = query
        query_sum = query_sum + row_sum(query * query)
        key = dot(mine[...], wk[:, tile]) + dot(theirs[...], wkt[:, tile])
        k_out[:, tile] = key
        key_sum = key_sum + row_sum(key * key)
    total_out[...] = columns_to_rows([query_sum, key_sum])


def value_kernel(mine, theirs, wv, wvt, v_out):
    for tile in tiles(wv.shape[1]):
        v_out[:, tile] = (dot(mine[...], wv[:, tile]) + dot(theirs[...], wvt[:, tile])).astype(BF16)


def attention_kernel(
    chunk,
    queries,
    keys,
    values,
    totals,
    totals_over,
    qgain,
    kgain,
    cosine,
    sine_part,
    wo,
    wot,
    *rest,
):
    if chunk == 0:
        q_rot, k_rot, mixed, logs, partial = rest
    else:
        q_rot, k_rot, mixed, logs, partial = rest[4:]
        keep_rows(zip(rest[:4], rest[4:]))
    rows = slice(chunk * CHUNK, (chunk + 1) * CHUNK)
    query_total, key_total = rows_to_columns(totals[...] + totals_over[...], 2)
    query = queries[rows, :] * rms_scale(query_total[rows]) * qgain[...]
    key = keys[rows, :] * rms_scale(key_total[rows]) * kgain[...]
    q_rot[rows, :] = (turn(query, cosine[rows, :], sine_part[rows, :]) * FACTOR).astype(BF16)
    k_rot[rows, :] = turn(key, cosine[rows, :], sine_part[rows, :]).astype(BF16)
    visible = lower_triangle()
    lane = lax.broadcasted_iota(jnp.int32, (CHUNK, LANES), 1)
    log_tile = jnp.zeros((CHUNK, LANES), F32)
    for at, tile in enumerate(tiles(queries.shape[1], LANES)):
        total = jnp.zeros((CHUNK, LANES), F32)
        for index in range(2):
            query_head = only(head_mask(CHUNK, index), q_rot[rows, tile])
            scores = []
            for block in range(chunk + 1):
                part = dot_t(query_head, k_rot[block * CHUNK : (block + 1) * CHUNK, tile])
                scores.append(jnp.where(visible, part, MASKED) if block == chunk else part)
            peak = jnp.max(scores[0], axis=1, keepdims=True)
            for part in scores[1:]:
                peak = jnp.maximum(peak, jnp.max(part, axis=1, keepdims=True))
            scores = [jnp.exp(part - peak) for part in scores]
            denominator = sum(row_sum(part) for part in scores)
            inverse = 1.0 / denominator
            for block, part in enumerate(scores):
                value_rows = values[block * CHUNK : (block + 1) * CHUNK, tile]
                total = total + dot(
                    (part * inverse).astype(BF16), only(head_mask(CHUNK, index), value_rows)
                )
            log_tile = jnp.where(lane == 2 * at + index, peak + jnp.log(denominator), log_tile)
        mixed[rows, tile] = total.astype(BF16)
    logs[rows, :] = log_tile
    low = mixed[rows, :]
    half = wo.shape[1]
    partial[:, :half] = dot(low, wo[...]).astype(BF16)
    partial[:, half:] = dot(low, wot[...]).astype(BF16)


def forward_kernel(
    chunk, part, part_over, mine, theirs, gain, wg, wgt, wu, wut, wd, wdt, *rest
):
    if chunk == 0:
        low_mine, low_theirs, active, hidden, gate, up, partial = rest
    else:
        low_mine, low_theirs, active, hidden, gate, up, partial = rest[3:]
        keep_rows(zip(rest[:3], rest[3:]))
    rows = slice(chunk * CHUNK, (chunk + 1) * CHUNK)
    branch, scale = branch_of(part, part_over)
    half = mine.shape[1]
    normed = branch * scale * gain[...]
    for at, side, low in ((0, mine, low_mine), (half, theirs, low_theirs)):
        value = side[rows, :].astype(F32) + normed[:, at : at + half]
        hidden[:, at : at + half] = value
        low[rows, :] = value.astype(BF16)
    for tile in tiles(wg.shape[1]):
        left, right = low_mine[rows, :], low_theirs[rows, :]
        gate_act = dot(left, wg[:, tile]) + dot(right, wgt[:, tile])
        up_act = dot(left, wu[:, tile]) + dot(right, wut[:, tile])
        gate[:, tile] = gate_act
        up[:, tile] = up_act
        active[rows, tile] = (gate_act * jax.nn.sigmoid(gate_act) * up_act).astype(BF16)
    low = active[rows, :]
    partial[:, :half] = dot(low, wd[...]).astype(BF16)
    partial[:, half:] = dot(low, wdt[...]).astype(BF16)


def ff_norm_back_kernel(
    chunk, part, part_over, hidden, cot_mine, cot_theirs, gain, *rest
):
    if chunk == 0:
        gff_mine, gff_theirs, out_mine, out_theirs, grad_gain = rest
    else:
        gain_before = rest[0]
        gff_mine, gff_theirs, out_mine, out_theirs, grad_gain = rest[3:]
        keep_rows(zip(rest[1:3], rest[3:]))
    rows = slice(chunk * CHUNK, (chunk + 1) * CHUNK)
    branch, scale = branch_of(part, part_over)
    half = cot_mine.shape[1]
    block_out = hidden[...] + branch * scale * gain[...]
    out_mine[...] = block_out[:, :half]
    out_theirs[...] = block_out[:, half:]
    upstream = jnp.concatenate([cot_mine[rows, :], cot_theirs[rows, :]], axis=1).astype(F32)
    grad_branch, gained = norm_back(branch, scale, gain[...], upstream)
    grad_gain[...] = gained if chunk == 0 else gain_before[...] + gained
    gff_mine[rows, :] = grad_branch[:, :half].astype(BF16)
    gff_theirs[rows, :] = grad_branch[:, half:].astype(BF16)


def backward_kernel(
    chunk, gff_mine, gff_theirs, gate, up, wd, wdt, wg, wgt, wu, wut, *rest
):
    if chunk == 0:
        ggate, gup, partial = rest
    else:
        ggate, gup, partial = rest[2:]
        keep_rows(zip(rest[:2], rest[2:]))
    rows = slice(chunk * CHUNK, (chunk + 1) * CHUNK)
    half = wd.shape[1]
    for tile in tiles(wg.shape[1]):
        grad_act = dot_t(gff_mine[rows, :], wd[tile, :]) + dot_t(gff_theirs[rows, :], wdt[tile, :])
        gate_act = gate[:, tile]
        sig = jax.nn.sigmoid(gate_act)
        ggate[rows, tile] = (
            grad_act * up[:, tile] * sig * (1.0 + gate_act * (1.0 - sig))
        ).astype(BF16)
        gup[rows, tile] = (grad_act * gate_act * sig).astype(BF16)
    left, right = ggate[rows, :], gup[rows, :]
    for tile in tiles(half):
        partial[:, tile] = (dot_t(left, wg[tile, :]) + dot_t(right, wu[tile, :])).astype(BF16)
        there = slice(half + tile.start, half + tile.stop)
        partial[:, there] = (dot_t(left, wgt[tile, :]) + dot_t(right, wut[tile, :])).astype(BF16)


def attention_back_kernel(
    chunk,
    grad_part,
    grad_over,
    cot_mine,
    cot_theirs,
    part,
    part_over,
    gain,
    wo,
    wot,
    q_rot,
    k_rot,
    values,
    logs,
    queries,
    keys,
    totals,
    totals_over,
    qgain,
    kgain,
    cosine,
    sine_part,
    *rest,
):
    half = wo.shape[1]
    width = queries.shape[1]
    if chunk == 0:
        gat_mine, gat_theirs, gh_mine, gh_theirs, gqn, grad_gain, column, gk_sum, gv_sum = rest
    else:
        gain_before, column_in, gk_in, gv_in = rest[:4]
        gat_mine, gat_theirs, gh_mine, gh_theirs, gqn, grad_gain, gkn, gv_low, inner_out = rest[6:]
        keep_rows(zip(rest[4:6], rest[6:]))
    rows = slice(chunk * CHUNK, (chunk + 1) * CHUNK)
    seen = (chunk + 1) * CHUNK
    branch, scale = branch_of(part, part_over)
    grad_hidden = (
        jnp.concatenate([cot_mine[rows, :], cot_theirs[rows, :]], axis=1).astype(F32)
        + grad_part[...].astype(F32)
        + grad_over[...].astype(F32)
    )
    gh_mine[...] = grad_hidden[:, :half]
    gh_theirs[...] = grad_hidden[:, half:]
    grad_branch, gained = norm_back(branch, scale, gain[...], grad_hidden)
    grad_gain[...] = gained if chunk == 0 else gain_before[...] + gained
    gat_mine[rows, :] = grad_branch[:, :half].astype(BF16)
    gat_theirs[rows, :] = grad_branch[:, half:].astype(BF16)
    grad_mixed = (
        dot_t(gat_mine[rows, :], wo[...]) + dot_t(gat_theirs[rows, :], wot[...])
    ).astype(BF16)
    visible = lower_triangle()
    query_total, key_total = rows_to_columns(totals[...] + totals_over[...], 2)
    query_inner = jnp.zeros((CHUNK, 1), F32)
    key_inner = jnp.zeros((seen, 1), F32)
    for at, tile in enumerate(tiles(width, LANES)):
        grad_query = jnp.zeros((CHUNK, LANES), F32)
        grad_key = [jnp.zeros((CHUNK, LANES), F32) for _ in range(chunk + 1)]
        grad_value = [jnp.zeros((CHUNK, LANES), F32) for _ in range(chunk + 1)]
        for index in range(2):
            mask = head_mask(CHUNK, index)
            query_head = only(mask, q_rot[rows, tile])
            grad_head = only(mask, grad_mixed[:, tile])
            log_column = logs[rows, 2 * at + index : 2 * at + index + 1]
            weights, grads = [], []
            for block in range(chunk + 1):
                span = slice(block * CHUNK, (block + 1) * CHUNK)
                scores = dot_t(query_head, k_rot[span, tile])
                if block == chunk:
                    scores = jnp.where(visible, scores, MASKED)
                weights.append(jnp.exp(scores - log_column))
                grads.append(dot_t(grad_head, values[span, tile]))
            inner = sum(row_sum(w * g) for w, g in zip(weights, grads))
            for block in range(chunk + 1):
                span = slice(block * CHUNK, (block + 1) * CHUNK)
                weight = weights[block]
                grad_scores = (weight * (grads[block] - inner)).astype(BF16)
                grad_value[block] = grad_value[block] + t_dot(weight.astype(BF16), grad_head)
                grad_query = grad_query + dot(grad_scores, only(mask, k_rot[span, tile]))
                grad_key[block] = grad_key[block] + t_dot(grad_scores, query_head)
        back = turn(grad_query * FACTOR, cosine[rows, :], -sine_part[rows, :])
        gqn[:, tile] = back
        query_inner = query_inner + row_sum(back * qgain[:, tile] * queries[rows, tile])
        if chunk == 0:
            gk_sum[:, tile] = grad_key[0]
            gv_sum[:, tile] = grad_value[0]
        else:
            key_all = jnp.concatenate([gk_in[:, tile] + grad_key[0], grad_key[1]], axis=0)
            value_all = jnp.concatenate([gv_in[:, tile] + grad_value[0], grad_value[1]], axis=0)
            gv_low[:, tile] = value_all.astype(BF16)
            back = turn(key_all, cosine[...], -sine_part[...])
            gkn[:, tile] = back
            key_inner = key_inner + row_sum(back * kgain[:, tile] * keys[:, tile])
    if chunk == 0:
        column[...] = jnp.broadcast_to(query_inner, (CHUNK, LANES))
    else:
        query_inner = jnp.concatenate([column_in[:, :1], query_inner], axis=0)
        inner_out[...] = columns_to_rows([query_inner, key_inner])


def query_key_back_kernel(
    gqn_first, gqn_second, gkn, queries, keys, totals, totals_over, inner, inner_over, qgain, kgain,
    gq, gk, qg, kg,
):
    query_total, key_total = rows_to_columns(totals[...] + totals_over[...], 2)
    query_inner, key_inner = rows_to_columns(inner[...] + inner_over[...], 2)
    gqn = jnp.concatenate([gqn_first[...], gqn_second[...]], axis=0)
    for raw, back, total, sums, gain, low, gained in (
        (queries, gqn, query_total, query_inner, qgain, gq, qg),
        (keys, gkn[...], key_total, key_inner, kgain, gk, kg),
    ):
        scale = rms_scale(total)
        value = raw[...]
        low[...] = (
            scale * (back * gain[...]) - value * (scale * scale * scale * sums / D)
        ).astype(BF16)
        gained[...] = jnp.sum(back * value * scale, axis=0, keepdims=True)


def weight_kernel(blocks, me, left, left_far, *rest):
    count = (len(rest) - 2) // 2
    rights, rights_far, (keep, give) = rest[:count], rest[count : 2 * count], rest[2 * count :]
    high = left.shape[1]
    size = high // blocks
    for tile in tiles(high):
        at = 0
        for right, right_far in zip(rights, rights_far):
            columns = slice(at, at + right.shape[1])
            value = (
                t_dot(left[:, tile], right[...]) + t_dot(left_far[:, tile], right_far[...])
            ).astype(BF16)
            first = tile.start
            while first < tile.stop:
                block = first // size
                last = min(tile.stop, (block + 1) * size)
                place = block ^ me[0]
                piece = value[first - tile.start : last - tile.start]
                for out, least in ((keep, 0), (give, blocks // 2)):

                    @pl.when((place >= least) & (place < least + blocks // 2))
                    def _():
                        to = (place - least) * size + (first - block * size)
                        to = pl.multiple_of(to, math.gcd(size, TILE))
                        out[pl.ds(to, last - first), columns] = piece

                first = last
            at += right.shape[1]


def halve_kernel(mine, received, keep, give):
    half = keep.shape[0]
    for out, span in ((give, slice(half, 2 * half)), (keep, slice(0, half))):
        out[...] = (mine[span, :].astype(F32) + received[span, :].astype(F32)).astype(BF16)


def add_kernel(mine, received, out):
    out[...] = (mine[...].astype(F32) + received[...].astype(F32)).astype(BF16)


def join_kernel(mine, received, out):
    half = mine.shape[0]
    out[:half] = mine[...]
    out[half:] = received[...]


def finish_kernel(blocks, me, low, high, *outs):
    half = blocks // 2
    size = low.shape[0] // half
    for place in range(blocks):
        source = low if place < half else high
        at = (place % half) * size
        to = pl.multiple_of((place ^ me[0]) * size, size)
        column = 0
        for out in outs:
            width = out.shape[1]
            out[pl.ds(to, size), :] = source[at : at + size, column : column + width].astype(F32)
            column += width


def input_back_kernel(
    gq, gk, gv, wq, wqt, wk, wkt, wv, wvt, *rest
):
    gh_mine, gh_theirs = rest[:2], rest[2:4]
    stays, moves, across, corner = rest[4:]
    for tile in tiles(wq.shape[0]):
        mine = (
            dot_t(gq[...], wq[tile, :]) + dot_t(gk[...], wk[tile, :]) + dot_t(gv[...], wv[tile, :])
        )
        theirs = (
            dot_t(gq[...], wqt[tile, :])
            + dot_t(gk[...], wkt[tile, :])
            + dot_t(gv[...], wvt[tile, :])
        )
        for chunk in range(2):
            rows = slice(chunk * CHUNK, (chunk + 1) * CHUNK)
            stays[rows, tile] = gh_mine[chunk][:, tile] + mine[rows]
            moves[rows, tile] = gh_theirs[chunk][:, tile] + theirs[rows]
        across[:, tile] = mine.astype(BF16)
        corner[:, tile] = theirs.astype(BF16)


def dp_exchange(values, bit):
    size = lax.axis_size("dp")
    return lax.ppermute(values, "dp", [(i, i ^ (1 << bit)) for i in range(size)])


def dp_bits():
    return lax.axis_size("dp").bit_length() - 1


class Chain:
    def __init__(self, name, order, widths, keep, give):
        self.name, self.order, self.widths = name, order, widths
        self.keep, self.give = keep, give
        self.received = dp_exchange(give, order[0])
        self.stage = 0

    def step(self, me, after):
        bits = len(self.order)
        stage = self.stage
        self.stage += 1
        name = f"{self.name}_{stage}"
        high, wide = self.keep.shape
        moved = high * wide
        if stage < bits - 1:
            self.keep, self.give = call(
                halve_kernel,
                [shape((high // 2, wide))] * 2,
                [self.keep, self.received],
                moved,
                name,
                after=after,
            )
            self.received = dp_exchange(self.give, self.order[stage + 1])
            return self.give
        if stage == bits - 1:
            (self.keep,) = call(
                add_kernel,
                [shape((high, wide))],
                [self.keep, self.received],
                moved,
                name,
                after=after,
            )
            for bit in range(bits, dp_bits()):
                total = self.keep.astype(F32) + dp_exchange(self.keep, bit).astype(F32)
                self.keep = total.astype(BF16)
        elif stage < 2 * bits - 1:
            (self.keep,) = call(
                join_kernel,
                [shape((2 * high, wide))],
                [self.keep, self.received],
                moved,
                name,
                after=after,
            )
        else:
            self.out = call(
                functools.partial(finish_kernel, 1 << bits),
                [shape((2 * high, w), F32) for w in self.widths],
                [me, self.keep, self.received],
                moved,
                name,
                scalars=1,
                after=after,
            )
            return self.out[0]
        self.received = dp_exchange(self.keep, self.order[2 * bits - 2 - stage])
        return self.keep


def dp_total_small(values):
    for bit in range(dp_bits()):
        values = values + dp_exchange(values, bit)
    return values


def on_device(
    block_in,
    w_query,
    w_key,
    w_value,
    w_output,
    w_gate,
    w_up,
    w_down,
    qnorm_gain,
    knorm_gain,
    attn_gain,
    mlp_gain,
    cotangent,
):
    rows, half = block_in.shape
    width = w_query.shape[1]
    ff = w_gate.shape[1]
    pair = ("row", "col")
    row_position = lax.axis_index("row")
    col_position = lax.axis_index("col")
    same = row_position == col_position
    flags = jnp.where(same, 1, 0).astype(jnp.int32).reshape(1)
    scatter_bits = min(3, dp_bits())
    blocks = 1 << scatter_bits
    forth = list(range(scatter_bits))

    def block_of(order):
        index = jnp.int32(0)
        for bit in order:
            index = 2 * index + ((lax.axis_index("dp") >> bit) & 1).astype(jnp.int32)
        return index.reshape(1)

    late = forth[1:] + forth[:1]

    to_over = [(0, 1), (3, 2)]
    to_corner = [(1, 2), (2, 1)]
    to_beside = [(2, 0), (1, 3)]
    from_same = [(0, 2), (3, 1)]

    in_over = lax.ppermute(block_in, pair, to_over)
    in_corner = lax.ppermute(block_in, pair, to_corner)
    in_beside = lax.ppermute(block_in, pair, to_beside)
    wq_far, wk_far, wv_far = swap(w_query, "row"), swap(w_key, "row"), swap(w_value, "row")
    wo_far = swap(w_output, "row")
    gains = jnp.stack([attn_gain, mlp_gain])
    gains = jnp.concatenate([gains, swap(gains, "row")], axis=1)
    attn_gain_full, mlp_gain_full = gains[0:1], gains[1:2]
    qgain, kgain = qnorm_gain[None], knorm_gain[None]
    cosine, sine_part = rope_tables(rows)

    queries, keys, totals, in_mine, in_theirs = call(
        query_key_kernel,
        [shape((rows, width), F32)] * 2 + [shape((8, rows), F32)] + [shape((rows, half))] * 2,
        [flags, block_in, in_over, in_beside, in_corner, w_query, wq_far, w_key, wk_far],
        4 * rows * D * width,
        "query_key",
        scalars=1,
    )
    totals_over = swap(totals, "col")
    (values,) = call(
        value_kernel,
        [shape((rows, width))],
        [in_mine, in_theirs, w_value, wv_far],
        2 * rows * D * width,
        "value",
    )

    wg_far, wu_far, wd_far = swap(w_gate, "row"), swap(w_up, "row"), swap(w_down, "row")
    cot_over = lax.ppermute(cotangent, pair, to_over)
    cot_corner = lax.ppermute(cotangent, pair, to_corner)
    cot_beside = lax.ppermute(cotangent, pair, to_beside)
    cot_mine = jnp.where(same, cotangent, cot_over)
    cot_theirs = jnp.where(same, cot_beside, cot_corner)

    attention_args = [
        queries,
        keys,
        values,
        totals,
        totals_over,
        qgain,
        kgain,
        cosine,
        sine_part,
        w_output,
        wo_far,
    ]
    attention_outs = [shape((rows, width))] * 3 + [
        shape((rows, LANES), F32),
        shape((CHUNK, D)),
    ]
    parts, parts_over = [], []
    kept = []
    for chunk in range(2):
        *kept, partial = call(
            functools.partial(attention_kernel, chunk),
            attention_outs,
            attention_args + kept,
            (1 + chunk) * 2e9 * 0.25 + 4 * CHUNK * width * half,
            f"attention_{chunk}",
        )
        parts.append(partial)
        parts_over.append(swap(partial, "col"))
    q_rot, k_rot, mixed, logs = kept
    mixed_far = swap(mixed, "row")

    ff_weights = [w_gate, wg_far, w_up, wu_far, w_down, wd_far]
    ff_parts, ff_over, hidden, gate, up = [], [], [], [], []
    kept = []
    for chunk in range(2):
        args = [parts[chunk], parts_over[chunk], in_mine, in_theirs, attn_gain_full] + ff_weights
        low_mine, low_theirs, active, hid, gate_act, up_act, partial = call(
            functools.partial(forward_kernel, chunk),
            [shape((rows, half))] * 2
            + [shape((rows, ff)), shape((CHUNK, D), F32)]
            + [shape((CHUNK, ff), F32)] * 2
            + [shape((CHUNK, D))],
            args + kept,
            6 * CHUNK * D * ff,
            f"forward_{chunk}",
        )
        kept = [low_mine, low_theirs, active]
        hidden.append(hid)
        gate.append(gate_act)
        up.append(up_act)
        ff_parts.append(partial)
        ff_over.append(swap(partial, "col"))
    low_far = swap(low_theirs, "row")
    active_far = swap(active, "row")

    def weight_grad(name, order, left, left_far, rights, rights_far, after):
        high = left.shape[1]
        widths = [r.shape[1] for r in rights]
        keep, give = call(
            functools.partial(weight_kernel, blocks),
            [shape((high // 2, sum(widths)))] * 2,
            [block_of(order), left, left_far, *rights, *rights_far],
            4 * rows * high * sum(widths),
            name,
            scalars=1,
            after=after,
        )
        return Chain(name, order, widths, keep, give)

    back_weights = [w_down, wd_far, w_gate, wg_far, w_up, wu_far]
    grad_parts, grad_over = [], []
    kept, kept_back = [], []
    out_mine, out_theirs = [], []
    mlp_part = None
    chains = {}
    for chunk in range(2):
        args = [
            ff_parts[chunk],
            ff_over[chunk],
            hidden[chunk],
            cot_mine,
            cot_theirs,
            mlp_gain_full,
        ]
        if chunk:
            args.append(mlp_part)
        gff_mine, gff_theirs, *outs, mlp_part = call(
            functools.partial(ff_norm_back_kernel, chunk),
            [shape((rows, half))] * 2 + [shape((CHUNK, half), F32)] * 2 + [shape((1, D), F32)],
            args + kept,
            40 * CHUNK * D,
            f"ff_norm_back_{chunk}",
        )
        kept = [gff_mine, gff_theirs]
        out_mine.append(outs[0])
        out_theirs.append(outs[1])
        after = ()
        if chunk:
            gff_far = swap(gff_theirs, "row")
            chains["down"] = weight_grad(
                "down", forth, active, active_far, [gff_mine], [gff_far], ()
            )
            after = (chains["down"].give,)
        args = [gff_mine, gff_theirs, gate[chunk], up[chunk]] + back_weights
        *kept_back, partial = call(
            functools.partial(backward_kernel, chunk),
            [shape((rows, ff))] * 2 + [shape((CHUNK, D))],
            args + kept_back,
            6 * CHUNK * D * ff,
            f"backward_{chunk}",
            after=after,
        )
        grad_parts.append(partial)
        grad_over.append(swap(partial, "col"))
    ggate, gup = kept_back

    ggate_far, gup_far = swap(ggate, "row"), swap(gup, "row")
    chains["gate"] = weight_grad("gate", forth, low_mine, low_far, [ggate], [ggate_far], (partial,))
    chains["up"] = weight_grad(
        "up", forth, low_mine, low_far, [gup], [gup_far], (chains["gate"].give,)
    )
    latest = chains["up"].give

    def step(*names):
        nonlocal latest
        for name in names:
            if chains[name].stage == 2 * scatter_bits:
                continue
            latest = chains[name].step(block_of(chains[name].order), (latest,))

    for chunk in range(2):
        args = [
            grad_parts[chunk],
            grad_over[chunk],
            cot_mine,
            cot_theirs,
            parts[chunk],
            parts_over[chunk],
            attn_gain_full,
            w_output,
            wo_far,
            q_rot,
            k_rot,
            values,
            logs,
            queries,
            keys,
            totals,
            totals_over,
            qgain,
            kgain,
            cosine,
            sine_part,
        ]
        outs = [shape((rows, half))] * 2 + [shape((CHUNK, half), F32)] * 3 + [shape((1, D), F32)]
        if chunk == 0:
            outs += [
                shape((CHUNK, LANES), F32),
                shape((CHUNK, width), F32),
                shape((CHUNK, width), F32),
            ]
            gat_mine, gat_theirs, gm, gt, gqn, attn_part, column, gk_sum, gv_sum = call(
                functools.partial(attention_back_kernel, chunk),
                outs,
                args,
                2e9,
                "attention_back_0",
                after=(latest,),
            )
            latest = column
            gh_mine, gh_theirs = [gm], [gt]
            step("down")
        else:
            outs += [
                shape((rows, width), F32),
                shape((rows, width)),
                shape((8, rows), F32),
            ]
            args += [attn_part, column, gk_sum, gv_sum, gat_mine, gat_theirs]
            gat_mine, gat_theirs, gm, gt, gqn_second, attn_part, gkn, gv, inner = call(
                functools.partial(attention_back_kernel, chunk),
                outs,
                args,
                3e9,
                "attention_back_1",
                after=(latest,),
            )
            latest = inner
            gh_mine.append(gm)
            gh_theirs.append(gt)
    inner_over = swap(inner, "col")
    gat_far = swap(gat_theirs, "row")
    chains["out"] = weight_grad(
        "out", late, mixed, mixed_far, [gat_mine], [gat_far], (latest,)
    )
    latest = chains["out"].give
    step("down")
    gq, gk, qgain_part, kgain_part = call(
        query_key_back_kernel,
        [shape((rows, width))] * 2 + [shape((1, width), F32)] * 2,
        [gqn, gqn_second, gkn, queries, keys, totals, totals_over, inner, inner_over, qgain, kgain],
        40 * rows * width,
        "query_key_back",
        after=(latest,),
    )
    gq_far, gk_far, gv_far = swap(gq, "row"), swap(gk, "row"), swap(gv, "row")
    in_fix = lax.ppermute(in_theirs, pair, to_beside)
    in_far = jnp.where(same, in_fix, block_in)
    chains["qkv"] = weight_grad(
        "qkv", forth, in_mine, in_far, [gq, gk, gv], [gq_far, gk_far, gv_far], (gq,)
    )
    latest = chains["qkv"].give
    step("out", "gate")

    stays, moves, across, corner = call(
        input_back_kernel,
        [shape((rows, half), F32)] * 2 + [shape((rows, half))] * 2,
        [gq, gk, gv, w_query, wq_far, w_key, wk_far, w_value, wv_far, *gh_mine, *gh_theirs],
        12 * rows * width * half,
        "input_back",
        after=(latest,),
    )
    latest = across
    across = lax.ppermute(across, pair, [(1, 0), (2, 3)])
    corner = lax.ppermute(corner, pair, to_corner)
    moves = lax.ppermute(moves, pair, from_same)
    grad_input = jnp.where(same, stays, moves) + jnp.where(same, across, corner).astype(F32)
    out_beside = lax.ppermute(jnp.concatenate(out_theirs, axis=0), pair, from_same)
    block_out = jnp.where(same, jnp.concatenate(out_mine, axis=0), out_beside)

    gain_mine = jnp.concatenate(
        [mlp_part[0, :half], attn_part[0, :half], qgain_part[0], kgain_part[0]]
    )
    gain_give = jnp.concatenate(
        [mlp_part[0, half:], attn_part[0, half:], qgain_part[0], kgain_part[0]]
    )
    gain_total = dp_total_small(gain_mine + swap(gain_give, "row"))
    grad_mlpgain, grad_attngain, grad_qgain, grad_kgain = jnp.split(
        gain_total, [half, 2 * half, 2 * half + width]
    )

    step("down", "out", "gate", "out", "down", "up", "out", "gate", "down", "out", "up")
    step("gate", "out", "qkv", "up", "gate", "qkv", "up", "down", "qkv", "up", "qkv")
    step("gate", "qkv", "up", "qkv")
    for chain in chains.values():
        while chain.stage < 2 * scatter_bits:
            step(chain.name)
    (grad_down,) = chains["down"].out
    (grad_gate,) = chains["gate"].out
    (grad_up,) = chains["up"].out
    (grad_out,) = chains["out"].out
    grad_query, grad_key, grad_value = chains["qkv"].out
    return (
        block_out,
        grad_input,
        grad_query,
        grad_key,
        grad_value,
        grad_out,
        grad_gate,
        grad_up,
        grad_down,
        grad_qgain,
        grad_kgain,
        grad_attngain,
        grad_mlpgain,
    )


def solution(mesh):
    tokens = P(("dp", "col"), "row")
    grid, turned = P("row", "col"), P("col", "row")
    in_specs = (
        tokens,
        grid,
        grid,
        grid,
        turned,
        grid,
        grid,
        turned,
        P("col"),
        P("col"),
        P("row"),
        P("row"),
        tokens,
    )
    out_specs = (
        tokens,
        tokens,
        grid,
        grid,
        grid,
        turned,
        grid,
        grid,
        turned,
        P("col"),
        P("col"),
        P("row"),
        P("row"),
    )
    return jax.shard_map(
        on_device, mesh=mesh, in_specs=in_specs, out_specs=out_specs, check_vma=False
    )
```

```python
import functools
import math

import jax
import jax.numpy as jnp
import numpy as np
from jax import lax
from jax.experimental import pallas as pl
from jax.experimental.pallas import tpu as pltpu
from jax.sharding import PartitionSpec as P

D = 1024
HEAD = 64
SEQ = 512
EPSILON = 1e-06
ROPE_BASE = 500000.0
MASKED = -1e30
CHUNK = 256
TILE = 256
LANES = 128
FACTOR = 1.0 / math.sqrt(HEAD)

F32 = jnp.float32
BF16 = jnp.bfloat16


def swap(values, axis):
    return lax.ppermute(values, axis, [(0, 1), (1, 0)])


def dot(left, right):
    return jnp.dot(left, right, preferred_element_type=F32)


def dot_t(left, right):
    return lax.dot_general(left, right, (((1,), (1,)), ((), ())), preferred_element_type=F32)


def t_dot(left, right):
    return lax.dot_general(left, right, (((0,), (0,)), ((), ())), preferred_element_type=F32)


def shape(dims, kind=BF16):
    return jax.ShapeDtypeStruct(dims, kind)


def call(kernel, outs, args, flops, name, scratch=(), after=()):
    count = len(args)
    skip = len(after)
    vmem = pl.BlockSpec(memory_space=pltpu.VMEM)
    moved = sum(math.prod(o.shape) * o.dtype.itemsize for o in outs)
    moved += sum(math.prod(a.shape) * a.dtype.itemsize for a in args)

    def body(*refs):
        kernel(*refs[:count], *refs[count + skip :])

    return pl.pallas_call(
        body,
        out_shape=tuple(outs),
        in_specs=[vmem] * count + [pl.BlockSpec(memory_space=pl.ANY)] * skip,
        out_specs=tuple([vmem] * len(outs)),
        scratch_shapes=scratch,
        compiler_params=pltpu.CompilerParams(
            vmem_limit_bytes=12 << 20, fuse_transposed_lhs_in_matmul=True
        ),
        cost_estimate=pl.CostEstimate(
            flops=int(flops), bytes_accessed=int(moved), transcendentals=0
        ),
        name=name,
    )(*args, *after)


def tiles(extent, size=TILE):
    return [slice(at, min(at + size, extent)) for at in range(0, extent, size)]


def row_sum(values):
    return jnp.sum(values, axis=1, keepdims=True)


def columns_to_rows(columns):
    count = columns[0].shape[0]
    lane = lax.broadcasted_iota(jnp.int32, (count, LANES), 1)
    packed = jnp.zeros((count, LANES), F32)
    for index, column in enumerate(columns):
        packed = jnp.where(lane == index, column, packed)
    return packed.T[:8]


def rows_to_columns(rows, count):
    turned = jnp.concatenate([rows] * (LANES // 8), axis=0).T
    return [turned[:, i : i + 1] for i in range(count)]


def rms_scale(total):
    return lax.rsqrt(total / D + EPSILON)


def turn(values, cosine, sine_part):
    lane = lax.broadcasted_iota(jnp.int32, cosine.shape, 1)
    first = (lane % HEAD) < HEAD // 2
    out = []
    for tile in tiles(values.shape[1], LANES):
        part = values[:, tile]
        other = jnp.where(
            first, pltpu.roll(part, LANES - HEAD // 2, 1), pltpu.roll(part, HEAD // 2, 1)
        )
        out.append(part * cosine + other * sine_part)
    return jnp.concatenate(out, axis=1)


def rope_tables(count):
    half = HEAD // 2
    frequency = np.exp(np.arange(half, dtype=np.float32) * np.float32(-2.0 * math.log(ROPE_BASE) / HEAD))
    angles = np.arange(count).astype(np.float32)[:, None] * frequency[None, :]
    cosine, sine_part = np.cos(angles), np.sin(angles)
    repeats = LANES // HEAD
    return (
        jnp.asarray(np.concatenate([cosine, cosine] * repeats, axis=1)),
        jnp.asarray(np.concatenate([-sine_part, sine_part] * repeats, axis=1)),
    )


def lower_triangle():
    rows = lax.broadcasted_iota(jnp.int32, (CHUNK, CHUNK), 0)
    cols = lax.broadcasted_iota(jnp.int32, (CHUNK, CHUNK), 1)
    return rows >= cols


def keep_rows(pairs):
    for before, out in pairs:
        out[:CHUNK] = before[:CHUNK]


def head_mask(count, index):
    lane = lax.broadcasted_iota(jnp.int32, (count, LANES), 1)
    return (lane < HEAD) if index == 0 else (lane >= HEAD)


def only(mask, values):
    return jnp.where(mask, values, jnp.zeros_like(values))


def branch_of(mine, theirs):
    branch = mine[...].astype(F32) + theirs[...].astype(F32)
    return branch, rms_scale(row_sum(branch * branch))


def gain_of(mine, theirs, index):
    row = slice(index, index + 1)
    return jnp.concatenate([mine[row, :], theirs[row, :]], axis=1)


def on_own_chip():
    return lax.axis_index("row") == lax.axis_index("col")


def block_of(order):
    index = 0
    for bit in order:
        index = 2 * index + ((lax.axis_index("dp") >> bit) & 1)
    return index


def norm_back(branch, scale, gain_vec, grad_out):
    weighted = grad_out * gain_vec
    inner = row_sum(weighted * branch)
    grad_branch = scale * weighted - branch * (scale * scale * scale * inner / D)
    grad_gain = jnp.sum(grad_out * branch * scale, axis=0, keepdims=True)
    return grad_branch, grad_gain


def pack_kernel(*refs):
    out = refs[-1]
    out[...] = jnp.zeros(out.shape, F32)
    for index, row in enumerate(refs[:-1]):
        out[index : index + 1, :] = row[...]


def choose_kernel(first, other, out):
    out[...] = jnp.where(on_own_chip(), first[...], other[...])


def choose_two_kernel(first, other, beside, corner, out, out_theirs):
    choose_kernel(first, other, out)
    choose_kernel(beside, corner, out_theirs)


def query_key_kernel(
    block, over, beside, corner, wq, wqt, wk, wkt, q_out, k_out, total_out, mine, theirs
):
    choose_two_kernel(block, over, beside, corner, mine, theirs)
    query_sum = 0.0
    key_sum = 0.0
    for tile in tiles(wq.shape[1]):
        query = dot(mine[...], wq[:, tile]) + dot(theirs[...], wqt[:, tile])
        q_out[:, tile] = query
        query_sum = query_sum + row_sum(query * query)
        key = dot(mine[...], wk[:, tile]) + dot(theirs[...], wkt[:, tile])
        k_out[:, tile] = key
        key_sum = key_sum + row_sum(key * key)
    total_out[...] = columns_to_rows([query_sum, key_sum])


def value_kernel(mine, theirs, wv, wvt, v_out):
    for tile in tiles(wv.shape[1]):
        v_out[:, tile] = (dot(mine[...], wv[:, tile]) + dot(theirs[...], wvt[:, tile])).astype(BF16)


def attention_kernel(
    chunk,
    queries,
    keys,
    values,
    totals,
    totals_over,
    qgain,
    kgain,
    cosine,
    sine_part,
    wo,
    wot,
    *rest,
):
    if chunk == 0:
        q_rot, k_rot, mixed, logs, partial = rest
    else:
        q_rot, k_rot, mixed, logs, partial = rest[4:]
        keep_rows(zip(rest[:4], rest[4:]))
    rows = slice(chunk * CHUNK, (chunk + 1) * CHUNK)
    query_total, key_total = rows_to_columns(totals[...] + totals_over[...], 2)
    query = queries[rows, :] * rms_scale(query_total[rows]) * qgain[...]
    key = keys[rows, :] * rms_scale(key_total[rows]) * kgain[...]
    q_rot[rows, :] = (turn(query, cosine[rows, :], sine_part[rows, :]) * FACTOR).astype(BF16)
    k_rot[rows, :] = turn(key, cosine[rows, :], sine_part[rows, :]).astype(BF16)
    visible = lower_triangle()
    lane = lax.broadcasted_iota(jnp.int32, (CHUNK, LANES), 1)
    log_tile = jnp.zeros((CHUNK, LANES), F32)
    for at, tile in enumerate(tiles(queries.shape[1], LANES)):
        total = jnp.zeros((CHUNK, LANES), F32)
        for index in range(2):
            query_head = only(head_mask(CHUNK, index), q_rot[rows, tile])
            scores = []
            for block in range(chunk + 1):
                part = dot_t(query_head, k_rot[block * CHUNK : (block + 1) * CHUNK, tile])
                scores.append(jnp.where(visible, part, MASKED) if block == chunk else part)
            peak = jnp.max(scores[0], axis=1, keepdims=True)
            for part in scores[1:]:
                peak = jnp.maximum(peak, jnp.max(part, axis=1, keepdims=True))
            scores = [jnp.exp(part - peak) for part in scores]
            denominator = sum(row_sum(part) for part in scores)
            inverse = 1.0 / denominator
            for block, part in enumerate(scores):
                value_rows = values[block * CHUNK : (block + 1) * CHUNK, tile]
                total = total + dot(
                    (part * inverse).astype(BF16), only(head_mask(CHUNK, index), value_rows)
                )
            log_tile = jnp.where(lane == 2 * at + index, peak + jnp.log(denominator), log_tile)
        mixed[rows, tile] = total.astype(BF16)
    logs[rows, :] = log_tile
    low = mixed[rows, :]
    half = wo.shape[1]
    partial[:, :half] = dot(low, wo[...]).astype(BF16)
    partial[:, half:] = dot(low, wot[...]).astype(BF16)


def forward_kernel(
    chunk, part, part_over, mine, theirs, gains, gains_far, wg, wgt, wu, wut, wd, wdt, *rest
):
    if chunk == 0:
        low_mine, low_theirs, active, hidden, gate, up, partial = rest
    else:
        low_mine, low_theirs, active, hidden, gate, up, partial = rest[3:]
        keep_rows(zip(rest[:3], rest[3:]))
    rows = slice(chunk * CHUNK, (chunk + 1) * CHUNK)
    branch, scale = branch_of(part, part_over)
    half = mine.shape[1]
    normed = branch * scale * gain_of(gains, gains_far, 0)
    for at, side, low in ((0, mine, low_mine), (half, theirs, low_theirs)):
        value = side[rows, :].astype(F32) + normed[:, at : at + half]
        hidden[:, at : at + half] = value
        low[rows, :] = value.astype(BF16)
    for tile in tiles(wg.shape[1]):
        left, right = low_mine[rows, :], low_theirs[rows, :]
        gate_act = dot(left, wg[:, tile]) + dot(right, wgt[:, tile])
        up_act = dot(left, wu[:, tile]) + dot(right, wut[:, tile])
        gate[:, tile] = gate_act
        up[:, tile] = up_act
        active[rows, tile] = (gate_act * jax.nn.sigmoid(gate_act) * up_act).astype(BF16)
    low = active[rows, :]
    partial[:, :half] = dot(low, wd[...]).astype(BF16)
    partial[:, half:] = dot(low, wdt[...]).astype(BF16)


def ff_norm_back_kernel(
    chunk, part, part_over, hidden, cot_mine, cot_theirs, gains, gains_far, *rest
):
    if chunk == 0:
        gff_mine, gff_theirs, out_mine, out_theirs, grad_gain = rest
    else:
        gain_before = rest[0]
        gff_mine, gff_theirs, out_mine, out_theirs, grad_gain = rest[3:]
        keep_rows(zip(rest[1:3], rest[3:]))
    rows = slice(chunk * CHUNK, (chunk + 1) * CHUNK)
    branch, scale = branch_of(part, part_over)
    half = cot_mine.shape[1]
    gain = gain_of(gains, gains_far, 1)
    block_out = hidden[...] + branch * scale * gain
    out_mine[...] = block_out[:, :half]
    out_theirs[...] = block_out[:, half:]
    upstream = jnp.concatenate([cot_mine[rows, :], cot_theirs[rows, :]], axis=1).astype(F32)
    grad_branch, gained = norm_back(branch, scale, gain, upstream)
    grad_gain[...] = gained if chunk == 0 else gain_before[...] + gained
    gff_mine[rows, :] = grad_branch[:, :half].astype(BF16)
    gff_theirs[rows, :] = grad_branch[:, half:].astype(BF16)


def backward_kernel(
    chunk, gff_mine, gff_theirs, gate, up, wd, wdt, wg, wgt, wu, wut, *rest
):
    if chunk == 0:
        ggate, gup, partial = rest
    else:
        ggate, gup, partial = rest[2:]
        keep_rows(zip(rest[:2], rest[2:]))
    rows = slice(chunk * CHUNK, (chunk + 1) * CHUNK)
    half = wd.shape[1]
    for tile in tiles(wg.shape[1]):
        grad_act = dot_t(gff_mine[rows, :], wd[tile, :]) + dot_t(gff_theirs[rows, :], wdt[tile, :])
        gate_act = gate[:, tile]
        sig = jax.nn.sigmoid(gate_act)
        ggate[rows, tile] = (
            grad_act * up[:, tile] * sig * (1.0 + gate_act * (1.0 - sig))
        ).astype(BF16)
        gup[rows, tile] = (grad_act * gate_act * sig).astype(BF16)
    left, right = ggate[rows, :], gup[rows, :]
    for tile in tiles(half):
        partial[:, tile] = (dot_t(left, wg[tile, :]) + dot_t(right, wu[tile, :])).astype(BF16)
        there = slice(half + tile.start, half + tile.stop)
        partial[:, there] = (dot_t(left, wgt[tile, :]) + dot_t(right, wut[tile, :])).astype(BF16)


def attention_back_kernel(
    chunk,
    grad_part,
    grad_over,
    cot_mine,
    cot_theirs,
    part,
    part_over,
    gains,
    gains_far,
    wo,
    wot,
    q_rot,
    k_rot,
    values,
    logs,
    queries,
    keys,
    totals,
    totals_over,
    qgain,
    kgain,
    cosine,
    sine_part,
    *rest,
):
    half = wo.shape[1]
    width = queries.shape[1]
    if chunk == 0:
        gat_mine, gat_theirs, gh_mine, gh_theirs, gqn, grad_gain, column, gk_sum, gv_sum = rest
    else:
        gain_before, column_in, gk_in, gv_in = rest[:4]
        gat_mine, gat_theirs, gh_mine, gh_theirs, gqn, grad_gain, gkn, gv_low, inner_out = rest[6:]
        keep_rows(zip(rest[4:6], rest[6:]))
    rows = slice(chunk * CHUNK, (chunk + 1) * CHUNK)
    seen = (chunk + 1) * CHUNK
    branch, scale = branch_of(part, part_over)
    grad_hidden = (
        jnp.concatenate([cot_mine[rows, :], cot_theirs[rows, :]], axis=1).astype(F32)
        + grad_part[...].astype(F32)
        + grad_over[...].astype(F32)
    )
    gh_mine[...] = grad_hidden[:, :half]
    gh_theirs[...] = grad_hidden[:, half:]
    grad_branch, gained = norm_back(branch, scale, gain_of(gains, gains_far, 0), grad_hidden)
    grad_gain[...] = gained if chunk == 0 else gain_before[...] + gained
    gat_mine[rows, :] = grad_branch[:, :half].astype(BF16)
    gat_theirs[rows, :] = grad_branch[:, half:].astype(BF16)
    grad_mixed = (
        dot_t(gat_mine[rows, :], wo[...]) + dot_t(gat_theirs[rows, :], wot[...])
    ).astype(BF16)
    visible = lower_triangle()
    query_total, key_total = rows_to_columns(totals[...] + totals_over[...], 2)
    query_inner = jnp.zeros((CHUNK, 1), F32)
    key_inner = jnp.zeros((seen, 1), F32)
    for at, tile in enumerate(tiles(width, LANES)):
        grad_query = jnp.zeros((CHUNK, LANES), F32)
        grad_key = [jnp.zeros((CHUNK, LANES), F32) for _ in range(chunk + 1)]
        grad_value = [jnp.zeros((CHUNK, LANES), F32) for _ in range(chunk + 1)]
        for index in range(2):
            mask = head_mask(CHUNK, index)
            query_head = only(mask, q_rot[rows, tile])
            grad_head = only(mask, grad_mixed[:, tile])
            log_column = logs[rows, 2 * at + index : 2 * at + index + 1]
            weights, grads = [], []
            for block in range(chunk + 1):
                span = slice(block * CHUNK, (block + 1) * CHUNK)
                scores = dot_t(query_head, k_rot[span, tile])
                if block == chunk:
                    scores = jnp.where(visible, scores, MASKED)
                weights.append(jnp.exp(scores - log_column))
                grads.append(dot_t(grad_head, values[span, tile]))
            inner = sum(row_sum(w * g) for w, g in zip(weights, grads))
            for block in range(chunk + 1):
                span = slice(block * CHUNK, (block + 1) * CHUNK)
                weight = weights[block]
                grad_scores = (weight * (grads[block] - inner)).astype(BF16)
                grad_value[block] = grad_value[block] + t_dot(weight.astype(BF16), grad_head)
                grad_query = grad_query + dot(grad_scores, only(mask, k_rot[span, tile]))
                grad_key[block] = grad_key[block] + t_dot(grad_scores, query_head)
        back = turn(grad_query * FACTOR, cosine[rows, :], -sine_part[rows, :])
        gqn[:, tile] = back
        query_inner = query_inner + row_sum(back * qgain[:, tile] * queries[rows, tile])
        if chunk == 0:
            gk_sum[:, tile] = grad_key[0]
            gv_sum[:, tile] = grad_value[0]
        else:
            key_all = jnp.concatenate([gk_in[:, tile] + grad_key[0], grad_key[1]], axis=0)
            value_all = jnp.concatenate([gv_in[:, tile] + grad_value[0], grad_value[1]], axis=0)
            gv_low[:, tile] = value_all.astype(BF16)
            back = turn(key_all, cosine[...], -sine_part[...])
            gkn[:, tile] = back
            key_inner = key_inner + row_sum(back * kgain[:, tile] * keys[:, tile])
    if chunk == 0:
        column[...] = jnp.broadcast_to(query_inner, (CHUNK, LANES))
    else:
        query_inner = jnp.concatenate([column_in[:, :1], query_inner], axis=0)
        inner_out[...] = columns_to_rows([query_inner, key_inner])


def query_key_back_kernel(
    gqn_first,
    gqn_second,
    gkn,
    queries,
    keys,
    totals,
    totals_over,
    inner,
    inner_over,
    qgain,
    kgain,
    mlp_part,
    attn_part,
    gq,
    gk,
    gain_mine,
    gain_give,
):
    half = gain_mine.shape[1]
    for out, columns in ((gain_mine, slice(0, half)), (gain_give, slice(half, 2 * half))):
        out[...] = jnp.zeros(out.shape, F32)
        out[0:1, :] = mlp_part[:, columns]
        out[1:2, :] = attn_part[:, columns]
    query_total, key_total = rows_to_columns(totals[...] + totals_over[...], 2)
    query_inner, key_inner = rows_to_columns(inner[...] + inner_over[...], 2)
    gqn = jnp.concatenate([gqn_first[...], gqn_second[...]], axis=0)
    for at, raw, back, total, sums, gain, low in (
        (2, queries, gqn, query_total, query_inner, qgain, gq),
        (3, keys, gkn[...], key_total, key_inner, kgain, gk),
    ):
        scale = rms_scale(total)
        value = raw[...]
        low[...] = (
            scale * (back * gain[...]) - value * (scale * scale * scale * sums / D)
        ).astype(BF16)
        gained = jnp.sum(back * value * scale, axis=0, keepdims=True)
        gain_mine[at : at + 1, :] = gained
        gain_give[at : at + 1, :] = gained


def weight_kernel(order, widths, *refs):
    keep, give, plain = refs[-3:]
    at = 0
    for index, width in enumerate(widths):
        left, left_far, right, right_far = refs[4 * index : 4 * index + 4]
        for tile in tiles(left.shape[1]):
            plain[tile, at : at + width] = (
                t_dot(left[:, tile], right[...]) + t_dot(left_far[:, tile], right_far[...])
            ).astype(BF16)
        at += width
    blocks = 1 << len(order)
    size = plain.shape[0] // blocks
    me = block_of(order)
    for place in range(blocks):
        out = keep if place < blocks // 2 else give
        to = (place % (blocks // 2)) * size
        block = pl.multiple_of((place ^ me) * size, size)
        out[to : to + size, :] = plain[pl.ds(block, size), :]


def halve_kernel(mine, received, keep, give):
    half = keep.shape[0]
    for out, span in ((give, slice(half, 2 * half)), (keep, slice(0, half))):
        out[...] = (mine[span, :].astype(F32) + received[span, :].astype(F32)).astype(BF16)


def add_kernel(mine, received, out):
    out[...] = (mine[...].astype(F32) + received[...].astype(F32)).astype(BF16)


def join_kernel(mine, received, out):
    half = mine.shape[0]
    out[:half] = mine[...]
    out[half:] = received[...]


def finish_kernel(order, low, high, *outs):
    blocks = 1 << len(order)
    half = blocks // 2
    size = low.shape[0] // half
    me = block_of(order)
    for place in range(blocks):
        source = low if place < half else high
        at = (place % half) * size
        to = pl.multiple_of((place ^ me) * size, size)
        column = 0
        for out in outs:
            width = out.shape[1]
            out[pl.ds(to, size), :] = source[at : at + size, column : column + width].astype(F32)
            column += width


def total_kernel(mine, received, out):
    out[...] = mine[...] + received[...]


def gains_out_kernel(mine, received, *outs):
    for index, out in enumerate(outs):
        out[...] = mine[index : index + 1, :] + received[index : index + 1, :]


def block_out_kernel(first, second, beside_first, beside_second, out):
    for chunk, (mine, beside) in enumerate(((first, beside_first), (second, beside_second))):
        rows = slice(chunk * CHUNK, (chunk + 1) * CHUNK)
        out[rows, :] = jnp.where(on_own_chip(), mine[...], beside[...])


def grad_input_kernel(stays, moves, across, corner, out):
    own = on_own_chip()
    out[...] = jnp.where(own, stays[...], moves[...]) + jnp.where(
        own, across[...], corner[...]
    ).astype(F32)


def input_back_kernel(
    gq, gk, gv, wq, wqt, wk, wkt, wv, wvt, *rest
):
    gh_mine, gh_theirs = rest[:2], rest[2:4]
    stays, moves, across, corner = rest[4:]
    for tile in tiles(wq.shape[0]):
        mine = (
            dot_t(gq[...], wq[tile, :]) + dot_t(gk[...], wk[tile, :]) + dot_t(gv[...], wv[tile, :])
        )
        theirs = (
            dot_t(gq[...], wqt[tile, :])
            + dot_t(gk[...], wkt[tile, :])
            + dot_t(gv[...], wvt[tile, :])
        )
        for chunk in range(2):
            rows = slice(chunk * CHUNK, (chunk + 1) * CHUNK)
            stays[rows, tile] = gh_mine[chunk][:, tile] + mine[rows]
            moves[rows, tile] = gh_theirs[chunk][:, tile] + theirs[rows]
        across[:, tile] = mine.astype(BF16)
        corner[:, tile] = theirs.astype(BF16)


def dp_exchange(values, bit):
    size = lax.axis_size("dp")
    return lax.ppermute(values, "dp", [(i, i ^ (1 << bit)) for i in range(size)])


def dp_bits():
    return lax.axis_size("dp").bit_length() - 1


class Chain:
    def __init__(self, name, order, widths, keep, give):
        self.name, self.order, self.widths = name, order, widths
        self.keep, self.give = keep, give
        self.received = dp_exchange(give, order[0])
        self.stage = 0

    def step(self, after):
        bits = len(self.order)
        stage = self.stage
        self.stage += 1
        name = f"{self.name}_{stage}"
        high, wide = self.keep.shape
        moved = high * wide
        if stage < bits - 1:
            self.keep, self.give = call(
                halve_kernel,
                [shape((high // 2, wide))] * 2,
                [self.keep, self.received],
                moved,
                name,
                after=after,
            )
            self.received = dp_exchange(self.give, self.order[stage + 1])
            return self.give
        if stage == bits - 1:
            (self.keep,) = call(
                add_kernel,
                [shape((high, wide))],
                [self.keep, self.received],
                moved,
                name,
                after=after,
            )
            for bit in range(bits, dp_bits()):
                total = self.keep.astype(F32) + dp_exchange(self.keep, bit).astype(F32)
                self.keep = total.astype(BF16)
        elif stage < 2 * bits - 1:
            (self.keep,) = call(
                join_kernel,
                [shape((2 * high, wide))],
                [self.keep, self.received],
                moved,
                name,
                after=after,
            )
        else:
            self.out = call(
                functools.partial(finish_kernel, self.order),
                [shape((2 * high, w), F32) for w in self.widths],
                [self.keep, self.received],
                moved,
                name,
                after=after,
            )
            return self.out[0]
        self.received = dp_exchange(self.keep, self.order[2 * bits - 2 - stage])
        return self.keep


def on_device(
    block_in,
    w_query,
    w_key,
    w_value,
    w_output,
    w_gate,
    w_up,
    w_down,
    qnorm_gain,
    knorm_gain,
    attn_gain,
    mlp_gain,
    cotangent,
):
    rows, half = block_in.shape
    width = w_query.shape[1]
    ff = w_gate.shape[1]
    pair = ("row", "col")
    scatter_bits = min(3, dp_bits())
    forth = list(range(scatter_bits))
    late = forth[1:] + forth[:1]

    to_over = [(0, 1), (3, 2)]
    to_corner = [(1, 2), (2, 1)]
    to_beside = [(2, 0), (1, 3)]
    from_same = [(0, 2), (3, 1)]

    in_over = lax.ppermute(block_in, pair, to_over)
    in_corner = lax.ppermute(block_in, pair, to_corner)
    in_beside = lax.ppermute(block_in, pair, to_beside)
    wq_far, wk_far, wv_far = swap(w_query, "row"), swap(w_key, "row"), swap(w_value, "row")
    wo_far = swap(w_output, "row")
    (gains,) = call(
        pack_kernel, [shape((8, half), F32)], [attn_gain[None], mlp_gain[None]], 0, "gains"
    )
    gains_far = swap(gains, "row")
    qgain, kgain = qnorm_gain[None], knorm_gain[None]
    cosine, sine_part = rope_tables(rows)

    def in_turn(value, before):
        return lax.optimization_barrier((value, before))

    cotangent, in_corner = in_turn(cotangent, in_corner)
    cot_over = lax.ppermute(cotangent, pair, to_over)
    cot_corner = lax.ppermute(cotangent, pair, to_corner)
    cot_beside = lax.ppermute(cotangent, pair, to_beside)

    queries, keys, totals, in_mine, in_theirs = call(
        query_key_kernel,
        [shape((rows, width), F32)] * 2 + [shape((8, rows), F32)] + [shape((rows, half))] * 2,
        [block_in, in_over, in_beside, in_corner, w_query, wq_far, w_key, wk_far],
        4 * rows * D * width,
        "query_key",
    )
    totals_over = swap(totals, "col")
    (values,) = call(
        value_kernel,
        [shape((rows, width))],
        [in_mine, in_theirs, w_value, wv_far],
        2 * rows * D * width,
        "value",
    )
    wg_far, wu_far, wd_far = swap(w_gate, "row"), swap(w_up, "row"), swap(w_down, "row")
    in_fix = lax.ppermute(in_theirs, pair, to_beside)
    cot_mine, cot_theirs = call(
        choose_two_kernel,
        [shape((rows, half))] * 2,
        [cotangent, cot_over, cot_beside, cot_corner],
        rows * D,
        "cotangent",
    )

    attention_args = [
        queries,
        keys,
        values,
        totals,
        totals_over,
        qgain,
        kgain,
        cosine,
        sine_part,
        w_output,
        wo_far,
    ]
    attention_outs = [shape((rows, width))] * 3 + [
        shape((rows, LANES), F32),
        shape((CHUNK, D)),
    ]
    parts, parts_over = [], []
    kept = []
    for chunk in range(2):
        *kept, partial = call(
            functools.partial(attention_kernel, chunk),
            attention_outs,
            attention_args + kept,
            (1 + chunk) * 5e8 + 4 * CHUNK * width * half,
            f"attention_{chunk}",
            after=() if chunk else (cot_mine,),
        )
        if chunk:
            partial, parts_over[0] = in_turn(partial, parts_over[0])
        parts.append(partial)
        parts_over.append(swap(partial, "col"))
    q_rot, k_rot, mixed, logs = kept
    mixed_far = swap(mixed, "row")
    (in_far,) = call(
        choose_kernel,
        [shape((rows, half))],
        [in_fix, block_in],
        rows * half,
        "in_far",
        after=(mixed,),
    )

    ff_weights = [w_gate, wg_far, w_up, wu_far, w_down, wd_far]
    ff_parts, ff_over, hidden, gate, up = [], [], [], [], []
    kept = []
    for chunk in range(2):
        low_mine, low_theirs, active, hid, gate_act, up_act, partial = call(
            functools.partial(forward_kernel, chunk),
            [shape((rows, half))] * 2
            + [shape((rows, ff)), shape((CHUNK, D), F32)]
            + [shape((CHUNK, ff), F32)] * 2
            + [shape((CHUNK, D))],
            [parts[chunk], parts_over[chunk], in_mine, in_theirs, gains, gains_far]
            + ff_weights
            + kept,
            6 * CHUNK * D * ff,
            f"forward_{chunk}",
            after=(in_far,),
        )
        kept = [low_mine, low_theirs, active]
        hidden.append(hid)
        gate.append(gate_act)
        up.append(up_act)
        if chunk:
            partial, ff_over[0] = in_turn(partial, ff_over[0])
        else:
            partial, parts_over[1] = in_turn(partial, parts_over[1])
        ff_parts.append(partial)
        ff_over.append(swap(partial, "col"))
    low_far = swap(low_theirs, "row")
    active_far = swap(active, "row")

    def weight_grad(name, order, products, after):
        high = products[0][0].shape[1]
        widths = [right.shape[1] for _, _, right, _ in products]
        keep, give = call(
            functools.partial(weight_kernel, order, widths),
            [shape((high // 2, sum(widths)))] * 2,
            [array for product in products for array in product],
            4 * rows * high * sum(widths),
            name,
            scratch=[pltpu.VMEM((high, sum(widths)), BF16)],
            after=after,
        )
        return Chain(name, order, widths, keep, give)

    back_weights = [w_down, wd_far, w_gate, wg_far, w_up, wu_far]
    grad_parts, grad_over = [], []
    kept, kept_back = [], []
    out_mine, out_beside = [], []
    mlp_part = None
    chains = {}
    for chunk in range(2):
        args = [
            ff_parts[chunk],
            ff_over[chunk],
            hidden[chunk],
            cot_mine,
            cot_theirs,
            gains,
            gains_far,
        ]
        if chunk:
            args.append(mlp_part)
        gff_mine, gff_theirs, mine, theirs, mlp_part = call(
            functools.partial(ff_norm_back_kernel, chunk),
            [shape((rows, half))] * 2 + [shape((CHUNK, half), F32)] * 2 + [shape((1, D), F32)],
            args + kept,
            40 * CHUNK * D,
            f"ff_norm_back_{chunk}",
        )
        kept = [gff_mine, gff_theirs]
        out_mine.append(mine)
        out_beside.append(lax.ppermute(theirs, pair, from_same))
        after = ()
        if chunk:
            gff_far = swap(gff_theirs, "row")
            chains["down"] = weight_grad(
                "down", forth, [(active, active_far, gff_mine, gff_far)], ()
            )
            after = (chains["down"].give,)
        *kept_back, partial = call(
            functools.partial(backward_kernel, chunk),
            [shape((rows, ff))] * 2 + [shape((CHUNK, D))],
            [gff_mine, gff_theirs, gate[chunk], up[chunk]] + back_weights + kept_back,
            6 * CHUNK * D * ff,
            f"backward_{chunk}",
            after=after,
        )
        if chunk:
            partial, grad_over[0] = in_turn(partial, grad_over[0])
        else:
            partial, ff_over[1] = in_turn(partial, ff_over[1])
        grad_parts.append(partial)
        grad_over.append(swap(partial, "col"))
    ggate, gup = kept_back

    ggate_far, gup_far = swap(ggate, "row"), swap(gup, "row")
    chains["gate"] = weight_grad(
        "gate", forth, [(low_mine, low_far, ggate, ggate_far)], (kept_back[0],)
    )
    chains["up"] = weight_grad(
        "up", forth, [(low_mine, low_far, gup, gup_far)], (chains["gate"].give,)
    )
    latest = chains["up"].give

    def step(*names):
        nonlocal latest
        for name in names:
            if chains[name].stage == 2 * scatter_bits:
                continue
            latest = chains[name].step((latest,))

    gh_mine, gh_theirs, gqn = [], [], []
    for chunk in range(2):
        args = [
            grad_parts[chunk],
            grad_over[chunk],
            cot_mine,
            cot_theirs,
            parts[chunk],
            parts_over[chunk],
            gains,
            gains_far,
            w_output,
            wo_far,
            q_rot,
            k_rot,
            values,
            logs,
            queries,
            keys,
            totals,
            totals_over,
            qgain,
            kgain,
            cosine,
            sine_part,
        ]
        outs = [shape((rows, half))] * 2 + [shape((CHUNK, half), F32)] * 3 + [shape((1, D), F32)]
        if chunk == 0:
            outs += [shape((CHUNK, LANES), F32)] + [shape((CHUNK, width), F32)] * 2
        else:
            outs += [shape((rows, width), F32), shape((rows, width)), shape((8, rows), F32)]
            args += [attn_part, column, gk_sum, gv_sum, gat_mine, gat_theirs]
        gat_mine, gat_theirs, gm, gt, gq_turned, attn_part, *more = call(
            functools.partial(attention_back_kernel, chunk),
            outs,
            args,
            2e9 + 1e9 * chunk,
            f"attention_back_{chunk}",
            after=(latest,),
        )
        gh_mine.append(gm)
        gh_theirs.append(gt)
        gqn.append(gq_turned)
        if chunk == 0:
            column, gk_sum, gv_sum = more
            latest = column
            step("down")
        else:
            gkn, gv, inner = more
            latest = inner
    inner_over = swap(inner, "col")
    gat_far, gv_far = swap(gat_theirs, "row"), swap(gv, "row")
    step("down", "gate")
    chains["out_value"] = weight_grad(
        "out_value",
        late,
        [(mixed, mixed_far, gat_mine, gat_far), (in_mine, in_far, gv, gv_far)],
        (latest,),
    )
    latest = chains["out_value"].give
    step("down")
    gq, gk, gain_mine, gain_give = call(
        query_key_back_kernel,
        [shape((rows, width))] * 2 + [shape((8, half), F32)] * 2,
        [
            *gqn,
            gkn,
            queries,
            keys,
            totals,
            totals_over,
            inner,
            inner_over,
            qgain,
            kgain,
            mlp_part,
            attn_part,
        ],
        40 * rows * width,
        "query_key_back",
        after=(latest,),
    )
    gq_far, gk_far = swap(gq, "row"), swap(gk, "row")
    gain_far = swap(gain_give, "row")
    chains["query_key"] = weight_grad(
        "query_key",
        forth,
        [(in_mine, in_far, gq, gq_far), (in_mine, in_far, gk, gk_far)],
        (gq,),
    )
    latest = chains["query_key"].give
    step("gate", "down")
    stays, moves, across, corner = call(
        input_back_kernel,
        [shape((rows, half), F32)] * 2 + [shape((rows, half))] * 2,
        [gq, gk, gv, w_query, wq_far, w_key, wk_far, w_value, wv_far, *gh_mine, *gh_theirs],
        12 * rows * width * half,
        "input_back",
        after=(latest,),
    )
    latest = across
    across = lax.ppermute(across, pair, [(1, 0), (2, 3)])
    corner = lax.ppermute(corner, pair, to_corner)
    moves = lax.ppermute(moves, pair, from_same)

    def gain_step(mine, received):
        nonlocal latest
        (latest,) = call(
            total_kernel, [shape(mine.shape, F32)], [mine, received], 0, "gain_sum", after=(latest,)
        )
        return latest

    step("up", "out_value", "gate", "down")
    gain_total = gain_step(gain_mine, gain_far)
    step("up", "query_key", "gate", "out_value")
    for bit in range(dp_bits() - 1):
        gain_total = gain_step(gain_total, dp_exchange(gain_total, bit))
        step("query_key", "up")
    (block_out,) = call(
        block_out_kernel,
        [shape((rows, half), F32)],
        [*out_mine, *out_beside],
        rows * half,
        "block_out",
        after=(latest,),
    )
    (grad_input,) = call(
        grad_input_kernel,
        [shape((rows, half), F32)],
        [stays, moves, across, corner],
        rows * half,
        "grad_input",
        after=(block_out,),
    )
    latest = grad_input
    step("out_value", "gate", "out_value", "query_key", "down", "up", "query_key", "out_value")
    step("up", "query_key", "gate", "out_value", "up", "query_key")
    gain_out = call(
        gains_out_kernel,
        [shape((1, half), F32)] * 2 + [shape((1, width), F32)] * 2,
        [gain_total, dp_exchange(gain_total, dp_bits() - 1)],
        0,
        "gains_out",
    )
    grad_mlpgain, grad_attngain, grad_qgain, grad_kgain = [row[0] for row in gain_out]
    for chain in chains.values():
        while chain.stage < 2 * scatter_bits:
            step(chain.name)
    (grad_down,) = chains["down"].out
    (grad_gate,) = chains["gate"].out
    (grad_up,) = chains["up"].out
    grad_out, grad_value = chains["out_value"].out
    grad_query, grad_key = chains["query_key"].out
    return (
        block_out,
        grad_input,
        grad_query,
        grad_key,
        grad_value,
        grad_out,
        grad_gate,
        grad_up,
        grad_down,
        grad_qgain,
        grad_kgain,
        grad_attngain,
        grad_mlpgain,
    )


def solution(mesh):
    tokens = P(("dp", "col"), "row")
    grid, turned = P("row", "col"), P("col", "row")
    in_specs = (
        tokens,
        grid,
        grid,
        grid,
        turned,
        grid,
        grid,
        turned,
        P("col"),
        P("col"),
        P("row"),
        P("row"),
        tokens,
    )
    out_specs = (
        tokens,
        tokens,
        grid,
        grid,
        grid,
        turned,
        grid,
        grid,
        turned,
        P("col"),
        P("col"),
        P("row"),
        P("row"),
    )
    return jax.shard_map(
        on_device, mesh=mesh, in_specs=in_specs, out_specs=out_specs, check_vma=False
    )
```

```python
import functools
import math

import jax
import jax.numpy as jnp
import numpy as np
from jax import lax
from jax.experimental import pallas as pl
from jax.experimental.pallas import tpu as pltpu
from jax.sharding import PartitionSpec as P

D = 1024
HEAD = 64
SEQ = 512
EPSILON = 1e-06
ROPE_BASE = 500000.0
MASKED = -1e30
CHUNK = 256
TILE = 256
LANES = 128
FACTOR = 1.0 / math.sqrt(HEAD)

F32 = jnp.float32
BF16 = jnp.bfloat16


def swap(values, axis):
    return lax.ppermute(values, axis, [(0, 1), (1, 0)])


def dot(left, right):
    return jnp.dot(left, right, preferred_element_type=F32)


def dot_t(left, right):
    return lax.dot_general(left, right, (((1,), (1,)), ((), ())), preferred_element_type=F32)


def t_dot(left, right):
    return lax.dot_general(left, right, (((0,), (0,)), ((), ())), preferred_element_type=F32)


def shape(dims, kind=BF16):
    return jax.ShapeDtypeStruct(dims, kind)


def call(kernel, outs, args, name, scratch=(), after=()):
    count = len(args)
    skip = len(after)
    vmem = pl.BlockSpec(memory_space=pltpu.VMEM)
    def body(*refs):
        kernel(*refs[:count], *refs[count + skip :])

    return pl.pallas_call(
        body,
        out_shape=tuple(outs),
        in_specs=[vmem] * count + [pl.BlockSpec(memory_space=pl.ANY)] * skip,
        out_specs=tuple([vmem] * len(outs)),
        scratch_shapes=scratch,
        compiler_params=pltpu.CompilerParams(
            vmem_limit_bytes=12 << 20, fuse_transposed_lhs_in_matmul=True
        ),
        cost_estimate=pl.CostEstimate(flops=1, bytes_accessed=1, transcendentals=0),
        name=name,
    )(*args, *after)


def tiles(extent, size=TILE):
    return [slice(at, min(at + size, extent)) for at in range(0, extent, size)]


def row_sum(values):
    return jnp.sum(values, axis=1, keepdims=True)


def columns_to_rows(columns):
    count = columns[0].shape[0]
    lane = lax.broadcasted_iota(jnp.int32, (count, LANES), 1)
    packed = jnp.zeros((count, LANES), F32)
    for index, column in enumerate(columns):
        packed = jnp.where(lane == index, column, packed)
    return packed.T[:8]


def rows_to_columns(rows, count):
    turned = jnp.concatenate([rows] * (LANES // 8), axis=0).T
    return [turned[:, i : i + 1] for i in range(count)]


def rms_scale(total):
    return lax.rsqrt(total / D + EPSILON)


def turn(values, cosine, sine_part):
    lane = lax.broadcasted_iota(jnp.int32, cosine.shape, 1)
    first = (lane % HEAD) < HEAD // 2
    out = []
    for tile in tiles(values.shape[1], LANES):
        part = values[:, tile]
        other = jnp.where(
            first, pltpu.roll(part, LANES - HEAD // 2, 1), pltpu.roll(part, HEAD // 2, 1)
        )
        out.append(part * cosine + other * sine_part)
    return jnp.concatenate(out, axis=1)


def rope_tables(count):
    half = HEAD // 2
    frequency = np.exp(np.arange(half, dtype=np.float32) * np.float32(-2.0 * math.log(ROPE_BASE) / HEAD))
    angles = np.arange(count).astype(np.float32)[:, None] * frequency[None, :]
    cosine, sine_part = np.cos(angles), np.sin(angles)
    repeats = LANES // HEAD
    return (
        jnp.asarray(np.concatenate([cosine, cosine] * repeats, axis=1)),
        jnp.asarray(np.concatenate([-sine_part, sine_part] * repeats, axis=1)),
    )


def lower_triangle():
    rows = lax.broadcasted_iota(jnp.int32, (CHUNK, CHUNK), 0)
    cols = lax.broadcasted_iota(jnp.int32, (CHUNK, CHUNK), 1)
    return rows >= cols


def keep_rows(pairs):
    for before, out in pairs:
        out[:CHUNK] = before[:CHUNK]


def head_mask(count, index):
    lane = lax.broadcasted_iota(jnp.int32, (count, LANES), 1)
    return (lane < HEAD) if index == 0 else (lane >= HEAD)


def only(mask, values):
    return jnp.where(mask, values, jnp.zeros_like(values))


def branch_of(mine, theirs):
    branch = mine[...].astype(F32) + theirs[...].astype(F32)
    return branch, rms_scale(row_sum(branch * branch))


def gain_of(mine, theirs, index):
    row = slice(index, index + 1)
    return jnp.concatenate([mine[row, :], theirs[row, :]], axis=1)


def on_own_chip():
    return lax.axis_index("row") == lax.axis_index("col")


def block_of(order):
    index = 0
    for bit in order:
        index = 2 * index + ((lax.axis_index("dp") >> bit) & 1)
    return index


def norm_back(branch, scale, gain_vec, grad_out):
    weighted = grad_out * gain_vec
    inner = row_sum(weighted * branch)
    grad_branch = scale * weighted - branch * (scale * scale * scale * inner / D)
    grad_gain = jnp.sum(grad_out * branch * scale, axis=0, keepdims=True)
    return grad_branch, grad_gain


def pack_kernel(*refs):
    out = refs[-1]
    out[...] = jnp.zeros(out.shape, F32)
    for index, row in enumerate(refs[:-1]):
        out[index : index + 1, :] = row[...]


def stack_kernel(*refs):
    out = refs[-1]
    at = 0
    for part in refs[:-1]:
        out[at : at + part.shape[0], :] = part[...]
        at += part.shape[0]


def split_rows(ref, count):
    high = ref.shape[0] // count
    return [ref.at[i * high : (i + 1) * high] for i in range(count)]


def choose_kernel(first, other, out):
    out[...] = jnp.where(on_own_chip(), first[...], other[...])


def choose_two_kernel(first, other, beside, corner, out, out_theirs):
    choose_kernel(first, other, out)
    choose_kernel(beside, corner, out_theirs)


def query_key_kernel(
    block, over, beside, corner, wq, wk, w_far, q_out, k_out, total_out, mine, theirs
):
    choose_two_kernel(block, over, beside, corner, mine, theirs)
    wqt, wkt, _, _ = split_rows(w_far, 4)
    query_sum = 0.0
    key_sum = 0.0
    for tile in tiles(wq.shape[1]):
        query = dot(mine[...], wq[:, tile]) + dot(theirs[...], wqt[:, tile])
        q_out[:, tile] = query
        query_sum = query_sum + row_sum(query * query)
        key = dot(mine[...], wk[:, tile]) + dot(theirs[...], wkt[:, tile])
        k_out[:, tile] = key
        key_sum = key_sum + row_sum(key * key)
    total_out[...] = columns_to_rows([query_sum, key_sum])


def value_kernel(mine, theirs, wv, w_far, v_out):
    wvt = split_rows(w_far, 4)[2]
    for tile in tiles(wv.shape[1]):
        v_out[:, tile] = (dot(mine[...], wv[:, tile]) + dot(theirs[...], wvt[:, tile])).astype(BF16)


def attention_kernel(
    chunk,
    queries,
    keys,
    values,
    totals,
    totals_over,
    qgain,
    kgain,
    cosine,
    sine_part,
    wo,
    w_far,
    *rest,
):
    wot = split_rows(w_far, 4)[3]
    if chunk == 0:
        q_rot, k_rot, mixed, logs, partial = rest
    else:
        q_rot, k_rot, mixed, logs, partial = rest[4:]
        keep_rows(zip(rest[:4], rest[4:]))
    rows = slice(chunk * CHUNK, (chunk + 1) * CHUNK)
    query_total, key_total = rows_to_columns(totals[...] + totals_over[...], 2)
    query = queries[rows, :] * rms_scale(query_total[rows]) * qgain[...]
    key = keys[rows, :] * rms_scale(key_total[rows]) * kgain[...]
    q_rot[rows, :] = (turn(query, cosine[rows, :], sine_part[rows, :]) * FACTOR).astype(BF16)
    k_rot[rows, :] = turn(key, cosine[rows, :], sine_part[rows, :]).astype(BF16)
    visible = lower_triangle()
    lane = lax.broadcasted_iota(jnp.int32, (CHUNK, LANES), 1)
    log_tile = jnp.zeros((CHUNK, LANES), F32)
    for at, tile in enumerate(tiles(queries.shape[1], LANES)):
        total = jnp.zeros((CHUNK, LANES), F32)
        for index in range(2):
            query_head = only(head_mask(CHUNK, index), q_rot[rows, tile])
            scores = []
            for block in range(chunk + 1):
                part = dot_t(query_head, k_rot[block * CHUNK : (block + 1) * CHUNK, tile])
                scores.append(jnp.where(visible, part, MASKED) if block == chunk else part)
            peak = jnp.max(scores[0], axis=1, keepdims=True)
            for part in scores[1:]:
                peak = jnp.maximum(peak, jnp.max(part, axis=1, keepdims=True))
            scores = [jnp.exp(part - peak) for part in scores]
            denominator = sum(row_sum(part) for part in scores)
            inverse = 1.0 / denominator
            for block, part in enumerate(scores):
                value_rows = values[block * CHUNK : (block + 1) * CHUNK, tile]
                total = total + dot(
                    (part * inverse).astype(BF16), only(head_mask(CHUNK, index), value_rows)
                )
            log_tile = jnp.where(lane == 2 * at + index, peak + jnp.log(denominator), log_tile)
        mixed[rows, tile] = total.astype(BF16)
    logs[rows, :] = log_tile
    low = mixed[rows, :]
    half = wo.shape[1]
    partial[:, :half] = dot(low, wo[...]).astype(BF16)
    partial[:, half:] = dot(low, wot[...]).astype(BF16)


def forward_kernel(
    chunk, part, part_over, mine, theirs, gains, gains_far, wg, wu, wgu_far, wd, wdt, *rest
):
    if chunk == 0:
        low_mine, side, hidden, gate, up, partial = rest
    else:
        low_mine, side, hidden, gate, up, partial = rest[2:]
        keep_rows(zip(rest[:2], rest[2:]))
    rows = slice(chunk * CHUNK, (chunk + 1) * CHUNK)
    wgt, wut = split_rows(wgu_far, 2)
    branch, scale = branch_of(part, part_over)
    half, ff = mine.shape[1], wg.shape[1]
    normed = branch * scale * gain_of(gains, gains_far, 0)
    value = mine[rows, :].astype(F32) + normed[:, :half]
    hidden[:, :half] = value
    low_mine[rows, :] = value.astype(BF16)
    value = theirs[rows, :].astype(F32) + normed[:, half:]
    hidden[:, half:] = value
    side[rows, ff:] = value.astype(BF16)
    for tile in tiles(ff):
        left, right = low_mine[rows, :], side[rows, ff:]
        gate_act = dot(left, wg[:, tile]) + dot(right, wgt[:, tile])
        up_act = dot(left, wu[:, tile]) + dot(right, wut[:, tile])
        gate[:, tile] = gate_act
        up[:, tile] = up_act
        side[rows, tile] = (gate_act * jax.nn.sigmoid(gate_act) * up_act).astype(BF16)
    low = side[rows, :ff]
    partial[:, :half] = dot(low, wd[...]).astype(BF16)
    partial[:, half:] = dot(low, wdt[...]).astype(BF16)


def ff_norm_back_kernel(
    chunk, part, part_over, hidden, cot_mine, cot_theirs, gains, gains_far, *rest
):
    if chunk == 0:
        gff_mine, gff_theirs, out_mine, out_theirs, grad_gain = rest
    else:
        gain_before = rest[0]
        gff_mine, gff_theirs, out_mine, out_theirs, grad_gain = rest[5:]
        keep_rows(zip(rest[1:5], rest[5:]))
    rows = slice(chunk * CHUNK, (chunk + 1) * CHUNK)
    branch, scale = branch_of(part, part_over)
    half = cot_mine.shape[1]
    gain = gain_of(gains, gains_far, 1)
    block_out = hidden[...] + branch * scale * gain
    out_mine[rows, :] = block_out[:, :half]
    out_theirs[rows, :] = block_out[:, half:]
    upstream = jnp.concatenate([cot_mine[rows, :], cot_theirs[rows, :]], axis=1).astype(F32)
    grad_branch, gained = norm_back(branch, scale, gain, upstream)
    grad_gain[...] = gained if chunk == 0 else gain_before[...] + gained
    gff_mine[rows, :] = grad_branch[:, :half].astype(BF16)
    gff_theirs[rows, :] = grad_branch[:, half:].astype(BF16)


def backward_kernel(
    chunk, gff_mine, gff_theirs, gate, up, wd, wdt, wg, wu, wgu_far, *rest
):
    if chunk == 0:
        grads, partial = rest
    else:
        grads, partial = rest[1:]
        keep_rows([rest[:2]])
    rows = slice(chunk * CHUNK, (chunk + 1) * CHUNK)
    wgt, wut = split_rows(wgu_far, 2)
    half, ff = wd.shape[1], wg.shape[1]
    for tile in tiles(ff):
        grad_act = dot_t(gff_mine[rows, :], wd[tile, :]) + dot_t(gff_theirs[rows, :], wdt[tile, :])
        gate_act = gate[:, tile]
        sig = jax.nn.sigmoid(gate_act)
        grads[rows, tile] = (
            grad_act * up[:, tile] * sig * (1.0 + gate_act * (1.0 - sig))
        ).astype(BF16)
        there = slice(ff + tile.start, ff + tile.stop)
        grads[rows, there] = (grad_act * gate_act * sig).astype(BF16)
    left, right = grads[rows, :ff], grads[rows, ff:]
    for tile in tiles(half):
        partial[:, tile] = (dot_t(left, wg[tile, :]) + dot_t(right, wu[tile, :])).astype(BF16)
        there = slice(half + tile.start, half + tile.stop)
        partial[:, there] = (dot_t(left, wgt[tile, :]) + dot_t(right, wut[tile, :])).astype(BF16)


def attention_back_kernel(
    chunk,
    grad_part,
    grad_over,
    cot_mine,
    cot_theirs,
    part,
    part_over,
    gains,
    gains_far,
    wo,
    w_far,
    q_rot,
    k_rot,
    values,
    logs,
    queries,
    keys,
    totals,
    totals_over,
    qgain,
    kgain,
    cosine,
    sine_part,
    *rest,
):
    half = wo.shape[1]
    width = queries.shape[1]
    if chunk == 0:
        gat_mine, side, gh_mine, gh_theirs, gqn, grad_gain, column, gk_sum, gv_sum = rest
    else:
        gain_before, column_in, gk_in, gv_in = rest[:4]
        gat_mine, side, gh_mine, gh_theirs, gqn, grad_gain, gkn, inner_out = rest[6:]
        keep_rows(zip(rest[4:6], rest[6:]))
    wot = split_rows(w_far, 4)[3]
    rows = slice(chunk * CHUNK, (chunk + 1) * CHUNK)
    seen = (chunk + 1) * CHUNK
    branch, scale = branch_of(part, part_over)
    grad_hidden = (
        jnp.concatenate([cot_mine[rows, :], cot_theirs[rows, :]], axis=1).astype(F32)
        + grad_part[...].astype(F32)
        + grad_over[...].astype(F32)
    )
    gh_mine[...] = grad_hidden[:, :half]
    gh_theirs[...] = grad_hidden[:, half:]
    grad_branch, gained = norm_back(branch, scale, gain_of(gains, gains_far, 0), grad_hidden)
    grad_gain[...] = gained if chunk == 0 else gain_before[...] + gained
    gat_mine[rows, :] = grad_branch[:, :half].astype(BF16)
    side[rows, :half] = grad_branch[:, half:].astype(BF16)
    grad_mixed = (
        dot_t(gat_mine[rows, :], wo[...]) + dot_t(side[rows, :half], wot[...])
    ).astype(BF16)
    visible = lower_triangle()
    query_total, key_total = rows_to_columns(totals[...] + totals_over[...], 2)
    query_inner = jnp.zeros((CHUNK, 1), F32)
    key_inner = jnp.zeros((seen, 1), F32)
    for at, tile in enumerate(tiles(width, LANES)):
        grad_query = jnp.zeros((CHUNK, LANES), F32)
        grad_key = [jnp.zeros((CHUNK, LANES), F32) for _ in range(chunk + 1)]
        grad_value = [jnp.zeros((CHUNK, LANES), F32) for _ in range(chunk + 1)]
        for index in range(2):
            mask = head_mask(CHUNK, index)
            query_head = only(mask, q_rot[rows, tile])
            grad_head = only(mask, grad_mixed[:, tile])
            log_column = logs[rows, 2 * at + index : 2 * at + index + 1]
            weights, grads = [], []
            for block in range(chunk + 1):
                span = slice(block * CHUNK, (block + 1) * CHUNK)
                scores = dot_t(query_head, k_rot[span, tile])
                if block == chunk:
                    scores = jnp.where(visible, scores, MASKED)
                weights.append(jnp.exp(scores - log_column))
                grads.append(dot_t(grad_head, values[span, tile]))
            inner = sum(row_sum(w * g) for w, g in zip(weights, grads))
            for block in range(chunk + 1):
                span = slice(block * CHUNK, (block + 1) * CHUNK)
                weight = weights[block]
                grad_scores = (weight * (grads[block] - inner)).astype(BF16)
                grad_value[block] = grad_value[block] + t_dot(weight.astype(BF16), grad_head)
                grad_query = grad_query + dot(grad_scores, only(mask, k_rot[span, tile]))
                grad_key[block] = grad_key[block] + t_dot(grad_scores, query_head)
        back = turn(grad_query * FACTOR, cosine[rows, :], -sine_part[rows, :])
        gqn[:, tile] = back
        query_inner = query_inner + row_sum(back * qgain[:, tile] * queries[rows, tile])
        if chunk == 0:
            gk_sum[:, tile] = grad_key[0]
            gv_sum[:, tile] = grad_value[0]
        else:
            key_all = jnp.concatenate([gk_in[:, tile] + grad_key[0], grad_key[1]], axis=0)
            value_all = jnp.concatenate([gv_in[:, tile] + grad_value[0], grad_value[1]], axis=0)
            side[:, half + tile.start : half + tile.stop] = value_all.astype(BF16)
            back = turn(key_all, cosine[...], -sine_part[...])
            gkn[:, tile] = back
            key_inner = key_inner + row_sum(back * kgain[:, tile] * keys[:, tile])
    if chunk == 0:
        column[...] = jnp.broadcast_to(query_inner, (CHUNK, LANES))
    else:
        query_inner = jnp.concatenate([column_in[:, :1], query_inner], axis=0)
        inner_out[...] = columns_to_rows([query_inner, key_inner])


def query_key_back_kernel(
    gqn_first,
    gqn_second,
    gkn,
    queries,
    keys,
    totals,
    totals_over,
    inner,
    inner_over,
    qgain,
    kgain,
    mlp_part,
    attn_part,
    grads,
    gain_mine,
    gain_give,
):
    width = queries.shape[1]
    half = gain_mine.shape[1]
    for out, columns in ((gain_mine, slice(0, half)), (gain_give, slice(half, 2 * half))):
        out[...] = jnp.zeros(out.shape, F32)
        out[0:1, :] = mlp_part[:, columns]
        out[1:2, :] = attn_part[:, columns]
    query_total, key_total = rows_to_columns(totals[...] + totals_over[...], 2)
    query_inner, key_inner = rows_to_columns(inner[...] + inner_over[...], 2)
    gqn = jnp.concatenate([gqn_first[...], gqn_second[...]], axis=0)
    for at, raw, back, total, sums, gain, low in (
        (2, queries, gqn, query_total, query_inner, qgain, grads.at[:, :width]),
        (3, keys, gkn[...], key_total, key_inner, kgain, grads.at[:, width:]),
    ):
        scale = rms_scale(total)
        value = raw[...]
        low[...] = (
            scale * (back * gain[...]) - value * (scale * scale * scale * sums / D)
        ).astype(BF16)
        gained = jnp.sum(back * value * scale, axis=0, keepdims=True)
        gain_mine[at : at + 1, :] = gained
        gain_give[at : at + 1, :] = gained


def weight_kernel(order, products, *refs):
    keep, give, plain = refs[-3:]

    def view(operand):
        index, start, stop = operand
        return refs[index].at[:, start:stop]

    at = 0
    for product in products:
        left, left_far, right, right_far = [view(operand) for operand in product]
        width = product[2][2] - product[2][1]
        for tile in tiles(plain.shape[0]):
            plain[tile, at : at + width] = (
                t_dot(left[:, tile], right[...]) + t_dot(left_far[:, tile], right_far[...])
            ).astype(BF16)
        at += width
    blocks = 1 << len(order)
    size = plain.shape[0] // blocks
    me = block_of(order)
    for place in range(blocks):
        out = keep if place < blocks // 2 else give
        to = (place % (blocks // 2)) * size
        block = pl.multiple_of((place ^ me) * size, size)
        out[to : to + size, :] = plain[pl.ds(block, size), :]


def halve_kernel(mine, received, keep, give):
    half = keep.shape[0]
    for out, span in ((give, slice(half, 2 * half)), (keep, slice(0, half))):
        out[...] = (mine[span, :].astype(F32) + received[span, :].astype(F32)).astype(BF16)


def add_kernel(mine, received, out):
    out[...] = (mine[...].astype(F32) + received[...].astype(F32)).astype(BF16)


def join_kernel(mine, received, out):
    half = mine.shape[0]
    out[:half] = mine[...]
    out[half:] = received[...]


def finish_kernel(order, low, high, *outs):
    blocks = 1 << len(order)
    half = blocks // 2
    size = low.shape[0] // half
    me = block_of(order)
    for place in range(blocks):
        source = low if place < half else high
        at = (place % half) * size
        to = pl.multiple_of((place ^ me) * size, size)
        column = 0
        for out in outs:
            width = out.shape[1]
            out[pl.ds(to, size), :] = source[at : at + size, column : column + width].astype(F32)
            column += width


def total_kernel(mine, received, out):
    out[...] = mine[...] + received[...]


def gains_out_kernel(mine, received, *outs):
    for index, out in enumerate(outs):
        out[...] = mine[index : index + 1, :] + received[index : index + 1, :]


def grad_input_kernel(stays, moves, across, corner, out):
    own = on_own_chip()
    out[...] = jnp.where(own, stays[...], moves[...]) + jnp.where(
        own, across[...], corner[...]
    ).astype(F32)


def input_back_kernel(
    grads, side, wq, wk, wv, w_far, *rest
):
    width = wq.shape[1]
    gq, gk = grads.at[:, :width], grads.at[:, width:]
    gv = side.at[:, side.shape[1] - width :]
    wqt, wkt, wvt, _ = split_rows(w_far, 4)
    gh_mine, gh_theirs = rest[:2], rest[2:4]
    stays, moves, across, corner = rest[4:]
    for tile in tiles(wq.shape[0]):
        mine = (
            dot_t(gq[...], wq[tile, :]) + dot_t(gk[...], wk[tile, :]) + dot_t(gv[...], wv[tile, :])
        )
        theirs = (
            dot_t(gq[...], wqt[tile, :])
            + dot_t(gk[...], wkt[tile, :])
            + dot_t(gv[...], wvt[tile, :])
        )
        for chunk in range(2):
            rows = slice(chunk * CHUNK, (chunk + 1) * CHUNK)
            stays[rows, tile] = gh_mine[chunk][:, tile] + mine[rows]
            moves[rows, tile] = gh_theirs[chunk][:, tile] + theirs[rows]
        across[:, tile] = mine.astype(BF16)
        corner[:, tile] = theirs.astype(BF16)


def dp_exchange(values, bit):
    size = lax.axis_size("dp")
    return lax.ppermute(values, "dp", [(i, i ^ (1 << bit)) for i in range(size)])


def dp_bits():
    return lax.axis_size("dp").bit_length() - 1


class Chain:
    def __init__(self, name, order, widths, keep, give):
        self.name, self.order, self.widths = name, order, widths
        self.keep, self.give = keep, give
        self.received = dp_exchange(give, order[0])
        self.stage = 0

    def step(self, after):
        bits = len(self.order)
        stage = self.stage
        self.stage += 1
        name = f"{self.name}_{stage}"
        high, wide = self.keep.shape
        if stage < bits - 1:
            self.keep, self.give = call(
                halve_kernel,
                [shape((high // 2, wide))] * 2,
                [self.keep, self.received],
                name,
                after=after,
            )
            self.received = dp_exchange(self.give, self.order[stage + 1])
            return self.give
        if stage == bits - 1:
            (self.keep,) = call(
                add_kernel,
                [shape((high, wide))],
                [self.keep, self.received],
                name,
                after=after,
            )
            for bit in range(bits, dp_bits()):
                total = self.keep.astype(F32) + dp_exchange(self.keep, bit).astype(F32)
                self.keep = total.astype(BF16)
        elif stage < 2 * bits - 1:
            (self.keep,) = call(
                join_kernel,
                [shape((2 * high, wide))],
                [self.keep, self.received],
                name,
                after=after,
            )
        else:
            self.out = call(
                functools.partial(finish_kernel, self.order),
                [shape((2 * high, w), F32) for w in self.widths],
                [self.keep, self.received],
                name,
                after=after,
            )
            return self.out[0]
        self.received = dp_exchange(self.keep, self.order[2 * bits - 2 - stage])
        return self.keep


def on_device(
    block_in,
    w_query,
    w_key,
    w_value,
    w_output,
    w_gate,
    w_up,
    w_down,
    qnorm_gain,
    knorm_gain,
    attn_gain,
    mlp_gain,
    cotangent,
):
    rows, half = block_in.shape
    width = w_query.shape[1]
    ff = w_gate.shape[1]
    pair = ("row", "col")
    scatter_bits = min(3, dp_bits())
    forth = list(range(scatter_bits))
    late = forth[1:] + forth[:1]

    to_over = [(0, 1), (3, 2)]
    to_corner = [(1, 2), (2, 1)]
    to_beside = [(2, 0), (1, 3)]
    from_same = [(0, 2), (3, 1)]

    in_over = lax.ppermute(block_in, pair, to_over)
    in_corner = lax.ppermute(block_in, pair, to_corner)
    in_beside = lax.ppermute(block_in, pair, to_beside)
    (packed,) = call(
        stack_kernel,
        [shape((4 * half, width))],
        [w_query, w_key, w_value, w_output],
        "attention_weights",
    )
    w_far = swap(packed, "row")
    (packed,) = call(stack_kernel, [shape((2 * half, ff))], [w_gate, w_up], "ff_weights")
    (gains,) = call(
        pack_kernel, [shape((8, half), F32)], [attn_gain[None], mlp_gain[None]], "gains"
    )
    qgain, kgain = qnorm_gain[None], knorm_gain[None]
    cosine, sine_part = rope_tables(rows)

    def in_turn(value, before):
        return lax.optimization_barrier((value, before))

    cotangent, in_corner = in_turn(cotangent, in_corner)
    cot_over = lax.ppermute(cotangent, pair, to_over)
    cot_corner = lax.ppermute(cotangent, pair, to_corner)
    cot_beside = lax.ppermute(cotangent, pair, to_beside)

    queries, keys, totals, in_mine, in_theirs = call(
        query_key_kernel,
        [shape((rows, width), F32)] * 2 + [shape((8, rows), F32)] + [shape((rows, half))] * 2,
        [block_in, in_over, in_beside, in_corner, w_query, w_key, w_far],
        "query_key",
    )
    totals_over = swap(totals, "col")
    (values,) = call(
        value_kernel,
        [shape((rows, width))],
        [in_mine, in_theirs, w_value, w_far],
        "value",
    )
    wgu_far = swap(packed, "row")
    wd_far = swap(w_down, "row")
    in_fix = lax.ppermute(in_theirs, pair, to_beside)
    (in_far,) = call(choose_kernel, [shape((rows, half))], [in_fix, block_in], "in_far")
    cot_mine, cot_theirs = call(
        choose_two_kernel,
        [shape((rows, half))] * 2,
        [cotangent, cot_over, cot_beside, cot_corner],
        "cotangent",
    )

    attention_args = [
        queries,
        keys,
        values,
        totals,
        totals_over,
        qgain,
        kgain,
        cosine,
        sine_part,
        w_output,
        w_far,
    ]
    attention_outs = [shape((rows, width))] * 3 + [
        shape((rows, LANES), F32),
        shape((CHUNK, D)),
    ]
    parts, parts_over = [], []
    kept = []
    for chunk in range(2):
        *kept, partial = call(
            functools.partial(attention_kernel, chunk),
            attention_outs,
            attention_args + kept,
            f"attention_{chunk}",
            after=(in_far, wd_far) if chunk else (cot_mine, wgu_far),
        )
        if chunk:
            partial, parts_over[0] = in_turn(partial, parts_over[0])
        parts.append(partial)
        parts_over.append(swap(partial, "col"))
    q_rot, k_rot, mixed, logs = kept
    mixed_far = swap(mixed, "row")
    gains_far = swap(gains, "row")

    ff_parts, ff_over, hidden, gate, up = [], [], [], [], []
    kept = []
    for chunk in range(2):
        low_mine, side, hid, gate_act, up_act, partial = call(
            functools.partial(forward_kernel, chunk),
            [shape((rows, half)), shape((rows, ff + half)), shape((CHUNK, D), F32)]
            + [shape((CHUNK, ff), F32)] * 2
            + [shape((CHUNK, D))],
            [parts[chunk], parts_over[chunk], in_mine, in_theirs, gains, gains_far]
            + [w_gate, w_up, wgu_far, w_down, wd_far]
            + kept,
            f"forward_{chunk}",
            after=(mixed_far,),
        )
        kept = [low_mine, side]
        hidden.append(hid)
        gate.append(gate_act)
        up.append(up_act)
        if chunk:
            partial, ff_over[0] = in_turn(partial, ff_over[0])
        else:
            partial, parts_over[1] = in_turn(partial, parts_over[1])
        ff_parts.append(partial)
        ff_over.append(swap(partial, "col"))
    side_far = swap(side, "row")

    def weight_grad(name, order, arrays, products, after):
        high = products[0][0][2] - products[0][0][1]
        widths = [right[2] - right[1] for _, _, right, _ in products]
        keep, give = call(
            functools.partial(weight_kernel, order, products),
            [shape((high // 2, sum(widths)))] * 2,
            arrays,
            name,
            scratch=[pltpu.VMEM((high, sum(widths)), BF16)],
            after=after,
        )
        return Chain(name, order, widths, keep, give)

    grad_parts, grad_over = [], []
    kept, kept_back = [], []
    mlp_part = None
    chains = {}
    for chunk in range(2):
        args = [
            ff_parts[chunk],
            ff_over[chunk],
            hidden[chunk],
            cot_mine,
            cot_theirs,
            gains,
            gains_far,
        ]
        if chunk:
            args.append(mlp_part)
        *kept, mlp_part = call(
            functools.partial(ff_norm_back_kernel, chunk),
            [shape((rows, half))] * 2 + [shape((rows, half), F32)] * 2 + [shape((1, D), F32)],
            args + kept,
            f"ff_norm_back_{chunk}",
            after=(side_far,),
        )
        gff_mine, gff_theirs, out_mine, out_theirs = kept
        after = ()
        if chunk:
            gff_far = swap(gff_theirs, "row")
            chains["down"] = weight_grad(
                "down",
                forth,
                [side, side_far, gff_mine, gff_far],
                [((0, 0, ff), (1, 0, ff), (2, 0, half), (3, 0, half))],
                (),
            )
            after = (chains["down"].give,)
        grads, partial = call(
            functools.partial(backward_kernel, chunk),
            [shape((rows, 2 * ff)), shape((CHUNK, D))],
            [gff_mine, gff_theirs, gate[chunk], up[chunk], w_down, wd_far, w_gate, w_up, wgu_far]
            + kept_back,
            f"backward_{chunk}",
            after=after,
        )
        kept_back = [grads]
        if chunk:
            partial, grad_over[0] = in_turn(partial, grad_over[0])
        else:
            partial, ff_over[1] = in_turn(partial, ff_over[1])
        grad_parts.append(partial)
        grad_over.append(swap(partial, "col"))
    out_beside = lax.ppermute(out_theirs, pair, from_same)
    grads_far = swap(grads, "row")

    def ff_grad(name, start, after):
        span = (start, start + ff)
        return weight_grad(
            name,
            forth,
            [low_mine, side_far, grads, grads_far],
            [((0, 0, half), (1, ff, ff + half), (2, *span), (3, *span))],
            after,
        )

    chains["gate"] = ff_grad("gate", 0, (out_beside,))
    latest = chains["gate"].give

    def step(*names):
        nonlocal latest
        for name in names:
            if chains[name].stage == 2 * scatter_bits:
                continue
            latest = chains[name].step((latest,))

    gh_mine, gh_theirs, gqn = [], [], []
    for chunk in range(2):
        args = [
            grad_parts[chunk],
            grad_over[chunk],
            cot_mine,
            cot_theirs,
            parts[chunk],
            parts_over[chunk],
            gains,
            gains_far,
            w_output,
            w_far,
            q_rot,
            k_rot,
            values,
            logs,
            queries,
            keys,
            totals,
            totals_over,
            qgain,
            kgain,
            cosine,
            sine_part,
        ]
        outs = [shape((rows, half)), shape((rows, half + width))]
        outs += [shape((CHUNK, half), F32)] * 2 + [shape((CHUNK, width), F32), shape((1, D), F32)]
        if chunk == 0:
            outs += [shape((CHUNK, LANES), F32)] + [shape((CHUNK, width), F32)] * 2
        else:
            outs += [shape((rows, width), F32), shape((8, rows), F32)]
            args += [attn_part, column, gk_sum, gv_sum, gat_mine, side_back]
        gat_mine, side_back, gm, gt, gq_turned, attn_part, *more = call(
            functools.partial(attention_back_kernel, chunk),
            outs,
            args,
            f"attention_back_{chunk}",
            after=(latest,),
        )
        gh_mine.append(gm)
        gh_theirs.append(gt)
        gqn.append(gq_turned)
        if chunk == 0:
            column, gk_sum, gv_sum = more
            latest = column
            step("down")
            chains["up"] = ff_grad("up", ff, (latest,))
            latest = chains["up"].give
        else:
            gkn, inner = more
            latest = inner
    inner_over = swap(inner, "col")
    side_back_far = swap(side_back, "row")
    step("down", "gate")
    chains["out_value"] = weight_grad(
        "out_value",
        late,
        [mixed, mixed_far, gat_mine, side_back_far, in_mine, in_far, side_back],
        [
            ((0, 0, width), (1, 0, width), (2, 0, half), (3, 0, half)),
            ((4, 0, half), (5, 0, half), (6, half, half + width), (3, half, half + width)),
        ],
        (latest,),
    )
    latest = chains["out_value"].give
    step("down")
    grads_back, gain_mine, gain_give = call(
        query_key_back_kernel,
        [shape((rows, 2 * width))] + [shape((8, half), F32)] * 2,
        [
            *gqn,
            gkn,
            queries,
            keys,
            totals,
            totals_over,
            inner,
            inner_over,
            qgain,
            kgain,
            mlp_part,
            attn_part,
        ],
        "query_key_back",
        after=(latest,),
    )
    grads_back_far = swap(grads_back, "row")
    chains["query_key"] = weight_grad(
        "query_key",
        forth,
        [in_mine, in_far, grads_back, grads_back_far],
        [
            ((0, 0, half), (1, 0, half), (2, 0, width), (3, 0, width)),
            ((0, 0, half), (1, 0, half), (2, width, 2 * width), (3, width, 2 * width)),
        ],
        (),
    )
    latest = chains["query_key"].give
    gain_far = swap(gain_give, "row")
    step("gate", "down")
    stays, moves, across, corner = call(
        input_back_kernel,
        [shape((rows, half), F32)] * 2 + [shape((rows, half))] * 2,
        [grads_back, side_back, w_query, w_key, w_value, w_far, *gh_mine, *gh_theirs],
        "input_back",
        after=(latest,),
    )
    latest = across
    across = lax.ppermute(across, pair, [(1, 0), (2, 3)])
    corner = lax.ppermute(corner, pair, to_corner)
    moves = lax.ppermute(moves, pair, from_same)

    def gain_step(mine, received):
        nonlocal latest
        (latest,) = call(
            total_kernel, [shape(mine.shape, F32)], [mine, received], "gain_sum", after=(latest,)
        )
        return latest

    step("up", "out_value", "gate", "down")
    gain_total = gain_step(gain_mine, gain_far)
    step("up", "query_key", "gate", "out_value")
    for bit in range(dp_bits() - 1):
        gain_total = gain_step(gain_total, dp_exchange(gain_total, bit))
        step("query_key", "up")
    (block_out,) = call(
        choose_kernel,
        [shape((rows, half), F32)],
        [out_mine, out_beside],
        "block_out",
        after=(latest,),
    )
    (grad_input,) = call(
        grad_input_kernel,
        [shape((rows, half), F32)],
        [stays, moves, across, corner],
        "grad_input",
        after=(block_out,),
    )
    latest = grad_input
    step("out_value", "gate", "out_value", "query_key", "down", "up", "query_key", "out_value")
    step("up", "query_key", "gate", "out_value", "up", "query_key")
    gain_out = call(
        gains_out_kernel,
        [shape((1, half), F32)] * 2 + [shape((1, width), F32)] * 2,
        [gain_total, dp_exchange(gain_total, dp_bits() - 1)],
        "gains_out",
    )
    grad_mlpgain, grad_attngain, grad_qgain, grad_kgain = [row[0] for row in gain_out]
    for chain in chains.values():
        while chain.stage < 2 * scatter_bits:
            step(chain.name)
    (grad_down,) = chains["down"].out
    (grad_gate,) = chains["gate"].out
    (grad_up,) = chains["up"].out
    grad_out, grad_value = chains["out_value"].out
    grad_query, grad_key = chains["query_key"].out
    return (
        block_out,
        grad_input,
        grad_query,
        grad_key,
        grad_value,
        grad_out,
        grad_gate,
        grad_up,
        grad_down,
        grad_qgain,
        grad_kgain,
        grad_attngain,
        grad_mlpgain,
    )


def solution(mesh):
    tokens = P(("dp", "col"), "row")
    grid, turned = P("row", "col"), P("col", "row")
    in_specs = (
        tokens,
        grid,
        grid,
        grid,
        turned,
        grid,
        grid,
        turned,
        P("col"),
        P("col"),
        P("row"),
        P("row"),
        tokens,
    )
    out_specs = (
        tokens,
        tokens,
        grid,
        grid,
        grid,
        turned,
        grid,
        grid,
        turned,
        P("col"),
        P("col"),
        P("row"),
        P("row"),
    )
    return jax.shard_map(
        on_device, mesh=mesh, in_specs=in_specs, out_specs=out_specs, check_vma=False
    )
```

```python
import functools
import math

import jax
import jax.numpy as jnp
import numpy as np
from jax import lax
from jax.experimental import pallas as pl
from jax.experimental.pallas import tpu as pltpu
from jax.sharding import PartitionSpec as P

D = 1024
HEAD = 64
SEQ = 512
EPSILON = 1e-06
ROPE_BASE = 500000.0
MASKED = -1e30
CHUNK = 256
TILE = 256
LANES = 128
FACTOR = 1.0 / math.sqrt(HEAD)

F32 = jnp.float32
BF16 = jnp.bfloat16


def swap(values, axis):
    return lax.ppermute(values, axis, [(0, 1), (1, 0)])


def dot(left, right):
    return jnp.dot(left, right, preferred_element_type=F32)


def dot_t(left, right):
    return lax.dot_general(left, right, (((1,), (1,)), ((), ())), preferred_element_type=F32)


def t_dot(left, right):
    return lax.dot_general(left, right, (((0,), (0,)), ((), ())), preferred_element_type=F32)


def shape(dims, kind=BF16):
    return jax.ShapeDtypeStruct(dims, kind)


def call(kernel, outs, args, name, scratch=(), after=()):
    count = len(args)
    skip = len(after)
    vmem = pl.BlockSpec(memory_space=pltpu.VMEM)
    def body(*refs):
        kernel(*refs[:count], *refs[count + skip :])

    return pl.pallas_call(
        body,
        out_shape=tuple(outs),
        in_specs=[vmem] * count + [pl.BlockSpec(memory_space=pl.ANY)] * skip,
        out_specs=tuple([vmem] * len(outs)),
        scratch_shapes=scratch,
        compiler_params=pltpu.CompilerParams(
            vmem_limit_bytes=12 << 20, fuse_transposed_lhs_in_matmul=True
        ),
        cost_estimate=pl.CostEstimate(flops=1, bytes_accessed=1, transcendentals=0),
        name=name,
    )(*args, *after)


def tiles(extent, size=TILE):
    return [slice(at, min(at + size, extent)) for at in range(0, extent, size)]


def row_sum(values):
    return jnp.sum(values, axis=1, keepdims=True)


def columns_to_rows(columns):
    count = columns[0].shape[0]
    lane = lax.broadcasted_iota(jnp.int32, (count, LANES), 1)
    packed = jnp.zeros((count, LANES), F32)
    for index, column in enumerate(columns):
        packed = jnp.where(lane == index, column, packed)
    return packed.T[:8]


def rows_to_columns(rows, count):
    turned = jnp.concatenate([rows] * (LANES // 8), axis=0).T
    return [turned[:, i : i + 1] for i in range(count)]


def rms_scale(total):
    return lax.rsqrt(total / D + EPSILON)


def turn(values, cosine, sine_part):
    lane = lax.broadcasted_iota(jnp.int32, cosine.shape, 1)
    first = (lane % HEAD) < HEAD // 2
    out = []
    for tile in tiles(values.shape[1], LANES):
        part = values[:, tile]
        other = jnp.where(
            first, pltpu.roll(part, LANES - HEAD // 2, 1), pltpu.roll(part, HEAD // 2, 1)
        )
        out.append(part * cosine + other * sine_part)
    return jnp.concatenate(out, axis=1)


def rope_tables(count):
    half = HEAD // 2
    frequency = np.exp(np.arange(half, dtype=np.float32) * np.float32(-2.0 * math.log(ROPE_BASE) / HEAD))
    angles = np.arange(count).astype(np.float32)[:, None] * frequency[None, :]
    cosine, sine_part = np.cos(angles), np.sin(angles)
    repeats = LANES // HEAD
    return (
        jnp.asarray(np.concatenate([cosine, cosine] * repeats, axis=1)),
        jnp.asarray(np.concatenate([-sine_part, sine_part] * repeats, axis=1)),
    )


def lower_triangle():
    rows = lax.broadcasted_iota(jnp.int32, (CHUNK, CHUNK), 0)
    cols = lax.broadcasted_iota(jnp.int32, (CHUNK, CHUNK), 1)
    return rows >= cols


def keep_rows(pairs):
    for before, out in pairs:
        out[:CHUNK] = before[:CHUNK]


def head_mask(count, index):
    lane = lax.broadcasted_iota(jnp.int32, (count, LANES), 1)
    return (lane < HEAD) if index == 0 else (lane >= HEAD)


def only(mask, values):
    return jnp.where(mask, values, jnp.zeros_like(values))


def branch_of(mine, theirs):
    branch = mine[...].astype(F32) + theirs[...].astype(F32)
    return branch, rms_scale(row_sum(branch * branch))


def gain_of(mine, theirs, index):
    row = slice(index, index + 1)
    return jnp.concatenate([mine[row, :], theirs[row, :]], axis=1)


def on_own_chip():
    return lax.axis_index("row") == lax.axis_index("col")


def own_half():
    return lax.axis_index("dp") & 1


def is_inner():
    place = lax.axis_index("dp") >> 1
    return (place == 1) | (place == 2)


def norm_back(branch, scale, gain_vec, grad_out):
    weighted = grad_out * gain_vec
    inner = row_sum(weighted * branch)
    grad_branch = scale * weighted - branch * (scale * scale * scale * inner / D)
    grad_gain = jnp.sum(grad_out * branch * scale, axis=0, keepdims=True)
    return grad_branch, grad_gain


def pack_kernel(*refs):
    out = refs[-1]
    out[...] = jnp.zeros(out.shape, F32)
    for index, row in enumerate(refs[:-1]):
        out[index : index + 1, :] = row[...]


def choose_kernel(first, other, out):
    out[...] = jnp.where(on_own_chip(), first[...], other[...])


def choose_two_kernel(first, other, beside, corner, out, out_theirs):
    choose_kernel(first, other, out)
    choose_kernel(beside, corner, out_theirs)


def query_key_kernel(
    block, over, beside, corner, wq, wqt, wk, wkt, q_out, k_out, total_out, mine, theirs
):
    choose_two_kernel(block, over, beside, corner, mine, theirs)
    query_sum = 0.0
    key_sum = 0.0
    for tile in tiles(wq.shape[1]):
        query = dot(mine[...], wq[:, tile]) + dot(theirs[...], wqt[:, tile])
        q_out[:, tile] = query
        query_sum = query_sum + row_sum(query * query)
        key = dot(mine[...], wk[:, tile]) + dot(theirs[...], wkt[:, tile])
        k_out[:, tile] = key
        key_sum = key_sum + row_sum(key * key)
    total_out[...] = columns_to_rows([query_sum, key_sum])


def value_kernel(mine, theirs, wv, wvt, v_out):
    for tile in tiles(wv.shape[1]):
        v_out[:, tile] = (dot(mine[...], wv[:, tile]) + dot(theirs[...], wvt[:, tile])).astype(BF16)


def attention_kernel(
    chunk,
    queries,
    keys,
    values,
    totals,
    totals_over,
    qgain,
    kgain,
    cosine,
    sine_part,
    wo,
    wot,
    *rest,
):
    if chunk == 0:
        q_rot, k_rot, mixed, logs, partial = rest
    else:
        q_rot, k_rot, mixed, logs, partial = rest[4:]
        keep_rows(zip(rest[:4], rest[4:]))
    rows = slice(chunk * CHUNK, (chunk + 1) * CHUNK)
    query_total, key_total = rows_to_columns(totals[...] + totals_over[...], 2)
    query = queries[rows, :] * rms_scale(query_total[rows]) * qgain[...]
    key = keys[rows, :] * rms_scale(key_total[rows]) * kgain[...]
    q_rot[rows, :] = (turn(query, cosine[rows, :], sine_part[rows, :]) * FACTOR).astype(BF16)
    k_rot[rows, :] = turn(key, cosine[rows, :], sine_part[rows, :]).astype(BF16)
    visible = lower_triangle()
    lane = lax.broadcasted_iota(jnp.int32, (CHUNK, LANES), 1)
    log_tile = jnp.zeros((CHUNK, LANES), F32)
    for at, tile in enumerate(tiles(queries.shape[1], LANES)):
        total = jnp.zeros((CHUNK, LANES), F32)
        for index in range(2):
            query_head = only(head_mask(CHUNK, index), q_rot[rows, tile])
            scores = []
            for block in range(chunk + 1):
                part = dot_t(query_head, k_rot[block * CHUNK : (block + 1) * CHUNK, tile])
                scores.append(jnp.where(visible, part, MASKED) if block == chunk else part)
            peak = jnp.max(scores[0], axis=1, keepdims=True)
            for part in scores[1:]:
                peak = jnp.maximum(peak, jnp.max(part, axis=1, keepdims=True))
            scores = [jnp.exp(part - peak) for part in scores]
            denominator = sum(row_sum(part) for part in scores)
            inverse = 1.0 / denominator
            for block, part in enumerate(scores):
                value_rows = values[block * CHUNK : (block + 1) * CHUNK, tile]
                total = total + dot(
                    (part * inverse).astype(BF16), only(head_mask(CHUNK, index), value_rows)
                )
            log_tile = jnp.where(lane == 2 * at + index, peak + jnp.log(denominator), log_tile)
        mixed[rows, tile] = total.astype(BF16)
    logs[rows, :] = log_tile
    low = mixed[rows, :]
    half = wo.shape[1]
    partial[:, :half] = dot(low, wo[...]).astype(BF16)
    partial[:, half:] = dot(low, wot[...]).astype(BF16)


def forward_kernel(
    chunk, part, part_over, mine, theirs, gains, gains_far, wg, wgt, wu, wut, wd, wdt, *rest
):
    if chunk == 0:
        low_mine, side, hidden, gate, up, partial = rest
    else:
        low_mine, side, hidden, gate, up, partial = rest[2:]
        keep_rows(zip(rest[:2], rest[2:]))
    rows = slice(chunk * CHUNK, (chunk + 1) * CHUNK)
    branch, scale = branch_of(part, part_over)
    half, ff = mine.shape[1], wg.shape[1]
    normed = branch * scale * gain_of(gains, gains_far, 0)
    value = mine[rows, :].astype(F32) + normed[:, :half]
    hidden[:, :half] = value
    low_mine[rows, :] = value.astype(BF16)
    value = theirs[rows, :].astype(F32) + normed[:, half:]
    hidden[:, half:] = value
    side[rows, ff:] = value.astype(BF16)
    for tile in tiles(ff):
        left, right = low_mine[rows, :], side[rows, ff:]
        gate_act = dot(left, wg[:, tile]) + dot(right, wgt[:, tile])
        up_act = dot(left, wu[:, tile]) + dot(right, wut[:, tile])
        gate[:, tile] = gate_act
        up[:, tile] = up_act
        side[rows, tile] = (gate_act * jax.nn.sigmoid(gate_act) * up_act).astype(BF16)
    low = side[rows, :ff]
    partial[:, :half] = dot(low, wd[...]).astype(BF16)
    partial[:, half:] = dot(low, wdt[...]).astype(BF16)


def ff_norm_back_kernel(
    chunk, part, part_over, hidden, cot_mine, cot_theirs, gains, gains_far, *rest
):
    if chunk == 0:
        gff_mine, gff_theirs, out_mine, out_theirs, grad_gain = rest
    else:
        gain_before = rest[0]
        gff_mine, gff_theirs, out_mine, out_theirs, grad_gain = rest[5:]
        keep_rows(zip(rest[1:5], rest[5:]))
    rows = slice(chunk * CHUNK, (chunk + 1) * CHUNK)
    branch, scale = branch_of(part, part_over)
    half = cot_mine.shape[1]
    gain = gain_of(gains, gains_far, 1)
    block_out = hidden[...] + branch * scale * gain
    out_mine[rows, :] = block_out[:, :half]
    out_theirs[rows, :] = block_out[:, half:]
    upstream = jnp.concatenate([cot_mine[rows, :], cot_theirs[rows, :]], axis=1).astype(F32)
    grad_branch, gained = norm_back(branch, scale, gain, upstream)
    grad_gain[...] = gained if chunk == 0 else gain_before[...] + gained
    gff_mine[rows, :] = grad_branch[:, :half].astype(BF16)
    gff_theirs[rows, :] = grad_branch[:, half:].astype(BF16)


def backward_kernel(
    chunk, gff_mine, gff_theirs, gate, up, wd, wdt, wg, wgt, wu, wut, *rest
):
    if chunk == 0:
        grads, partial = rest
    else:
        grads, partial = rest[1:]
        keep_rows([rest[:2]])
    rows = slice(chunk * CHUNK, (chunk + 1) * CHUNK)
    half, ff = wd.shape[1], wg.shape[1]
    for tile in tiles(ff):
        grad_act = dot_t(gff_mine[rows, :], wd[tile, :]) + dot_t(gff_theirs[rows, :], wdt[tile, :])
        gate_act = gate[:, tile]
        sig = jax.nn.sigmoid(gate_act)
        grads[rows, tile] = (
            grad_act * up[:, tile] * sig * (1.0 + gate_act * (1.0 - sig))
        ).astype(BF16)
        there = slice(ff + tile.start, ff + tile.stop)
        grads[rows, there] = (grad_act * gate_act * sig).astype(BF16)
    left, right = grads[rows, :ff], grads[rows, ff:]
    for tile in tiles(half):
        partial[:, tile] = (dot_t(left, wg[tile, :]) + dot_t(right, wu[tile, :])).astype(BF16)
        there = slice(half + tile.start, half + tile.stop)
        partial[:, there] = (dot_t(left, wgt[tile, :]) + dot_t(right, wut[tile, :])).astype(BF16)


def attention_back_kernel(
    chunk,
    grad_part,
    grad_over,
    cot_mine,
    cot_theirs,
    part,
    part_over,
    gains,
    gains_far,
    wo,
    wot,
    q_rot,
    k_rot,
    values,
    logs,
    queries,
    keys,
    totals,
    totals_over,
    qgain,
    kgain,
    cosine,
    sine_part,
    *rest,
):
    half = wo.shape[1]
    width = queries.shape[1]
    if chunk == 0:
        gat_mine, side, gh_mine, gh_theirs, gqn, grad_gain, column, gk_sum, gv_sum = rest
    else:
        gain_before, column_in, gk_in, gv_in = rest[:4]
        gat_mine, side, gh_mine, gh_theirs, gqn, grad_gain, gkn, inner_out = rest[6:]
        keep_rows(zip(rest[4:6], rest[6:]))
    rows = slice(chunk * CHUNK, (chunk + 1) * CHUNK)
    seen = (chunk + 1) * CHUNK
    branch, scale = branch_of(part, part_over)
    grad_hidden = (
        jnp.concatenate([cot_mine[rows, :], cot_theirs[rows, :]], axis=1).astype(F32)
        + grad_part[...].astype(F32)
        + grad_over[...].astype(F32)
    )
    gh_mine[...] = grad_hidden[:, :half]
    gh_theirs[...] = grad_hidden[:, half:]
    grad_branch, gained = norm_back(branch, scale, gain_of(gains, gains_far, 0), grad_hidden)
    grad_gain[...] = gained if chunk == 0 else gain_before[...] + gained
    gat_mine[rows, :] = grad_branch[:, :half].astype(BF16)
    side[rows, :half] = grad_branch[:, half:].astype(BF16)
    grad_mixed = (
        dot_t(gat_mine[rows, :], wo[...]) + dot_t(side[rows, :half], wot[...])
    ).astype(BF16)
    visible = lower_triangle()
    query_total, key_total = rows_to_columns(totals[...] + totals_over[...], 2)
    query_inner = jnp.zeros((CHUNK, 1), F32)
    key_inner = jnp.zeros((seen, 1), F32)
    for at, tile in enumerate(tiles(width, LANES)):
        grad_query = jnp.zeros((CHUNK, LANES), F32)
        grad_key = [jnp.zeros((CHUNK, LANES), F32) for _ in range(chunk + 1)]
        grad_value = [jnp.zeros((CHUNK, LANES), F32) for _ in range(chunk + 1)]
        for index in range(2):
            mask = head_mask(CHUNK, index)
            query_head = only(mask, q_rot[rows, tile])
            grad_head = only(mask, grad_mixed[:, tile])
            log_column = logs[rows, 2 * at + index : 2 * at + index + 1]
            weights, grads = [], []
            for block in range(chunk + 1):
                span = slice(block * CHUNK, (block + 1) * CHUNK)
                scores = dot_t(query_head, k_rot[span, tile])
                if block == chunk:
                    scores = jnp.where(visible, scores, MASKED)
                weights.append(jnp.exp(scores - log_column))
                grads.append(dot_t(grad_head, values[span, tile]))
            inner = sum(row_sum(w * g) for w, g in zip(weights, grads))
            for block in range(chunk + 1):
                span = slice(block * CHUNK, (block + 1) * CHUNK)
                weight = weights[block]
                grad_scores = (weight * (grads[block] - inner)).astype(BF16)
                grad_value[block] = grad_value[block] + t_dot(weight.astype(BF16), grad_head)
                grad_query = grad_query + dot(grad_scores, only(mask, k_rot[span, tile]))
                grad_key[block] = grad_key[block] + t_dot(grad_scores, query_head)
        back = turn(grad_query * FACTOR, cosine[rows, :], -sine_part[rows, :])
        gqn[:, tile] = back
        query_inner = query_inner + row_sum(back * qgain[:, tile] * queries[rows, tile])
        if chunk == 0:
            gk_sum[:, tile] = grad_key[0]
            gv_sum[:, tile] = grad_value[0]
        else:
            key_all = jnp.concatenate([gk_in[:, tile] + grad_key[0], grad_key[1]], axis=0)
            value_all = jnp.concatenate([gv_in[:, tile] + grad_value[0], grad_value[1]], axis=0)
            side[:, half + tile.start : half + tile.stop] = value_all.astype(BF16)
            back = turn(key_all, cosine[...], -sine_part[...])
            gkn[:, tile] = back
            key_inner = key_inner + row_sum(back * kgain[:, tile] * keys[:, tile])
    if chunk == 0:
        column[...] = jnp.broadcast_to(query_inner, (CHUNK, LANES))
    else:
        query_inner = jnp.concatenate([column_in[:, :1], query_inner], axis=0)
        inner_out[...] = columns_to_rows([query_inner, key_inner])


def query_key_back_kernel(
    gqn_first,
    gqn_second,
    gkn,
    queries,
    keys,
    totals,
    totals_over,
    inner,
    inner_over,
    qgain,
    kgain,
    mlp_part,
    attn_part,
    grads,
    gain_mine,
    gain_give,
):
    width = queries.shape[1]
    half = gain_mine.shape[1]
    for out, columns in ((gain_mine, slice(0, half)), (gain_give, slice(half, 2 * half))):
        out[...] = jnp.zeros(out.shape, F32)
        out[0:1, :] = mlp_part[:, columns]
        out[1:2, :] = attn_part[:, columns]
    query_total, key_total = rows_to_columns(totals[...] + totals_over[...], 2)
    query_inner, key_inner = rows_to_columns(inner[...] + inner_over[...], 2)
    gqn = jnp.concatenate([gqn_first[...], gqn_second[...]], axis=0)
    for at, raw, back, total, sums, gain, low in (
        (2, queries, gqn, query_total, query_inner, qgain, grads.at[:, :width]),
        (3, keys, gkn[...], key_total, key_inner, kgain, grads.at[:, width:]),
    ):
        scale = rms_scale(total)
        value = raw[...]
        low[...] = (
            scale * (back * gain[...]) - value * (scale * scale * scale * sums / D)
        ).astype(BF16)
        gained = jnp.sum(back * value * scale, axis=0, keepdims=True)
        gain_mine[at : at + 1, :] = gained
        gain_give[at : at + 1, :] = gained


def weight_kernel(count, products, *refs):
    keep, *give, plain = refs[-2 - count :]

    def view(operand):
        index, start, stop = operand
        return refs[index].at[:, start:stop]

    at = 0
    for product in products:
        left, left_far, right, right_far = [view(operand) for operand in product]
        width = product[2][2] - product[2][1]
        for tile in tiles(plain.shape[0]):
            plain[tile, at : at + width] = (
                t_dot(left[:, tile], right[...]) + t_dot(left_far[:, tile], right_far[...])
            ).astype(BF16)
        at += width
    half = keep.shape[0]
    mine = pl.multiple_of(own_half() * half, half)
    theirs = pl.multiple_of((1 - own_half()) * half, half)
    keep[...] = plain[pl.ds(mine, half), :]
    size = half // count
    for index, out in enumerate(give):
        out[...] = plain[pl.ds(theirs + index * size, size), :]


def add_kernel(mine, *rest):
    out = rest[-1]
    at = 0
    for piece in rest[:-1]:
        rows = slice(at, at + piece.shape[0])
        out[rows, :] = (mine[rows, :].astype(F32) + piece[...].astype(F32)).astype(BF16)
        at = rows.stop


def inner_kernel(mine, received, out):
    out[...] = jnp.where(is_inner(), mine[...], received[...])


def finish_kernel(mine, received, *outs):
    half = mine.shape[0]
    for place, source in enumerate((mine, received)):
        to = pl.multiple_of((own_half() ^ place) * half, half)
        column = 0
        for out in outs:
            width = out.shape[1]
            out[pl.ds(to, half), :] = source[:, column : column + width].astype(F32)
            column += width


def total_kernel(mine, received, out):
    out[...] = mine[...] + received[...]


def gains_out_kernel(mine, received, *outs):
    for index, out in enumerate(outs):
        out[...] = mine[index : index + 1, :] + received[index : index + 1, :]


def grad_input_kernel(stays, moves, across, corner, out):
    own = on_own_chip()
    out[...] = jnp.where(own, stays[...], moves[...]) + jnp.where(
        own, across[...], corner[...]
    ).astype(F32)


def input_back_kernel(
    grads, side, wq, wqt, wk, wkt, wv, wvt, *rest
):
    width = wq.shape[1]
    gq, gk = grads.at[:, :width], grads.at[:, width:]
    gv = side.at[:, side.shape[1] - width :]
    gh_mine, gh_theirs = rest[:2], rest[2:4]
    stays, moves, across, corner = rest[4:]
    for tile in tiles(wq.shape[0]):
        mine = (
            dot_t(gq[...], wq[tile, :]) + dot_t(gk[...], wk[tile, :]) + dot_t(gv[...], wv[tile, :])
        )
        theirs = (
            dot_t(gq[...], wqt[tile, :])
            + dot_t(gk[...], wkt[tile, :])
            + dot_t(gv[...], wvt[tile, :])
        )
        for chunk in range(2):
            rows = slice(chunk * CHUNK, (chunk + 1) * CHUNK)
            stays[rows, tile] = gh_mine[chunk][:, tile] + mine[rows]
            moves[rows, tile] = gh_theirs[chunk][:, tile] + theirs[rows]
        across[:, tile] = mine.astype(BF16)
        corner[:, tile] = theirs.astype(BF16)


def dp_exchange(values, bit):
    size = lax.axis_size("dp")
    return lax.ppermute(values, "dp", [(i, i ^ (1 << bit)) for i in range(size)])


def dp_bits():
    return lax.axis_size("dp").bit_length() - 1


def along_line(values, moves):
    pairs = [(2 * a + half, 2 * b + half) for a, b in moves for half in range(2)]
    return lax.ppermute(values, "dp", pairs)


def in_turn(operands, received):
    return lax.optimization_barrier((operands, received))


class Chain:
    def __init__(self, name, widths, keep, give):
        self.name, self.widths, self.keep, self.give = name, widths, keep, give
        self.back = False
        self.received = None

    def kernel(self, body, args, part, after, outs=None):
        out = call(
            body, outs or [shape(self.keep.shape)], args, f"{self.name}_{part}", after=after
        )
        if outs is None:
            (self.keep,) = out
        else:
            self.out = out
        return out[0]

    def combine(self, body, part, after):
        return self.kernel(body, [self.keep, *self.received], part, after)

    def finish(self, after):
        high = 2 * self.keep.shape[0]
        outs = [shape((high, w), F32) for w in self.widths]
        return self.kernel(finish_kernel, [self.keep, *self.received], "out", after, outs)


LINE = ((0, 1), (3, 2)), ((1, 2), (2, 1)), ((1, 0), (2, 3))


class Lanes:
    def __init__(self):
        self.line = [None, None, None]
        self.latest = None

    def send_y(self, chain, before=None):
        operands = [chain.keep] if chain.back else list(chain.give)
        if before is not None:
            operands, before.received = in_turn(operands, before.received)
        chain.received = [dp_exchange(piece, 0) for piece in operands]

    def pass_on(self, index, chain):
        before, self.line[index] = self.line[index], chain
        if before is not None and chain is not None:
            chain.keep, before.received = in_turn(chain.keep, before.received)
        if chain is not None:
            chain.received = [along_line(chain.keep, LINE[index])]
        return before

    def advance(self, chain, following=None):
        if following is not None:
            self.send_y(following, chain)
        done = None
        if chain.back:
            done, chain = chain, None
        else:
            self.latest = chain.combine(add_kernel, "y", (self.latest,))
            if lax.axis_size("dp") != 8:
                for bit in range(1, dp_bits()):
                    other = dp_exchange(chain.keep, bit).astype(F32)
                    chain.keep = (chain.keep.astype(F32) + other).astype(BF16)
                chain.back = True
                chain = None
        for index, (body, part) in enumerate(
            ((add_kernel, "in"), (add_kernel, "across"), (inner_kernel, "out"))
        ):
            chain = self.pass_on(index, chain)
            if chain is not None:
                self.latest = chain.combine(body, f"z_{part}", (self.latest,))
        if chain is not None:
            chain.back = True
        if done is not None:
            self.latest = done.finish((self.latest,))


def on_device(
    block_in,
    w_query,
    w_key,
    w_value,
    w_output,
    w_gate,
    w_up,
    w_down,
    qnorm_gain,
    knorm_gain,
    attn_gain,
    mlp_gain,
    cotangent,
):
    rows, half = block_in.shape
    width = w_query.shape[1]
    ff = w_gate.shape[1]
    pair = ("row", "col")

    to_over = [(0, 1), (3, 2)]
    to_corner = [(1, 2), (2, 1)]
    to_beside = [(2, 0), (1, 3)]
    from_same = [(0, 2), (3, 1)]

    in_over = lax.ppermute(block_in, pair, to_over)
    in_corner = lax.ppermute(block_in, pair, to_corner)
    in_beside = lax.ppermute(block_in, pair, to_beside)
    wq_far, wk_far = swap(w_query, "row"), swap(w_key, "row")
    (gains,) = call(
        pack_kernel, [shape((8, half), F32)], [attn_gain[None], mlp_gain[None]], "gains"
    )
    qgain, kgain = qnorm_gain[None], knorm_gain[None]
    cosine, sine_part = rope_tables(rows)

    (cotangent, wv_give, wo_give), (in_corner,) = in_turn(
        [cotangent, w_value, w_output], [in_corner]
    )
    cot_over = lax.ppermute(cotangent, pair, to_over)
    cot_corner = lax.ppermute(cotangent, pair, to_corner)
    wv_far, wo_far = swap(wv_give, "row"), swap(wo_give, "row")

    queries, keys, totals, in_mine, in_theirs = call(
        query_key_kernel,
        [shape((rows, width), F32)] * 2 + [shape((8, rows), F32)] + [shape((rows, half))] * 2,
        [block_in, in_over, in_beside, in_corner, w_query, wq_far, w_key, wk_far],
        "query_key",
    )
    totals_over = swap(totals, "col")
    (values,) = call(
        value_kernel,
        [shape((rows, width))],
        [in_mine, in_theirs, w_value, wv_far],
        "value",
    )
    given = [w_gate, w_up, w_down, gains, cotangent]
    given, (totals_over,) = in_turn(given, [totals_over])
    wg_far, wu_far, wd_far, gains_far = [swap(value, "row") for value in given[:4]]
    cot_beside = lax.ppermute(given[4], pair, to_beside)
    (cot_mine,) = call(
        choose_kernel, [shape((rows, half))], [cotangent, cot_over], "cotangent_mine"
    )
    (cot_theirs,) = call(
        choose_kernel, [shape((rows, half))], [cot_beside, cot_corner], "cotangent_theirs"
    )

    attention_args = [
        queries,
        keys,
        values,
        totals,
        totals_over,
        qgain,
        kgain,
        cosine,
        sine_part,
        w_output,
        wo_far,
    ]
    attention_outs = [shape((rows, width))] * 3 + [
        shape((rows, LANES), F32),
        shape((CHUNK, D)),
    ]
    *kept, first = call(
        functools.partial(attention_kernel, 0), attention_outs, attention_args, "attention_0",
        after=(cot_mine, cot_theirs),
    )
    first_over = swap(first, "col")
    *kept, second = call(
        functools.partial(attention_kernel, 1), attention_outs, attention_args + kept, "attention_1"
    )
    q_rot, k_rot, mixed, logs = kept
    (second, mixed, in_theirs), (first_over,) = in_turn([second, mixed, in_theirs], [first_over])
    second_over = swap(second, "col")
    mixed_far = swap(mixed, "row")
    in_fix = lax.ppermute(in_theirs, pair, to_beside)
    parts = [first, second]
    def forward(chunk, over, kept, after):
        return call(
            functools.partial(forward_kernel, chunk),
            [shape((rows, half)), shape((rows, ff + half)), shape((CHUNK, D), F32)]
            + [shape((CHUNK, ff), F32)] * 2
            + [shape((CHUNK, D))],
            [parts[chunk], over, in_mine, in_theirs, gains, gains_far]
            + [w_gate, wg_far, w_up, wu_far, w_down, wd_far]
            + kept,
            f"forward_{chunk}",
            after=after,
        )

    low_mine, side, *saved, ff_first = forward(0, first_over, [], ())
    saved_all = [saved]
    (in_far,) = call(
        choose_kernel, [shape((rows, half))], [in_fix, block_in], "in_far", after=(ff_first,)
    )
    (ff_first,), (second_over,) = in_turn([ff_first], [second_over])
    parts_over = [first_over, second_over]
    ff_first_over = swap(ff_first, "col")
    low_mine, side, *saved, ff_second = forward(
        1, second_over, [low_mine, side], (in_far, mixed_far)
    )
    saved_all.append(saved)
    (ff_second, side), (ff_first_over,) = in_turn([ff_second, side], [ff_first_over])
    ff_second_over = swap(ff_second, "col")
    side_far = swap(side, "row")

    def weight_grad(name, arrays, products, after, count=1):
        high = products[0][0][2] - products[0][0][1]
        widths = [right[2] - right[1] for _, _, right, _ in products]
        keep, *give = call(
            functools.partial(weight_kernel, count, products),
            [shape((high // 2, sum(widths)))]
            + [shape((high // 2 // count, sum(widths)))] * count,
            arrays,
            name,
            scratch=[pltpu.VMEM((high, sum(widths)), BF16)],
            after=after,
        )
        return Chain(name, widths, keep, give)

    def ff_norm_back(chunk, mine, over, more, after):
        return call(
            functools.partial(ff_norm_back_kernel, chunk),
            [shape((rows, half))] * 2 + [shape((rows, half), F32)] * 2 + [shape((1, D), F32)],
            [mine, over, saved_all[chunk][0], cot_mine, cot_theirs, gains, gains_far, *more],
            f"ff_norm_back_{chunk}",
            after=after,
        )

    def backward(chunk, more, after):
        return call(
            functools.partial(backward_kernel, chunk),
            [shape((rows, 2 * ff)), shape((CHUNK, D))],
            [gff_mine, gff_theirs, *saved_all[chunk][1:]]
            + [w_down, wd_far, w_gate, wg_far, w_up, wu_far]
            + more,
            f"backward_{chunk}",
            after=after,
        )

    *kept, mlp_part = ff_norm_back(0, ff_first, ff_first_over, [], ())
    gff_mine, gff_theirs, _, _ = kept
    grads, gh_first = backward(0, [], ())
    (gh_first,), (ff_second_over,) = in_turn([gh_first], [ff_second_over])
    gh_first_over = swap(gh_first, "col")
    *kept, mlp_part = ff_norm_back(
        1, ff_second, ff_second_over, [mlp_part, *kept], (side_far,)
    )
    gff_mine, gff_theirs, out_mine, out_theirs = kept
    gff_far = swap(gff_theirs, "row")
    grads, gh_second = backward(1, [grads], ())
    lanes = Lanes()
    down = weight_grad(
        "down",
        [side, side_far, gff_mine, gff_far],
        [((0, 0, ff), (1, 0, ff), (2, 0, half), (3, 0, half))],
        (gh_second,),
    )
    lanes.send_y(down)
    (gh_second, grads), (gh_first_over, down.keep) = in_turn(
        [gh_second, grads], [gh_first_over, down.keep]
    )
    gh_second_over = swap(gh_second, "col")
    grads_far = swap(grads, "row")
    grad_parts, grad_over = [gh_first, gh_second], [gh_first_over, gh_second_over]

    def ff_grad(name, start, after):
        span = (start, start + ff)
        return weight_grad(
            name,
            [low_mine, side_far, grads, grads_far],
            [((0, 0, half), (1, ff, ff + half), (2, *span), (3, *span))],
            after,
        )

    latest = down.keep
    gh_mine, gh_theirs, gqn = [], [], []
    for chunk in range(2):
        args = [
            grad_parts[chunk],
            grad_over[chunk],
            cot_mine,
            cot_theirs,
            parts[chunk],
            parts_over[chunk],
            gains,
            gains_far,
            w_output,
            wo_far,
            q_rot,
            k_rot,
            values,
            logs,
            queries,
            keys,
            totals,
            totals_over,
            qgain,
            kgain,
            cosine,
            sine_part,
        ]
        outs = [shape((rows, half)), shape((rows, half + width))]
        outs += [shape((CHUNK, half), F32)] * 2 + [shape((CHUNK, width), F32), shape((1, D), F32)]
        if chunk == 0:
            outs += [shape((CHUNK, LANES), F32)] + [shape((CHUNK, width), F32)] * 2
        else:
            outs += [shape((rows, width), F32), shape((8, rows), F32)]
            args += [attn_part, column, gk_sum, gv_sum, gat_mine, side_back]
        gat_mine, side_back, gm, gt, gq_turned, attn_part, *more = call(
            functools.partial(attention_back_kernel, chunk),
            outs,
            args,
            f"attention_back_{chunk}",
            after=(latest,),
        )
        gh_mine.append(gm)
        gh_theirs.append(gt)
        gqn.append(gq_turned)
        if chunk == 0:
            column, gk_sum, gv_sum = more
            gate = ff_grad("gate", 0, (column,))
            lanes.send_y(gate)
            up = ff_grad("up", ff, (gate.keep,))
            latest = up.keep
        else:
            gkn, inner = more
    (inner, side_back), down.received = in_turn([inner, side_back], down.received)
    inner_over = swap(inner, "col")
    side_back_far = swap(side_back, "row")
    lanes.latest = inner
    lanes.advance(down, up)
    out_value = weight_grad(
        "out_value",
        [mixed, mixed_far, gat_mine, side_back_far, in_mine, in_far, side_back],
        [
            ((0, 0, width), (1, 0, width), (2, 0, half), (3, 0, half)),
            ((4, 0, half), (5, 0, half), (6, half, half + width), (3, half, half + width)),
        ],
        (lanes.latest,),
    )
    grads_back, gain_mine, gain_give = call(
        query_key_back_kernel,
        [shape((rows, 2 * width))] + [shape((8, half), F32)] * 2,
        [
            *gqn,
            gkn,
            queries,
            keys,
            totals,
            totals_over,
            inner,
            inner_over,
            qgain,
            kgain,
            mlp_part,
            attn_part,
        ],
        "query_key_back",
        after=(out_value.keep,),
    )
    grads_back_far = swap(grads_back, "row")
    lanes.latest = grads_back
    lanes.advance(gate)
    query_key = weight_grad(
        "query_key",
        [in_mine, in_far, grads_back, grads_back_far],
        [
            ((0, 0, half), (1, 0, half), (2, 0, width), (3, 0, width)),
            ((0, 0, half), (1, 0, half), (2, width, 2 * width), (3, width, 2 * width)),
        ],
        (lanes.latest,),
    )
    latest = query_key.keep
    stays, moves, across, corner = call(
        input_back_kernel,
        [shape((rows, half), F32)] * 2 + [shape((rows, half))] * 2,
        [grads_back, side_back, w_query, wq_far, w_key, wk_far, w_value, wv_far]
        + [*gh_mine, *gh_theirs],
        "input_back",
        after=(latest,),
    )
    lanes.latest = across
    gain_total = gain_mine
    gain_next = swap(gain_give, "row")
    moves = lax.ppermute(moves, pair, from_same)

    def gain_step(bit):
        nonlocal gain_total, gain_next
        (gain_total,) = call(
            total_kernel,
            [shape(gain_total.shape, F32)],
            [gain_total, gain_next],
            "gain_sum",
            after=(lanes.latest,),
        )
        lanes.latest = gain_total
        gain_next = dp_exchange(gain_total, bit)

    lanes.advance(up, out_value)
    gain_step(0)
    across = lax.ppermute(across, pair, [(1, 0), (2, 3)])
    lanes.advance(out_value, query_key)
    (corner,), (across,) = in_turn([corner], [across])
    corner = lax.ppermute(corner, pair, to_corner)
    for bit in range(1, dp_bits() - 1):
        gain_step(bit)
    lanes.advance(query_key, down)
    (grad_input,) = call(
        grad_input_kernel,
        [shape((rows, half), F32)],
        [stays, moves, across, corner],
        "grad_input",
        after=(lanes.latest,),
    )
    lanes.latest = grad_input
    gain_step(dp_bits() - 1)
    out_beside = lax.ppermute(out_theirs, pair, from_same)
    lanes.advance(down, gate)
    (block_out,) = call(
        choose_kernel,
        [shape((rows, half), F32)],
        [out_mine, out_beside],
        "block_out",
        after=(lanes.latest,),
    )
    gain_out = call(
        gains_out_kernel,
        [shape((1, half), F32)] * 2 + [shape((1, width), F32)] * 2,
        [gain_total, gain_next],
        "gains_out",
        after=(block_out,),
    )
    grad_mlpgain, grad_attngain, grad_qgain, grad_kgain = [row[0] for row in gain_out]
    lanes.latest = gain_out[0]
    lanes.advance(gate, up)
    lanes.advance(up, out_value)
    lanes.advance(out_value, query_key)
    lanes.advance(query_key)
    (grad_down,) = down.out
    (grad_gate,) = gate.out
    (grad_up,) = up.out
    grad_out, grad_value = out_value.out
    grad_query, grad_key = query_key.out
    return (
        block_out,
        grad_input,
        grad_query,
        grad_key,
        grad_value,
        grad_out,
        grad_gate,
        grad_up,
        grad_down,
        grad_qgain,
        grad_kgain,
        grad_attngain,
        grad_mlpgain,
    )


def solution(mesh):
    tokens = P(("dp", "col"), "row")
    grid, turned = P("row", "col"), P("col", "row")
    in_specs = (
        tokens,
        grid,
        grid,
        grid,
        turned,
        grid,
        grid,
        turned,
        P("col"),
        P("col"),
        P("row"),
        P("row"),
        tokens,
    )
    out_specs = (
        tokens,
        tokens,
        grid,
        grid,
        grid,
        turned,
        grid,
        grid,
        turned,
        P("col"),
        P("col"),
        P("row"),
        P("row"),
    )
    return jax.shard_map(
        on_device, mesh=mesh, in_specs=in_specs, out_specs=out_specs, check_vma=False
    )
```

```python
import functools
import math

import jax
import jax.numpy as jnp
import numpy as np
from jax import lax
from jax.experimental import pallas as pl
from jax.experimental.pallas import tpu as pltpu
from jax.sharding import PartitionSpec as P

D = 1024
HEAD = 64
SEQ = 512
EPSILON = 1e-06
ROPE_BASE = 500000.0
MASKED = -1e30
CHUNK = 256
PIECES = 2
TILE = 256
LANES = 128
FACTOR = 1.0 / math.sqrt(HEAD)

F32 = jnp.float32
BF16 = jnp.bfloat16


def swap(values, axis):
    return lax.ppermute(values, axis, [(0, 1), (1, 0)])


def dot(left, right):
    return jnp.dot(left, right, preferred_element_type=F32)


def dot_t(left, right):
    return lax.dot_general(left, right, (((1,), (1,)), ((), ())), preferred_element_type=F32)


def t_dot(left, right):
    return lax.dot_general(left, right, (((0,), (0,)), ((), ())), preferred_element_type=F32)


def shape(dims, kind=BF16):
    return jax.ShapeDtypeStruct(dims, kind)


def call(kernel, outs, args, name, scratch=(), after=()):
    count = len(args)
    skip = len(after)
    vmem = pl.BlockSpec(memory_space=pltpu.VMEM)
    def body(*refs):
        kernel(*refs[:count], *refs[count + skip :])

    return pl.pallas_call(
        body,
        out_shape=tuple(outs),
        in_specs=[vmem] * count + [pl.BlockSpec(memory_space=pl.ANY)] * skip,
        out_specs=tuple([vmem] * len(outs)),
        scratch_shapes=scratch,
        compiler_params=pltpu.CompilerParams(
            vmem_limit_bytes=12 << 20, fuse_transposed_lhs_in_matmul=True
        ),
        cost_estimate=pl.CostEstimate(flops=1, bytes_accessed=1, transcendentals=0),
        name=name,
    )(*args, *after)


def tiles(extent, size=TILE):
    return [slice(at, min(at + size, extent)) for at in range(0, extent, size)]


def row_sum(values):
    return jnp.sum(values, axis=1, keepdims=True)


def columns_to_rows(columns):
    count = columns[0].shape[0]
    lane = lax.broadcasted_iota(jnp.int32, (count, LANES), 1)
    packed = jnp.zeros((count, LANES), F32)
    for index, column in enumerate(columns):
        packed = jnp.where(lane == index, column, packed)
    return packed.T[:8]


def rows_to_columns(rows, count):
    turned = jnp.concatenate([rows] * (LANES // 8), axis=0).T
    return [turned[:, i : i + 1] for i in range(count)]


def rms_scale(total):
    return lax.rsqrt(total / D + EPSILON)


def turn(values, cosine, sine_part):
    lane = lax.broadcasted_iota(jnp.int32, cosine.shape, 1)
    first = (lane % HEAD) < HEAD // 2
    out = []
    for tile in tiles(values.shape[1], LANES):
        part = values[:, tile]
        other = jnp.where(
            first, pltpu.roll(part, LANES - HEAD // 2, 1), pltpu.roll(part, HEAD // 2, 1)
        )
        out.append(part * cosine + other * sine_part)
    return jnp.concatenate(out, axis=1)


def rope_tables(count):
    half = HEAD // 2
    frequency = np.exp(np.arange(half, dtype=np.float32) * np.float32(-2.0 * math.log(ROPE_BASE) / HEAD))
    angles = np.arange(count).astype(np.float32)[:, None] * frequency[None, :]
    cosine, sine_part = np.cos(angles), np.sin(angles)
    repeats = LANES // HEAD
    return (
        jnp.asarray(np.concatenate([cosine, cosine] * repeats, axis=1)),
        jnp.asarray(np.concatenate([-sine_part, sine_part] * repeats, axis=1)),
    )


def lower_triangle():
    rows = lax.broadcasted_iota(jnp.int32, (CHUNK, CHUNK), 0)
    cols = lax.broadcasted_iota(jnp.int32, (CHUNK, CHUNK), 1)
    return rows >= cols


def keep_rows(pairs):
    for before, out in pairs:
        out[:CHUNK] = before[:CHUNK]


def head_mask(count, index):
    lane = lax.broadcasted_iota(jnp.int32, (count, LANES), 1)
    return (lane < HEAD) if index == 0 else (lane >= HEAD)


def only(mask, values):
    return jnp.where(mask, values, jnp.zeros_like(values))


def total_of(mine, theirs):
    return jnp.concatenate(
        [a[...].astype(F32) + b[...].astype(F32) for a, b in zip(mine, theirs)], axis=0
    )


def branch_of(mine, theirs):
    branch = total_of(mine, theirs)
    return branch, rms_scale(row_sum(branch * branch))


def store_pieces(pieces, columns, values):
    at = 0
    for piece in pieces:
        high = piece.shape[0]
        piece[:, columns] = values[at : at + high].astype(BF16)
        at += high


def gain_of(mine, theirs, index):
    row = slice(index, index + 1)
    return jnp.concatenate([mine[row, :], theirs[row, :]], axis=1)


def on_own_chip():
    return lax.axis_index("row") == lax.axis_index("col")


def own_half():
    return lax.axis_index("dp") & 1


def is_inner():
    place = lax.axis_index("dp") >> 1
    return (place == 1) | (place == 2)


def norm_back(branch, scale, gain_vec, grad_out):
    weighted = grad_out * gain_vec
    inner = row_sum(weighted * branch)
    grad_branch = scale * weighted - branch * (scale * scale * scale * inner / D)
    grad_gain = jnp.sum(grad_out * branch * scale, axis=0, keepdims=True)
    return grad_branch, grad_gain


def pack_kernel(*refs):
    out = refs[-1]
    out[...] = jnp.zeros(out.shape, F32)
    for index, row in enumerate(refs[:-1]):
        out[index : index + 1, :] = row[...]


def choose_kernel(first, other, out):
    out[...] = jnp.where(on_own_chip(), first[...], other[...])


def choose_two_kernel(first, other, beside, corner, out, out_theirs):
    choose_kernel(first, other, out)
    choose_kernel(beside, corner, out_theirs)


def query_key_kernel(
    block, over, beside, corner, wq, wqt, wk, wkt, q_out, k_out, total_out, mine, theirs
):
    choose_two_kernel(block, over, beside, corner, mine, theirs)
    query_sum = 0.0
    key_sum = 0.0
    for tile in tiles(wq.shape[1]):
        query = dot(mine[...], wq[:, tile]) + dot(theirs[...], wqt[:, tile])
        q_out[:, tile] = query
        query_sum = query_sum + row_sum(query * query)
        key = dot(mine[...], wk[:, tile]) + dot(theirs[...], wkt[:, tile])
        k_out[:, tile] = key
        key_sum = key_sum + row_sum(key * key)
    total_out[...] = columns_to_rows([query_sum, key_sum])


def value_kernel(mine, theirs, wv, wvt, v_out):
    for tile in tiles(wv.shape[1]):
        v_out[:, tile] = (dot(mine[...], wv[:, tile]) + dot(theirs[...], wvt[:, tile])).astype(BF16)


def attention_kernel(
    chunk,
    queries,
    keys,
    values,
    totals,
    totals_over,
    qgain,
    kgain,
    cosine,
    sine_part,
    wo,
    wot,
    *rest,
):
    if chunk == 0:
        q_rot, k_rot, mixed, logs, *partial = rest
    else:
        q_rot, k_rot, mixed, logs, *partial = rest[4:]
        keep_rows(zip(rest[:4], rest[4:]))
    rows = slice(chunk * CHUNK, (chunk + 1) * CHUNK)
    query_total, key_total = rows_to_columns(totals[...] + totals_over[...], 2)
    query = queries[rows, :] * rms_scale(query_total[rows]) * qgain[...]
    key = keys[rows, :] * rms_scale(key_total[rows]) * kgain[...]
    q_rot[rows, :] = (turn(query, cosine[rows, :], sine_part[rows, :]) * FACTOR).astype(BF16)
    k_rot[rows, :] = turn(key, cosine[rows, :], sine_part[rows, :]).astype(BF16)
    visible = lower_triangle()
    lane = lax.broadcasted_iota(jnp.int32, (CHUNK, LANES), 1)
    log_tile = jnp.zeros((CHUNK, LANES), F32)
    for at, tile in enumerate(tiles(queries.shape[1], LANES)):
        total = jnp.zeros((CHUNK, LANES), F32)
        for index in range(2):
            query_head = only(head_mask(CHUNK, index), q_rot[rows, tile])
            scores = []
            for block in range(chunk + 1):
                part = dot_t(query_head, k_rot[block * CHUNK : (block + 1) * CHUNK, tile])
                scores.append(jnp.where(visible, part, MASKED) if block == chunk else part)
            peak = jnp.max(scores[0], axis=1, keepdims=True)
            for part in scores[1:]:
                peak = jnp.maximum(peak, jnp.max(part, axis=1, keepdims=True))
            scores = [jnp.exp(part - peak) for part in scores]
            denominator = sum(row_sum(part) for part in scores)
            inverse = 1.0 / denominator
            for block, part in enumerate(scores):
                value_rows = values[block * CHUNK : (block + 1) * CHUNK, tile]
                total = total + dot(
                    (part * inverse).astype(BF16), only(head_mask(CHUNK, index), value_rows)
                )
            log_tile = jnp.where(lane == 2 * at + index, peak + jnp.log(denominator), log_tile)
        mixed[rows, tile] = total.astype(BF16)
    logs[rows, :] = log_tile
    low = mixed[rows, :]
    half = wo.shape[1]
    store_pieces(partial, slice(0, half), dot(low, wo[...]))
    store_pieces(partial, slice(half, 2 * half), dot(low, wot[...]))


def forward_kernel(
    chunk, *refs
):
    part, part_over = refs[:PIECES], refs[PIECES : 2 * PIECES]
    forward_body(chunk, part, part_over, *refs[2 * PIECES :])


def forward_body(
    chunk, part, part_over, mine, theirs, gains, gains_far, wg, wgt, wu, wut, wd, wdt, *rest
):
    if chunk == 0:
        low_mine, side, hidden, gate, up, *partial = rest
    else:
        mixed = rest[0]
        low_mine, side, hidden, gate, up, *partial = rest[3:]
        keep_rows(zip(rest[1:3], rest[3:]))
        at = wg.shape[1] + mine.shape[1]
        side[:, at : at + mixed.shape[1]] = mixed[...]
        side[:, at + mixed.shape[1] :] = theirs[...]
    rows = slice(chunk * CHUNK, (chunk + 1) * CHUNK)
    branch, scale = branch_of(part, part_over)
    half, ff = mine.shape[1], wg.shape[1]
    normed = branch * scale * gain_of(gains, gains_far, 0)
    value = mine[rows, :].astype(F32) + normed[:, :half]
    hidden[:, :half] = value
    low_mine[rows, :] = value.astype(BF16)
    value = theirs[rows, :].astype(F32) + normed[:, half:]
    hidden[:, half:] = value
    side[rows, ff : ff + half] = value.astype(BF16)
    for tile in tiles(ff):
        left, right = low_mine[rows, :], side[rows, ff : ff + half]
        gate_act = dot(left, wg[:, tile]) + dot(right, wgt[:, tile])
        up_act = dot(left, wu[:, tile]) + dot(right, wut[:, tile])
        gate[:, tile] = gate_act
        up[:, tile] = up_act
        side[rows, tile] = (gate_act * jax.nn.sigmoid(gate_act) * up_act).astype(BF16)
    low = side[rows, :ff]
    store_pieces(partial, slice(0, half), dot(low, wd[...]))
    store_pieces(partial, slice(half, 2 * half), dot(low, wdt[...]))


def ff_norm_back_kernel(
    chunk, *refs
):
    part, part_over = refs[:PIECES], refs[PIECES : 2 * PIECES]
    hidden, cot_mine, cot_theirs, gains, gains_far, *rest = refs[2 * PIECES :]
    if chunk == 0:
        gff_mine, gff_theirs, out_mine, out_theirs, grad_gain = rest
    else:
        gain_before = rest[0]
        gff_mine, gff_theirs, out_mine, out_theirs, grad_gain = rest[5:]
        keep_rows(zip(rest[1:5], rest[5:]))
    rows = slice(chunk * CHUNK, (chunk + 1) * CHUNK)
    branch, scale = branch_of(part, part_over)
    half = cot_mine.shape[1]
    gain = gain_of(gains, gains_far, 1)
    block_out = hidden[...] + branch * scale * gain
    out_mine[rows, :] = block_out[:, :half]
    out_theirs[rows, :] = block_out[:, half:]
    upstream = jnp.concatenate([cot_mine[rows, :], cot_theirs[rows, :]], axis=1).astype(F32)
    grad_branch, gained = norm_back(branch, scale, gain, upstream)
    grad_gain[...] = gained if chunk == 0 else gain_before[...] + gained
    gff_mine[rows, :] = grad_branch[:, :half].astype(BF16)
    gff_theirs[rows, :] = grad_branch[:, half:].astype(BF16)


def backward_kernel(
    chunk, gff_mine, gff_theirs, gate, up, wd, wdt, wg, wgt, wu, wut, *rest
):
    if chunk == 0:
        grads, *partial = rest
    else:
        grads, *partial = rest[1:]
        keep_rows([rest[:2]])
    rows = slice(chunk * CHUNK, (chunk + 1) * CHUNK)
    half, ff = wd.shape[1], wg.shape[1]
    for tile in tiles(ff):
        grad_act = dot_t(gff_mine[rows, :], wd[tile, :]) + dot_t(gff_theirs[rows, :], wdt[tile, :])
        gate_act = gate[:, tile]
        sig = jax.nn.sigmoid(gate_act)
        grads[rows, tile] = (
            grad_act * up[:, tile] * sig * (1.0 + gate_act * (1.0 - sig))
        ).astype(BF16)
        there = slice(ff + tile.start, ff + tile.stop)
        grads[rows, there] = (grad_act * gate_act * sig).astype(BF16)
    left, right = grads[rows, :ff], grads[rows, ff:]
    for tile in tiles(half):
        store_pieces(partial, tile, dot_t(left, wg[tile, :]) + dot_t(right, wu[tile, :]))
        there = slice(half + tile.start, half + tile.stop)
        store_pieces(partial, there, dot_t(left, wgt[tile, :]) + dot_t(right, wut[tile, :]))


def attention_back_kernel(chunk, *refs):
    grad_part, grad_over, part, part_over = [
        refs[i * PIECES : (i + 1) * PIECES] for i in range(4)
    ]
    (
        cot_mine,
        cot_theirs,
        gains,
        gains_far,
        wo,
        wot,
        q_rot,
        k_rot,
        values,
        logs,
        queries,
        keys,
        totals,
        totals_over,
        qgain,
        kgain,
        cosine,
        sine_part,
        *rest,
    ) = refs[4 * PIECES :]
    half = wo.shape[1]
    width = queries.shape[1]
    if chunk == 0:
        gat_mine, side, gh_mine, gh_theirs, gqn, grad_gain, column, gk_sum, gv_sum = rest
    else:
        gain_before, column_in, gk_in, gv_in = rest[:4]
        gat_mine, side, gh_mine, gh_theirs, gqn, grad_gain, gkn, gv_low, inner_out = rest[6:]
        keep_rows(zip(rest[4:6], rest[6:]))
    rows = slice(chunk * CHUNK, (chunk + 1) * CHUNK)
    seen = (chunk + 1) * CHUNK
    branch, scale = branch_of(part, part_over)
    grad_hidden = (
        jnp.concatenate([cot_mine[rows, :], cot_theirs[rows, :]], axis=1).astype(F32)
        + total_of(grad_part, grad_over)
    )
    gh_mine[...] = grad_hidden[:, :half]
    gh_theirs[...] = grad_hidden[:, half:]
    grad_branch, gained = norm_back(branch, scale, gain_of(gains, gains_far, 0), grad_hidden)
    grad_gain[...] = gained if chunk == 0 else gain_before[...] + gained
    gat_mine[rows, :] = grad_branch[:, :half].astype(BF16)
    side[rows, :] = grad_branch[:, half:].astype(BF16)
    grad_mixed = (
        dot_t(gat_mine[rows, :], wo[...]) + dot_t(side[rows, :], wot[...])
    ).astype(BF16)
    visible = lower_triangle()
    query_total, key_total = rows_to_columns(totals[...] + totals_over[...], 2)
    query_inner = jnp.zeros((CHUNK, 1), F32)
    key_inner = jnp.zeros((seen, 1), F32)
    for at, tile in enumerate(tiles(width, LANES)):
        grad_query = jnp.zeros((CHUNK, LANES), F32)
        grad_key = [jnp.zeros((CHUNK, LANES), F32) for _ in range(chunk + 1)]
        grad_value = [jnp.zeros((CHUNK, LANES), F32) for _ in range(chunk + 1)]
        for index in range(2):
            mask = head_mask(CHUNK, index)
            query_head = only(mask, q_rot[rows, tile])
            grad_head = only(mask, grad_mixed[:, tile])
            log_column = logs[rows, 2 * at + index : 2 * at + index + 1]
            weights, grads = [], []
            for block in range(chunk + 1):
                span = slice(block * CHUNK, (block + 1) * CHUNK)
                scores = dot_t(query_head, k_rot[span, tile])
                if block == chunk:
                    scores = jnp.where(visible, scores, MASKED)
                weights.append(jnp.exp(scores - log_column))
                grads.append(dot_t(grad_head, values[span, tile]))
            inner = sum(row_sum(w * g) for w, g in zip(weights, grads))
            for block in range(chunk + 1):
                span = slice(block * CHUNK, (block + 1) * CHUNK)
                weight = weights[block]
                grad_scores = (weight * (grads[block] - inner)).astype(BF16)
                grad_value[block] = grad_value[block] + t_dot(weight.astype(BF16), grad_head)
                grad_query = grad_query + dot(grad_scores, only(mask, k_rot[span, tile]))
                grad_key[block] = grad_key[block] + t_dot(grad_scores, query_head)
        back = turn(grad_query * FACTOR, cosine[rows, :], -sine_part[rows, :])
        gqn[:, tile] = back
        query_inner = query_inner + row_sum(back * qgain[:, tile] * queries[rows, tile])
        if chunk == 0:
            gk_sum[:, tile] = grad_key[0]
            gv_sum[:, tile] = grad_value[0]
        else:
            key_all = jnp.concatenate([gk_in[:, tile] + grad_key[0], grad_key[1]], axis=0)
            value_all = jnp.concatenate([gv_in[:, tile] + grad_value[0], grad_value[1]], axis=0)
            gv_low[:, tile] = value_all.astype(BF16)
            back = turn(key_all, cosine[...], -sine_part[...])
            gkn[:, tile] = back
            key_inner = key_inner + row_sum(back * kgain[:, tile] * keys[:, tile])
    if chunk == 0:
        column[...] = jnp.broadcast_to(query_inner, (CHUNK, LANES))
    else:
        query_inner = jnp.concatenate([column_in[:, :1], query_inner], axis=0)
        inner_out[...] = columns_to_rows([query_inner, key_inner])


def query_key_back_kernel(
    gqn_first,
    gqn_second,
    gkn,
    queries,
    keys,
    totals,
    totals_over,
    inner,
    inner_over,
    qgain,
    kgain,
    mlp_part,
    attn_part,
    grads,
    gain_mine,
    gain_give,
):
    width = queries.shape[1]
    half = gain_mine.shape[1]
    for out, columns in ((gain_mine, slice(0, half)), (gain_give, slice(half, 2 * half))):
        out[...] = jnp.zeros(out.shape, F32)
        out[0:1, :] = mlp_part[:, columns]
        out[1:2, :] = attn_part[:, columns]
    query_total, key_total = rows_to_columns(totals[...] + totals_over[...], 2)
    query_inner, key_inner = rows_to_columns(inner[...] + inner_over[...], 2)
    gqn = jnp.concatenate([gqn_first[...], gqn_second[...]], axis=0)
    for at, raw, back, total, sums, gain, low in (
        (2, queries, gqn, query_total, query_inner, qgain, grads.at[:, :width]),
        (3, keys, gkn[...], key_total, key_inner, kgain, grads.at[:, width:]),
    ):
        scale = rms_scale(total)
        value = raw[...]
        low[...] = (
            scale * (back * gain[...]) - value * (scale * scale * scale * sums / D)
        ).astype(BF16)
        gained = jnp.sum(back * value * scale, axis=0, keepdims=True)
        gain_mine[at : at + 1, :] = gained
        gain_give[at : at + 1, :] = gained


GAIN_ROWS = 16


def weight_kernel(with_gains, products, *refs):
    keep, give, plain = refs[-3:]

    def view(operand):
        index, start, stop = operand
        return refs[index].at[:, start:stop]

    at = 0
    for product in products:
        left, left_far, right, right_far = [view(operand) for operand in product]
        width = product[2][2] - product[2][1]
        for tile in tiles(plain.shape[0]):
            plain[tile, at : at + width] = (
                t_dot(left[:, tile], right[...]) + t_dot(left_far[:, tile], right_far[...])
            ).astype(BF16)
        at += width
    half = plain.shape[0] // 2
    mine = pl.multiple_of(own_half() * half, half)
    theirs = pl.multiple_of((1 - own_half()) * half, half)
    keep[:half, :] = plain[pl.ds(mine, half), :]
    give[:half, :] = plain[pl.ds(theirs, half), :]
    if with_gains:
        gains = refs[-5][...] + refs[-4][...]
        width = gains.shape[1]
        row = lax.broadcasted_iota(jnp.int32, (GAIN_ROWS, width), 0)
        for at in range(0, plain.shape[1], width):
            index = 2 * at // width
            first = jnp.broadcast_to(gains[index : index + 1, :], row.shape)
            second = jnp.broadcast_to(gains[index + 1 : index + 2, :], row.shape)
            rows = jnp.where(row == 0, first, jnp.where(row == 1, second, 0.0)).astype(BF16)
            keep[half:, at : at + width] = rows
            give[half:, at : at + width] = rows


def add_kernel(mine, *rest):
    out = rest[-1]
    at = 0
    for piece in rest[:-1]:
        rows = slice(at, at + piece.shape[0])
        out[rows, :] = (mine[rows, :].astype(F32) + piece[...].astype(F32)).astype(BF16)
        at = rows.stop


def inner_kernel(mine, received, out):
    out[...] = jnp.where(is_inner(), mine[...], received[...])


def finish_kernel(mine, received, *outs):
    half = outs[0].shape[0] // 2
    for place, source in enumerate((mine, received)):
        to = pl.multiple_of((own_half() ^ place) * half, half)
        column = 0
        for out in outs:
            width = out.shape[1]
            out[pl.ds(to, half), :] = source[:half, column : column + width].astype(F32)
            column += width


def in_far_kernel(side_far, block, out):
    out[...] = jnp.where(on_own_chip(), side_far[:, side_far.shape[1] - out.shape[1] :], block[...])


def gains_out_kernel(total, *outs):
    width = outs[0].shape[1]
    rows = total[total.shape[0] - GAIN_ROWS :, :].astype(F32)
    for index, out in enumerate(outs):
        at = index // 2 * width
        out[...] = rows[index % 2 : index % 2 + 1, at : at + width]


def grad_input_kernel(stays, moves, across, corner, out):
    own = on_own_chip()
    out[...] = jnp.where(own, stays[...], moves[...]) + jnp.where(
        own, across[...], corner[...]
    ).astype(F32)


def input_back_kernel(
    grads, gv, wq, wqt, wk, wkt, wv, wvt, *rest
):
    width = wq.shape[1]
    gq, gk = grads.at[:, :width], grads.at[:, width:]
    gh_mine, gh_theirs = rest[:2], rest[2:4]
    stays, moves, across, corner = rest[4:]
    for tile in tiles(wq.shape[0]):
        mine = (
            dot_t(gq[...], wq[tile, :]) + dot_t(gk[...], wk[tile, :]) + dot_t(gv[...], wv[tile, :])
        )
        theirs = (
            dot_t(gq[...], wqt[tile, :])
            + dot_t(gk[...], wkt[tile, :])
            + dot_t(gv[...], wvt[tile, :])
        )
        for chunk in range(2):
            rows = slice(chunk * CHUNK, (chunk + 1) * CHUNK)
            stays[rows, tile] = gh_mine[chunk][:, tile] + mine[rows]
            moves[rows, tile] = gh_theirs[chunk][:, tile] + theirs[rows]
        across[:, tile] = mine.astype(BF16)
        corner[:, tile] = theirs.astype(BF16)


def dp_exchange(values, bit):
    size = lax.axis_size("dp")
    return lax.ppermute(values, "dp", [(i, i ^ (1 << bit)) for i in range(size)])


def dp_bits():
    return lax.axis_size("dp").bit_length() - 1


def along_line(values, moves):
    pairs = [(2 * a + half, 2 * b + half) for a, b in moves for half in range(2)]
    return lax.ppermute(values, "dp", pairs)


def in_turn(operands, received):
    return lax.optimization_barrier((operands, received))


class Chain:
    def __init__(self, name, high, widths, keep, give):
        self.name, self.high, self.widths, self.keep, self.give = name, high, widths, keep, give
        self.back = False
        self.received = None

    def kernel(self, body, args, part, after, outs=None):
        out = call(
            body, outs or [shape(self.keep.shape)], args, f"{self.name}_{part}", after=after
        )
        if outs is None:
            (self.keep,) = out
        else:
            self.out = out
        return out[0]

    def combine(self, body, part, after):
        return self.kernel(body, [self.keep, *self.received], part, after)

    def finish(self, after):
        outs = [shape((self.high, w), F32) for w in self.widths]
        return self.kernel(finish_kernel, [self.keep, *self.received], "out", after, outs)


LINE = ((0, 1), (3, 2)), ((1, 2), (2, 1)), ((1, 0), (2, 3))


class Lanes:
    def __init__(self):
        self.line = [None, None, None]
        self.latest = None

    def send_y(self, chain, before=None):
        operands = [chain.keep if chain.back else chain.give]
        if before is not None:
            operands, before.received = in_turn(operands, before.received)
        chain.received = [dp_exchange(piece, 0) for piece in operands]

    def pass_on(self, index, chain):
        before, self.line[index] = self.line[index], chain
        if before is not None and chain is not None:
            chain.keep, before.received = in_turn(chain.keep, before.received)
        if chain is not None:
            chain.received = [along_line(chain.keep, LINE[index])]
        return before

    def advance(self, chain, following=None, after=()):
        if following is not None:
            self.send_y(following, chain)
        done = None
        if chain.back:
            done, chain = chain, None
        else:
            self.latest = chain.combine(add_kernel, "y", (self.latest, *after))
            if lax.axis_size("dp") != 8:
                for bit in range(1, dp_bits()):
                    other = dp_exchange(chain.keep, bit).astype(F32)
                    chain.keep = (chain.keep.astype(F32) + other).astype(BF16)
                chain.back = True
                chain = None
        for index, (body, part) in enumerate(
            ((add_kernel, "in"), (add_kernel, "across"), (inner_kernel, "out"))
        ):
            chain = self.pass_on(index, chain)
            if chain is not None:
                self.latest = chain.combine(body, f"z_{part}", (self.latest,))
        if chain is not None:
            chain.back = True
        if done is not None:
            self.latest = done.finish((self.latest,))


def on_device(
    block_in,
    w_query,
    w_key,
    w_value,
    w_output,
    w_gate,
    w_up,
    w_down,
    qnorm_gain,
    knorm_gain,
    attn_gain,
    mlp_gain,
    cotangent,
):
    rows, half = block_in.shape
    width = w_query.shape[1]
    ff = w_gate.shape[1]
    pair = ("row", "col")

    to_over = [(0, 1), (3, 2)]
    to_corner = [(1, 2), (2, 1)]
    to_beside = [(2, 0), (1, 3)]
    from_same = [(0, 2), (3, 1)]

    in_over = lax.ppermute(block_in, pair, to_over)
    in_corner = lax.ppermute(block_in, pair, to_corner)
    in_beside = lax.ppermute(block_in, pair, to_beside)
    wq_far, wk_far = swap(w_query, "row"), swap(w_key, "row")
    (gains,) = call(
        pack_kernel, [shape((8, half), F32)], [attn_gain[None], mlp_gain[None]], "gains"
    )
    qgain, kgain = qnorm_gain[None], knorm_gain[None]
    cosine, sine_part = rope_tables(rows)

    (cotangent, wv_give, wo_give), (in_corner, in_over) = in_turn(
        [cotangent, w_value, w_output], [in_corner, in_over]
    )
    cot_over = lax.ppermute(cotangent, pair, to_over)
    cot_corner = lax.ppermute(cotangent, pair, to_corner)
    wv_far, wo_far = swap(wv_give, "row"), swap(wo_give, "row")

    queries, keys, totals, in_mine, in_theirs = call(
        query_key_kernel,
        [shape((rows, width), F32)] * 2 + [shape((8, rows), F32)] + [shape((rows, half))] * 2,
        [block_in, in_over, in_beside, in_corner, w_query, wq_far, w_key, wk_far],
        "query_key",
    )
    totals_over = swap(totals, "col")
    (values,) = call(
        value_kernel,
        [shape((rows, width))],
        [in_mine, in_theirs, w_value, wv_far],
        "value",
    )
    (cot_mine,) = call(
        choose_kernel, [shape((rows, half))], [cotangent, cot_over], "cotangent_mine"
    )
    given, (totals_over,) = in_turn([gains, cotangent], [totals_over])
    gains_far = swap(given[0], "row")
    cot_beside = lax.ppermute(given[1], pair, to_beside)
    (cot_theirs,) = call(
        choose_kernel, [shape((rows, half))], [cot_beside, cot_corner], "cotangent_theirs"
    )

    attention_args = [
        queries,
        keys,
        values,
        totals,
        totals_over,
        qgain,
        kgain,
        cosine,
        sine_part,
        w_output,
        wo_far,
    ]
    partial = [shape((CHUNK // PIECES, D))] * PIECES
    attention_outs = [shape((rows, width))] * 3 + [shape((rows, LANES), F32), *partial]

    def send_over(pieces, before=None):
        if before is not None:
            for index in range(PIECES):
                (pieces[index],), (before[index],) = in_turn([pieces[index]], [before[index]])
        return [swap(piece, "col") for piece in pieces]

    *kept, first_a, first_b = call(
        functools.partial(attention_kernel, 0),
        attention_outs,
        attention_args,
        "attention_0",
        after=(cot_mine, cot_theirs, gains_far),
    )
    first = [first_a, first_b]
    given, kept[-1:] = in_turn([w_gate, w_up, w_down], kept[-1:])
    wg_far, wu_far, wd_far = [swap(value, "row") for value in given]
    first_over = send_over(first)
    *kept, second_a, second_b = call(
        functools.partial(attention_kernel, 1),
        attention_outs,
        attention_args + kept,
        "attention_1",
    )
    q_rot, k_rot, mixed, logs = kept
    second = [second_a, second_b]
    second_over = send_over(second, first_over)
    parts, parts_over = [first, second], [first_over, second_over]

    side_width = ff + half + width + half

    def forward(chunk, over, kept, after):
        return call(
            functools.partial(forward_kernel, chunk),
            [shape((rows, half)), shape((rows, side_width)), shape((CHUNK, D), F32)]
            + [shape((CHUNK, ff), F32)] * 2
            + partial,
            [*parts[chunk], *over, in_mine, in_theirs, gains, gains_far]
            + [w_gate, wg_far, w_up, wu_far, w_down, wd_far]
            + kept,
            f"forward_{chunk}",
            after=after,
        )

    low_mine, side, *saved = forward(0, first_over, [], ())
    saved_all, ff_first = [saved[:3]], saved[3:]
    ff_first_over = send_over(ff_first, second_over)
    low_mine, side, *saved = forward(1, second_over, [mixed, low_mine, side], ())
    saved_all.append(saved[:3])
    ff_second = saved[3:]
    ff_second_over = send_over(ff_second, ff_first_over)

    def weight_grad(name, arrays, products, after, gains=()):
        high = products[0][0][2] - products[0][0][1]
        widths = [right[2] - right[1] for _, _, right, _ in products]
        extra = GAIN_ROWS if gains else 0
        keep, give = call(
            functools.partial(weight_kernel, bool(gains), products),
            [shape((high // 2 + extra, sum(widths)))] * 2,
            [*arrays, *gains],
            name,
            scratch=[pltpu.VMEM((high, sum(widths)), BF16)],
            after=after,
        )
        return Chain(name, high, widths, keep, give)

    def ff_norm_back(chunk, mine, over, more, after):
        return call(
            functools.partial(ff_norm_back_kernel, chunk),
            [shape((rows, half))] * 2 + [shape((rows, half), F32)] * 2 + [shape((1, D), F32)],
            [*mine, *over, saved_all[chunk][0], cot_mine, cot_theirs, gains, gains_far, *more],
            f"ff_norm_back_{chunk}",
            after=after,
        )

    def backward(chunk, more, after):
        return call(
            functools.partial(backward_kernel, chunk),
            [shape((rows, 2 * ff)), *partial],
            [gff_mine, gff_theirs, *saved_all[chunk][1:]]
            + [w_down, wd_far, w_gate, wg_far, w_up, wu_far]
            + more,
            f"backward_{chunk}",
            after=after,
        )

    *kept, mlp_part = ff_norm_back(0, ff_first, ff_first_over, [], ())
    gff_mine, gff_theirs, _, _ = kept
    grads, *gh_first = backward(0, [], ())
    gh_first_over = send_over(gh_first, ff_second_over)
    *kept, mlp_part = ff_norm_back(
        1, ff_second, ff_second_over, [mlp_part, *kept], ()
    )
    gff_mine, gff_theirs, out_mine, out_theirs = kept
    (side,), (gff_theirs,) = in_turn([side], [gff_theirs])
    side_far = swap(side, "row")
    gff_far = swap(gff_theirs, "row")
    out_beside = lax.ppermute(out_theirs, pair, from_same)
    grads, *gh_second = backward(1, [grads], ())
    lanes = Lanes()
    down = weight_grad(
        "down",
        [side, side_far, gff_mine, gff_far],
        [((0, 0, ff), (1, 0, ff), (2, 0, half), (3, 0, half))],
        (grads,),
    )
    (block_out,) = call(
        choose_kernel,
        [shape((rows, half), F32)],
        [out_mine, out_beside],
        "block_out",
        after=(down.keep,),
    )
    (in_far,) = call(
        in_far_kernel, [shape((rows, half))], [side_far, block_in], "in_far", after=(block_out,)
    )
    lanes.send_y(down)
    (gh_second, grads), (gh_first_over, down.keep, in_far) = in_turn(
        [gh_second, grads], [gh_first_over, down.keep, in_far]
    )
    gh_second_over = send_over(gh_second)
    grads_far = swap(grads, "row")
    grad_parts, grad_over = [gh_first, gh_second], [gh_first_over, gh_second_over]

    def ff_grad(name, start, after):
        span = (start, start + ff)
        return weight_grad(
            name,
            [low_mine, side_far, grads, grads_far],
            [((0, 0, half), (1, ff, ff + half), (2, *span), (3, *span))],
            after,
        )

    latest = down.keep
    gh_mine, gh_theirs, gqn = [], [], []
    for chunk in range(2):
        args = [
            *grad_parts[chunk],
            *grad_over[chunk],
            *parts[chunk],
            *parts_over[chunk],
            cot_mine,
            cot_theirs,
            gains,
            gains_far,
            w_output,
            wo_far,
            q_rot,
            k_rot,
            values,
            logs,
            queries,
            keys,
            totals,
            totals_over,
            qgain,
            kgain,
            cosine,
            sine_part,
        ]
        outs = [shape((rows, half))] * 2
        outs += [shape((CHUNK, half), F32)] * 2 + [shape((CHUNK, width), F32), shape((1, D), F32)]
        if chunk == 0:
            outs += [shape((CHUNK, LANES), F32)] + [shape((CHUNK, width), F32)] * 2
        else:
            outs += [shape((rows, width), F32), shape((rows, width)), shape((8, rows), F32)]
            args += [attn_part, column, gk_sum, gv_sum, gat_mine, gat_theirs]
        gat_mine, gat_theirs, gm, gt, gq_turned, attn_part, *more = call(
            functools.partial(attention_back_kernel, chunk),
            outs,
            args,
            f"attention_back_{chunk}",
            after=(latest,),
        )
        gh_mine.append(gm)
        gh_theirs.append(gt)
        gqn.append(gq_turned)
        if chunk == 0:
            column, gk_sum, gv_sum = more
            up = ff_grad("up", ff, (column,))
            gate = ff_grad("gate", 0, (up.keep,))
            lanes.latest = gate.keep
            lanes.advance(down, gate, grad_over[1])
            latest = lanes.latest
        else:
            gkn, gv, inner = more
    inner_over = swap(inner, "col")
    gat_far, gv_far = swap(gat_theirs, "row"), swap(gv, "row")
    grads_back, gain_mine, gain_give = call(
        query_key_back_kernel,
        [shape((rows, 2 * width))] + [shape((8, half), F32)] * 2,
        [
            *gqn,
            gkn,
            queries,
            keys,
            totals,
            totals_over,
            inner,
            inner_over,
            qgain,
            kgain,
            mlp_part,
            attn_part,
        ],
        "query_key_back",
        after=(gv,),
    )
    grads_back_far = swap(grads_back, "row")
    gain_far = swap(gain_give, "row")
    lanes.latest = grads_back
    lanes.advance(gate, up)
    out_value = weight_grad(
        "out_value",
        [mixed, side_far, gat_mine, gat_far, in_mine, in_far, gv, gv_far],
        [
            ((0, 0, width), (1, ff + half, ff + half + width), (2, 0, half), (3, 0, half)),
            ((4, 0, half), (5, 0, half), (6, 0, width), (7, 0, width)),
        ],
        (lanes.latest,),
    )
    lanes.latest = out_value.keep
    query_key = weight_grad(
        "query_key",
        [in_mine, in_far, grads_back, grads_back_far],
        [
            ((0, 0, half), (1, 0, half), (2, 0, width), (3, 0, width)),
            ((0, 0, half), (1, 0, half), (2, width, 2 * width), (3, width, 2 * width)),
        ],
        (lanes.latest,),
        (gain_mine, gain_far),
    )
    latest = query_key.keep
    stays, moves, across, corner = call(
        input_back_kernel,
        [shape((rows, half), F32)] * 2 + [shape((rows, half))] * 2,
        [grads_back, gv, w_query, wq_far, w_key, wk_far, w_value, wv_far]
        + [*gh_mine, *gh_theirs],
        "input_back",
        after=(latest,),
    )
    lanes.latest = across
    moves = lax.ppermute(moves, pair, from_same)
    across = lax.ppermute(across, pair, [(1, 0), (2, 3)])
    lanes.advance(up, out_value)
    (corner,), (across,) = in_turn([corner], [across])
    corner = lax.ppermute(corner, pair, to_corner)
    lanes.advance(out_value, query_key)
    lanes.advance(query_key, down)
    (grad_input,) = call(
        grad_input_kernel,
        [shape((rows, half), F32)],
        [stays, moves, across, corner],
        "grad_input",
        after=(lanes.latest,),
    )
    lanes.latest = grad_input
    lanes.advance(down, gate)
    lanes.advance(gate, up)
    lanes.advance(up, out_value)
    lanes.advance(out_value, query_key)
    gain_out = call(
        gains_out_kernel,
        [shape((1, half), F32)] * 2 + [shape((1, width), F32)] * 2,
        [query_key.keep],
        "gains_out",
        after=(lanes.latest,),
    )
    grad_mlpgain, grad_attngain, grad_qgain, grad_kgain = [row[0] for row in gain_out]
    lanes.latest = gain_out[0]
    lanes.advance(query_key)
    (grad_down,) = down.out
    (grad_gate,) = gate.out
    (grad_up,) = up.out
    grad_out, grad_value = out_value.out
    grad_query, grad_key = query_key.out
    return (
        block_out,
        grad_input,
        grad_query,
        grad_key,
        grad_value,
        grad_out,
        grad_gate,
        grad_up,
        grad_down,
        grad_qgain,
        grad_kgain,
        grad_attngain,
        grad_mlpgain,
    )


def solution(mesh):
    tokens = P(("dp", "col"), "row")
    grid, turned = P("row", "col"), P("col", "row")
    in_specs = (
        tokens,
        grid,
        grid,
        grid,
        turned,
        grid,
        grid,
        turned,
        P("col"),
        P("col"),
        P("row"),
        P("row"),
        tokens,
    )
    out_specs = (
        tokens,
        tokens,
        grid,
        grid,
        grid,
        turned,
        grid,
        grid,
        turned,
        P("col"),
        P("col"),
        P("row"),
        P("row"),
    )
    return jax.shard_map(
        on_device, mesh=mesh, in_specs=in_specs, out_specs=out_specs, check_vma=False
    )
```

```python
import functools
import math

import jax
import jax.numpy as jnp
import numpy as np
from jax import lax
from jax.experimental import pallas as pl
from jax.experimental.pallas import tpu as pltpu
from jax.sharding import PartitionSpec as P

D = 1024
HEAD = 64
SEQ = 512
EPSILON = 1e-06
ROPE_BASE = 500000.0
MASKED = -1e30
CHUNK = 256
PIECES = 2
TILE = 256
LANES = 128
FACTOR = 1.0 / math.sqrt(HEAD)

F32 = jnp.float32
BF16 = jnp.bfloat16


def swap(values, axis):
    return lax.ppermute(values, axis, [(0, 1), (1, 0)])


def dot(left, right):
    return jnp.dot(left, right, preferred_element_type=F32)


def dot_t(left, right):
    return lax.dot_general(left, right, (((1,), (1,)), ((), ())), preferred_element_type=F32)


def t_dot(left, right):
    return lax.dot_general(left, right, (((0,), (0,)), ((), ())), preferred_element_type=F32)


def shape(dims, kind=BF16):
    return jax.ShapeDtypeStruct(dims, kind)


def call(kernel, outs, args, name, scratch=(), after=(), far=(), flops=1):
    count, skip, fetched = len(args), len(after), len(far)
    vmem = pl.BlockSpec(memory_space=pltpu.VMEM)
    anywhere = pl.BlockSpec(memory_space=pl.ANY)
    buffers = [pltpu.VMEM(a.shape, a.dtype) for a in far]
    if fetched:
        buffers.append(pltpu.SemaphoreType.DMA((fetched,)))

    def body(*refs):
        sources, refs = refs[:fetched], refs[fetched:]
        copies = []
        if fetched:
            refs, local = refs[: -fetched - 1], refs[-fetched - 1 :]
            copies = [
                pltpu.make_async_copy(source, local[i], local[-1].at[i])
                for i, source in enumerate(sources)
            ]
            for copy in copies:
                copy.start()
            for copy in copies:
                copy.wait()
            sources = local[:-1]
        kernel(*sources, *refs[:count], *refs[count + skip :])

    return pl.pallas_call(
        body,
        out_shape=tuple(outs),
        in_specs=[anywhere] * fetched + [vmem] * count + [anywhere] * skip,
        out_specs=tuple([vmem] * len(outs)),
        scratch_shapes=[*scratch, *buffers],
        compiler_params=pltpu.CompilerParams(
            vmem_limit_bytes=12 << 20, fuse_transposed_lhs_in_matmul=True
        ),
        cost_estimate=pl.CostEstimate(flops=int(flops), bytes_accessed=1, transcendentals=0),
        name=name,
    )(*far, *args, *after)


def tiles(extent, size=TILE):
    return [slice(at, min(at + size, extent)) for at in range(0, extent, size)]


def row_sum(values):
    return jnp.sum(values, axis=1, keepdims=True)


def columns_to_rows(columns):
    count = columns[0].shape[0]
    lane = lax.broadcasted_iota(jnp.int32, (count, LANES), 1)
    packed = jnp.zeros((count, LANES), F32)
    for index, column in enumerate(columns):
        packed = jnp.where(lane == index, column, packed)
    return packed.T[:8]


def rows_to_columns(rows, count):
    turned = jnp.concatenate([rows] * (LANES // 8), axis=0).T
    return [turned[:, i : i + 1] for i in range(count)]


def rms_scale(total):
    return lax.rsqrt(total / D + EPSILON)


def turn(values, cosine, sine_part):
    lane = lax.broadcasted_iota(jnp.int32, cosine.shape, 1)
    first = (lane % HEAD) < HEAD // 2
    out = []
    for tile in tiles(values.shape[1], LANES):
        part = values[:, tile]
        other = jnp.where(
            first, pltpu.roll(part, LANES - HEAD // 2, 1), pltpu.roll(part, HEAD // 2, 1)
        )
        out.append(part * cosine + other * sine_part)
    return jnp.concatenate(out, axis=1)


def rope_tables(count):
    half = HEAD // 2
    frequency = np.exp(np.arange(half, dtype=np.float32) * np.float32(-2.0 * math.log(ROPE_BASE) / HEAD))
    angles = np.arange(count).astype(np.float32)[:, None] * frequency[None, :]
    cosine, sine_part = np.cos(angles), np.sin(angles)
    repeats = LANES // HEAD
    return (
        jnp.asarray(np.concatenate([cosine, cosine] * repeats, axis=1)),
        jnp.asarray(np.concatenate([-sine_part, sine_part] * repeats, axis=1)),
    )


def lower_triangle():
    rows = lax.broadcasted_iota(jnp.int32, (CHUNK, CHUNK), 0)
    cols = lax.broadcasted_iota(jnp.int32, (CHUNK, CHUNK), 1)
    return rows >= cols


def keep_rows(pairs):
    for before, out in pairs:
        out[:CHUNK] = before[:CHUNK]


def head_mask(count, index):
    lane = lax.broadcasted_iota(jnp.int32, (count, LANES), 1)
    return (lane < HEAD) if index == 0 else (lane >= HEAD)


def only(mask, values):
    return jnp.where(mask, values, jnp.zeros_like(values))


def total_of(mine, theirs):
    return jnp.concatenate(
        [a[...].astype(F32) + b[...].astype(F32) for a, b in zip(mine, theirs)], axis=0
    )


def branch_of(mine, theirs):
    branch = total_of(mine, theirs)
    return branch, rms_scale(row_sum(branch * branch))


def store_pieces(pieces, columns, values):
    at = 0
    for piece in pieces:
        high = piece.shape[0]
        piece[:, columns] = values[at : at + high].astype(BF16)
        at += high


def gain_of(mine, theirs, index):
    row = slice(index, index + 1)
    return jnp.concatenate([mine[row, :], theirs[row, :]], axis=1)


def on_own_chip():
    return lax.axis_index("row") == lax.axis_index("col")


def own_half():
    return lax.axis_index("dp") & 1


def is_inner():
    place = lax.axis_index("dp") >> 1
    return (place == 1) | (place == 2)


def norm_back(branch, scale, gain_vec, grad_out):
    weighted = grad_out * gain_vec
    inner = row_sum(weighted * branch)
    grad_branch = scale * weighted - branch * (scale * scale * scale * inner / D)
    grad_gain = jnp.sum(grad_out * branch * scale, axis=0, keepdims=True)
    return grad_branch, grad_gain


def pack_kernel(*refs):
    out = refs[-1]
    out[...] = jnp.zeros(out.shape, F32)
    for index, row in enumerate(refs[:-1]):
        out[index : index + 1, :] = row[...]


def choose_kernel(first, other, out):
    out[...] = jnp.where(on_own_chip(), first[...], other[...])


def choose_two_kernel(first, other, beside, corner, out, out_theirs):
    choose_kernel(first, other, out)
    choose_kernel(beside, corner, out_theirs)


def query_key_kernel(
    block, wq, wk, over, beside, corner, wqt, wkt, q_out, k_out, total_out, mine, theirs
):
    choose_two_kernel(block, over, beside, corner, mine, theirs)
    query_sum = 0.0
    key_sum = 0.0
    for tile in tiles(wq.shape[1]):
        query = dot(mine[...], wq[:, tile]) + dot(theirs[...], wqt[:, tile])
        q_out[:, tile] = query
        query_sum = query_sum + row_sum(query * query)
        key = dot(mine[...], wk[:, tile]) + dot(theirs[...], wkt[:, tile])
        k_out[:, tile] = key
        key_sum = key_sum + row_sum(key * key)
    total_out[...] = columns_to_rows([query_sum, key_sum])


def value_kernel(mine, theirs, wv, wvt, v_out):
    for tile in tiles(wv.shape[1]):
        v_out[:, tile] = (dot(mine[...], wv[:, tile]) + dot(theirs[...], wvt[:, tile])).astype(BF16)


def attention_kernel(
    chunk,
    queries,
    keys,
    values,
    totals,
    totals_over,
    qgain,
    kgain,
    cosine,
    sine_part,
    wo,
    wot,
    *rest,
):
    if chunk == 0:
        q_rot, k_rot, mixed, logs, *partial = rest
    else:
        q_rot, k_rot, mixed, logs, *partial = rest[4:]
        keep_rows(zip(rest[:4], rest[4:]))
    rows = slice(chunk * CHUNK, (chunk + 1) * CHUNK)
    query_total, key_total = rows_to_columns(totals[...] + totals_over[...], 2)
    query = queries[rows, :] * rms_scale(query_total[rows]) * qgain[...]
    key = keys[rows, :] * rms_scale(key_total[rows]) * kgain[...]
    q_rot[rows, :] = (turn(query, cosine[rows, :], sine_part[rows, :]) * FACTOR).astype(BF16)
    k_rot[rows, :] = turn(key, cosine[rows, :], sine_part[rows, :]).astype(BF16)
    visible = lower_triangle()
    lane = lax.broadcasted_iota(jnp.int32, (CHUNK, LANES), 1)
    log_tile = jnp.zeros((CHUNK, LANES), F32)
    for at, tile in enumerate(tiles(queries.shape[1], LANES)):
        total = jnp.zeros((CHUNK, LANES), F32)
        for index in range(2):
            query_head = only(head_mask(CHUNK, index), q_rot[rows, tile])
            scores = []
            for block in range(chunk + 1):
                part = dot_t(query_head, k_rot[block * CHUNK : (block + 1) * CHUNK, tile])
                scores.append(jnp.where(visible, part, MASKED) if block == chunk else part)
            peak = jnp.max(scores[0], axis=1, keepdims=True)
            for part in scores[1:]:
                peak = jnp.maximum(peak, jnp.max(part, axis=1, keepdims=True))
            scores = [jnp.exp(part - peak) for part in scores]
            denominator = sum(row_sum(part) for part in scores)
            inverse = 1.0 / denominator
            for block, part in enumerate(scores):
                value_rows = values[block * CHUNK : (block + 1) * CHUNK, tile]
                total = total + dot(
                    (part * inverse).astype(BF16), only(head_mask(CHUNK, index), value_rows)
                )
            log_tile = jnp.where(lane == 2 * at + index, peak + jnp.log(denominator), log_tile)
        mixed[rows, tile] = total.astype(BF16)
    logs[rows, :] = log_tile
    low = mixed[rows, :]
    half = wo.shape[1]
    store_pieces(partial, slice(0, half), dot(low, wo[...]))
    store_pieces(partial, slice(half, 2 * half), dot(low, wot[...]))


def forward_kernel(
    chunk, *refs
):
    part, part_over = refs[:PIECES], refs[PIECES : 2 * PIECES]
    forward_body(chunk, part, part_over, *refs[2 * PIECES :])


def forward_body(
    chunk, part, part_over, mine, theirs, gains, gains_far, wg, wgt, wu, wut, wd, wdt, *rest
):
    if chunk == 0:
        low_mine, side, hidden, gate, up, *partial = rest
    else:
        mixed = rest[0]
        low_mine, side, hidden, gate, up, *partial = rest[3:]
        keep_rows(zip(rest[1:3], rest[3:]))
        at = wg.shape[1] + mine.shape[1]
        side[:, at : at + mixed.shape[1]] = mixed[...]
        side[:, at + mixed.shape[1] :] = theirs[...]
    rows = slice(chunk * CHUNK, (chunk + 1) * CHUNK)
    branch, scale = branch_of(part, part_over)
    half, ff = mine.shape[1], wg.shape[1]
    normed = branch * scale * gain_of(gains, gains_far, 0)
    value = mine[rows, :].astype(F32) + normed[:, :half]
    hidden[:, :half] = value
    low_mine[rows, :] = value.astype(BF16)
    value = theirs[rows, :].astype(F32) + normed[:, half:]
    hidden[:, half:] = value
    side[rows, ff : ff + half] = value.astype(BF16)
    for tile in tiles(ff):
        left, right = low_mine[rows, :], side[rows, ff : ff + half]
        gate_act = dot(left, wg[:, tile]) + dot(right, wgt[:, tile])
        up_act = dot(left, wu[:, tile]) + dot(right, wut[:, tile])
        gate[:, tile] = gate_act
        up[:, tile] = up_act
        side[rows, tile] = (gate_act * jax.nn.sigmoid(gate_act) * up_act).astype(BF16)
    low = side[rows, :ff]
    store_pieces(partial, slice(0, half), dot(low, wd[...]))
    store_pieces(partial, slice(half, 2 * half), dot(low, wdt[...]))


def ff_norm_back_kernel(
    chunk, *refs
):
    part, part_over = refs[:PIECES], refs[PIECES : 2 * PIECES]
    hidden, cot_mine, cot_theirs, gains, gains_far, *rest = refs[2 * PIECES :]
    if chunk == 0:
        gff_mine, gff_theirs, out_mine, out_theirs, grad_gain = rest
    else:
        gain_before = rest[0]
        gff_mine, gff_theirs, out_mine, out_theirs, grad_gain = rest[5:]
        keep_rows(zip(rest[1:5], rest[5:]))
    rows = slice(chunk * CHUNK, (chunk + 1) * CHUNK)
    branch, scale = branch_of(part, part_over)
    half = cot_mine.shape[1]
    gain = gain_of(gains, gains_far, 1)
    block_out = hidden[...] + branch * scale * gain
    out_mine[rows, :] = block_out[:, :half]
    out_theirs[rows, :] = block_out[:, half:]
    upstream = jnp.concatenate([cot_mine[rows, :], cot_theirs[rows, :]], axis=1).astype(F32)
    grad_branch, gained = norm_back(branch, scale, gain, upstream)
    grad_gain[...] = gained if chunk == 0 else gain_before[...] + gained
    gff_mine[rows, :] = grad_branch[:, :half].astype(BF16)
    gff_theirs[rows, :] = grad_branch[:, half:].astype(BF16)


def backward_kernel(
    chunk, gff_mine, gff_theirs, gate, up, wd, wdt, wg, wgt, wu, wut, *rest
):
    if chunk == 0:
        grads, *partial = rest
    else:
        grads, *partial = rest[1:]
        keep_rows([rest[:2]])
    rows = slice(chunk * CHUNK, (chunk + 1) * CHUNK)
    half, ff = wd.shape[1], wg.shape[1]
    for tile in tiles(ff):
        grad_act = dot_t(gff_mine[rows, :], wd[tile, :]) + dot_t(gff_theirs[rows, :], wdt[tile, :])
        gate_act = gate[:, tile]
        sig = jax.nn.sigmoid(gate_act)
        grads[rows, tile] = (
            grad_act * up[:, tile] * sig * (1.0 + gate_act * (1.0 - sig))
        ).astype(BF16)
        there = slice(ff + tile.start, ff + tile.stop)
        grads[rows, there] = (grad_act * gate_act * sig).astype(BF16)
    left, right = grads[rows, :ff], grads[rows, ff:]
    for tile in tiles(half):
        store_pieces(partial, tile, dot_t(left, wg[tile, :]) + dot_t(right, wu[tile, :]))
        there = slice(half + tile.start, half + tile.stop)
        store_pieces(partial, there, dot_t(left, wgt[tile, :]) + dot_t(right, wut[tile, :]))


def attention_back_kernel(chunk, *refs):
    grad_part, grad_over, part, part_over = [
        refs[i * PIECES : (i + 1) * PIECES] for i in range(4)
    ]
    (
        cot_mine,
        cot_theirs,
        gains,
        gains_far,
        wo,
        wot,
        q_rot,
        k_rot,
        values,
        logs,
        queries,
        keys,
        totals,
        totals_over,
        qgain,
        kgain,
        cosine,
        sine_part,
        *rest,
    ) = refs[4 * PIECES :]
    half = wo.shape[1]
    width = queries.shape[1]
    if chunk == 0:
        gat_mine, side, gh_mine, gh_theirs, gqn, grad_gain, column, gk_sum, gv_sum = rest
    else:
        gain_before, column_in, gk_in, gv_in = rest[:4]
        gat_mine, side, gh_mine, gh_theirs, gqn, grad_gain, gkn, gv_low, inner_out = rest[6:]
        keep_rows(zip(rest[4:6], rest[6:]))
    rows = slice(chunk * CHUNK, (chunk + 1) * CHUNK)
    seen = (chunk + 1) * CHUNK
    branch, scale = branch_of(part, part_over)
    grad_hidden = (
        jnp.concatenate([cot_mine[rows, :], cot_theirs[rows, :]], axis=1).astype(F32)
        + total_of(grad_part, grad_over)
    )
    gh_mine[...] = grad_hidden[:, :half]
    gh_theirs[...] = grad_hidden[:, half:]
    grad_branch, gained = norm_back(branch, scale, gain_of(gains, gains_far, 0), grad_hidden)
    grad_gain[...] = gained if chunk == 0 else gain_before[...] + gained
    gat_mine[rows, :] = grad_branch[:, :half].astype(BF16)
    side[rows, :] = grad_branch[:, half:].astype(BF16)
    grad_mixed = (
        dot_t(gat_mine[rows, :], wo[...]) + dot_t(side[rows, :], wot[...])
    ).astype(BF16)
    visible = lower_triangle()
    query_total, key_total = rows_to_columns(totals[...] + totals_over[...], 2)
    query_inner = jnp.zeros((CHUNK, 1), F32)
    key_inner = jnp.zeros((seen, 1), F32)
    for at, tile in enumerate(tiles(width, LANES)):
        grad_query = jnp.zeros((CHUNK, LANES), F32)
        grad_key = [jnp.zeros((CHUNK, LANES), F32) for _ in range(chunk + 1)]
        grad_value = [jnp.zeros((CHUNK, LANES), F32) for _ in range(chunk + 1)]
        for index in range(2):
            mask = head_mask(CHUNK, index)
            query_head = only(mask, q_rot[rows, tile])
            grad_head = only(mask, grad_mixed[:, tile])
            log_column = logs[rows, 2 * at + index : 2 * at + index + 1]
            weights, grads = [], []
            for block in range(chunk + 1):
                span = slice(block * CHUNK, (block + 1) * CHUNK)
                scores = dot_t(query_head, k_rot[span, tile])
                if block == chunk:
                    scores = jnp.where(visible, scores, MASKED)
                weights.append(jnp.exp(scores - log_column))
                grads.append(dot_t(grad_head, values[span, tile]))
            inner = sum(row_sum(w * g) for w, g in zip(weights, grads))
            for block in range(chunk + 1):
                span = slice(block * CHUNK, (block + 1) * CHUNK)
                weight = weights[block]
                grad_scores = (weight * (grads[block] - inner)).astype(BF16)
                grad_value[block] = grad_value[block] + t_dot(weight.astype(BF16), grad_head)
                grad_query = grad_query + dot(grad_scores, only(mask, k_rot[span, tile]))
                grad_key[block] = grad_key[block] + t_dot(grad_scores, query_head)
        back = turn(grad_query * FACTOR, cosine[rows, :], -sine_part[rows, :])
        gqn[:, tile] = back
        query_inner = query_inner + row_sum(back * qgain[:, tile] * queries[rows, tile])
        if chunk == 0:
            gk_sum[:, tile] = grad_key[0]
            gv_sum[:, tile] = grad_value[0]
        else:
            key_all = jnp.concatenate([gk_in[:, tile] + grad_key[0], grad_key[1]], axis=0)
            value_all = jnp.concatenate([gv_in[:, tile] + grad_value[0], grad_value[1]], axis=0)
            gv_low[:, tile] = value_all.astype(BF16)
            back = turn(key_all, cosine[...], -sine_part[...])
            gkn[:, tile] = back
            key_inner = key_inner + row_sum(back * kgain[:, tile] * keys[:, tile])
    if chunk == 0:
        column[...] = jnp.broadcast_to(query_inner, (CHUNK, LANES))
    else:
        query_inner = jnp.concatenate([column_in[:, :1], query_inner], axis=0)
        inner_out[...] = columns_to_rows([query_inner, key_inner])


def query_key_back_kernel(
    gqn_first,
    gqn_second,
    gkn,
    queries,
    keys,
    totals,
    totals_over,
    inner,
    inner_over,
    qgain,
    kgain,
    mlp_part,
    attn_part,
    grads,
    gain_mine,
    gain_give,
):
    width = queries.shape[1]
    half = gain_mine.shape[1]
    for out, columns in ((gain_mine, slice(0, half)), (gain_give, slice(half, 2 * half))):
        out[...] = jnp.zeros(out.shape, F32)
        out[0:1, :] = mlp_part[:, columns]
        out[1:2, :] = attn_part[:, columns]
    query_total, key_total = rows_to_columns(totals[...] + totals_over[...], 2)
    query_inner, key_inner = rows_to_columns(inner[...] + inner_over[...], 2)
    gqn = jnp.concatenate([gqn_first[...], gqn_second[...]], axis=0)
    for at, raw, back, total, sums, gain, low in (
        (2, queries, gqn, query_total, query_inner, qgain, grads.at[:, :width]),
        (3, keys, gkn[...], key_total, key_inner, kgain, grads.at[:, width:]),
    ):
        scale = rms_scale(total)
        value = raw[...]
        low[...] = (
            scale * (back * gain[...]) - value * (scale * scale * scale * sums / D)
        ).astype(BF16)
        gained = jnp.sum(back * value * scale, axis=0, keepdims=True)
        gain_mine[at : at + 1, :] = gained
        gain_give[at : at + 1, :] = gained


GAIN_ROWS = 16


def plain_weight_kernel(products, *refs):
    plain = refs[-1]

    def view(operand):
        index, start, stop = operand
        return refs[index].at[:, start:stop]

    at = 0
    for product in products:
        left, left_far, right, right_far = [view(operand) for operand in product]
        width = product[2][2] - product[2][1]
        for tile in tiles(plain.shape[0]):
            plain[tile, at : at + width] = (
                t_dot(left[:, tile], right[...]) + t_dot(left_far[:, tile], right_far[...])
            ).astype(BF16)
        at += width


def copy_kernel(values, out):
    out[...] = values[...]


def split_kernel(total, *outs):
    at = 0
    for out in outs:
        out[...] = total[:, at : at + out.shape[1]].astype(F32)
        at += out.shape[1]


def weight_kernel(with_gains, products, *refs):
    keep, give, plain = refs[-3:]
    plain_weight_kernel(products, *refs[:-3], plain)
    half = plain.shape[0] // 2
    mine = pl.multiple_of(own_half() * half, half)
    theirs = pl.multiple_of((1 - own_half()) * half, half)
    keep[:half, :] = plain[pl.ds(mine, half), :]
    give[:half, :] = plain[pl.ds(theirs, half), :]
    if with_gains:
        gains = refs[-5][...] + refs[-4][...]
        width = gains.shape[1]
        row = lax.broadcasted_iota(jnp.int32, (GAIN_ROWS, width), 0)
        for at in range(0, plain.shape[1], width):
            index = 2 * at // width
            first = jnp.broadcast_to(gains[index : index + 1, :], row.shape)
            second = jnp.broadcast_to(gains[index + 1 : index + 2, :], row.shape)
            rows = jnp.where(row == 0, first, jnp.where(row == 1, second, 0.0)).astype(BF16)
            keep[half:, at : at + width] = rows
            give[half:, at : at + width] = rows


def add_kernel(mine, *rest):
    out = rest[-1]
    at = 0
    for piece in rest[:-1]:
        rows = slice(at, at + piece.shape[0])
        out[rows, :] = (mine[rows, :].astype(F32) + piece[...].astype(F32)).astype(BF16)
        at = rows.stop


def inner_kernel(mine, received, out):
    out[...] = jnp.where(is_inner(), mine[...], received[...])


def finish_kernel(mine, received, *outs):
    half = outs[0].shape[0] // 2
    for place, source in enumerate((mine, received)):
        to = pl.multiple_of((own_half() ^ place) * half, half)
        column = 0
        for out in outs:
            width = out.shape[1]
            out[pl.ds(to, half), :] = source[:half, column : column + width].astype(F32)
            column += width


def in_far_kernel(side_far, block, out):
    out[...] = jnp.where(on_own_chip(), side_far[:, side_far.shape[1] - out.shape[1] :], block[...])


def gains_out_kernel(total, *outs):
    width = outs[0].shape[1]
    rows = total[total.shape[0] - GAIN_ROWS :, :].astype(F32)
    for index, out in enumerate(outs):
        at = index // 2 * width
        out[...] = rows[index % 2 : index % 2 + 1, at : at + width]


def grad_input_kernel(stays, moves, across, corner, out):
    own = on_own_chip()
    out[...] = jnp.where(own, stays[...], moves[...]) + jnp.where(
        own, across[...], corner[...]
    ).astype(F32)


def input_back_kernel(
    grads, gv, wq, wqt, wk, wkt, wv, wvt, *rest
):
    width = wq.shape[1]
    gq, gk = grads.at[:, :width], grads.at[:, width:]
    gh_mine, gh_theirs = rest[:2], rest[2:4]
    stays, moves, across, corner = rest[4:]
    for tile in tiles(wq.shape[0]):
        mine = (
            dot_t(gq[...], wq[tile, :]) + dot_t(gk[...], wk[tile, :]) + dot_t(gv[...], wv[tile, :])
        )
        theirs = (
            dot_t(gq[...], wqt[tile, :])
            + dot_t(gk[...], wkt[tile, :])
            + dot_t(gv[...], wvt[tile, :])
        )
        for chunk in range(2):
            rows = slice(chunk * CHUNK, (chunk + 1) * CHUNK)
            stays[rows, tile] = gh_mine[chunk][:, tile] + mine[rows]
            moves[rows, tile] = gh_theirs[chunk][:, tile] + theirs[rows]
        across[:, tile] = mine.astype(BF16)
        corner[:, tile] = theirs.astype(BF16)


def dp_exchange(values, bit):
    size = lax.axis_size("dp")
    return lax.ppermute(values, "dp", [(i, i ^ (1 << bit)) for i in range(size)])


def dp_bits():
    return lax.axis_size("dp").bit_length() - 1


def along_line(values, moves):
    pairs = [(2 * a + half, 2 * b + half) for a, b in moves for half in range(2)]
    return lax.ppermute(values, "dp", pairs)


def in_turn(operands, received):
    return lax.optimization_barrier((operands, received))


class Chain:
    def __init__(self, name, high, widths, keep, give):
        self.name, self.high, self.widths, self.keep, self.give = name, high, widths, keep, give
        self.back = False
        self.received = None

    def kernel(self, body, args, part, after, outs=None):
        out = call(
            body, outs or [shape(self.keep.shape)], args, f"{self.name}_{part}", after=after
        )
        if outs is None:
            (self.keep,) = out
        else:
            self.out = out
        return out[0]

    def combine(self, body, part, after):
        return self.kernel(body, [self.keep, *self.received], part, after)

    def finish(self, after):
        outs = [shape((self.high, w), F32) for w in self.widths]
        return self.kernel(finish_kernel, [self.keep, *self.received], "out", after, outs)


LINE = ((0, 1), (3, 2)), ((1, 2), (2, 1)), ((1, 0), (2, 3))


class Lanes:
    def __init__(self):
        self.line = [None, None, None]
        self.latest = None

    def send_y(self, chain, before=None):
        operands = [chain.keep if chain.back else chain.give]
        if before is not None:
            operands, before.received = in_turn(operands, before.received)
        chain.received = [dp_exchange(piece, 0) for piece in operands]

    def pass_on(self, index, chain):
        before, self.line[index] = self.line[index], chain
        if before is not None and chain is not None:
            chain.keep, before.received = in_turn(chain.keep, before.received)
        if chain is not None:
            chain.received = [along_line(chain.keep, LINE[index])]
        return before

    def advance(self, chain, following=None, after=()):
        current = chain
        late = following is not None and following is self.line[2]
        if following is not None and not late:
            self.send_y(following, chain)
        done = None
        if chain.back:
            done, chain = chain, None
        else:
            self.latest = chain.combine(add_kernel, "y", (self.latest, *after))
            if lax.axis_size("dp") != 8:
                for bit in range(1, dp_bits()):
                    other = dp_exchange(chain.keep, bit).astype(F32)
                    chain.keep = (chain.keep.astype(F32) + other).astype(BF16)
                chain.back = True
                chain = None
        for index, (body, part) in enumerate(
            ((add_kernel, "in"), (add_kernel, "across"), (inner_kernel, "out"))
        ):
            chain = self.pass_on(index, chain)
            if chain is not None:
                self.latest = chain.combine(body, f"z_{part}", (self.latest,))
        if chain is not None:
            chain.back = True
        if late:
            self.send_y(following, current)
        if done is not None:
            self.latest = done.finish((self.latest,))


def on_device(
    block_in,
    w_query,
    w_key,
    w_value,
    w_output,
    w_gate,
    w_up,
    w_down,
    qnorm_gain,
    knorm_gain,
    attn_gain,
    mlp_gain,
    cotangent,
):
    rows, half = block_in.shape
    width = w_query.shape[1]
    ff = w_gate.shape[1]
    pair = ("row", "col")

    to_over = [(0, 1), (3, 2)]
    to_corner = [(1, 2), (2, 1)]
    to_beside = [(2, 0), (1, 3)]
    from_same = [(0, 2), (3, 1)]

    in_over = lax.ppermute(block_in, pair, to_over)
    in_corner = lax.ppermute(block_in, pair, to_corner)
    in_beside = lax.ppermute(block_in, pair, to_beside)
    wq_far, wk_far = swap(w_query, "row"), swap(w_key, "row")
    (gains,) = call(
        pack_kernel, [shape((8, half), F32)], [attn_gain[None], mlp_gain[None]], "gains"
    )
    qgain, kgain = qnorm_gain[None], knorm_gain[None]
    cosine, sine_part = rope_tables(rows)

    (cotangent, wv_give, wo_give), (in_corner, in_over) = in_turn(
        [cotangent, w_value, w_output], [in_corner, in_over]
    )
    cot_over = lax.ppermute(cotangent, pair, to_over)
    cot_corner = lax.ppermute(cotangent, pair, to_corner)
    wv_far, wo_far = swap(wv_give, "row"), swap(wo_give, "row")

    queries, keys, totals, in_mine, in_theirs = call(
        query_key_kernel,
        [shape((rows, width), F32)] * 2 + [shape((8, rows), F32)] + [shape((rows, half))] * 2,
        [in_over, in_beside, in_corner, wq_far, wk_far],
        "query_key",
        far=[block_in, w_query, w_key],
    )
    totals_over = swap(totals, "col")
    (values,) = call(
        value_kernel,
        [shape((rows, width))],
        [in_mine, in_theirs, w_value, wv_far],
        "value",
    )
    (cot_mine,) = call(
        choose_kernel, [shape((rows, half))], [cotangent, cot_over], "cotangent_mine"
    )
    (gains,), (values,) = in_turn([gains], [values])
    gains_far = swap(gains, "row")
    attention_args = [
        queries,
        keys,
        values,
        totals,
        totals_over,
        qgain,
        kgain,
        cosine,
        sine_part,
        w_output,
        wo_far,
    ]
    partial = [shape((CHUNK // PIECES, D))] * PIECES
    attention_outs = [shape((rows, width))] * 3 + [shape((rows, LANES), F32), *partial]

    def send_over(pieces, before=None):
        if before is not None:
            for index in range(PIECES):
                (pieces[index],), (before[index],) = in_turn([pieces[index]], [before[index]])
        return [swap(piece, "col") for piece in pieces]

    *kept, first_a, first_b = call(
        functools.partial(attention_kernel, 0),
        attention_outs,
        attention_args,
        "attention_0",
        after=(cot_mine, gains_far),
    )
    first = [first_a, first_b]
    given, (kept[-1], cot_corner) = in_turn([w_gate, w_up, w_down], [kept[-1], cot_corner])
    wg_far, wu_far, wd_far = [swap(value, "row") for value in given]
    first_over = send_over(first)
    *kept, second_a, second_b = call(
        functools.partial(attention_kernel, 1),
        attention_outs,
        attention_args + kept,
        "attention_1",
    )
    q_rot, k_rot, mixed, logs = kept
    second = [second_a, second_b]
    second_over = send_over(second, first_over)
    parts, parts_over = [first, second], [first_over, second_over]

    side_width = ff + half + width + half

    def forward(chunk, over, kept, after):
        return call(
            functools.partial(forward_kernel, chunk),
            [shape((rows, half)), shape((rows, side_width)), shape((CHUNK, D), F32)]
            + [shape((CHUNK, ff), F32)] * 2
            + partial,
            [*parts[chunk], *over, in_mine, in_theirs, gains, gains_far]
            + [w_gate, wg_far, w_up, wu_far, w_down, wd_far]
            + kept,
            f"forward_{chunk}",
            after=after,
        )

    low_mine, side, *saved = forward(0, first_over, [], ())
    saved_all, ff_first = [saved[:3]], saved[3:]
    (cotangent,), (low_mine,) = in_turn([cotangent], [low_mine])
    cot_beside = lax.ppermute(cotangent, pair, to_beside)
    (cot_theirs,) = call(
        choose_kernel, [shape((rows, half))], [cot_beside, cot_corner], "cotangent_theirs"
    )
    ff_first_over = send_over(ff_first, second_over)
    low_mine, side, *saved = forward(1, second_over, [mixed, low_mine, side], ())
    saved_all.append(saved[:3])
    ff_second = saved[3:]
    ff_second_over = send_over(ff_second, ff_first_over)

    def weight_grad(name, arrays, products, after, gains=()):
        high = products[0][0][2] - products[0][0][1]
        widths = [right[2] - right[1] for _, _, right, _ in products]
        extra = GAIN_ROWS if gains else 0
        keep, give = call(
            functools.partial(weight_kernel, bool(gains), products),
            [shape((high // 2 + extra, sum(widths)))] * 2,
            [*arrays, *gains],
            name,
            scratch=[pltpu.VMEM((high, sum(widths)), BF16)],
            after=after,
        )
        return Chain(name, high, widths, keep, give)

    def ff_norm_back(chunk, mine, over, more, after):
        return call(
            functools.partial(ff_norm_back_kernel, chunk),
            [shape((rows, half))] * 2 + [shape((rows, half), F32)] * 2 + [shape((1, D), F32)],
            [*mine, *over, saved_all[chunk][0], cot_mine, cot_theirs, gains, gains_far, *more],
            f"ff_norm_back_{chunk}",
            after=after,
        )

    def backward(chunk, more, after):
        return call(
            functools.partial(backward_kernel, chunk),
            [shape((rows, 2 * ff)), *partial],
            [gff_mine, gff_theirs, *saved_all[chunk][1:]]
            + [w_down, wd_far, w_gate, wg_far, w_up, wu_far]
            + more,
            f"backward_{chunk}",
            after=after,
        )

    *kept, mlp_part = ff_norm_back(0, ff_first, ff_first_over, [], ())
    gff_mine, gff_theirs, _, _ = kept
    grads, *gh_first = backward(0, [], ())
    gh_first_over = send_over(gh_first, ff_second_over)
    *kept, mlp_part = ff_norm_back(
        1, ff_second, ff_second_over, [mlp_part, *kept], ()
    )
    gff_mine, gff_theirs, out_mine, out_theirs = kept
    (side,), (gff_theirs,) = in_turn([side], [gff_theirs])
    side_far = swap(side, "row")
    gff_far = swap(gff_theirs, "row")
    out_beside = lax.ppermute(out_theirs, pair, from_same)
    grads, *gh_second = backward(1, [grads], ())
    lanes = Lanes()
    down = weight_grad(
        "down",
        [side, side_far, gff_mine, gff_far],
        [((0, 0, ff), (1, 0, ff), (2, 0, half), (3, 0, half))],
        (grads,),
    )
    (block_out,) = call(
        choose_kernel,
        [shape((rows, half), F32)],
        [out_mine, out_beside],
        "block_out",
        after=(down.keep,),
    )
    (in_far,) = call(
        in_far_kernel, [shape((rows, half))], [side_far, block_in], "in_far", after=(block_out,)
    )
    lanes.send_y(down)
    (gh_second, grads), (gh_first_over, down.keep, in_far) = in_turn(
        [gh_second, grads], [gh_first_over, down.keep, in_far]
    )
    gh_second_over = send_over(gh_second)
    grads_far = swap(grads, "row")
    grad_parts, grad_over = [gh_first, gh_second], [gh_first_over, gh_second_over]

    def ff_grad(name, start, after):
        span = (start, start + ff)
        return weight_grad(
            name,
            [low_mine, side_far, grads, grads_far],
            [((0, 0, half), (1, ff, ff + half), (2, *span), (3, *span))],
            after,
        )

    latest = down.keep
    gh_mine, gh_theirs, gqn = [], [], []
    for chunk in range(2):
        args = [
            *grad_parts[chunk],
            *grad_over[chunk],
            *parts[chunk],
            *parts_over[chunk],
            cot_mine,
            cot_theirs,
            gains,
            gains_far,
            w_output,
            wo_far,
            q_rot,
            k_rot,
            values,
            logs,
            queries,
            keys,
            totals,
            totals_over,
            qgain,
            kgain,
            cosine,
            sine_part,
        ]
        outs = [shape((rows, half))] * 2
        outs += [shape((CHUNK, half), F32)] * 2 + [shape((CHUNK, width), F32), shape((1, D), F32)]
        if chunk == 0:
            outs += [shape((CHUNK, LANES), F32)] + [shape((CHUNK, width), F32)] * 2
        else:
            outs += [shape((rows, width), F32), shape((rows, width)), shape((8, rows), F32)]
            args += [attn_part, column, gk_sum, gv_sum, gat_mine, gat_theirs]
        gat_mine, gat_theirs, gm, gt, gq_turned, attn_part, *more = call(
            functools.partial(attention_back_kernel, chunk),
            outs,
            args,
            f"attention_back_{chunk}",
            after=(latest,),
            flops=3e10 if chunk else 1,
        )
        gh_mine.append(gm)
        gh_theirs.append(gt)
        gqn.append(gq_turned)
        if chunk == 0:
            column, gk_sum, gv_sum = more
            up = ff_grad("up", ff, (column,))
            gate = ff_grad("gate", 0, (up.keep,))
            lanes.latest = gate.keep
            lanes.advance(down, gate, grad_over[1])
            latest = lanes.latest
        else:
            gkn, gv, inner = more
    inner_over = swap(inner, "col")
    gat_far, gv_far = swap(gat_theirs, "row"), swap(gv, "row")
    grads_back, gain_mine, gain_give = call(
        query_key_back_kernel,
        [shape((rows, 2 * width))] + [shape((8, half), F32)] * 2,
        [
            *gqn,
            gkn,
            queries,
            keys,
            totals,
            totals_over,
            inner,
            inner_over,
            qgain,
            kgain,
            mlp_part,
            attn_part,
        ],
        "query_key_back",
        after=(gv,),
    )
    grads_back_far = swap(grads_back, "row")
    gain_far = swap(gain_give, "row")
    lanes.latest = grads_back
    lanes.advance(gate, up)
    (out_value,) = call(
        functools.partial(
            plain_weight_kernel,
            [
                ((0, 0, width), (1, ff + half, ff + half + width), (2, 0, half), (3, 0, half)),
                ((4, 0, half), (5, 0, half), (6, 0, width), (7, 0, width)),
            ],
        ),
        [shape((half, 2 * width))],
        [mixed, side_far, gat_mine, gat_far, in_mine, in_far, gv, gv_far],
        "out_value",
        after=(lanes.latest,),
    )
    out_value_part = lax.psum_scatter(out_value, "dp", scatter_dimension=0, tiled=True)
    lanes.latest = out_value
    query_key = weight_grad(
        "query_key",
        [in_mine, in_far, grads_back, grads_back_far],
        [
            ((0, 0, half), (1, 0, half), (2, 0, width), (3, 0, width)),
            ((0, 0, half), (1, 0, half), (2, width, 2 * width), (3, width, 2 * width)),
        ],
        (lanes.latest,),
        (gain_mine, gain_far),
    )
    lanes.latest = query_key.keep
    lanes.advance(up, query_key)
    stays, moves, across, corner = call(
        input_back_kernel,
        [shape((rows, half), F32)] * 2 + [shape((rows, half))] * 2,
        [grads_back, gv, w_query, wq_far, w_key, wk_far, w_value, wv_far]
        + [*gh_mine, *gh_theirs],
        "input_back",
        after=(lanes.latest,),
    )
    lanes.latest = across
    moves = lax.ppermute(moves, pair, from_same)
    across = lax.ppermute(across, pair, [(1, 0), (2, 3)])
    (corner,), (across,) = in_turn([corner], [across])
    corner = lax.ppermute(corner, pair, to_corner)
    lanes.advance(query_key, down)
    (out_value_part,) = call(
        copy_kernel,
        [shape(out_value_part.shape)],
        [out_value_part],
        "out_value_part",
        after=(lanes.latest,),
    )
    lanes.latest = out_value_part
    out_value_total = lax.all_gather(out_value_part, "dp", axis=0, tiled=True)
    (grad_input,) = call(
        grad_input_kernel,
        [shape((rows, half), F32)],
        [stays, moves, across, corner],
        "grad_input",
        after=(lanes.latest,),
    )
    lanes.latest = grad_input
    lanes.advance(down, gate)
    lanes.advance(gate, up)
    lanes.advance(up, query_key)
    grad_out, grad_value = call(
        split_kernel,
        [shape((half, width), F32)] * 2,
        [out_value_total],
        "out_value_out",
        after=(lanes.latest,),
    )
    lanes.latest = grad_out
    gain_out = call(
        gains_out_kernel,
        [shape((1, half), F32)] * 2 + [shape((1, width), F32)] * 2,
        [query_key.keep],
        "gains_out",
        after=(lanes.latest,),
    )
    grad_mlpgain, grad_attngain, grad_qgain, grad_kgain = [row[0] for row in gain_out]
    lanes.latest = gain_out[0]
    lanes.advance(query_key)
    (grad_down,) = down.out
    (grad_gate,) = gate.out
    (grad_up,) = up.out
    grad_query, grad_key = query_key.out
    return (
        block_out,
        grad_input,
        grad_query,
        grad_key,
        grad_value,
        grad_out,
        grad_gate,
        grad_up,
        grad_down,
        grad_qgain,
        grad_kgain,
        grad_attngain,
        grad_mlpgain,
    )


def solution(mesh):
    tokens = P(("dp", "col"), "row")
    grid, turned = P("row", "col"), P("col", "row")
    in_specs = (
        tokens,
        grid,
        grid,
        grid,
        turned,
        grid,
        grid,
        turned,
        P("col"),
        P("col"),
        P("row"),
        P("row"),
        tokens,
    )
    out_specs = (
        tokens,
        tokens,
        grid,
        grid,
        grid,
        turned,
        grid,
        grid,
        turned,
        P("col"),
        P("col"),
        P("row"),
        P("row"),
    )
    return jax.shard_map(
        on_device, mesh=mesh, in_specs=in_specs, out_specs=out_specs, check_vma=False
    )
```

```python
import functools
import math

import jax
import jax.numpy as jnp
import numpy as np
from jax import lax
from jax.experimental import pallas as pl
from jax.experimental.pallas import tpu as pltpu
from jax.sharding import PartitionSpec as P

D = 1024
HEAD = 64
SEQ = 512
EPSILON = 1e-06
ROPE_BASE = 500000.0
MASKED = -1e30
CHUNK = 256
PIECES = 2
TILE = 256
LANES = 128
FACTOR = 1.0 / math.sqrt(HEAD)

F32 = jnp.float32
BF16 = jnp.bfloat16


def swap(values, axis):
    return lax.ppermute(values, axis, [(0, 1), (1, 0)])


def dot(left, right):
    return jnp.dot(left, right, preferred_element_type=F32)


def dot_t(left, right):
    return lax.dot_general(left, right, (((1,), (1,)), ((), ())), preferred_element_type=F32)


def t_dot(left, right):
    return lax.dot_general(left, right, (((0,), (0,)), ((), ())), preferred_element_type=F32)


def shape(dims, kind=BF16):
    return jax.ShapeDtypeStruct(dims, kind)


def call(kernel, outs, args, name, scratch=(), after=(), far=(), flops=1):
    count, skip, fetched = len(args), len(after), len(far)
    vmem = pl.BlockSpec(memory_space=pltpu.VMEM)
    anywhere = pl.BlockSpec(memory_space=pl.ANY)
    buffers = [pltpu.VMEM(a.shape, a.dtype) for a in far]
    if fetched:
        buffers.append(pltpu.SemaphoreType.DMA((fetched,)))

    def body(*refs):
        sources, refs = refs[:fetched], refs[fetched:]
        copies = []
        if fetched:
            refs, local = refs[: -fetched - 1], refs[-fetched - 1 :]
            copies = [
                pltpu.make_async_copy(source, local[i], local[-1].at[i])
                for i, source in enumerate(sources)
            ]
            for copy in copies:
                copy.start()
            for copy in copies:
                copy.wait()
            sources = local[:-1]
        kernel(*sources, *refs[:count], *refs[count + skip :])

    return pl.pallas_call(
        body,
        out_shape=tuple(outs),
        in_specs=[pl.BlockSpec(memory_space=pltpu.HBM)] * fetched + [vmem] * count + [anywhere] * skip,
        out_specs=tuple([vmem] * len(outs)),
        scratch_shapes=[*scratch, *buffers],
        compiler_params=pltpu.CompilerParams(
            vmem_limit_bytes=12 << 20, fuse_transposed_lhs_in_matmul=True
        ),
        cost_estimate=pl.CostEstimate(flops=int(flops), bytes_accessed=1, transcendentals=0),
        name=name,
    )(*far, *args, *after)


def tiles(extent, size=TILE):
    return [slice(at, min(at + size, extent)) for at in range(0, extent, size)]


def row_sum(values):
    return jnp.sum(values, axis=1, keepdims=True)


def columns_to_rows(columns):
    count = columns[0].shape[0]
    lane = lax.broadcasted_iota(jnp.int32, (count, LANES), 1)
    packed = jnp.zeros((count, LANES), F32)
    for index, column in enumerate(columns):
        packed = jnp.where(lane == index, column, packed)
    return packed.T[:8]


def rows_to_columns(rows, count):
    turned = jnp.concatenate([rows] * (LANES // 8), axis=0).T
    return [turned[:, i : i + 1] for i in range(count)]


def rms_scale(total):
    return lax.rsqrt(total / D + EPSILON)


def turn(values, cosine, sine_part):
    lane = lax.broadcasted_iota(jnp.int32, cosine.shape, 1)
    first = (lane % HEAD) < HEAD // 2
    out = []
    for tile in tiles(values.shape[1], LANES):
        part = values[:, tile]
        other = jnp.where(
            first, pltpu.roll(part, LANES - HEAD // 2, 1), pltpu.roll(part, HEAD // 2, 1)
        )
        out.append(part * cosine + other * sine_part)
    return jnp.concatenate(out, axis=1)


def rope_tables(count):
    half = HEAD // 2
    frequency = np.exp(np.arange(half, dtype=np.float32) * np.float32(-2.0 * math.log(ROPE_BASE) / HEAD))
    angles = np.arange(count).astype(np.float32)[:, None] * frequency[None, :]
    cosine, sine_part = np.cos(angles), np.sin(angles)
    repeats = LANES // HEAD
    return (
        jnp.asarray(np.concatenate([cosine, cosine] * repeats, axis=1)),
        jnp.asarray(np.concatenate([-sine_part, sine_part] * repeats, axis=1)),
    )


def lower_triangle():
    rows = lax.broadcasted_iota(jnp.int32, (CHUNK, CHUNK), 0)
    cols = lax.broadcasted_iota(jnp.int32, (CHUNK, CHUNK), 1)
    return rows >= cols


def keep_rows(pairs):
    for before, out in pairs:
        out[:CHUNK] = before[:CHUNK]


def head_mask(count, index):
    lane = lax.broadcasted_iota(jnp.int32, (count, LANES), 1)
    return (lane < HEAD) if index == 0 else (lane >= HEAD)


def only(mask, values):
    return jnp.where(mask, values, jnp.zeros_like(values))


def total_of(mine, theirs):
    return jnp.concatenate(
        [a[...].astype(F32) + b[...].astype(F32) for a, b in zip(mine, theirs)], axis=0
    )


def branch_of(mine, theirs):
    branch = total_of(mine, theirs)
    return branch, rms_scale(row_sum(branch * branch))


def store_pieces(pieces, columns, values):
    at = 0
    for piece in pieces:
        high = piece.shape[0]
        piece[:, columns] = values[at : at + high].astype(BF16)
        at += high


def gain_of(mine, theirs, index):
    row = slice(index, index + 1)
    return jnp.concatenate([mine[row, :], theirs[row, :]], axis=1)


def on_own_chip():
    return lax.axis_index("row") == lax.axis_index("col")


def own_half():
    return lax.axis_index("dp") & 1


def is_inner():
    place = lax.axis_index("dp") >> 1
    return (place == 1) | (place == 2)


def norm_back(branch, scale, gain_vec, grad_out):
    weighted = grad_out * gain_vec
    inner = row_sum(weighted * branch)
    grad_branch = scale * weighted - branch * (scale * scale * scale * inner / D)
    grad_gain = jnp.sum(grad_out * branch * scale, axis=0, keepdims=True)
    return grad_branch, grad_gain


def pack_kernel(*refs):
    out = refs[-1]
    out[...] = jnp.zeros(out.shape, F32)
    for index, row in enumerate(refs[:-1]):
        out[index : index + 1, :] = row[...]


def choose_kernel(first, other, out):
    out[...] = jnp.where(on_own_chip(), first[...], other[...])


def choose_two_kernel(first, other, beside, corner, out, out_theirs):
    choose_kernel(first, other, out)
    choose_kernel(beside, corner, out_theirs)


def query_key_kernel(
    block, wq, wk, over, beside, corner, wqt, wkt, q_out, k_out, total_out, mine, theirs
):
    choose_two_kernel(block, over, beside, corner, mine, theirs)
    query_sum = 0.0
    key_sum = 0.0
    for tile in tiles(wq.shape[1]):
        query = dot(mine[...], wq[:, tile]) + dot(theirs[...], wqt[:, tile])
        q_out[:, tile] = query
        query_sum = query_sum + row_sum(query * query)
        key = dot(mine[...], wk[:, tile]) + dot(theirs[...], wkt[:, tile])
        k_out[:, tile] = key
        key_sum = key_sum + row_sum(key * key)
    total_out[...] = columns_to_rows([query_sum, key_sum])


def value_kernel(mine, theirs, wv, wvt, v_out):
    for tile in tiles(wv.shape[1]):
        v_out[:, tile] = (dot(mine[...], wv[:, tile]) + dot(theirs[...], wvt[:, tile])).astype(BF16)


def attention_kernel(
    chunk,
    queries,
    keys,
    values,
    totals,
    totals_over,
    qgain,
    kgain,
    cosine,
    sine_part,
    wo,
    wot,
    *rest,
):
    if chunk == 0:
        q_rot, k_rot, mixed, logs, *partial = rest
    else:
        q_rot, k_rot, mixed, logs, *partial = rest[4:]
        keep_rows(zip(rest[:4], rest[4:]))
    rows = slice(chunk * CHUNK, (chunk + 1) * CHUNK)
    query_total, key_total = rows_to_columns(totals[...] + totals_over[...], 2)
    query = queries[rows, :] * rms_scale(query_total[rows]) * qgain[...]
    key = keys[rows, :] * rms_scale(key_total[rows]) * kgain[...]
    q_rot[rows, :] = (turn(query, cosine[rows, :], sine_part[rows, :]) * FACTOR).astype(BF16)
    k_rot[rows, :] = turn(key, cosine[rows, :], sine_part[rows, :]).astype(BF16)
    visible = lower_triangle()
    lane = lax.broadcasted_iota(jnp.int32, (CHUNK, LANES), 1)
    log_tile = jnp.zeros((CHUNK, LANES), F32)
    for at, tile in enumerate(tiles(queries.shape[1], LANES)):
        total = jnp.zeros((CHUNK, LANES), F32)
        for index in range(2):
            query_head = only(head_mask(CHUNK, index), q_rot[rows, tile])
            scores = []
            for block in range(chunk + 1):
                part = dot_t(query_head, k_rot[block * CHUNK : (block + 1) * CHUNK, tile])
                scores.append(jnp.where(visible, part, MASKED) if block == chunk else part)
            peak = jnp.max(scores[0], axis=1, keepdims=True)
            for part in scores[1:]:
                peak = jnp.maximum(peak, jnp.max(part, axis=1, keepdims=True))
            scores = [jnp.exp(part - peak) for part in scores]
            denominator = sum(row_sum(part) for part in scores)
            inverse = 1.0 / denominator
            for block, part in enumerate(scores):
                value_rows = values[block * CHUNK : (block + 1) * CHUNK, tile]
                total = total + dot(
                    (part * inverse).astype(BF16), only(head_mask(CHUNK, index), value_rows)
                )
            log_tile = jnp.where(lane == 2 * at + index, peak + jnp.log(denominator), log_tile)
        mixed[rows, tile] = total.astype(BF16)
    logs[rows, :] = log_tile
    low = mixed[rows, :]
    half = wo.shape[1]
    store_pieces(partial, slice(0, half), dot(low, wo[...]))
    store_pieces(partial, slice(half, 2 * half), dot(low, wot[...]))


def forward_kernel(
    chunk, *refs
):
    part, part_over = refs[:PIECES], refs[PIECES : 2 * PIECES]
    forward_body(chunk, part, part_over, *refs[2 * PIECES :])


def forward_body(
    chunk, part, part_over, mine, theirs, gains, gains_far, wg, wgt, wu, wut, wd, wdt, *rest
):
    if chunk == 0:
        low_mine, side, hidden, gate, up, *partial = rest
    else:
        mixed = rest[0]
        low_mine, side, hidden, gate, up, *partial = rest[3:]
        keep_rows(zip(rest[1:3], rest[3:]))
        at = wg.shape[1] + mine.shape[1]
        side[:, at : at + mixed.shape[1]] = mixed[...]
        side[:, at + mixed.shape[1] :] = theirs[...]
    rows = slice(chunk * CHUNK, (chunk + 1) * CHUNK)
    branch, scale = branch_of(part, part_over)
    half, ff = mine.shape[1], wg.shape[1]
    normed = branch * scale * gain_of(gains, gains_far, 0)
    value = mine[rows, :].astype(F32) + normed[:, :half]
    hidden[:, :half] = value
    low_mine[rows, :] = value.astype(BF16)
    value = theirs[rows, :].astype(F32) + normed[:, half:]
    hidden[:, half:] = value
    side[rows, ff : ff + half] = value.astype(BF16)
    for tile in tiles(ff):
        left, right = low_mine[rows, :], side[rows, ff : ff + half]
        gate_act = dot(left, wg[:, tile]) + dot(right, wgt[:, tile])
        up_act = dot(left, wu[:, tile]) + dot(right, wut[:, tile])
        gate[:, tile] = gate_act
        up[:, tile] = up_act
        side[rows, tile] = (gate_act * jax.nn.sigmoid(gate_act) * up_act).astype(BF16)
    low = side[rows, :ff]
    store_pieces(partial, slice(0, half), dot(low, wd[...]))
    store_pieces(partial, slice(half, 2 * half), dot(low, wdt[...]))


def ff_norm_back_kernel(
    chunk, *refs
):
    part, part_over = refs[:PIECES], refs[PIECES : 2 * PIECES]
    hidden, cot_mine, cot_theirs, gains, gains_far, *rest = refs[2 * PIECES :]
    if chunk == 0:
        gff_mine, gff_theirs, out_mine, out_theirs, grad_gain = rest
    else:
        gain_before = rest[0]
        gff_mine, gff_theirs, out_mine, out_theirs, grad_gain = rest[5:]
        keep_rows(zip(rest[1:5], rest[5:]))
    rows = slice(chunk * CHUNK, (chunk + 1) * CHUNK)
    branch, scale = branch_of(part, part_over)
    half = cot_mine.shape[1]
    gain = gain_of(gains, gains_far, 1)
    block_out = hidden[...] + branch * scale * gain
    out_mine[rows, :] = block_out[:, :half]
    out_theirs[rows, :] = block_out[:, half:]
    upstream = jnp.concatenate([cot_mine[rows, :], cot_theirs[rows, :]], axis=1).astype(F32)
    grad_branch, gained = norm_back(branch, scale, gain, upstream)
    grad_gain[...] = gained if chunk == 0 else gain_before[...] + gained
    gff_mine[rows, :] = grad_branch[:, :half].astype(BF16)
    gff_theirs[rows, :] = grad_branch[:, half:].astype(BF16)


def backward_kernel(
    chunk, gff_mine, gff_theirs, gate, up, wd, wdt, wg, wgt, wu, wut, *rest
):
    if chunk == 0:
        grads, *partial = rest
    else:
        grads, *partial = rest[1:]
        keep_rows([rest[:2]])
    rows = slice(chunk * CHUNK, (chunk + 1) * CHUNK)
    half, ff = wd.shape[1], wg.shape[1]
    for tile in tiles(ff):
        grad_act = dot_t(gff_mine[rows, :], wd[tile, :]) + dot_t(gff_theirs[rows, :], wdt[tile, :])
        gate_act = gate[:, tile]
        sig = jax.nn.sigmoid(gate_act)
        grads[rows, tile] = (
            grad_act * up[:, tile] * sig * (1.0 + gate_act * (1.0 - sig))
        ).astype(BF16)
        there = slice(ff + tile.start, ff + tile.stop)
        grads[rows, there] = (grad_act * gate_act * sig).astype(BF16)
    left, right = grads[rows, :ff], grads[rows, ff:]
    for tile in tiles(half):
        store_pieces(partial, tile, dot_t(left, wg[tile, :]) + dot_t(right, wu[tile, :]))
        there = slice(half + tile.start, half + tile.stop)
        store_pieces(partial, there, dot_t(left, wgt[tile, :]) + dot_t(right, wut[tile, :]))


def attention_back_kernel(chunk, *refs):
    grad_part, grad_over, part, part_over = [
        refs[i * PIECES : (i + 1) * PIECES] for i in range(4)
    ]
    (
        cot_mine,
        cot_theirs,
        gains,
        gains_far,
        wo,
        wot,
        q_rot,
        k_rot,
        values,
        logs,
        queries,
        keys,
        totals,
        totals_over,
        qgain,
        kgain,
        cosine,
        sine_part,
        *rest,
    ) = refs[4 * PIECES :]
    half = wo.shape[1]
    width = queries.shape[1]
    if chunk == 0:
        gat_mine, side, gh_mine, gh_theirs, gqn, grad_gain, column, gk_sum, gv_sum = rest
    else:
        gain_before, column_in, gk_in, gv_in = rest[:4]
        gat_mine, side, gh_mine, gh_theirs, gqn, grad_gain, gkn, gv_low, inner_out = rest[6:]
        keep_rows(zip(rest[4:6], rest[6:]))
    rows = slice(chunk * CHUNK, (chunk + 1) * CHUNK)
    seen = (chunk + 1) * CHUNK
    branch, scale = branch_of(part, part_over)
    grad_hidden = (
        jnp.concatenate([cot_mine[rows, :], cot_theirs[rows, :]], axis=1).astype(F32)
        + total_of(grad_part, grad_over)
    )
    gh_mine[...] = grad_hidden[:, :half]
    gh_theirs[...] = grad_hidden[:, half:]
    grad_branch, gained = norm_back(branch, scale, gain_of(gains, gains_far, 0), grad_hidden)
    grad_gain[...] = gained if chunk == 0 else gain_before[...] + gained
    gat_mine[rows, :] = grad_branch[:, :half].astype(BF16)
    side[rows, :] = grad_branch[:, half:].astype(BF16)
    grad_mixed = (
        dot_t(gat_mine[rows, :], wo[...]) + dot_t(side[rows, :], wot[...])
    ).astype(BF16)
    visible = lower_triangle()
    query_total, key_total = rows_to_columns(totals[...] + totals_over[...], 2)
    query_inner = jnp.zeros((CHUNK, 1), F32)
    key_inner = jnp.zeros((seen, 1), F32)
    for at, tile in enumerate(tiles(width, LANES)):
        grad_query = jnp.zeros((CHUNK, LANES), F32)
        grad_key = [jnp.zeros((CHUNK, LANES), F32) for _ in range(chunk + 1)]
        grad_value = [jnp.zeros((CHUNK, LANES), F32) for _ in range(chunk + 1)]
        for index in range(2):
            mask = head_mask(CHUNK, index)
            query_head = only(mask, q_rot[rows, tile])
            grad_head = only(mask, grad_mixed[:, tile])
            log_column = logs[rows, 2 * at + index : 2 * at + index + 1]
            weights, grads = [], []
            for block in range(chunk + 1):
                span = slice(block * CHUNK, (block + 1) * CHUNK)
                scores = dot_t(query_head, k_rot[span, tile])
                if block == chunk:
                    scores = jnp.where(visible, scores, MASKED)
                weights.append(jnp.exp(scores - log_column))
                grads.append(dot_t(grad_head, values[span, tile]))
            inner = sum(row_sum(w * g) for w, g in zip(weights, grads))
            for block in range(chunk + 1):
                span = slice(block * CHUNK, (block + 1) * CHUNK)
                weight = weights[block]
                grad_scores = (weight * (grads[block] - inner)).astype(BF16)
                grad_value[block] = grad_value[block] + t_dot(weight.astype(BF16), grad_head)
                grad_query = grad_query + dot(grad_scores, only(mask, k_rot[span, tile]))
                grad_key[block] = grad_key[block] + t_dot(grad_scores, query_head)
        back = turn(grad_query * FACTOR, cosine[rows, :], -sine_part[rows, :])
        gqn[:, tile] = back
        query_inner = query_inner + row_sum(back * qgain[:, tile] * queries[rows, tile])
        if chunk == 0:
            gk_sum[:, tile] = grad_key[0]
            gv_sum[:, tile] = grad_value[0]
        else:
            key_all = jnp.concatenate([gk_in[:, tile] + grad_key[0], grad_key[1]], axis=0)
            value_all = jnp.concatenate([gv_in[:, tile] + grad_value[0], grad_value[1]], axis=0)
            gv_low[:, tile] = value_all.astype(BF16)
            back = turn(key_all, cosine[...], -sine_part[...])
            gkn[:, tile] = back
            key_inner = key_inner + row_sum(back * kgain[:, tile] * keys[:, tile])
    if chunk == 0:
        column[...] = jnp.broadcast_to(query_inner, (CHUNK, LANES))
    else:
        query_inner = jnp.concatenate([column_in[:, :1], query_inner], axis=0)
        inner_out[...] = columns_to_rows([query_inner, key_inner])


def query_key_back_kernel(
    gqn_first,
    gqn_second,
    gkn,
    queries,
    keys,
    totals,
    totals_over,
    inner,
    inner_over,
    qgain,
    kgain,
    mlp_part,
    attn_part,
    grads,
    gain_mine,
    gain_give,
):
    width = queries.shape[1]
    half = gain_mine.shape[1]
    for out, columns in ((gain_mine, slice(0, half)), (gain_give, slice(half, 2 * half))):
        out[...] = jnp.zeros(out.shape, F32)
        out[0:1, :] = mlp_part[:, columns]
        out[1:2, :] = attn_part[:, columns]
    query_total, key_total = rows_to_columns(totals[...] + totals_over[...], 2)
    query_inner, key_inner = rows_to_columns(inner[...] + inner_over[...], 2)
    gqn = jnp.concatenate([gqn_first[...], gqn_second[...]], axis=0)
    for at, raw, back, total, sums, gain, low in (
        (2, queries, gqn, query_total, query_inner, qgain, grads.at[:, :width]),
        (3, keys, gkn[...], key_total, key_inner, kgain, grads.at[:, width:]),
    ):
        scale = rms_scale(total)
        value = raw[...]
        low[...] = (
            scale * (back * gain[...]) - value * (scale * scale * scale * sums / D)
        ).astype(BF16)
        gained = jnp.sum(back * value * scale, axis=0, keepdims=True)
        gain_mine[at : at + 1, :] = gained
        gain_give[at : at + 1, :] = gained


GAIN_ROWS = 16


def plain_weight_kernel(products, *refs):
    plain = refs[-1]

    def view(operand):
        index, start, stop = operand
        return refs[index].at[:, start:stop]

    at = 0
    for product in products:
        left, left_far, right, right_far = [view(operand) for operand in product]
        width = product[2][2] - product[2][1]
        for tile in tiles(plain.shape[0]):
            plain[tile, at : at + width] = (
                t_dot(left[:, tile], right[...]) + t_dot(left_far[:, tile], right_far[...])
            ).astype(BF16)
        at += width


def weight_kernel(with_gains, products, *refs):
    keep, give, plain = refs[-3:]
    plain_weight_kernel(products, *refs[:-3], plain)
    half = plain.shape[0] // 2
    mine = pl.multiple_of(own_half() * half, half)
    theirs = pl.multiple_of((1 - own_half()) * half, half)
    keep[:half, :] = plain[pl.ds(mine, half), :]
    give[:half, :] = plain[pl.ds(theirs, half), :]
    if with_gains:
        gains = refs[-5][...] + refs[-4][...]
        width = gains.shape[1]
        rows = jnp.concatenate([gains, jnp.zeros_like(gains)], axis=0)
        rest = jnp.zeros((GAIN_ROWS, plain.shape[1] - width), F32)
        rows = jnp.concatenate([rows, rest], axis=1).astype(BF16)
        keep[half:, :] = rows
        give[half:, :] = rows


def add_kernel(mine, *rest):
    out = rest[-1]
    at = 0
    for piece in rest[:-1]:
        rows = slice(at, at + piece.shape[0])
        out[rows, :] = (mine[rows, :].astype(F32) + piece[...].astype(F32)).astype(BF16)
        at = rows.stop


def inner_kernel(mine, received, out):
    out[...] = jnp.where(is_inner(), mine[...], received[...])


def finish_kernel(mine, received, *outs):
    half = outs[0].shape[0] // 2
    for place, source in enumerate((mine, received)):
        to = pl.multiple_of((own_half() ^ place) * half, half)
        column = 0
        for out in outs:
            width = out.shape[1]
            out[pl.ds(to, half), :] = source[:half, column : column + width].astype(F32)
            column += width


def in_far_kernel(side_far, block, out):
    out[...] = jnp.where(on_own_chip(), side_far[:, side_far.shape[1] - out.shape[1] :], block[...])


def gains_out_kernel(total, *outs):
    rows = total[total.shape[0] - GAIN_ROWS :, :].astype(F32)
    for index, out in enumerate(outs):
        out[...] = rows[index : index + 1, : out.shape[1]]


def finish_rest_kernel(mine, received, query_first, query, key):
    half = query.shape[0] // 2
    split = query_first.shape[1]
    more = query.shape[1] - split
    query[:, :split] = query_first[...]
    for place, source in enumerate((mine, received)):
        to = pl.multiple_of((own_half() ^ place) * half, half)
        query[pl.ds(to, half), split:] = source[:half, :more].astype(F32)
        key[pl.ds(to, half), :] = source[:half, more:].astype(F32)


def grad_input_kernel(stays, moves, across, corner, out):
    own = on_own_chip()
    out[...] = jnp.where(own, stays[...], moves[...]) + jnp.where(
        own, across[...], corner[...]
    ).astype(F32)


def input_back_kernel(
    grads, gv, wq, wqt, wk, wkt, wv, wvt, *rest
):
    width = wq.shape[1]
    gq, gk = grads.at[:, :width], grads.at[:, width:]
    gh_mine, gh_theirs = rest[:2], rest[2:4]
    stays, moves, across, corner = rest[4:]
    for tile in tiles(wq.shape[0]):
        mine = (
            dot_t(gq[...], wq[tile, :]) + dot_t(gk[...], wk[tile, :]) + dot_t(gv[...], wv[tile, :])
        )
        theirs = (
            dot_t(gq[...], wqt[tile, :])
            + dot_t(gk[...], wkt[tile, :])
            + dot_t(gv[...], wvt[tile, :])
        )
        for chunk in range(2):
            rows = slice(chunk * CHUNK, (chunk + 1) * CHUNK)
            stays[rows, tile] = gh_mine[chunk][:, tile] + mine[rows]
            moves[rows, tile] = gh_theirs[chunk][:, tile] + theirs[rows]
        across[:, tile] = mine.astype(BF16)
        corner[:, tile] = theirs.astype(BF16)


def dp_exchange(values, bit):
    size = lax.axis_size("dp")
    return lax.ppermute(values, "dp", [(i, i ^ (1 << bit)) for i in range(size)])


def dp_bits():
    return lax.axis_size("dp").bit_length() - 1


def along_line(values, moves):
    pairs = [(2 * a + half, 2 * b + half) for a, b in moves for half in range(2)]
    return lax.ppermute(values, "dp", pairs)


def in_turn(operands, received):
    return lax.optimization_barrier((operands, received))


class Chain:
    def __init__(self, name, high, widths, keep, give):
        self.name, self.high, self.widths, self.keep, self.give = name, high, widths, keep, give
        self.back = False
        self.received = None

    def kernel(self, body, args, part, after, outs=None):
        out = call(
            body, outs or [shape(self.keep.shape)], args, f"{self.name}_{part}", after=after
        )
        if outs is None:
            (self.keep,) = out
        else:
            self.out = out
        return out[0]

    def combine(self, body, part, after):
        return self.kernel(body, [self.keep, *self.received], part, after)

    def finish(self, after):
        outs = [shape((self.high, w), F32) for w in self.widths]
        return self.kernel(finish_kernel, [self.keep, *self.received], "out", after, outs)


LINE = ((0, 1), (3, 2)), ((1, 2), (2, 1)), ((1, 0), (2, 3))


class Lanes:
    def __init__(self):
        self.line = [None, None, None]
        self.latest = None

    def send_y(self, chain, before=None):
        operands = [chain.keep if chain.back else chain.give]
        if before is not None:
            operands, before.received = in_turn(operands, before.received)
        chain.received = [dp_exchange(piece, 0) for piece in operands]

    def pass_on(self, index, chain):
        before, self.line[index] = self.line[index], chain
        if before is not None and chain is not None:
            chain.keep, before.received = in_turn(chain.keep, before.received)
        if chain is not None:
            chain.received = [along_line(chain.keep, LINE[index])]
        return before

    def advance(self, chain, following=None, after=()):
        current = chain
        late = following is not None and following is self.line[2]
        if following is not None and not late:
            self.send_y(following, chain)
        done = None
        if chain.back:
            done, chain = chain, None
        else:
            self.latest = chain.combine(add_kernel, "y", (self.latest, *after))
            if lax.axis_size("dp") != 8:
                for bit in range(1, dp_bits()):
                    other = dp_exchange(chain.keep, bit).astype(F32)
                    chain.keep = (chain.keep.astype(F32) + other).astype(BF16)
                chain.back = True
                chain = None
        for index, (body, part) in enumerate(
            ((add_kernel, "in"), (add_kernel, "across"), (inner_kernel, "out"))
        ):
            chain = self.pass_on(index, chain)
            if chain is not None:
                self.latest = chain.combine(body, f"z_{part}", (self.latest,))
        if chain is not None:
            chain.back = True
        if late:
            self.send_y(following, current)
        if done is not None:
            self.latest = done.finish((self.latest,))


def on_device(
    block_in,
    w_query,
    w_key,
    w_value,
    w_output,
    w_gate,
    w_up,
    w_down,
    qnorm_gain,
    knorm_gain,
    attn_gain,
    mlp_gain,
    cotangent,
):
    rows, half = block_in.shape
    width = w_query.shape[1]
    ff = w_gate.shape[1]
    pair = ("row", "col")

    to_over = [(0, 1), (3, 2)]
    to_corner = [(1, 2), (2, 1)]
    to_beside = [(2, 0), (1, 3)]
    from_same = [(0, 2), (3, 1)]

    in_over = lax.ppermute(block_in, pair, to_over)
    in_corner = lax.ppermute(block_in, pair, to_corner)
    in_beside = lax.ppermute(block_in, pair, to_beside)
    wq_far, wk_far = swap(w_query, "row"), swap(w_key, "row")
    qgain, kgain = qnorm_gain[None], knorm_gain[None]
    cosine, sine_part = rope_tables(rows)

    (cotangent, wv_give, wo_give), (in_corner, in_over) = in_turn(
        [cotangent, w_value, w_output], [in_corner, in_over]
    )
    cot_over = lax.ppermute(cotangent, pair, to_over)
    cot_corner = lax.ppermute(cotangent, pair, to_corner)
    wv_far, wo_far = swap(wv_give, "row"), swap(wo_give, "row")

    queries, keys, totals, in_mine, in_theirs = call(
        query_key_kernel,
        [shape((rows, width), F32)] * 2 + [shape((8, rows), F32)] + [shape((rows, half))] * 2,
        [in_over, in_beside, in_corner, wq_far, wk_far],
        "query_key",
        far=[block_in, w_query, w_key],
    )
    totals_over = swap(totals, "col")
    (values,) = call(
        value_kernel,
        [shape((rows, width))],
        [in_mine, in_theirs, w_value, wv_far],
        "value",
    )
    (cot_mine,) = call(
        choose_kernel, [shape((rows, half))], [cotangent, cot_over], "cotangent_mine"
    )
    (gains,) = call(
        pack_kernel, [shape((8, half), F32)], [attn_gain[None], mlp_gain[None]], "gains", after=(values,)
    )
    (gains,), (values,) = in_turn([gains], [values])
    gains_far = swap(gains, "row")
    attention_args = [
        queries,
        keys,
        values,
        totals,
        totals_over,
        qgain,
        kgain,
        cosine,
        sine_part,
        w_output,
        wo_far,
    ]
    partial = [shape((CHUNK // PIECES, D))] * PIECES
    attention_outs = [shape((rows, width))] * 3 + [shape((rows, LANES), F32), *partial]

    def send_over(pieces, before=None):
        if before is not None:
            for index in range(PIECES):
                (pieces[index],), (before[index],) = in_turn([pieces[index]], [before[index]])
        return [swap(piece, "col") for piece in pieces]

    *kept, first_a, first_b = call(
        functools.partial(attention_kernel, 0),
        attention_outs,
        attention_args,
        "attention_0",
        after=(cot_mine, gains_far),
    )
    first = [first_a, first_b]
    given, (kept[-1], cot_corner) = in_turn([w_gate, w_up, w_down], [kept[-1], cot_corner])
    wg_far, wu_far, wd_far = [swap(value, "row") for value in given]
    first_over = send_over(first)
    *kept, second_a, second_b = call(
        functools.partial(attention_kernel, 1),
        attention_outs,
        attention_args + kept,
        "attention_1",
    )
    q_rot, k_rot, mixed, logs = kept
    second = [second_a, second_b]
    second_over = send_over(second, first_over)
    parts, parts_over = [first, second], [first_over, second_over]

    side_width = ff + half + width + half

    def forward(chunk, over, kept, after):
        return call(
            functools.partial(forward_kernel, chunk),
            [shape((rows, half)), shape((rows, side_width)), shape((CHUNK, D), F32)]
            + [shape((CHUNK, ff), F32)] * 2
            + partial,
            [*parts[chunk], *over, in_mine, in_theirs, gains, gains_far]
            + [w_gate, wg_far, w_up, wu_far, w_down, wd_far]
            + kept,
            f"forward_{chunk}",
            after=after,
        )

    low_mine, side, *saved = forward(0, first_over, [], ())
    saved_all, ff_first = [saved[:3]], saved[3:]
    (cotangent,), (low_mine,) = in_turn([cotangent], [low_mine])
    cot_beside = lax.ppermute(cotangent, pair, to_beside)
    (cot_theirs,) = call(
        choose_kernel, [shape((rows, half))], [cot_beside, cot_corner], "cotangent_theirs"
    )
    ff_first_over = send_over(ff_first, second_over)
    low_mine, side, *saved = forward(1, second_over, [mixed, low_mine, side], ())
    saved_all.append(saved[:3])
    ff_second = saved[3:]
    ff_second_over = send_over(ff_second, ff_first_over)

    def weight_grad(name, arrays, products, after, gains=()):
        high = products[0][0][2] - products[0][0][1]
        widths = [right[2] - right[1] for _, _, right, _ in products]
        extra = GAIN_ROWS if gains else 0
        keep, give = call(
            functools.partial(weight_kernel, bool(gains), products),
            [shape((high // 2 + extra, sum(widths)))] * 2,
            [*arrays, *gains],
            name,
            scratch=[pltpu.VMEM((high, sum(widths)), BF16)],
            after=after,
        )
        return Chain(name, high, widths, keep, give)

    def ff_norm_back(chunk, mine, over, more, after):
        return call(
            functools.partial(ff_norm_back_kernel, chunk),
            [shape((rows, half))] * 2 + [shape((rows, half), F32)] * 2 + [shape((1, D), F32)],
            [*mine, *over, saved_all[chunk][0], cot_mine, cot_theirs, gains, gains_far, *more],
            f"ff_norm_back_{chunk}",
            after=after,
        )

    def backward(chunk, more, after):
        return call(
            functools.partial(backward_kernel, chunk),
            [shape((rows, 2 * ff)), *partial],
            [gff_mine, gff_theirs, *saved_all[chunk][1:]]
            + [w_down, wd_far, w_gate, wg_far, w_up, wu_far]
            + more,
            f"backward_{chunk}",
            after=after,
        )

    *kept, mlp_part = ff_norm_back(0, ff_first, ff_first_over, [], ())
    gff_mine, gff_theirs, _, _ = kept
    grads, *gh_first = backward(0, [], ())
    gh_first_over = send_over(gh_first, ff_second_over)
    *kept, mlp_part = ff_norm_back(
        1, ff_second, ff_second_over, [mlp_part, *kept], ()
    )
    gff_mine, gff_theirs, out_mine, out_theirs = kept
    (side,), (gff_theirs,) = in_turn([side], [gff_theirs])
    side_far = swap(side, "row")
    gff_far = swap(gff_theirs, "row")
    out_beside = lax.ppermute(out_theirs, pair, from_same)
    grads, *gh_second = backward(1, [grads], ())
    lanes = Lanes()
    down = weight_grad(
        "down",
        [side, side_far, gff_mine, gff_far],
        [((0, 0, ff), (1, 0, ff), (2, 0, half), (3, 0, half))],
        (grads,),
    )
    (block_out,) = call(
        choose_kernel,
        [shape((rows, half), F32)],
        [out_mine, out_beside],
        "block_out",
        after=(down.keep,),
    )
    (in_far,) = call(
        in_far_kernel, [shape((rows, half))], [side_far, block_in], "in_far", after=(block_out,)
    )
    lanes.send_y(down)
    (gh_second, grads), (gh_first_over, down.keep, in_far) = in_turn(
        [gh_second, grads], [gh_first_over, down.keep, in_far]
    )
    gh_second_over = send_over(gh_second)
    grads_far = swap(grads, "row")
    grad_parts, grad_over = [gh_first, gh_second], [gh_first_over, gh_second_over]

    def ff_grad(name, start, after):
        span = (start, start + ff)
        return weight_grad(
            name,
            [low_mine, side_far, grads, grads_far],
            [((0, 0, half), (1, ff, ff + half), (2, *span), (3, *span))],
            after,
        )

    latest = down.keep
    gh_mine, gh_theirs, gqn = [], [], []
    for chunk in range(2):
        args = [
            *grad_parts[chunk],
            *grad_over[chunk],
            *parts[chunk],
            *parts_over[chunk],
            cot_mine,
            cot_theirs,
            gains,
            gains_far,
            w_output,
            wo_far,
            q_rot,
            k_rot,
            values,
            logs,
            queries,
            keys,
            totals,
            totals_over,
            qgain,
            kgain,
            cosine,
            sine_part,
        ]
        outs = [shape((rows, half))] * 2
        outs += [shape((CHUNK, half), F32)] * 2 + [shape((CHUNK, width), F32), shape((1, D), F32)]
        if chunk == 0:
            outs += [shape((CHUNK, LANES), F32)] + [shape((CHUNK, width), F32)] * 2
        else:
            outs += [shape((rows, width), F32), shape((rows, width)), shape((8, rows), F32)]
            args += [attn_part, column, gk_sum, gv_sum, gat_mine, gat_theirs]
        gat_mine, gat_theirs, gm, gt, gq_turned, attn_part, *more = call(
            functools.partial(attention_back_kernel, chunk),
            outs,
            args,
            f"attention_back_{chunk}",
            after=(latest,),
            flops=3e10 if chunk else 1,
        )
        gh_mine.append(gm)
        gh_theirs.append(gt)
        gqn.append(gq_turned)
        if chunk == 0:
            column, gk_sum, gv_sum = more
            up = ff_grad("up", ff, (column,))
            gate = ff_grad("gate", 0, (up.keep,))
            lanes.latest = gate.keep
            lanes.advance(down, gate, grad_over[1])
            latest = lanes.latest
        else:
            gkn, gv, inner = more
    inner_over = swap(inner, "col")
    gat_far, gv_far = swap(gat_theirs, "row"), swap(gv, "row")
    grads_back, gain_mine, gain_give = call(
        query_key_back_kernel,
        [shape((rows, 2 * width))] + [shape((8, half), F32)] * 2,
        [
            *gqn,
            gkn,
            queries,
            keys,
            totals,
            totals_over,
            inner,
            inner_over,
            qgain,
            kgain,
            mlp_part,
            attn_part,
        ],
        "query_key_back",
        after=(gv,),
    )
    grads_back_far = swap(grads_back, "row")
    gain_far = swap(gain_give, "row")
    lanes.latest = grads_back
    lanes.advance(gate, up)
    split = width * 3 // 4
    mixing = weight_grad(
        "mixing",
        [mixed, side_far, gat_mine, gat_far, in_mine, in_far, gv, gv_far]
        + [grads_back, grads_back_far],
        [
            ((0, 0, width), (1, ff + half, ff + half + width), (2, 0, half), (3, 0, half)),
            ((4, 0, half), (5, 0, half), (6, 0, width), (7, 0, width)),
            ((4, 0, half), (5, 0, half), (8, 0, split), (9, 0, split)),
        ],
        (lanes.latest,),
    )
    rest = (split, 2 * width)
    matching = weight_grad(
        "matching",
        [in_mine, in_far, grads_back, grads_back_far],
        [((0, 0, half), (1, 0, half), (2, *rest), (3, *rest))],
        (mixing.keep,),
        (gain_mine, gain_far),
    )
    mixing.widths = [half, width, split]
    lanes.latest = matching.keep
    lanes.advance(up, mixing)
    stays, moves, across, corner = call(
        input_back_kernel,
        [shape((rows, half), F32)] * 2 + [shape((rows, half))] * 2,
        [grads_back, gv, w_query, wq_far, w_key, wk_far, w_value, wv_far]
        + [*gh_mine, *gh_theirs],
        "input_back",
        after=(lanes.latest,),
    )
    lanes.latest = across
    moves = lax.ppermute(moves, pair, from_same)
    across = lax.ppermute(across, pair, [(1, 0), (2, 3)])
    lanes.advance(mixing, matching)
    (corner,), (across,) = in_turn([corner], [across])
    corner = lax.ppermute(corner, pair, to_corner)
    lanes.advance(matching, down)
    (grad_input,) = call(
        grad_input_kernel,
        [shape((rows, half), F32)],
        [stays, moves, across, corner],
        "grad_input",
        after=(lanes.latest,),
    )
    lanes.latest = grad_input
    lanes.advance(down, gate)
    lanes.advance(gate, up)
    lanes.advance(up, mixing)
    lanes.advance(mixing, matching)
    gain_out = call(
        gains_out_kernel,
        [shape((1, half), F32)] * 2 + [shape((1, width), F32)] * 2,
        [matching.keep],
        "gains_out",
        after=(lanes.latest,),
    )
    grad_mlpgain, grad_attngain, grad_qgain, grad_kgain = [row[0] for row in gain_out]
    lanes.latest = gain_out[0]
    grad_out, grad_value, query_first = mixing.out
    grad_query, grad_key = call(
        finish_rest_kernel,
        [shape((half, width), F32)] * 2,
        [matching.keep, *matching.received, query_first],
        "matching_out",
        after=(lanes.latest,),
    )
    (grad_down,) = down.out
    (grad_gate,) = gate.out
    (grad_up,) = up.out
    return (
        block_out,
        grad_input,
        grad_query,
        grad_key,
        grad_value,
        grad_out,
        grad_gate,
        grad_up,
        grad_down,
        grad_qgain,
        grad_kgain,
        grad_attngain,
        grad_mlpgain,
    )


def solution(mesh):
    tokens = P(("dp", "col"), "row")
    grid, turned = P("row", "col"), P("col", "row")
    in_specs = (
        tokens,
        grid,
        grid,
        grid,
        turned,
        grid,
        grid,
        turned,
        P("col"),
        P("col"),
        P("row"),
        P("row"),
        tokens,
    )
    out_specs = (
        tokens,
        tokens,
        grid,
        grid,
        grid,
        turned,
        grid,
        grid,
        turned,
        P("col"),
        P("col"),
        P("row"),
        P("row"),
    )
    return jax.shard_map(
        on_device, mesh=mesh, in_specs=in_specs, out_specs=out_specs, check_vma=False
    )
```

```python
import functools
import math

import jax
import jax.numpy as jnp
import numpy as np
from jax import lax
from jax.experimental import pallas as pl
from jax.experimental.pallas import tpu as pltpu
from jax.sharding import PartitionSpec as P

D = 1024
HEAD = 64
SEQ = 512
EPSILON = 1e-06
ROPE_BASE = 500000.0
MASKED = -1e30
CHUNK = 256
PIECES = 2
TILE = 256
LANES = 128
FACTOR = 1.0 / math.sqrt(HEAD)

F32 = jnp.float32
BF16 = jnp.bfloat16


def swap(values, axis):
    return lax.ppermute(values, axis, [(0, 1), (1, 0)])


def dot(left, right):
    return jnp.dot(left, right, preferred_element_type=F32)


def dot_t(left, right):
    return lax.dot_general(left, right, (((1,), (1,)), ((), ())), preferred_element_type=F32)


def t_dot(left, right):
    return lax.dot_general(left, right, (((0,), (0,)), ((), ())), preferred_element_type=F32)


def shape(dims, kind=BF16):
    return jax.ShapeDtypeStruct(dims, kind)


def call(kernel, outs, args, name, scratch=(), after=(), far=(), flops=1):
    count, skip, fetched = len(args), len(after), len(far)
    vmem = pl.BlockSpec(memory_space=pltpu.VMEM)
    anywhere = pl.BlockSpec(memory_space=pl.ANY)
    buffers = [pltpu.VMEM(a.shape, a.dtype) for a in far]
    if fetched:
        buffers.append(pltpu.SemaphoreType.DMA((fetched,)))

    def body(*refs):
        sources, refs = refs[:fetched], refs[fetched:]
        copies = []
        if fetched:
            refs, local = refs[: -fetched - 1], refs[-fetched - 1 :]
            copies = [
                pltpu.make_async_copy(source, local[i], local[-1].at[i])
                for i, source in enumerate(sources)
            ]
            for copy in copies:
                copy.start()
            for copy in copies:
                copy.wait()
            sources = local[:-1]
        kernel(*sources, *refs[:count], *refs[count + skip :])

    return pl.pallas_call(
        body,
        out_shape=tuple(outs),
        in_specs=[pl.BlockSpec(memory_space=pltpu.HBM)] * fetched + [vmem] * count + [anywhere] * skip,
        out_specs=tuple([vmem] * len(outs)),
        scratch_shapes=[*scratch, *buffers],
        compiler_params=pltpu.CompilerParams(
            vmem_limit_bytes=12 << 20, fuse_transposed_lhs_in_matmul=True
        ),
        cost_estimate=pl.CostEstimate(flops=int(flops), bytes_accessed=1, transcendentals=0),
        name=name,
    )(*far, *args, *after)


def tiles(extent, size=TILE):
    return [slice(at, min(at + size, extent)) for at in range(0, extent, size)]


def row_sum(values):
    return jnp.sum(values, axis=1, keepdims=True)


def columns_to_rows(columns):
    count = columns[0].shape[0]
    lane = lax.broadcasted_iota(jnp.int32, (count, LANES), 1)
    packed = jnp.zeros((count, LANES), F32)
    for index, column in enumerate(columns):
        packed = jnp.where(lane == index, column, packed)
    return packed.T[:8]


def rows_to_columns(rows, count):
    turned = jnp.concatenate([rows] * (LANES // 8), axis=0).T
    return [turned[:, i : i + 1] for i in range(count)]


def rms_scale(total):
    return lax.rsqrt(total / D + EPSILON)


def turn(values, cosine, sine_part):
    lane = lax.broadcasted_iota(jnp.int32, cosine.shape, 1)
    first = (lane % HEAD) < HEAD // 2
    out = []
    for tile in tiles(values.shape[1], LANES):
        part = values[:, tile]
        other = jnp.where(
            first, pltpu.roll(part, LANES - HEAD // 2, 1), pltpu.roll(part, HEAD // 2, 1)
        )
        out.append(part * cosine + other * sine_part)
    return jnp.concatenate(out, axis=1)


def rope_tables(count):
    half = HEAD // 2
    frequency = np.exp(np.arange(half, dtype=np.float32) * np.float32(-2.0 * math.log(ROPE_BASE) / HEAD))
    angles = np.arange(count).astype(np.float32)[:, None] * frequency[None, :]
    cosine, sine_part = np.cos(angles), np.sin(angles)
    repeats = LANES // HEAD
    return (
        jnp.asarray(np.concatenate([cosine, cosine] * repeats, axis=1)),
        jnp.asarray(np.concatenate([-sine_part, sine_part] * repeats, axis=1)),
    )


def lower_triangle():
    rows = lax.broadcasted_iota(jnp.int32, (CHUNK, CHUNK), 0)
    cols = lax.broadcasted_iota(jnp.int32, (CHUNK, CHUNK), 1)
    return rows >= cols


def keep_rows(pairs):
    for before, out in pairs:
        out[:CHUNK] = before[:CHUNK]


def head_mask(count, index):
    lane = lax.broadcasted_iota(jnp.int32, (count, LANES), 1)
    return (lane < HEAD) if index == 0 else (lane >= HEAD)


def only(mask, values):
    return jnp.where(mask, values, jnp.zeros_like(values))


def total_of(mine, theirs):
    return jnp.concatenate(
        [a[...].astype(F32) + b[...].astype(F32) for a, b in zip(mine, theirs)], axis=0
    )


def branch_of(mine, theirs):
    branch = total_of(mine, theirs)
    return branch, rms_scale(row_sum(branch * branch))


def store_pieces(pieces, columns, values):
    at = 0
    for piece in pieces:
        high = piece.shape[0]
        piece[:, columns] = values[at : at + high].astype(BF16)
        at += high


def gain_of(mine, theirs, index):
    row = slice(index, index + 1)
    return jnp.concatenate([mine[row, :], theirs[row, :]], axis=1)


def on_own_chip():
    return lax.axis_index("row") == lax.axis_index("col")


def own_half():
    return lax.axis_index("dp") & 1


def is_inner():
    place = lax.axis_index("dp") >> 1
    return (place == 1) | (place == 2)


def norm_back(branch, scale, gain_vec, grad_out):
    weighted = grad_out * gain_vec
    inner = row_sum(weighted * branch)
    grad_branch = scale * weighted - branch * (scale * scale * scale * inner / D)
    grad_gain = jnp.sum(grad_out * branch * scale, axis=0, keepdims=True)
    return grad_branch, grad_gain


def pack_kernel(*refs):
    out = refs[-1]
    out[...] = jnp.zeros(out.shape, F32)
    for index, row in enumerate(refs[:-1]):
        out[index : index + 1, :] = row[...]


def copy_kernel(*refs):
    count = len(refs) // 2
    for source, out in zip(refs[:count], refs[count:]):
        out[...] = source[...]


def choose_kernel(first, other, out):
    out[...] = jnp.where(on_own_chip(), first[...], other[...])


def choose_two_kernel(first, other, beside, corner, out, out_theirs):
    choose_kernel(first, other, out)
    choose_kernel(beside, corner, out_theirs)


def query_key_kernel(
    block, wq, wk, over, beside, corner, wqt, wkt, q_out, k_out, total_out, mine, theirs
):
    choose_two_kernel(block, over, beside, corner, mine, theirs)
    query_sum = 0.0
    key_sum = 0.0
    for tile in tiles(wq.shape[1]):
        query = dot(mine[...], wq[:, tile]) + dot(theirs[...], wqt[:, tile])
        q_out[:, tile] = query
        query_sum = query_sum + row_sum(query * query)
        key = dot(mine[...], wk[:, tile]) + dot(theirs[...], wkt[:, tile])
        k_out[:, tile] = key
        key_sum = key_sum + row_sum(key * key)
    total_out[...] = columns_to_rows([query_sum, key_sum])


def value_kernel(mine, theirs, wv, wvt, v_out):
    for tile in tiles(wv.shape[1]):
        v_out[:, tile] = (dot(mine[...], wv[:, tile]) + dot(theirs[...], wvt[:, tile])).astype(BF16)


def attention_kernel(
    chunk,
    queries,
    keys,
    values,
    totals,
    totals_over,
    qgain,
    kgain,
    cosine,
    sine_part,
    wo,
    wot,
    *rest,
):
    if chunk == 0:
        q_rot, k_rot, mixed, logs, *partial = rest
    else:
        q_rot, k_rot, mixed, logs, *partial = rest[4:]
        keep_rows(zip(rest[:4], rest[4:]))
    rows = slice(chunk * CHUNK, (chunk + 1) * CHUNK)
    query_total, key_total = rows_to_columns(totals[...] + totals_over[...], 2)
    query = queries[rows, :] * rms_scale(query_total[rows]) * qgain[...]
    key = keys[rows, :] * rms_scale(key_total[rows]) * kgain[...]
    q_rot[rows, :] = (turn(query, cosine[rows, :], sine_part[rows, :]) * FACTOR).astype(BF16)
    k_rot[rows, :] = turn(key, cosine[rows, :], sine_part[rows, :]).astype(BF16)
    visible = lower_triangle()
    lane = lax.broadcasted_iota(jnp.int32, (CHUNK, LANES), 1)
    log_tile = jnp.zeros((CHUNK, LANES), F32)
    for at, tile in enumerate(tiles(queries.shape[1], LANES)):
        total = jnp.zeros((CHUNK, LANES), F32)
        for index in range(2):
            query_head = only(head_mask(CHUNK, index), q_rot[rows, tile])
            scores = []
            for block in range(chunk + 1):
                part = dot_t(query_head, k_rot[block * CHUNK : (block + 1) * CHUNK, tile])
                scores.append(jnp.where(visible, part, MASKED) if block == chunk else part)
            peak = jnp.max(scores[0], axis=1, keepdims=True)
            for part in scores[1:]:
                peak = jnp.maximum(peak, jnp.max(part, axis=1, keepdims=True))
            scores = [jnp.exp(part - peak) for part in scores]
            denominator = sum(row_sum(part) for part in scores)
            inverse = 1.0 / denominator
            for block, part in enumerate(scores):
                value_rows = values[block * CHUNK : (block + 1) * CHUNK, tile]
                total = total + dot(
                    (part * inverse).astype(BF16), only(head_mask(CHUNK, index), value_rows)
                )
            log_tile = jnp.where(lane == 2 * at + index, peak + jnp.log(denominator), log_tile)
        mixed[rows, tile] = total.astype(BF16)
    logs[rows, :] = log_tile
    low = mixed[rows, :]
    half = wo.shape[1]
    store_pieces(partial, slice(0, half), dot(low, wo[...]))
    store_pieces(partial, slice(half, 2 * half), dot(low, wot[...]))


def forward_kernel(
    chunk, *refs
):
    part, part_over = refs[:PIECES], refs[PIECES : 2 * PIECES]
    forward_body(chunk, part, part_over, *refs[2 * PIECES :])


def forward_body(
    chunk, part, part_over, mine, theirs, gains, gains_far, wg, wgt, wu, wut, wd, wdt, *rest
):
    if chunk == 0:
        low_mine, side, hidden, gate, up, *partial = rest
    else:
        mixed = rest[0]
        low_mine, side, hidden, gate, up, *partial = rest[3:]
        keep_rows(zip(rest[1:3], rest[3:]))
        at = wg.shape[1] + mine.shape[1]
        side[:, at : at + mixed.shape[1]] = mixed[...]
        side[:, at + mixed.shape[1] :] = theirs[...]
    rows = slice(chunk * CHUNK, (chunk + 1) * CHUNK)
    branch, scale = branch_of(part, part_over)
    half, ff = mine.shape[1], wg.shape[1]
    normed = branch * scale * gain_of(gains, gains_far, 0)
    value = mine[rows, :].astype(F32) + normed[:, :half]
    hidden[:, :half] = value
    low_mine[rows, :] = value.astype(BF16)
    value = theirs[rows, :].astype(F32) + normed[:, half:]
    hidden[:, half:] = value
    side[rows, ff : ff + half] = value.astype(BF16)
    for tile in tiles(ff):
        left, right = low_mine[rows, :], side[rows, ff : ff + half]
        gate_act = dot(left, wg[:, tile]) + dot(right, wgt[:, tile])
        up_act = dot(left, wu[:, tile]) + dot(right, wut[:, tile])
        gate[:, tile] = gate_act
        up[:, tile] = up_act
        side[rows, tile] = (gate_act * jax.nn.sigmoid(gate_act) * up_act).astype(BF16)
    low = side[rows, :ff]
    store_pieces(partial, slice(0, half), dot(low, wd[...]))
    store_pieces(partial, slice(half, 2 * half), dot(low, wdt[...]))


def ff_norm_back_kernel(
    chunk, *refs
):
    part, part_over = refs[:PIECES], refs[PIECES : 2 * PIECES]
    hidden, cot_mine, cot_theirs, gains, gains_far, *rest = refs[2 * PIECES :]
    if chunk == 0:
        gff_mine, gff_theirs, out_mine, out_theirs, grad_gain = rest
    else:
        gain_before = rest[0]
        gff_mine, gff_theirs, out_mine, out_theirs, grad_gain = rest[5:]
        keep_rows(zip(rest[1:5], rest[5:]))
    rows = slice(chunk * CHUNK, (chunk + 1) * CHUNK)
    branch, scale = branch_of(part, part_over)
    half = cot_mine.shape[1]
    gain = gain_of(gains, gains_far, 1)
    block_out = hidden[...] + branch * scale * gain
    out_mine[rows, :] = block_out[:, :half]
    out_theirs[rows, :] = block_out[:, half:]
    upstream = jnp.concatenate([cot_mine[rows, :], cot_theirs[rows, :]], axis=1).astype(F32)
    grad_branch, gained = norm_back(branch, scale, gain, upstream)
    grad_gain[...] = gained if chunk == 0 else gain_before[...] + gained
    gff_mine[rows, :] = grad_branch[:, :half].astype(BF16)
    gff_theirs[rows, :] = grad_branch[:, half:].astype(BF16)


def backward_kernel(
    chunk, gff_mine, gff_theirs, gate, up, wd, wdt, wg, wgt, wu, wut, *rest
):
    if chunk == 0:
        grads, *partial = rest
    else:
        grads, *partial = rest[1:]
        keep_rows([rest[:2]])
    rows = slice(chunk * CHUNK, (chunk + 1) * CHUNK)
    half, ff = wd.shape[1], wg.shape[1]
    for tile in tiles(ff):
        grad_act = dot_t(gff_mine[rows, :], wd[tile, :]) + dot_t(gff_theirs[rows, :], wdt[tile, :])
        gate_act = gate[:, tile]
        sig = jax.nn.sigmoid(gate_act)
        grads[rows, tile] = (
            grad_act * up[:, tile] * sig * (1.0 + gate_act * (1.0 - sig))
        ).astype(BF16)
        there = slice(ff + tile.start, ff + tile.stop)
        grads[rows, there] = (grad_act * gate_act * sig).astype(BF16)
    left, right = grads[rows, :ff], grads[rows, ff:]
    for tile in tiles(half):
        store_pieces(partial, tile, dot_t(left, wg[tile, :]) + dot_t(right, wu[tile, :]))
        there = slice(half + tile.start, half + tile.stop)
        store_pieces(partial, there, dot_t(left, wgt[tile, :]) + dot_t(right, wut[tile, :]))


def attention_back_kernel(chunk, *refs):
    grad_part, grad_over, part, part_over = [
        refs[i * PIECES : (i + 1) * PIECES] for i in range(4)
    ]
    (
        cot_mine,
        cot_theirs,
        gains,
        gains_far,
        wo,
        wot,
        q_rot,
        k_rot,
        values,
        logs,
        queries,
        keys,
        totals,
        totals_over,
        qgain,
        kgain,
        cosine,
        sine_part,
        *rest,
    ) = refs[4 * PIECES :]
    half = wo.shape[1]
    width = queries.shape[1]
    if chunk == 0:
        gat_mine, side, gh_mine, gh_theirs, gqn, grad_gain, column, gk_sum, gv_sum = rest
    else:
        gain_before, column_in, gk_in, gv_in = rest[:4]
        gat_mine, side, gh_mine, gh_theirs, gqn, grad_gain, gkn, gv_low, inner_out = rest[6:]
        keep_rows(zip(rest[4:6], rest[6:]))
    rows = slice(chunk * CHUNK, (chunk + 1) * CHUNK)
    seen = (chunk + 1) * CHUNK
    branch, scale = branch_of(part, part_over)
    grad_hidden = (
        jnp.concatenate([cot_mine[rows, :], cot_theirs[rows, :]], axis=1).astype(F32)
        + total_of(grad_part, grad_over)
    )
    gh_mine[...] = grad_hidden[:, :half]
    gh_theirs[...] = grad_hidden[:, half:]
    grad_branch, gained = norm_back(branch, scale, gain_of(gains, gains_far, 0), grad_hidden)
    grad_gain[...] = gained if chunk == 0 else gain_before[...] + gained
    gat_mine[rows, :] = grad_branch[:, :half].astype(BF16)
    side[rows, :] = grad_branch[:, half:].astype(BF16)
    grad_mixed = (
        dot_t(gat_mine[rows, :], wo[...]) + dot_t(side[rows, :], wot[...])
    ).astype(BF16)
    visible = lower_triangle()
    query_total, key_total = rows_to_columns(totals[...] + totals_over[...], 2)
    query_inner = jnp.zeros((CHUNK, 1), F32)
    key_inner = jnp.zeros((seen, 1), F32)
    for at, tile in enumerate(tiles(width, LANES)):
        grad_query = jnp.zeros((CHUNK, LANES), F32)
        grad_key = [jnp.zeros((CHUNK, LANES), F32) for _ in range(chunk + 1)]
        grad_value = [jnp.zeros((CHUNK, LANES), F32) for _ in range(chunk + 1)]
        for index in range(2):
            mask = head_mask(CHUNK, index)
            query_head = only(mask, q_rot[rows, tile])
            grad_head = only(mask, grad_mixed[:, tile])
            log_column = logs[rows, 2 * at + index : 2 * at + index + 1]
            weights, grads = [], []
            for block in range(chunk + 1):
                span = slice(block * CHUNK, (block + 1) * CHUNK)
                scores = dot_t(query_head, k_rot[span, tile])
                if block == chunk:
                    scores = jnp.where(visible, scores, MASKED)
                weights.append(jnp.exp(scores - log_column))
                grads.append(dot_t(grad_head, values[span, tile]))
            inner = sum(row_sum(w * g) for w, g in zip(weights, grads))
            for block in range(chunk + 1):
                span = slice(block * CHUNK, (block + 1) * CHUNK)
                weight = weights[block]
                grad_scores = (weight * (grads[block] - inner)).astype(BF16)
                grad_value[block] = grad_value[block] + t_dot(weight.astype(BF16), grad_head)
                grad_query = grad_query + dot(grad_scores, only(mask, k_rot[span, tile]))
                grad_key[block] = grad_key[block] + t_dot(grad_scores, query_head)
        back = turn(grad_query * FACTOR, cosine[rows, :], -sine_part[rows, :])
        gqn[:, tile] = back
        query_inner = query_inner + row_sum(back * qgain[:, tile] * queries[rows, tile])
        if chunk == 0:
            gk_sum[:, tile] = grad_key[0]
            gv_sum[:, tile] = grad_value[0]
        else:
            key_all = jnp.concatenate([gk_in[:, tile] + grad_key[0], grad_key[1]], axis=0)
            value_all = jnp.concatenate([gv_in[:, tile] + grad_value[0], grad_value[1]], axis=0)
            gv_low[:, tile] = value_all.astype(BF16)
            back = turn(key_all, cosine[...], -sine_part[...])
            gkn[:, tile] = back
            key_inner = key_inner + row_sum(back * kgain[:, tile] * keys[:, tile])
    if chunk == 0:
        column[...] = jnp.broadcast_to(query_inner, (CHUNK, LANES))
    else:
        query_inner = jnp.concatenate([column_in[:, :1], query_inner], axis=0)
        inner_out[...] = columns_to_rows([query_inner, key_inner])


def query_key_back_kernel(
    gqn_first,
    gqn_second,
    gkn,
    queries,
    keys,
    totals,
    totals_over,
    inner,
    inner_over,
    qgain,
    kgain,
    mlp_part,
    attn_part,
    gq,
    gk,
    gain_mine,
    gain_give,
):
    half = gain_mine.shape[1]
    for out, columns in ((gain_mine, slice(0, half)), (gain_give, slice(half, 2 * half))):
        out[...] = jnp.zeros(out.shape, F32)
        out[0:1, :] = mlp_part[:, columns]
        out[1:2, :] = attn_part[:, columns]
    query_total, key_total = rows_to_columns(totals[...] + totals_over[...], 2)
    query_inner, key_inner = rows_to_columns(inner[...] + inner_over[...], 2)
    gqn = jnp.concatenate([gqn_first[...], gqn_second[...]], axis=0)
    for at, raw, back, total, sums, gain, low in (
        (2, queries, gqn, query_total, query_inner, qgain, gq),
        (3, keys, gkn[...], key_total, key_inner, kgain, gk),
    ):
        scale = rms_scale(total)
        value = raw[...]
        low[...] = (
            scale * (back * gain[...]) - value * (scale * scale * scale * sums / D)
        ).astype(BF16)
        gained = jnp.sum(back * value * scale, axis=0, keepdims=True)
        gain_mine[at : at + 1, :] = gained
        gain_give[at : at + 1, :] = gained


GAIN_ROWS = 16


def plain_weight_kernel(products, *refs):
    plain = refs[-1]

    def view(operand):
        index, start, stop = operand
        return refs[index].at[:, start:stop]

    at = 0
    for product in products:
        left, left_far, right, right_far = [view(operand) for operand in product]
        width = product[2][2] - product[2][1]
        for tile in tiles(plain.shape[0]):
            plain[tile, at : at + width] = (
                t_dot(left[:, tile], right[...]) + t_dot(left_far[:, tile], right_far[...])
            ).astype(BF16)
        at += width


def weight_kernel(with_gains, products, *refs):
    keep, give, plain = refs[-3:]
    plain_weight_kernel(products, *refs[:-3], plain)
    half = plain.shape[0] // 2
    mine = pl.multiple_of(own_half() * half, half)
    theirs = pl.multiple_of((1 - own_half()) * half, half)
    keep[:half, :] = plain[pl.ds(mine, half), :]
    give[:half, :] = plain[pl.ds(theirs, half), :]
    if with_gains:
        gains = refs[-5][...] + refs[-4][...]
        width = gains.shape[1]
        rows = jnp.concatenate([gains, jnp.zeros_like(gains)], axis=0)
        rest = jnp.zeros((GAIN_ROWS, plain.shape[1] - width), F32)
        rows = jnp.concatenate([rows, rest], axis=1).astype(BF16)
        keep[half:, :] = rows
        give[half:, :] = rows


def add_kernel(mine, *rest):
    out = rest[-1]
    at = 0
    for piece in rest[:-1]:
        rows = slice(at, at + piece.shape[0])
        out[rows, :] = (mine[rows, :].astype(F32) + piece[...].astype(F32)).astype(BF16)
        at = rows.stop


def inner_kernel(mine, received, out):
    out[...] = jnp.where(is_inner(), mine[...], received[...])


def finish_kernel(mine, received, *outs):
    half = outs[0].shape[0] // 2
    for place, source in enumerate((mine, received)):
        to = pl.multiple_of((own_half() ^ place) * half, half)
        column = 0
        for out in outs:
            width = out.shape[1]
            out[pl.ds(to, half), :] = source[:half, column : column + width].astype(F32)
            column += width


def in_far_kernel(side_far, block, out):
    out[...] = jnp.where(on_own_chip(), side_far[:, side_far.shape[1] - out.shape[1] :], block[...])


def gains_out_kernel(total, *outs):
    rows = total[total.shape[0] - GAIN_ROWS :, :].astype(F32)
    for index, out in enumerate(outs):
        out[...] = rows[index : index + 1, : out.shape[1]]


def finish_last_kernel(mine, received, query_more, first, second, query):
    split = query.shape[1] - query_more.shape[1]
    finish_kernel(mine, received, first, second, query.at[:, :split])
    query[:, split:] = query_more[...]


def grad_input_kernel(stays, moves, across, corner, out):
    own = on_own_chip()
    out[...] = jnp.where(own, stays[...], moves[...]) + jnp.where(
        own, across[...], corner[...]
    ).astype(F32)


def input_back_kernel(
    gq, gk, gv, wq, wqt, wk, wkt, wv, wvt, *rest
):
    gh_mine, gh_theirs = rest[:2], rest[2:4]
    stays, moves, across, corner = rest[4:]
    for tile in tiles(wq.shape[0]):
        mine = (
            dot_t(gq[...], wq[tile, :]) + dot_t(gk[...], wk[tile, :]) + dot_t(gv[...], wv[tile, :])
        )
        theirs = (
            dot_t(gq[...], wqt[tile, :])
            + dot_t(gk[...], wkt[tile, :])
            + dot_t(gv[...], wvt[tile, :])
        )
        for chunk in range(2):
            rows = slice(chunk * CHUNK, (chunk + 1) * CHUNK)
            stays[rows, tile] = gh_mine[chunk][:, tile] + mine[rows]
            moves[rows, tile] = gh_theirs[chunk][:, tile] + theirs[rows]
        across[:, tile] = mine.astype(BF16)
        corner[:, tile] = theirs.astype(BF16)


def dp_exchange(values, bit):
    size = lax.axis_size("dp")
    return lax.ppermute(values, "dp", [(i, i ^ (1 << bit)) for i in range(size)])


def dp_bits():
    return lax.axis_size("dp").bit_length() - 1


def along_line(values, moves):
    pairs = [(2 * a + half, 2 * b + half) for a, b in moves for half in range(2)]
    return lax.ppermute(values, "dp", pairs)


def in_turn(operands, received):
    return lax.optimization_barrier((operands, received))


class Chain:
    def __init__(self, name, high, widths, keep, give):
        self.name, self.high, self.widths, self.keep, self.give = name, high, widths, keep, give
        self.back = False
        self.received = None

    def kernel(self, body, args, part, after, outs=None):
        out = call(
            body, outs or [shape(self.keep.shape)], args, f"{self.name}_{part}", after=after
        )
        if outs is None:
            (self.keep,) = out
        else:
            self.out = out
        return out[0]

    def combine(self, body, part, after):
        return self.kernel(body, [self.keep, *self.received], part, after)

    def finish(self, after):
        outs = [shape((self.high, w), F32) for w in self.widths]
        return self.kernel(finish_kernel, [self.keep, *self.received], "out", after, outs)


LINE = ((0, 1), (3, 2)), ((1, 2), (2, 1)), ((1, 0), (2, 3))


class Lanes:
    def __init__(self):
        self.line = [None, None, None]
        self.latest = None

    def send_y(self, chain, before=None):
        operands = [chain.keep if chain.back else chain.give]
        if before is not None:
            operands, before.received = in_turn(operands, before.received)
        chain.received = [dp_exchange(piece, 0) for piece in operands]

    def pass_on(self, index, chain):
        before, self.line[index] = self.line[index], chain
        if before is not None and chain is not None:
            chain.keep, before.received = in_turn(chain.keep, before.received)
        if chain is not None:
            chain.received = [along_line(chain.keep, LINE[index])]
        return before

    def advance(self, chain, following=None, after=()):
        current = chain
        late = following is not None and following is self.line[2]
        if following is not None and not late:
            self.send_y(following, chain)
        done = None
        if chain.back:
            done, chain = chain, None
        else:
            self.latest = chain.combine(add_kernel, "y", (self.latest, *after))
            if lax.axis_size("dp") != 8:
                for bit in range(1, dp_bits()):
                    other = dp_exchange(chain.keep, bit).astype(F32)
                    chain.keep = (chain.keep.astype(F32) + other).astype(BF16)
                chain.back = True
                chain = None
        for index, (body, part) in enumerate(
            ((add_kernel, "in"), (add_kernel, "across"), (inner_kernel, "out"))
        ):
            chain = self.pass_on(index, chain)
            if chain is not None:
                self.latest = chain.combine(body, f"z_{part}", (self.latest,))
        if chain is not None:
            chain.back = True
        if late:
            self.send_y(following, current)
        if done is not None:
            self.latest = done.finish((self.latest,))


def on_device(
    block_in,
    w_query,
    w_key,
    w_value,
    w_output,
    w_gate,
    w_up,
    w_down,
    qnorm_gain,
    knorm_gain,
    attn_gain,
    mlp_gain,
    cotangent,
):
    rows, half = block_in.shape
    width = w_query.shape[1]
    ff = w_gate.shape[1]
    pair = ("row", "col")

    to_over = [(0, 1), (3, 2)]
    to_corner = [(1, 2), (2, 1)]
    to_beside = [(2, 0), (1, 3)]
    from_same = [(0, 2), (3, 1)]

    in_over = lax.ppermute(block_in, pair, to_over)
    in_corner = lax.ppermute(block_in, pair, to_corner)
    in_beside = lax.ppermute(block_in, pair, to_beside)
    wq_far, wk_far = swap(w_query, "row"), swap(w_key, "row")
    qgain, kgain = qnorm_gain[None], knorm_gain[None]
    cosine, sine_part = rope_tables(rows)

    near = call(
        copy_kernel,
        [shape((rows, half)), shape((half, width)), shape((half, width))],
        [block_in, w_query, w_key],
        "near",
    )
    (wv_give, wo_give), (in_corner, in_over, *near) = in_turn(
        [w_value, w_output], [in_corner, in_over, *near]
    )
    wv_far, wo_far = swap(wv_give, "row"), swap(wo_give, "row")

    queries, keys, totals, in_mine, in_theirs = call(
        query_key_kernel,
        [shape((rows, width), F32)] * 2 + [shape((8, rows), F32)] + [shape((rows, half))] * 2,
        [*near, in_over, in_beside, in_corner, wq_far, wk_far],
        "query_key",
    )
    totals_over = swap(totals, "col")
    (cotangent,), (in_mine,) = in_turn([cotangent], [in_mine])
    cot_over = lax.ppermute(cotangent, pair, to_over)
    cot_corner = lax.ppermute(cotangent, pair, to_corner)
    (values,) = call(
        value_kernel,
        [shape((rows, width))],
        [in_mine, in_theirs, w_value, wv_far],
        "value",
    )
    (gains,) = call(
        pack_kernel, [shape((8, half), F32)], [attn_gain[None], mlp_gain[None]], "gains", after=(values,)
    )
    (gains,), (values,) = in_turn([gains], [values])
    gains_far = swap(gains, "row")
    attention_args = [
        queries,
        keys,
        values,
        totals,
        totals_over,
        qgain,
        kgain,
        cosine,
        sine_part,
        w_output,
        wo_far,
    ]
    partial = [shape((CHUNK // PIECES, D))] * PIECES
    attention_outs = [shape((rows, width))] * 3 + [shape((rows, LANES), F32), *partial]

    def send_over(pieces, before=None):
        if before is not None:
            for index in range(PIECES):
                (pieces[index],), (before[index],) = in_turn([pieces[index]], [before[index]])
        return [swap(piece, "col") for piece in pieces]

    *kept, first_a, first_b = call(
        functools.partial(attention_kernel, 0),
        attention_outs,
        attention_args,
        "attention_0",
        after=(gains_far,),
    )
    first = [first_a, first_b]
    given, (kept[-1], cot_corner, cot_over) = in_turn(
        [w_gate, w_up, w_down], [kept[-1], cot_corner, cot_over]
    )
    wg_far, wu_far, wd_far = [swap(value, "row") for value in given]
    first_over = send_over(first)
    *kept, second_a, second_b = call(
        functools.partial(attention_kernel, 1),
        attention_outs,
        attention_args + kept,
        "attention_1",
    )
    q_rot, k_rot, mixed, logs = kept
    second = [second_a, second_b]
    second_over = send_over(second, first_over)
    parts, parts_over = [first, second], [first_over, second_over]

    side_width = ff + half + width + half

    def forward(chunk, over, kept, after):
        return call(
            functools.partial(forward_kernel, chunk),
            [shape((rows, half)), shape((rows, side_width)), shape((CHUNK, D), F32)]
            + [shape((CHUNK, ff), F32)] * 2
            + partial,
            [*parts[chunk], *over, in_mine, in_theirs, gains, gains_far]
            + [w_gate, wg_far, w_up, wu_far, w_down, wd_far]
            + kept,
            f"forward_{chunk}",
            after=after,
        )

    low_mine, side, *saved = forward(0, first_over, [], ())
    saved_all, ff_first = [saved[:3]], saved[3:]
    (cotangent,), (low_mine,) = in_turn([cotangent], [low_mine])
    cot_beside = lax.ppermute(cotangent, pair, to_beside)
    (cot_mine,) = call(
        choose_kernel, [shape((rows, half))], [cotangent, cot_over], "cotangent_mine"
    )
    (cot_theirs,) = call(
        choose_kernel, [shape((rows, half))], [cot_beside, cot_corner], "cotangent_theirs"
    )
    ff_first_over = send_over(ff_first, second_over)
    low_mine, side, *saved = forward(1, second_over, [mixed, low_mine, side], ())
    saved_all.append(saved[:3])
    ff_second = saved[3:]
    ff_second_over = send_over(ff_second, ff_first_over)

    def weight_grad(name, arrays, products, after, gains=()):
        high = products[0][0][2] - products[0][0][1]
        widths = [right[2] - right[1] for _, _, right, _ in products]
        extra = GAIN_ROWS if gains else 0
        keep, give = call(
            functools.partial(weight_kernel, bool(gains), products),
            [shape((high // 2 + extra, sum(widths)))] * 2,
            [*arrays, *gains],
            name,
            scratch=[pltpu.VMEM((high, sum(widths)), BF16)],
            after=after,
        )
        return Chain(name, high, widths, keep, give)

    def ff_norm_back(chunk, mine, over, more, after):
        return call(
            functools.partial(ff_norm_back_kernel, chunk),
            [shape((rows, half))] * 2 + [shape((rows, half), F32)] * 2 + [shape((1, D), F32)],
            [*mine, *over, saved_all[chunk][0], cot_mine, cot_theirs, gains, gains_far, *more],
            f"ff_norm_back_{chunk}",
            after=after,
        )

    def backward(chunk, more, after):
        return call(
            functools.partial(backward_kernel, chunk),
            [shape((rows, 2 * ff)), *partial],
            [gff_mine, gff_theirs, *saved_all[chunk][1:]]
            + [w_down, wd_far, w_gate, wg_far, w_up, wu_far]
            + more,
            f"backward_{chunk}",
            after=after,
        )

    *kept, mlp_part = ff_norm_back(0, ff_first, ff_first_over, [], ())
    gff_mine, gff_theirs, _, _ = kept
    grads, *gh_first = backward(0, [], ())
    gh_first_over = send_over(gh_first, ff_second_over)
    *kept, mlp_part = ff_norm_back(
        1, ff_second, ff_second_over, [mlp_part, *kept], ()
    )
    gff_mine, gff_theirs, out_mine, out_theirs = kept
    (side,), (gff_theirs,) = in_turn([side], [gff_theirs])
    side_far = swap(side, "row")
    gff_far = swap(gff_theirs, "row")
    out_beside = lax.ppermute(out_theirs, pair, from_same)
    grads, *gh_second = backward(1, [grads], ())
    lanes = Lanes()
    down = weight_grad(
        "down",
        [side, side_far, gff_mine, gff_far],
        [((0, 0, ff), (1, 0, ff), (2, 0, half), (3, 0, half))],
        (grads,),
    )
    (block_out,) = call(
        choose_kernel,
        [shape((rows, half), F32)],
        [out_mine, out_beside],
        "block_out",
        after=(down.keep,),
    )
    (in_far,) = call(
        in_far_kernel, [shape((rows, half))], [side_far, block_in], "in_far", after=(block_out,)
    )
    lanes.send_y(down)
    (gh_second, grads), (gh_first_over, down.keep, in_far) = in_turn(
        [gh_second, grads], [gh_first_over, down.keep, in_far]
    )
    gh_second_over = send_over(gh_second)
    grads_far = swap(grads, "row")
    grad_parts, grad_over = [gh_first, gh_second], [gh_first_over, gh_second_over]

    def ff_grad(name, start, after):
        span = (start, start + ff)
        return weight_grad(
            name,
            [low_mine, side_far, grads, grads_far],
            [((0, 0, half), (1, ff, ff + half), (2, *span), (3, *span))],
            after,
        )

    latest = down.keep
    gh_mine, gh_theirs, gqn = [], [], []
    for chunk in range(2):
        args = [
            *grad_parts[chunk],
            *grad_over[chunk],
            *parts[chunk],
            *parts_over[chunk],
            cot_mine,
            cot_theirs,
            gains,
            gains_far,
            w_output,
            wo_far,
            q_rot,
            k_rot,
            values,
            logs,
            queries,
            keys,
            totals,
            totals_over,
            qgain,
            kgain,
            cosine,
            sine_part,
        ]
        outs = [shape((rows, half))] * 2
        outs += [shape((CHUNK, half), F32)] * 2 + [shape((CHUNK, width), F32), shape((1, D), F32)]
        if chunk == 0:
            outs += [shape((CHUNK, LANES), F32)] + [shape((CHUNK, width), F32)] * 2
        else:
            outs += [shape((rows, width), F32), shape((rows, width)), shape((8, rows), F32)]
            args += [attn_part, column, gk_sum, gv_sum, gat_mine, gat_theirs]
        gat_mine, gat_theirs, gm, gt, gq_turned, attn_part, *more = call(
            functools.partial(attention_back_kernel, chunk),
            outs,
            args,
            f"attention_back_{chunk}",
            after=(latest, *(down.received if chunk else ())),
            flops=3e10 if chunk else 1,
        )
        gh_mine.append(gm)
        gh_theirs.append(gt)
        gqn.append(gq_turned)
        if chunk == 0:
            column, gk_sum, gv_sum = more
            up = ff_grad("up", ff, (column,))
            gate = ff_grad("gate", 0, (up.keep,))
            lanes.send_y(gate, down)
            latest = gate.keep
        else:
            gkn, gv, inner = more
    lanes.latest = inner
    lanes.advance(down)
    inner_over = swap(inner, "col")
    gat_far, gv_far = swap(gat_theirs, "row"), swap(gv, "row")
    gq, gk, gain_mine, gain_give = call(
        query_key_back_kernel,
        [shape((rows, width))] * 2 + [shape((8, half), F32)] * 2,
        [
            *gqn,
            gkn,
            queries,
            keys,
            totals,
            totals_over,
            inner,
            inner_over,
            qgain,
            kgain,
            mlp_part,
            attn_part,
        ],
        "query_key_back",
        after=(gv,),
    )
    gq_far, gk_far = swap(gq, "row"), swap(gk, "row")
    gain_far = swap(gain_give, "row")
    lanes.latest = gq
    lanes.advance(gate, up)
    split = width * 3 // 4
    matching = weight_grad(
        "matching",
        [in_mine, in_far, gq, gq_far, gk, gk_far],
        [
            ((0, 0, half), (1, 0, half), (2, split, width), (3, split, width)),
            ((0, 0, half), (1, 0, half), (4, 0, width), (5, 0, width)),
        ],
        (lanes.latest,),
        (gain_mine, gain_far),
    )
    mixing = weight_grad(
        "mixing",
        [mixed, side_far, gat_mine, gat_far, in_mine, in_far, gv, gv_far]
        + [gq, gq_far],
        [
            ((0, 0, width), (1, ff + half, ff + half + width), (2, 0, half), (3, 0, half)),
            ((4, 0, half), (5, 0, half), (6, 0, width), (7, 0, width)),
            ((4, 0, half), (5, 0, half), (8, 0, split), (9, 0, split)),
        ],
        (matching.keep,),
    )
    lanes.latest = mixing.keep
    lanes.advance(up, matching)
    stays, moves, across, corner = call(
        input_back_kernel,
        [shape((rows, half), F32)] * 2 + [shape((rows, half))] * 2,
        [gq, gk, gv, w_query, wq_far, w_key, wk_far, w_value, wv_far]
        + [*gh_mine, *gh_theirs],
        "input_back",
        after=(lanes.latest,),
    )
    lanes.latest = across
    moves = lax.ppermute(moves, pair, from_same)
    across = lax.ppermute(across, pair, [(1, 0), (2, 3)])
    lanes.advance(matching, mixing)
    (corner,), (across,) = in_turn([corner], [across])
    corner = lax.ppermute(corner, pair, to_corner)
    lanes.advance(mixing, down)
    (grad_input,) = call(
        grad_input_kernel,
        [shape((rows, half), F32)],
        [stays, moves, across, corner],
        "grad_input",
        after=(lanes.latest,),
    )
    lanes.latest = grad_input
    lanes.advance(down, gate)
    lanes.advance(gate, up)
    lanes.advance(up, matching)
    lanes.send_y(mixing, matching)
    key_more = call(
        finish_kernel,
        [shape((half, width - split), F32), shape((half, width), F32)],
        [matching.keep, *matching.received],
        "matching_out",
        after=(lanes.latest,),
    )
    query_more, grad_key = key_more
    lanes.latest = grad_key
    gain_out = call(
        gains_out_kernel,
        [shape((1, half), F32)] * 2 + [shape((1, width), F32)] * 2,
        [matching.keep],
        "gains_out",
        after=(lanes.latest,),
    )
    grad_mlpgain, grad_attngain, grad_qgain, grad_kgain = [row[0] for row in gain_out]
    lanes.latest = gain_out[0]
    grad_out, grad_value, grad_query = call(
        finish_last_kernel,
        [shape((half, width), F32)] * 3,
        [mixing.keep, *mixing.received, query_more],
        "mixing_out",
        after=(gain_out[0],),
    )
    (grad_down,) = down.out
    (grad_gate,) = gate.out
    (grad_up,) = up.out
    return (
        block_out,
        grad_input,
        grad_query,
        grad_key,
        grad_value,
        grad_out,
        grad_gate,
        grad_up,
        grad_down,
        grad_qgain,
        grad_kgain,
        grad_attngain,
        grad_mlpgain,
    )


def solution(mesh):
    tokens = P(("dp", "col"), "row")
    grid, turned = P("row", "col"), P("col", "row")
    in_specs = (
        tokens,
        grid,
        grid,
        grid,
        turned,
        grid,
        grid,
        turned,
        P("col"),
        P("col"),
        P("row"),
        P("row"),
        tokens,
    )
    out_specs = (
        tokens,
        tokens,
        grid,
        grid,
        grid,
        turned,
        grid,
        grid,
        turned,
        P("col"),
        P("col"),
        P("row"),
        P("row"),
    )
    return jax.shard_map(
        on_device, mesh=mesh, in_specs=in_specs, out_specs=out_specs, check_vma=False
    )
```

```python
import functools
import math

import jax
import jax.numpy as jnp
import numpy as np
from jax import lax
from jax.experimental import pallas as pl
from jax.experimental.pallas import tpu as pltpu
from jax.sharding import PartitionSpec as P

D = 1024
HEAD = 64
SEQ = 512
EPSILON = 1e-06
ROPE_BASE = 500000.0
MASKED = -1e30
CHUNK = 256
PIECES = 2
TILE = 256
LANES = 128
FACTOR = 1.0 / math.sqrt(HEAD)

F32 = jnp.float32
BF16 = jnp.bfloat16


def swap(values, axis):
    return lax.ppermute(values, axis, [(0, 1), (1, 0)])


def dot(left, right):
    return jnp.dot(left, right, preferred_element_type=F32)


def dot_t(left, right):
    return lax.dot_general(left, right, (((1,), (1,)), ((), ())), preferred_element_type=F32)


def t_dot(left, right):
    return lax.dot_general(left, right, (((0,), (0,)), ((), ())), preferred_element_type=F32)


def shape(dims, kind=BF16):
    return jax.ShapeDtypeStruct(dims, kind)


def call(kernel, outs, args, name, scratch=(), after=(), far=(), flops=1):
    count, skip, fetched = len(args), len(after), len(far)
    vmem = pl.BlockSpec(memory_space=pltpu.VMEM)
    anywhere = pl.BlockSpec(memory_space=pl.ANY)
    buffers = [pltpu.VMEM(a.shape, a.dtype) for a in far]
    if fetched:
        buffers.append(pltpu.SemaphoreType.DMA((fetched,)))

    def body(*refs):
        sources, refs = refs[:fetched], refs[fetched:]
        copies = []
        if fetched:
            refs, local = refs[: -fetched - 1], refs[-fetched - 1 :]
            copies = [
                pltpu.make_async_copy(source, local[i], local[-1].at[i])
                for i, source in enumerate(sources)
            ]
            for copy in copies:
                copy.start()
            for copy in copies:
                copy.wait()
            sources = local[:-1]
        kernel(*sources, *refs[:count], *refs[count + skip :])

    return pl.pallas_call(
        body,
        out_shape=tuple(outs),
        in_specs=[pl.BlockSpec(memory_space=pltpu.HBM)] * fetched + [vmem] * count + [anywhere] * skip,
        out_specs=tuple([vmem] * len(outs)),
        scratch_shapes=[*scratch, *buffers],
        compiler_params=pltpu.CompilerParams(
            vmem_limit_bytes=12 << 20, fuse_transposed_lhs_in_matmul=True
        ),
        cost_estimate=pl.CostEstimate(flops=int(flops), bytes_accessed=1, transcendentals=0),
        name=name,
    )(*far, *args, *after)


def tiles(extent, size=TILE):
    return [slice(at, min(at + size, extent)) for at in range(0, extent, size)]


def row_sum(values):
    return jnp.sum(values, axis=1, keepdims=True)


def columns_to_rows(columns):
    count = columns[0].shape[0]
    lane = lax.broadcasted_iota(jnp.int32, (count, LANES), 1)
    packed = jnp.zeros((count, LANES), F32)
    for index, column in enumerate(columns):
        packed = jnp.where(lane == index, column, packed)
    return packed.T[:8]


def rows_to_columns(rows, count):
    turned = jnp.concatenate([rows] * (LANES // 8), axis=0).T
    return [turned[:, i : i + 1] for i in range(count)]


def rms_scale(total):
    return lax.rsqrt(total / D + EPSILON)


def turn(values, cosine, sine_part):
    lane = lax.broadcasted_iota(jnp.int32, cosine.shape, 1)
    first = (lane % HEAD) < HEAD // 2
    out = []
    for tile in tiles(values.shape[1], LANES):
        part = values[:, tile]
        other = jnp.where(
            first, pltpu.roll(part, LANES - HEAD // 2, 1), pltpu.roll(part, HEAD // 2, 1)
        )
        out.append(part * cosine + other * sine_part)
    return jnp.concatenate(out, axis=1)


def rope_tables(count):
    half = HEAD // 2
    frequency = np.exp(np.arange(half, dtype=np.float32) * np.float32(-2.0 * math.log(ROPE_BASE) / HEAD))
    angles = np.arange(count).astype(np.float32)[:, None] * frequency[None, :]
    cosine, sine_part = np.cos(angles), np.sin(angles)
    repeats = LANES // HEAD
    return (
        jnp.asarray(np.concatenate([cosine, cosine] * repeats, axis=1)),
        jnp.asarray(np.concatenate([-sine_part, sine_part] * repeats, axis=1)),
    )


def lower_triangle():
    rows = lax.broadcasted_iota(jnp.int32, (CHUNK, CHUNK), 0)
    cols = lax.broadcasted_iota(jnp.int32, (CHUNK, CHUNK), 1)
    return rows >= cols


def keep_rows(pairs):
    for before, out in pairs:
        out[:CHUNK] = before[:CHUNK]


def head_mask(count, index):
    lane = lax.broadcasted_iota(jnp.int32, (count, LANES), 1)
    return (lane < HEAD) if index == 0 else (lane >= HEAD)


def only(mask, values):
    return jnp.where(mask, values, jnp.zeros_like(values))


def total_of(mine, theirs):
    return jnp.concatenate(
        [a[...].astype(F32) + b[...].astype(F32) for a, b in zip(mine, theirs)], axis=0
    )


def branch_of(mine, theirs):
    branch = total_of(mine, theirs)
    return branch, rms_scale(row_sum(branch * branch))


def store_pieces(pieces, columns, values):
    at = 0
    for piece in pieces:
        high = piece.shape[0]
        piece[:, columns] = values[at : at + high].astype(BF16)
        at += high


def gain_of(mine, theirs, index):
    row = slice(index, index + 1)
    return jnp.concatenate([mine[row, :], theirs[row, :]], axis=1)


def on_own_chip():
    return lax.axis_index("row") == lax.axis_index("col")


def own_half():
    return lax.axis_index("dp") & 1


def is_inner():
    place = lax.axis_index("dp") >> 1
    return (place == 1) | (place == 2)


def norm_back(branch, scale, gain_vec, grad_out):
    weighted = grad_out * gain_vec
    inner = row_sum(weighted * branch)
    grad_branch = scale * weighted - branch * (scale * scale * scale * inner / D)
    grad_gain = jnp.sum(grad_out * branch * scale, axis=0, keepdims=True)
    return grad_branch, grad_gain


def pack_kernel(*refs):
    out = refs[-1]
    out[...] = jnp.zeros(out.shape, F32)
    for index, row in enumerate(refs[:-1]):
        out[index : index + 1, :] = row[...]


def copy_kernel(*refs):
    count = len(refs) // 2
    for source, out in zip(refs[:count], refs[count:]):
        out[...] = source[...]


def pack_weights_kernel(wg, wu, wd, out):
    high, ff = wg.shape
    out[:, :ff] = wg[...]
    out[:, ff : 2 * ff] = wu[...]
    for index, rows in enumerate(tiles(ff, high)):
        at = 2 * ff + index * high
        out[: rows.stop - rows.start, at : at + high] = wd[rows, :]


def packed_weights(packed, ff):
    high = packed.shape[0]
    blocks = []
    for index, rows in enumerate(tiles(ff, high)):
        at = 2 * ff + index * high
        blocks.append((rows, packed.at[: rows.stop - rows.start, at : at + high]))
    return packed.at[:, :ff], packed.at[:, ff : 2 * ff], blocks


def choose_kernel(first, other, out):
    out[...] = jnp.where(on_own_chip(), first[...], other[...])


def choose_two_kernel(first, other, beside, corner, out, out_theirs):
    choose_kernel(first, other, out)
    choose_kernel(beside, corner, out_theirs)


def query_key_kernel(
    block, wq, wk, over, beside, corner, wqt, wkt, q_out, k_out, total_out, mine, theirs
):
    choose_two_kernel(block, over, beside, corner, mine, theirs)
    query_sum = 0.0
    key_sum = 0.0
    for tile in tiles(wq.shape[1]):
        query = dot(mine[...], wq[:, tile]) + dot(theirs[...], wqt[:, tile])
        q_out[:, tile] = query
        query_sum = query_sum + row_sum(query * query)
        key = dot(mine[...], wk[:, tile]) + dot(theirs[...], wkt[:, tile])
        k_out[:, tile] = key
        key_sum = key_sum + row_sum(key * key)
    total_out[...] = columns_to_rows([query_sum, key_sum])


def value_kernel(mine, theirs, wv, wvt, v_out):
    for tile in tiles(wv.shape[1]):
        v_out[:, tile] = (dot(mine[...], wv[:, tile]) + dot(theirs[...], wvt[:, tile])).astype(BF16)


def attention_kernel(
    chunk,
    queries,
    keys,
    values,
    totals,
    totals_over,
    qgain,
    kgain,
    cosine,
    sine_part,
    wo,
    wot,
    *rest,
):
    if chunk == 0:
        q_rot, k_rot, mixed, logs, *partial = rest
    else:
        q_rot, k_rot, mixed, logs, *partial = rest[4:]
        keep_rows(zip(rest[:4], rest[4:]))
    rows = slice(chunk * CHUNK, (chunk + 1) * CHUNK)
    query_total, key_total = rows_to_columns(totals[...] + totals_over[...], 2)
    query = queries[rows, :] * rms_scale(query_total[rows]) * qgain[...]
    key = keys[rows, :] * rms_scale(key_total[rows]) * kgain[...]
    q_rot[rows, :] = (turn(query, cosine[rows, :], sine_part[rows, :]) * FACTOR).astype(BF16)
    k_rot[rows, :] = turn(key, cosine[rows, :], sine_part[rows, :]).astype(BF16)
    visible = lower_triangle()
    lane = lax.broadcasted_iota(jnp.int32, (CHUNK, LANES), 1)
    log_tile = jnp.zeros((CHUNK, LANES), F32)
    for at, tile in enumerate(tiles(queries.shape[1], LANES)):
        total = jnp.zeros((CHUNK, LANES), F32)
        for index in range(2):
            query_head = only(head_mask(CHUNK, index), q_rot[rows, tile])
            scores = []
            for block in range(chunk + 1):
                part = dot_t(query_head, k_rot[block * CHUNK : (block + 1) * CHUNK, tile])
                scores.append(jnp.where(visible, part, MASKED) if block == chunk else part)
            peak = jnp.max(scores[0], axis=1, keepdims=True)
            for part in scores[1:]:
                peak = jnp.maximum(peak, jnp.max(part, axis=1, keepdims=True))
            scores = [jnp.exp(part - peak) for part in scores]
            denominator = sum(row_sum(part) for part in scores)
            inverse = 1.0 / denominator
            for block, part in enumerate(scores):
                value_rows = values[block * CHUNK : (block + 1) * CHUNK, tile]
                total = total + dot(
                    (part * inverse).astype(BF16), only(head_mask(CHUNK, index), value_rows)
                )
            log_tile = jnp.where(lane == 2 * at + index, peak + jnp.log(denominator), log_tile)
        mixed[rows, tile] = total.astype(BF16)
    logs[rows, :] = log_tile
    low = mixed[rows, :]
    half = wo.shape[1]
    store_pieces(partial, slice(0, half), dot(low, wo[...]))
    store_pieces(partial, slice(half, 2 * half), dot(low, wot[...]))


def forward_kernel(
    chunk, *refs
):
    part, part_over = refs[:PIECES], refs[PIECES : 2 * PIECES]
    forward_body(chunk, part, part_over, *refs[2 * PIECES :])


def forward_body(
    chunk, part, part_over, mine, theirs, gains, gains_far, wg, wu, wd, w_far, *rest
):
    if chunk == 0:
        low_mine, side, hidden, gate, up, *partial = rest
    else:
        mixed = rest[0]
        low_mine, side, hidden, gate, up, *partial = rest[3:]
        keep_rows(zip(rest[1:3], rest[3:]))
        at = wg.shape[1] + mine.shape[1]
        side[:, at : at + mixed.shape[1]] = mixed[...]
        side[:, at + mixed.shape[1] :] = theirs[...]
    rows = slice(chunk * CHUNK, (chunk + 1) * CHUNK)
    branch, scale = branch_of(part, part_over)
    half, ff = mine.shape[1], wg.shape[1]
    wgt, wut, wdt = packed_weights(w_far, ff)
    normed = branch * scale * gain_of(gains, gains_far, 0)
    value = mine[rows, :].astype(F32) + normed[:, :half]
    hidden[:, :half] = value
    low_mine[rows, :] = value.astype(BF16)
    value = theirs[rows, :].astype(F32) + normed[:, half:]
    hidden[:, half:] = value
    side[rows, ff : ff + half] = value.astype(BF16)
    for tile in tiles(ff):
        left, right = low_mine[rows, :], side[rows, ff : ff + half]
        gate_act = dot(left, wg[:, tile]) + dot(right, wgt[:, tile])
        up_act = dot(left, wu[:, tile]) + dot(right, wut[:, tile])
        gate[:, tile] = gate_act
        up[:, tile] = up_act
        side[rows, tile] = (gate_act * jax.nn.sigmoid(gate_act) * up_act).astype(BF16)
    low = side[rows, :ff]
    store_pieces(partial, slice(0, half), dot(low, wd[...]))
    theirs_part = sum(dot(side[rows, span], block[...]) for span, block in wdt)
    store_pieces(partial, slice(half, 2 * half), theirs_part)


def ff_norm_back_kernel(
    chunk, *refs
):
    part, part_over = refs[:PIECES], refs[PIECES : 2 * PIECES]
    hidden, cot_mine, cot_theirs, gains, gains_far, *rest = refs[2 * PIECES :]
    if chunk == 0:
        gff_mine, gff_theirs, out_mine, out_theirs, grad_gain = rest
    else:
        gain_before = rest[0]
        gff_mine, gff_theirs, out_mine, out_theirs, grad_gain = rest[5:]
        keep_rows(zip(rest[1:5], rest[5:]))
    rows = slice(chunk * CHUNK, (chunk + 1) * CHUNK)
    branch, scale = branch_of(part, part_over)
    half = cot_mine.shape[1]
    gain = gain_of(gains, gains_far, 1)
    block_out = hidden[...] + branch * scale * gain
    out_mine[rows, :] = block_out[:, :half]
    out_theirs[rows, :] = block_out[:, half:]
    upstream = jnp.concatenate([cot_mine[rows, :], cot_theirs[rows, :]], axis=1).astype(F32)
    grad_branch, gained = norm_back(branch, scale, gain, upstream)
    grad_gain[...] = gained if chunk == 0 else gain_before[...] + gained
    gff_mine[rows, :] = grad_branch[:, :half].astype(BF16)
    gff_theirs[rows, :] = grad_branch[:, half:].astype(BF16)


def backward_kernel(
    chunk, gff_mine, gff_theirs, gate, up, wg, wu, wd, w_far, *rest
):
    if chunk == 0:
        grads, *partial = rest
    else:
        grads, *partial = rest[1:]
        keep_rows([rest[:2]])
    rows = slice(chunk * CHUNK, (chunk + 1) * CHUNK)
    half, ff = wd.shape[1], wg.shape[1]
    wgt, wut, wdt = packed_weights(w_far, ff)
    for tile in tiles(ff):
        span, block = wdt[tile.start // wdt[0][0].stop]
        part = block[tile.start - span.start : tile.stop - span.start, :]
        grad_act = dot_t(gff_mine[rows, :], wd[tile, :]) + dot_t(gff_theirs[rows, :], part)
        gate_act = gate[:, tile]
        sig = jax.nn.sigmoid(gate_act)
        grads[rows, tile] = (
            grad_act * up[:, tile] * sig * (1.0 + gate_act * (1.0 - sig))
        ).astype(BF16)
        there = slice(ff + tile.start, ff + tile.stop)
        grads[rows, there] = (grad_act * gate_act * sig).astype(BF16)
    left, right = grads[rows, :ff], grads[rows, ff:]
    for tile in tiles(half):
        store_pieces(partial, tile, dot_t(left, wg[tile, :]) + dot_t(right, wu[tile, :]))
        there = slice(half + tile.start, half + tile.stop)
        store_pieces(partial, there, dot_t(left, wgt[tile, :]) + dot_t(right, wut[tile, :]))


def attention_back_kernel(chunk, *refs):
    grad_part, grad_over, part, part_over = [
        refs[i * PIECES : (i + 1) * PIECES] for i in range(4)
    ]
    (
        cot_mine,
        cot_theirs,
        gains,
        gains_far,
        wo,
        wot,
        q_rot,
        k_rot,
        values,
        logs,
        queries,
        keys,
        totals,
        totals_over,
        qgain,
        kgain,
        cosine,
        sine_part,
        *rest,
    ) = refs[4 * PIECES :]
    half = wo.shape[1]
    width = queries.shape[1]
    if chunk == 0:
        gat_mine, side, gh_mine, gh_theirs, gqn, grad_gain, column, gk_sum, gv_sum = rest
    else:
        gain_before, column_in, gk_in, gv_in = rest[:4]
        gat_mine, side, gh_mine, gh_theirs, gqn, grad_gain, gkn, gv_low, inner_out = rest[6:]
        keep_rows(zip(rest[4:6], rest[6:]))
    rows = slice(chunk * CHUNK, (chunk + 1) * CHUNK)
    seen = (chunk + 1) * CHUNK
    branch, scale = branch_of(part, part_over)
    grad_hidden = (
        jnp.concatenate([cot_mine[rows, :], cot_theirs[rows, :]], axis=1).astype(F32)
        + total_of(grad_part, grad_over)
    )
    gh_mine[...] = grad_hidden[:, :half]
    gh_theirs[...] = grad_hidden[:, half:]
    grad_branch, gained = norm_back(branch, scale, gain_of(gains, gains_far, 0), grad_hidden)
    grad_gain[...] = gained if chunk == 0 else gain_before[...] + gained
    gat_mine[rows, :] = grad_branch[:, :half].astype(BF16)
    side[rows, :] = grad_branch[:, half:].astype(BF16)
    grad_mixed = (
        dot_t(gat_mine[rows, :], wo[...]) + dot_t(side[rows, :], wot[...])
    ).astype(BF16)
    visible = lower_triangle()
    query_total, key_total = rows_to_columns(totals[...] + totals_over[...], 2)
    query_inner = jnp.zeros((CHUNK, 1), F32)
    key_inner = jnp.zeros((seen, 1), F32)
    for at, tile in enumerate(tiles(width, LANES)):
        grad_query = jnp.zeros((CHUNK, LANES), F32)
        grad_key = [jnp.zeros((CHUNK, LANES), F32) for _ in range(chunk + 1)]
        grad_value = [jnp.zeros((CHUNK, LANES), F32) for _ in range(chunk + 1)]
        for index in range(2):
            mask = head_mask(CHUNK, index)
            query_head = only(mask, q_rot[rows, tile])
            grad_head = only(mask, grad_mixed[:, tile])
            log_column = logs[rows, 2 * at + index : 2 * at + index + 1]
            weights, grads = [], []
            for block in range(chunk + 1):
                span = slice(block * CHUNK, (block + 1) * CHUNK)
                scores = dot_t(query_head, k_rot[span, tile])
                if block == chunk:
                    scores = jnp.where(visible, scores, MASKED)
                weights.append(jnp.exp(scores - log_column))
                grads.append(dot_t(grad_head, values[span, tile]))
            inner = sum(row_sum(w * g) for w, g in zip(weights, grads))
            for block in range(chunk + 1):
                span = slice(block * CHUNK, (block + 1) * CHUNK)
                weight = weights[block]
                grad_scores = (weight * (grads[block] - inner)).astype(BF16)
                grad_value[block] = grad_value[block] + t_dot(weight.astype(BF16), grad_head)
                grad_query = grad_query + dot(grad_scores, only(mask, k_rot[span, tile]))
                grad_key[block] = grad_key[block] + t_dot(grad_scores, query_head)
        back = turn(grad_query * FACTOR, cosine[rows, :], -sine_part[rows, :])
        gqn[:, tile] = back
        query_inner = query_inner + row_sum(back * qgain[:, tile] * queries[rows, tile])
        if chunk == 0:
            gk_sum[:, tile] = grad_key[0]
            gv_sum[:, tile] = grad_value[0]
        else:
            key_all = jnp.concatenate([gk_in[:, tile] + grad_key[0], grad_key[1]], axis=0)
            value_all = jnp.concatenate([gv_in[:, tile] + grad_value[0], grad_value[1]], axis=0)
            gv_low[:, tile] = value_all.astype(BF16)
            back = turn(key_all, cosine[...], -sine_part[...])
            gkn[:, tile] = back
            key_inner = key_inner + row_sum(back * kgain[:, tile] * keys[:, tile])
    if chunk == 0:
        column[...] = jnp.broadcast_to(query_inner, (CHUNK, LANES))
    else:
        query_inner = jnp.concatenate([column_in[:, :1], query_inner], axis=0)
        inner_out[...] = columns_to_rows([query_inner, key_inner])


def query_key_back_kernel(
    gqn_first,
    gqn_second,
    gkn,
    queries,
    keys,
    totals,
    totals_over,
    inner,
    inner_over,
    qgain,
    kgain,
    mlp_part,
    attn_part,
    grads,
    gain_mine,
    gain_give,
):
    width = queries.shape[1]
    half = gain_mine.shape[1]
    for out, columns in ((gain_mine, slice(0, half)), (gain_give, slice(half, 2 * half))):
        out[...] = jnp.zeros(out.shape, F32)
        out[0:1, :] = mlp_part[:, columns]
        out[1:2, :] = attn_part[:, columns]
    query_total, key_total = rows_to_columns(totals[...] + totals_over[...], 2)
    query_inner, key_inner = rows_to_columns(inner[...] + inner_over[...], 2)
    gqn = jnp.concatenate([gqn_first[...], gqn_second[...]], axis=0)
    for at, raw, back, total, sums, gain, low in (
        (2, queries, gqn, query_total, query_inner, qgain, grads.at[:, :width]),
        (3, keys, gkn[...], key_total, key_inner, kgain, grads.at[:, width:]),
    ):
        scale = rms_scale(total)
        value = raw[...]
        low[...] = (
            scale * (back * gain[...]) - value * (scale * scale * scale * sums / D)
        ).astype(BF16)
        gained = jnp.sum(back * value * scale, axis=0, keepdims=True)
        gain_mine[at : at + 1, :] = gained
        gain_give[at : at + 1, :] = gained


GAIN_ROWS = 16


def plain_weight_kernel(products, *refs):
    plain = refs[-1]

    def view(operand):
        index, start, stop = operand
        return refs[index].at[:, start:stop]

    at = 0
    for product in products:
        left, left_far, right, right_far = [view(operand) for operand in product]
        width = product[2][2] - product[2][1]
        for tile in tiles(plain.shape[0]):
            plain[tile, at : at + width] = (
                t_dot(left[:, tile], right[...]) + t_dot(left_far[:, tile], right_far[...])
            ).astype(BF16)
        at += width


def weight_kernel(with_gains, products, *refs):
    keep, give, plain = refs[-3:]
    plain_weight_kernel(products, *refs[:-3], plain)
    half = plain.shape[0] // 2
    mine = pl.multiple_of(own_half() * half, half)
    theirs = pl.multiple_of((1 - own_half()) * half, half)
    keep[:half, :] = plain[pl.ds(mine, half), :]
    give[:half, :] = plain[pl.ds(theirs, half), :]
    if with_gains:
        gains = refs[-5][...] + refs[-4][...]
        width = gains.shape[1]
        rows = jnp.concatenate([gains, jnp.zeros_like(gains)], axis=0)
        rest = jnp.zeros((GAIN_ROWS, plain.shape[1] - width), F32)
        rows = jnp.concatenate([rows, rest], axis=1).astype(BF16)
        keep[half:, :] = rows
        give[half:, :] = rows


def add_kernel(mine, *rest):
    out = rest[-1]
    at = 0
    for piece in rest[:-1]:
        rows = slice(at, at + piece.shape[0])
        out[rows, :] = (mine[rows, :].astype(F32) + piece[...].astype(F32)).astype(BF16)
        at = rows.stop


def inner_kernel(mine, received, out):
    out[...] = jnp.where(is_inner(), mine[...], received[...])


def finish_kernel(mine, received, *outs):
    half = outs[0].shape[0] // 2
    for place, source in enumerate((mine, received)):
        to = pl.multiple_of((own_half() ^ place) * half, half)
        column = 0
        for out in outs:
            width = out.shape[1]
            out[pl.ds(to, half), :] = source[:half, column : column + width].astype(F32)
            column += width


def in_far_kernel(side_far, block, out):
    out[...] = jnp.where(on_own_chip(), side_far[:, side_far.shape[1] - out.shape[1] :], block[...])


def gains_out_kernel(total, *outs):
    rows = total[total.shape[0] - GAIN_ROWS :, :].astype(F32)
    for index, out in enumerate(outs):
        out[...] = rows[index : index + 1, : out.shape[1]]


def finish_rest_kernel(mine, received, query_first, query, key):
    half = query.shape[0] // 2
    split = query_first.shape[1]
    more = query.shape[1] - split
    query[:, :split] = query_first[...]
    for place, source in enumerate((mine, received)):
        to = pl.multiple_of((own_half() ^ place) * half, half)
        query[pl.ds(to, half), split:] = source[:half, :more].astype(F32)
        key[pl.ds(to, half), :] = source[:half, more:].astype(F32)


def grad_input_kernel(stays, moves, across, corner, out):
    own = on_own_chip()
    out[...] = jnp.where(own, stays[...], moves[...]) + jnp.where(
        own, across[...], corner[...]
    ).astype(F32)


def input_back_kernel(
    grads, gv, wq, wqt, wk, wkt, wv, wvt, *rest
):
    width = wq.shape[1]
    gq, gk = grads.at[:, :width], grads.at[:, width:]
    gh_mine, gh_theirs = rest[:2], rest[2:4]
    stays, moves, across, corner = rest[4:]
    for tile in tiles(wq.shape[0]):
        mine = (
            dot_t(gq[...], wq[tile, :]) + dot_t(gk[...], wk[tile, :]) + dot_t(gv[...], wv[tile, :])
        )
        theirs = (
            dot_t(gq[...], wqt[tile, :])
            + dot_t(gk[...], wkt[tile, :])
            + dot_t(gv[...], wvt[tile, :])
        )
        for chunk in range(2):
            rows = slice(chunk * CHUNK, (chunk + 1) * CHUNK)
            stays[rows, tile] = gh_mine[chunk][:, tile] + mine[rows]
            moves[rows, tile] = gh_theirs[chunk][:, tile] + theirs[rows]
        across[:, tile] = mine.astype(BF16)
        corner[:, tile] = theirs.astype(BF16)


def dp_exchange(values, bit):
    size = lax.axis_size("dp")
    return lax.ppermute(values, "dp", [(i, i ^ (1 << bit)) for i in range(size)])


def dp_bits():
    return lax.axis_size("dp").bit_length() - 1


def along_line(values, moves):
    pairs = [(2 * a + half, 2 * b + half) for a, b in moves for half in range(2)]
    return lax.ppermute(values, "dp", pairs)


def in_turn(operands, received):
    return lax.optimization_barrier((operands, received))


class Chain:
    def __init__(self, name, high, widths, keep, give):
        self.name, self.high, self.widths, self.keep, self.give = name, high, widths, keep, give
        self.back = False
        self.received = None

    def kernel(self, body, args, part, after, outs=None):
        out = call(
            body, outs or [shape(self.keep.shape)], args, f"{self.name}_{part}", after=after
        )
        if outs is None:
            (self.keep,) = out
        else:
            self.out = out
        return out[0]

    def combine(self, body, part, after):
        return self.kernel(body, [self.keep, *self.received], part, after)

    def finish(self, after):
        outs = [shape((self.high, w), F32) for w in self.widths]
        return self.kernel(finish_kernel, [self.keep, *self.received], "out", after, outs)


LINE = ((0, 1), (3, 2)), ((1, 2), (2, 1)), ((1, 0), (2, 3))


class Lanes:
    def __init__(self):
        self.line = [None, None, None]
        self.latest = None

    def send_y(self, chain, before=None):
        operands = [chain.keep if chain.back else chain.give]
        if before is not None:
            operands, before.received = in_turn(operands, before.received)
        chain.received = [dp_exchange(piece, 0) for piece in operands]

    def pass_on(self, index, chain):
        before, self.line[index] = self.line[index], chain
        if before is not None and chain is not None:
            chain.keep, before.received = in_turn(chain.keep, before.received)
        if chain is not None:
            chain.received = [along_line(chain.keep, LINE[index])]
        return before

    def advance(self, chain, following=None, after=()):
        current = chain
        late = following is not None and following is self.line[2]
        if following is not None and not late:
            self.send_y(following, chain)
        done = None
        if chain.back:
            done, chain = chain, None
        else:
            self.latest = chain.combine(add_kernel, "y", (self.latest, *after))
            if lax.axis_size("dp") != 8:
                for bit in range(1, dp_bits()):
                    other = dp_exchange(chain.keep, bit).astype(F32)
                    chain.keep = (chain.keep.astype(F32) + other).astype(BF16)
                chain.back = True
                chain = None
        for index, (body, part) in enumerate(
            ((add_kernel, "in"), (add_kernel, "across"), (inner_kernel, "out"))
        ):
            chain = self.pass_on(index, chain)
            if chain is not None:
                self.latest = chain.combine(body, f"z_{part}", (self.latest,))
        if chain is not None:
            chain.back = True
        if late:
            self.send_y(following, current)
        if done is not None:
            self.latest = done.finish((self.latest,))


def on_device(
    block_in,
    w_query,
    w_key,
    w_value,
    w_output,
    w_gate,
    w_up,
    w_down,
    qnorm_gain,
    knorm_gain,
    attn_gain,
    mlp_gain,
    cotangent,
):
    rows, half = block_in.shape
    width = w_query.shape[1]
    ff = w_gate.shape[1]
    pair = ("row", "col")

    to_over = [(0, 1), (3, 2)]
    to_corner = [(1, 2), (2, 1)]
    to_beside = [(2, 0), (1, 3)]
    from_same = [(0, 2), (3, 1)]

    in_over = lax.ppermute(block_in, pair, to_over)
    in_corner = lax.ppermute(block_in, pair, to_corner)
    in_beside = lax.ppermute(block_in, pair, to_beside)
    wq_far, wk_far = swap(w_query, "row"), swap(w_key, "row")
    qgain, kgain = qnorm_gain[None], knorm_gain[None]
    cosine, sine_part = rope_tables(rows)

    near = call(
        copy_kernel,
        [shape((rows, half)), shape((half, width)), shape((half, width))],
        [block_in, w_query, w_key],
        "near",
    )
    (ff_weights,) = call(
        pack_weights_kernel,
        [shape((half, 2 * ff + -(-ff // half) * half))],
        [w_gate, w_up, w_down],
        "ff_weights",
        after=(near[0],),
    )
    (wv_give, wo_give), (in_corner, in_over, ff_weights, *near) = in_turn(
        [w_value, w_output], [in_corner, in_over, ff_weights, *near]
    )
    wv_far, wo_far = swap(wv_give, "row"), swap(wo_give, "row")

    queries, keys, totals, in_mine, in_theirs = call(
        query_key_kernel,
        [shape((rows, width), F32)] * 2 + [shape((8, rows), F32)] + [shape((rows, half))] * 2,
        [*near, in_over, in_beside, in_corner, wq_far, wk_far],
        "query_key",
    )
    totals_over = swap(totals, "col")
    (cotangent, ff_weights), (totals_over,) = in_turn([cotangent, ff_weights], [totals_over])
    cot_over = lax.ppermute(cotangent, pair, to_over)
    cot_corner = lax.ppermute(cotangent, pair, to_corner)
    w_far = swap(ff_weights, "row")
    (values,) = call(
        value_kernel,
        [shape((rows, width))],
        [in_mine, in_theirs, w_value, wv_far],
        "value",
    )
    (gains,) = call(
        pack_kernel, [shape((8, half), F32)], [attn_gain[None], mlp_gain[None]], "gains", after=(values,)
    )
    (gains,), (values,) = in_turn([gains], [values])
    gains_far = swap(gains, "row")
    attention_args = [
        queries,
        keys,
        values,
        totals,
        totals_over,
        qgain,
        kgain,
        cosine,
        sine_part,
        w_output,
        wo_far,
    ]
    partial = [shape((CHUNK // PIECES, D))] * PIECES
    attention_outs = [shape((rows, width))] * 3 + [shape((rows, LANES), F32), *partial]

    def send_over(pieces, before=None):
        if before is not None:
            for index in range(PIECES):
                (pieces[index],), (before[index],) = in_turn([pieces[index]], [before[index]])
        return [swap(piece, "col") for piece in pieces]

    *kept, first_a, first_b = call(
        functools.partial(attention_kernel, 0),
        attention_outs,
        attention_args,
        "attention_0",
        after=(gains_far,),
    )
    first = [first_a, first_b]
    first_over = send_over(first)
    *kept, second_a, second_b = call(
        functools.partial(attention_kernel, 1),
        attention_outs,
        attention_args + kept,
        "attention_1",
    )
    q_rot, k_rot, mixed, logs = kept
    second = [second_a, second_b]
    second_over = send_over(second, first_over)
    parts, parts_over = [first, second], [first_over, second_over]

    (cot_mine,) = call(
        choose_kernel, [shape((rows, half))], [cotangent, cot_over], "cotangent_mine"
    )
    side_width = ff + half + width + half

    def forward(chunk, over, kept, after):
        return call(
            functools.partial(forward_kernel, chunk),
            [shape((rows, half)), shape((rows, side_width)), shape((CHUNK, D), F32)]
            + [shape((CHUNK, ff), F32)] * 2
            + partial,
            [*parts[chunk], *over, in_mine, in_theirs, gains, gains_far]
            + [w_gate, w_up, w_down, w_far]
            + kept,
            f"forward_{chunk}",
            after=after,
        )

    low_mine, side, *saved = forward(0, first_over, [], (cot_mine, cot_corner))
    saved_all, ff_first = [saved[:3]], saved[3:]
    (cotangent,), (low_mine,) = in_turn([cotangent], [low_mine])
    cot_beside = lax.ppermute(cotangent, pair, to_beside)
    (cot_theirs,) = call(
        choose_kernel, [shape((rows, half))], [cot_beside, cot_corner], "cotangent_theirs"
    )
    ff_first_over = send_over(ff_first, second_over)
    low_mine, side, *saved = forward(1, second_over, [mixed, low_mine, side], ())
    saved_all.append(saved[:3])
    ff_second = saved[3:]
    ff_second_over = send_over(ff_second, ff_first_over)

    def weight_grad(name, arrays, products, after, gains=()):
        high = products[0][0][2] - products[0][0][1]
        widths = [right[2] - right[1] for _, _, right, _ in products]
        extra = GAIN_ROWS if gains else 0
        keep, give = call(
            functools.partial(weight_kernel, bool(gains), products),
            [shape((high // 2 + extra, sum(widths)))] * 2,
            [*arrays, *gains],
            name,
            scratch=[pltpu.VMEM((high, sum(widths)), BF16)],
            after=after,
        )
        return Chain(name, high, widths, keep, give)

    def ff_norm_back(chunk, mine, over, more, after):
        return call(
            functools.partial(ff_norm_back_kernel, chunk),
            [shape((rows, half))] * 2 + [shape((rows, half), F32)] * 2 + [shape((1, D), F32)],
            [*mine, *over, saved_all[chunk][0], cot_mine, cot_theirs, gains, gains_far, *more],
            f"ff_norm_back_{chunk}",
            after=after,
        )

    def backward(chunk, more, after):
        return call(
            functools.partial(backward_kernel, chunk),
            [shape((rows, 2 * ff)), *partial],
            [gff_mine, gff_theirs, *saved_all[chunk][1:]]
            + [w_gate, w_up, w_down, w_far]
            + more,
            f"backward_{chunk}",
            after=after,
        )

    *kept, mlp_part = ff_norm_back(0, ff_first, ff_first_over, [], ())
    gff_mine, gff_theirs, _, _ = kept
    grads, *gh_first = backward(0, [], ())
    gh_first_over = send_over(gh_first, ff_second_over)
    *kept, mlp_part = ff_norm_back(
        1, ff_second, ff_second_over, [mlp_part, *kept], ()
    )
    gff_mine, gff_theirs, out_mine, out_theirs = kept
    (side,), (gff_theirs,) = in_turn([side], [gff_theirs])
    side_far = swap(side, "row")
    gff_far = swap(gff_theirs, "row")
    out_beside = lax.ppermute(out_theirs, pair, from_same)
    grads, *gh_second = backward(1, [grads], ())
    lanes = Lanes()
    down = weight_grad(
        "down",
        [side, side_far, gff_mine, gff_far],
        [((0, 0, ff), (1, 0, ff), (2, 0, half), (3, 0, half))],
        (grads,),
    )
    (block_out,) = call(
        choose_kernel,
        [shape((rows, half), F32)],
        [out_mine, out_beside],
        "block_out",
        after=(down.keep,),
    )
    (in_far,) = call(
        in_far_kernel, [shape((rows, half))], [side_far, block_in], "in_far", after=(block_out,)
    )
    lanes.send_y(down)
    (gh_second, grads), (gh_first_over, down.keep, in_far) = in_turn(
        [gh_second, grads], [gh_first_over, down.keep, in_far]
    )
    gh_second_over = send_over(gh_second)
    grads_far = swap(grads, "row")
    grad_parts, grad_over = [gh_first, gh_second], [gh_first_over, gh_second_over]

    def ff_grad(name, start, after):
        span = (start, start + ff)
        return weight_grad(
            name,
            [low_mine, side_far, grads, grads_far],
            [((0, 0, half), (1, ff, ff + half), (2, *span), (3, *span))],
            after,
        )

    latest = down.keep
    gh_mine, gh_theirs, gqn = [], [], []
    for chunk in range(2):
        args = [
            *grad_parts[chunk],
            *grad_over[chunk],
            *parts[chunk],
            *parts_over[chunk],
            cot_mine,
            cot_theirs,
            gains,
            gains_far,
            w_output,
            wo_far,
            q_rot,
            k_rot,
            values,
            logs,
            queries,
            keys,
            totals,
            totals_over,
            qgain,
            kgain,
            cosine,
            sine_part,
        ]
        outs = [shape((rows, half))] * 2
        outs += [shape((CHUNK, half), F32)] * 2 + [shape((CHUNK, width), F32), shape((1, D), F32)]
        if chunk == 0:
            outs += [shape((CHUNK, LANES), F32)] + [shape((CHUNK, width), F32)] * 2
        else:
            outs += [shape((rows, width), F32), shape((rows, width)), shape((8, rows), F32)]
            args += [attn_part, column, gk_sum, gv_sum, gat_mine, gat_theirs]
        gat_mine, gat_theirs, gm, gt, gq_turned, attn_part, *more = call(
            functools.partial(attention_back_kernel, chunk),
            outs,
            args,
            f"attention_back_{chunk}",
            after=(latest,),
            flops=3e10 if chunk else 1,
        )
        gh_mine.append(gm)
        gh_theirs.append(gt)
        gqn.append(gq_turned)
        if chunk == 0:
            column, gk_sum, gv_sum = more
            up = ff_grad("up", ff, (column,))
            gate = ff_grad("gate", 0, (up.keep,))
            lanes.latest = gate.keep
            lanes.advance(down, gate, grad_over[1])
            latest = lanes.latest
        else:
            gkn, gv, inner = more
    inner_over = swap(inner, "col")
    gat_far, gv_far = swap(gat_theirs, "row"), swap(gv, "row")
    grads_back, gain_mine, gain_give = call(
        query_key_back_kernel,
        [shape((rows, 2 * width))] + [shape((8, half), F32)] * 2,
        [
            *gqn,
            gkn,
            queries,
            keys,
            totals,
            totals_over,
            inner,
            inner_over,
            qgain,
            kgain,
            mlp_part,
            attn_part,
        ],
        "query_key_back",
        after=(gv,),
    )
    grads_back_far = swap(grads_back, "row")
    gain_far = swap(gain_give, "row")
    lanes.latest = grads_back
    lanes.advance(gate, up)
    split = width * 3 // 4
    mixing = weight_grad(
        "mixing",
        [mixed, side_far, gat_mine, gat_far, in_mine, in_far, gv, gv_far]
        + [grads_back, grads_back_far],
        [
            ((0, 0, width), (1, ff + half, ff + half + width), (2, 0, half), (3, 0, half)),
            ((4, 0, half), (5, 0, half), (6, 0, width), (7, 0, width)),
            ((4, 0, half), (5, 0, half), (8, 0, split), (9, 0, split)),
        ],
        (lanes.latest,),
    )
    rest = (split, 2 * width)
    matching = weight_grad(
        "matching",
        [in_mine, in_far, grads_back, grads_back_far],
        [((0, 0, half), (1, 0, half), (2, *rest), (3, *rest))],
        (mixing.keep,),
        (gain_mine, gain_far),
    )
    mixing.widths = [half, width, split]
    lanes.latest = matching.keep
    lanes.advance(up, mixing)
    lanes.advance(mixing, matching)
    lanes.advance(matching, down)
    stays, moves, across, corner = call(
        input_back_kernel,
        [shape((rows, half), F32)] * 2 + [shape((rows, half))] * 2,
        [grads_back, gv, w_query, wq_far, w_key, wk_far, w_value, wv_far]
        + [*gh_mine, *gh_theirs],
        "input_back",
        after=(lanes.latest,),
    )
    lanes.latest = across
    moves = lax.ppermute(moves, pair, from_same)
    across = lax.ppermute(across, pair, [(1, 0), (2, 3)])
    lanes.advance(down, gate)
    (corner,), (across,) = in_turn([corner], [across])
    corner = lax.ppermute(corner, pair, to_corner)
    lanes.advance(gate, up)
    (grad_input,) = call(
        grad_input_kernel,
        [shape((rows, half), F32)],
        [stays, moves, across, corner],
        "grad_input",
        after=(lanes.latest,),
    )
    lanes.latest = grad_input
    lanes.advance(up, mixing)
    lanes.advance(mixing, matching)
    gain_out = call(
        gains_out_kernel,
        [shape((1, half), F32)] * 2 + [shape((1, width), F32)] * 2,
        [matching.keep],
        "gains_out",
        after=(lanes.latest,),
    )
    grad_mlpgain, grad_attngain, grad_qgain, grad_kgain = [row[0] for row in gain_out]
    lanes.latest = gain_out[0]
    grad_out, grad_value, query_first = mixing.out
    grad_query, grad_key = call(
        finish_rest_kernel,
        [shape((half, width), F32)] * 2,
        [matching.keep, *matching.received, query_first],
        "matching_out",
        after=(lanes.latest,),
    )
    (grad_down,) = down.out
    (grad_gate,) = gate.out
    (grad_up,) = up.out
    return (
        block_out,
        grad_input,
        grad_query,
        grad_key,
        grad_value,
        grad_out,
        grad_gate,
        grad_up,
        grad_down,
        grad_qgain,
        grad_kgain,
        grad_attngain,
        grad_mlpgain,
    )


def solution(mesh):
    tokens = P(("dp", "col"), "row")
    grid, turned = P("row", "col"), P("col", "row")
    in_specs = (
        tokens,
        grid,
        grid,
        grid,
        turned,
        grid,
        grid,
        turned,
        P("col"),
        P("col"),
        P("row"),
        P("row"),
        tokens,
    )
    out_specs = (
        tokens,
        tokens,
        grid,
        grid,
        grid,
        turned,
        grid,
        grid,
        turned,
        P("col"),
        P("col"),
        P("row"),
        P("row"),
    )
    return jax.shard_map(
        on_device, mesh=mesh, in_specs=in_specs, out_specs=out_specs, check_vma=False
    )
```

```python
import functools
import math

import jax
import jax.numpy as jnp
import numpy as np
from jax import lax
from jax.experimental import pallas as pl
from jax.experimental.pallas import tpu as pltpu
from jax.sharding import PartitionSpec as P

D = 1024
HEAD = 64
SEQ = 512
EPSILON = 1e-06
ROPE_BASE = 500000.0
MASKED = -1e30
CHUNK = 256
PIECES = 2
TILE = 256
LANES = 128
FACTOR = 1.0 / math.sqrt(HEAD)

F32 = jnp.float32
BF16 = jnp.bfloat16


def swap(values, axis):
    return lax.ppermute(values, axis, [(0, 1), (1, 0)])


def dot(left, right):
    return jnp.dot(left, right, preferred_element_type=F32)


def dot_t(left, right):
    return lax.dot_general(left, right, (((1,), (1,)), ((), ())), preferred_element_type=F32)


def t_dot(left, right):
    return lax.dot_general(left, right, (((0,), (0,)), ((), ())), preferred_element_type=F32)


def shape(dims, kind=BF16):
    return jax.ShapeDtypeStruct(dims, kind)


def call(kernel, outs, args, name, scratch=(), after=(), far=(), flops=1):
    count, skip, fetched = len(args), len(after), len(far)
    vmem = pl.BlockSpec(memory_space=pltpu.VMEM)
    anywhere = pl.BlockSpec(memory_space=pl.ANY)
    buffers = [pltpu.VMEM(a.shape, a.dtype) for a in far]
    if fetched:
        buffers.append(pltpu.SemaphoreType.DMA((fetched,)))

    def body(*refs):
        sources, refs = refs[:fetched], refs[fetched:]
        copies = []
        if fetched:
            refs, local = refs[: -fetched - 1], refs[-fetched - 1 :]
            copies = [
                pltpu.make_async_copy(source, local[i], local[-1].at[i])
                for i, source in enumerate(sources)
            ]
            for copy in copies:
                copy.start()
            for copy in copies:
                copy.wait()
            sources = local[:-1]
        kernel(*sources, *refs[:count], *refs[count + skip :])

    return pl.pallas_call(
        body,
        out_shape=tuple(outs),
        in_specs=[pl.BlockSpec(memory_space=pltpu.HBM)] * fetched + [vmem] * count + [anywhere] * skip,
        out_specs=tuple([vmem] * len(outs)),
        scratch_shapes=[*scratch, *buffers],
        compiler_params=pltpu.CompilerParams(
            vmem_limit_bytes=12 << 20, fuse_transposed_lhs_in_matmul=True
        ),
        cost_estimate=pl.CostEstimate(flops=int(flops), bytes_accessed=1, transcendentals=0),
        name=name,
    )(*far, *args, *after)


def tiles(extent, size=TILE):
    return [slice(at, min(at + size, extent)) for at in range(0, extent, size)]


def row_sum(values):
    return jnp.sum(values, axis=1, keepdims=True)


def columns_to_rows(columns):
    count = columns[0].shape[0]
    lane = lax.broadcasted_iota(jnp.int32, (count, LANES), 1)
    packed = jnp.zeros((count, LANES), F32)
    for index, column in enumerate(columns):
        packed = jnp.where(lane == index, column, packed)
    return packed.T[:8]


def rows_to_columns(rows, count):
    turned = jnp.concatenate([rows] * (LANES // 8), axis=0).T
    return [turned[:, i : i + 1] for i in range(count)]


def rms_scale(total):
    return lax.rsqrt(total / D + EPSILON)


def turn(values, cosine, sine_part):
    lane = lax.broadcasted_iota(jnp.int32, cosine.shape, 1)
    first = (lane % HEAD) < HEAD // 2
    out = []
    for tile in tiles(values.shape[1], LANES):
        part = values[:, tile]
        other = jnp.where(
            first, pltpu.roll(part, LANES - HEAD // 2, 1), pltpu.roll(part, HEAD // 2, 1)
        )
        out.append(part * cosine + other * sine_part)
    return jnp.concatenate(out, axis=1)


def rope_tables(count):
    half = HEAD // 2
    frequency = np.exp(np.arange(half, dtype=np.float32) * np.float32(-2.0 * math.log(ROPE_BASE) / HEAD))
    angles = np.arange(count).astype(np.float32)[:, None] * frequency[None, :]
    cosine, sine_part = np.cos(angles), np.sin(angles)
    repeats = LANES // HEAD
    return (
        jnp.asarray(np.concatenate([cosine, cosine] * repeats, axis=1)),
        jnp.asarray(np.concatenate([-sine_part, sine_part] * repeats, axis=1)),
    )


def lower_triangle():
    rows = lax.broadcasted_iota(jnp.int32, (CHUNK, CHUNK), 0)
    cols = lax.broadcasted_iota(jnp.int32, (CHUNK, CHUNK), 1)
    return rows >= cols


def keep_rows(pairs):
    for before, out in pairs:
        out[:CHUNK] = before[:CHUNK]


def head_mask(count, index):
    lane = lax.broadcasted_iota(jnp.int32, (count, LANES), 1)
    return (lane < HEAD) if index == 0 else (lane >= HEAD)


def only(mask, values):
    return jnp.where(mask, values, jnp.zeros_like(values))


def total_of(mine, theirs):
    return jnp.concatenate(
        [a[...].astype(F32) + b[...].astype(F32) for a, b in zip(mine, theirs)], axis=0
    )


def branch_of(mine, theirs):
    branch = total_of(mine, theirs)
    return branch, rms_scale(row_sum(branch * branch))


def store_pieces(pieces, columns, values):
    at = 0
    for piece in pieces:
        high = piece.shape[0]
        piece[:, columns] = values[at : at + high].astype(BF16)
        at += high


def gain_of(mine, theirs, index):
    row = slice(index, index + 1)
    return jnp.concatenate([mine[row, :], theirs[row, :]], axis=1)


def on_own_chip():
    return lax.axis_index("row") == lax.axis_index("col")


def own_half():
    return lax.axis_index("dp") & 1


def is_inner():
    place = lax.axis_index("dp") >> 1
    return (place == 1) | (place == 2)


def norm_back(branch, scale, gain_vec, grad_out):
    weighted = grad_out * gain_vec
    inner = row_sum(weighted * branch)
    grad_branch = scale * weighted - branch * (scale * scale * scale * inner / D)
    grad_gain = jnp.sum(grad_out * branch * scale, axis=0, keepdims=True)
    return grad_branch, grad_gain


def pack_kernel(*refs):
    out = refs[-1]
    out[...] = jnp.zeros(out.shape, F32)
    for index, row in enumerate(refs[:-1]):
        out[index : index + 1, :] = row[...]


def copy_kernel(*refs):
    count = len(refs) // 2
    for source, out in zip(refs[:count], refs[count:]):
        out[...] = source[...]


def pack_weights_kernel(wg, wu, wd, out):
    high, ff = wg.shape
    out[:, :ff] = wg[...]
    out[:, ff : 2 * ff] = wu[...]
    for index, rows in enumerate(tiles(ff, high)):
        at = 2 * ff + index * high
        out[: rows.stop - rows.start, at : at + high] = wd[rows, :]


def packed_weights(packed, ff):
    high = packed.shape[0]
    blocks = []
    for index, rows in enumerate(tiles(ff, high)):
        at = 2 * ff + index * high
        blocks.append((rows, packed.at[: rows.stop - rows.start, at : at + high]))
    return packed.at[:, :ff], packed.at[:, ff : 2 * ff], blocks


def choose_kernel(first, other, out):
    out[...] = jnp.where(on_own_chip(), first[...], other[...])


def choose_two_kernel(first, other, beside, corner, out, out_theirs):
    choose_kernel(first, other, out)
    choose_kernel(beside, corner, out_theirs)


def query_key_kernel(
    block, wq, wk, over, beside, corner, wqt, wkt, q_out, k_out, total_out, mine, theirs
):
    choose_two_kernel(block, over, beside, corner, mine, theirs)
    query_sum = 0.0
    key_sum = 0.0
    for tile in tiles(wq.shape[1]):
        query = dot(mine[...], wq[:, tile]) + dot(theirs[...], wqt[:, tile])
        q_out[:, tile] = query
        query_sum = query_sum + row_sum(query * query)
        key = dot(mine[...], wk[:, tile]) + dot(theirs[...], wkt[:, tile])
        k_out[:, tile] = key
        key_sum = key_sum + row_sum(key * key)
    total_out[...] = columns_to_rows([query_sum, key_sum])


def value_kernel(mine, theirs, wv, wvt, v_out):
    for tile in tiles(wv.shape[1]):
        v_out[:, tile] = (dot(mine[...], wv[:, tile]) + dot(theirs[...], wvt[:, tile])).astype(BF16)


def attention_kernel(
    chunk,
    queries,
    keys,
    values,
    totals,
    totals_over,
    qgain,
    kgain,
    cosine,
    sine_part,
    wo,
    wot,
    *rest,
):
    if chunk == 0:
        q_rot, k_rot, mixed, logs, *partial = rest
    else:
        q_rot, k_rot, mixed, logs, *partial = rest[4:]
        keep_rows(zip(rest[:4], rest[4:]))
    rows = slice(chunk * CHUNK, (chunk + 1) * CHUNK)
    query_total, key_total = rows_to_columns(totals[...] + totals_over[...], 2)
    query = queries[rows, :] * rms_scale(query_total[rows]) * qgain[...]
    key = keys[rows, :] * rms_scale(key_total[rows]) * kgain[...]
    q_rot[rows, :] = (turn(query, cosine[rows, :], sine_part[rows, :]) * FACTOR).astype(BF16)
    k_rot[rows, :] = turn(key, cosine[rows, :], sine_part[rows, :]).astype(BF16)
    visible = lower_triangle()
    lane = lax.broadcasted_iota(jnp.int32, (CHUNK, LANES), 1)
    log_tile = jnp.zeros((CHUNK, LANES), F32)
    for at, tile in enumerate(tiles(queries.shape[1], LANES)):
        total = jnp.zeros((CHUNK, LANES), F32)
        for index in range(2):
            query_head = only(head_mask(CHUNK, index), q_rot[rows, tile])
            scores = []
            for block in range(chunk + 1):
                part = dot_t(query_head, k_rot[block * CHUNK : (block + 1) * CHUNK, tile])
                scores.append(jnp.where(visible, part, MASKED) if block == chunk else part)
            peak = jnp.max(scores[0], axis=1, keepdims=True)
            for part in scores[1:]:
                peak = jnp.maximum(peak, jnp.max(part, axis=1, keepdims=True))
            scores = [jnp.exp(part - peak) for part in scores]
            denominator = sum(row_sum(part) for part in scores)
            inverse = 1.0 / denominator
            for block, part in enumerate(scores):
                value_rows = values[block * CHUNK : (block + 1) * CHUNK, tile]
                total = total + dot(
                    (part * inverse).astype(BF16), only(head_mask(CHUNK, index), value_rows)
                )
            log_tile = jnp.where(lane == 2 * at + index, peak + jnp.log(denominator), log_tile)
        mixed[rows, tile] = total.astype(BF16)
    logs[rows, :] = log_tile
    low = mixed[rows, :]
    half = wo.shape[1]
    store_pieces(partial, slice(0, half), dot(low, wo[...]))
    store_pieces(partial, slice(half, 2 * half), dot(low, wot[...]))


def forward_kernel(
    chunk, *refs
):
    part, part_over = refs[:PIECES], refs[PIECES : 2 * PIECES]
    forward_body(chunk, part, part_over, *refs[2 * PIECES :])


def forward_body(
    chunk, part, part_over, mine, theirs, gains, gains_far, wg, wu, wd, w_far, *rest
):
    if chunk == 0:
        low_mine, side, hidden, gate, up, *partial = rest
    else:
        mixed = rest[0]
        low_mine, side, hidden, gate, up, *partial = rest[3:]
        keep_rows(zip(rest[1:3], rest[3:]))
        at = wg.shape[1] + mine.shape[1]
        side[:, at : at + mixed.shape[1]] = mixed[...]
        side[:, at + mixed.shape[1] :] = theirs[...]
    rows = slice(chunk * CHUNK, (chunk + 1) * CHUNK)
    branch, scale = branch_of(part, part_over)
    half, ff = mine.shape[1], wg.shape[1]
    wgt, wut, wdt = packed_weights(w_far, ff)
    normed = branch * scale * gain_of(gains, gains_far, 0)
    value = mine[rows, :].astype(F32) + normed[:, :half]
    hidden[:, :half] = value
    low_mine[rows, :] = value.astype(BF16)
    value = theirs[rows, :].astype(F32) + normed[:, half:]
    hidden[:, half:] = value
    side[rows, ff : ff + half] = value.astype(BF16)
    for tile in tiles(ff):
        left, right = low_mine[rows, :], side[rows, ff : ff + half]
        gate_act = dot(left, wg[:, tile]) + dot(right, wgt[:, tile])
        up_act = dot(left, wu[:, tile]) + dot(right, wut[:, tile])
        gate[:, tile] = gate_act
        up[:, tile] = up_act
        side[rows, tile] = (gate_act * jax.nn.sigmoid(gate_act) * up_act).astype(BF16)
    low = side[rows, :ff]
    store_pieces(partial, slice(0, half), dot(low, wd[...]))
    theirs_part = sum(dot(side[rows, span], block[...]) for span, block in wdt)
    store_pieces(partial, slice(half, 2 * half), theirs_part)


def ff_norm_back_kernel(
    chunk, *refs
):
    part, part_over = refs[:PIECES], refs[PIECES : 2 * PIECES]
    hidden, cot_mine, cot_theirs, gains, gains_far, *rest = refs[2 * PIECES :]
    if chunk == 0:
        gff_mine, gff_theirs, out_mine, out_theirs, grad_gain = rest
    else:
        gain_before = rest[0]
        gff_mine, gff_theirs, out_mine, out_theirs, grad_gain = rest[5:]
        keep_rows(zip(rest[1:5], rest[5:]))
    rows = slice(chunk * CHUNK, (chunk + 1) * CHUNK)
    branch, scale = branch_of(part, part_over)
    half = cot_mine.shape[1]
    gain = gain_of(gains, gains_far, 1)
    block_out = hidden[...] + branch * scale * gain
    out_mine[rows, :] = block_out[:, :half]
    out_theirs[rows, :] = block_out[:, half:]
    upstream = jnp.concatenate([cot_mine[rows, :], cot_theirs[rows, :]], axis=1).astype(F32)
    grad_branch, gained = norm_back(branch, scale, gain, upstream)
    grad_gain[...] = gained if chunk == 0 else gain_before[...] + gained
    gff_mine[rows, :] = grad_branch[:, :half].astype(BF16)
    gff_theirs[rows, :] = grad_branch[:, half:].astype(BF16)


def backward_kernel(
    chunk, gff_mine, gff_theirs, gate, up, wg, wu, wd, w_far, *rest
):
    if chunk == 0:
        grads, *partial = rest
    else:
        grads, *partial = rest[1:]
        keep_rows([rest[:2]])
    rows = slice(chunk * CHUNK, (chunk + 1) * CHUNK)
    half, ff = wd.shape[1], wg.shape[1]
    wgt, wut, wdt = packed_weights(w_far, ff)
    for tile in tiles(ff):
        span, block = wdt[tile.start // wdt[0][0].stop]
        part = block[tile.start - span.start : tile.stop - span.start, :]
        grad_act = dot_t(gff_mine[rows, :], wd[tile, :]) + dot_t(gff_theirs[rows, :], part)
        gate_act = gate[:, tile]
        sig = jax.nn.sigmoid(gate_act)
        grads[rows, tile] = (
            grad_act * up[:, tile] * sig * (1.0 + gate_act * (1.0 - sig))
        ).astype(BF16)
        there = slice(ff + tile.start, ff + tile.stop)
        grads[rows, there] = (grad_act * gate_act * sig).astype(BF16)
    left, right = grads[rows, :ff], grads[rows, ff:]
    for tile in tiles(half):
        store_pieces(partial, tile, dot_t(left, wg[tile, :]) + dot_t(right, wu[tile, :]))
        there = slice(half + tile.start, half + tile.stop)
        store_pieces(partial, there, dot_t(left, wgt[tile, :]) + dot_t(right, wut[tile, :]))


def attention_back_kernel(chunk, *refs):
    grad_part, grad_over, part, part_over = [
        refs[i * PIECES : (i + 1) * PIECES] for i in range(4)
    ]
    (
        cot_mine,
        cot_theirs,
        gains,
        gains_far,
        wo,
        wot,
        q_rot,
        k_rot,
        values,
        logs,
        queries,
        keys,
        totals,
        totals_over,
        qgain,
        kgain,
        cosine,
        sine_part,
        *rest,
    ) = refs[4 * PIECES :]
    half = wo.shape[1]
    width = queries.shape[1]
    if chunk == 0:
        gat_mine, side, gh_mine, gh_theirs, gqn, grad_gain, column, gk_sum, gv_sum = rest
    else:
        gain_before, column_in, gk_in, gv_in = rest[:4]
        gat_mine, side, gh_mine, gh_theirs, gqn, grad_gain, gkn, gv_low, inner_out = rest[6:]
        keep_rows(zip(rest[4:6], rest[6:]))
    rows = slice(chunk * CHUNK, (chunk + 1) * CHUNK)
    seen = (chunk + 1) * CHUNK
    branch, scale = branch_of(part, part_over)
    grad_hidden = (
        jnp.concatenate([cot_mine[rows, :], cot_theirs[rows, :]], axis=1).astype(F32)
        + total_of(grad_part, grad_over)
    )
    gh_mine[...] = grad_hidden[:, :half]
    gh_theirs[...] = grad_hidden[:, half:]
    grad_branch, gained = norm_back(branch, scale, gain_of(gains, gains_far, 0), grad_hidden)
    grad_gain[...] = gained if chunk == 0 else gain_before[...] + gained
    gat_mine[rows, :] = grad_branch[:, :half].astype(BF16)
    side[rows, :] = grad_branch[:, half:].astype(BF16)
    grad_mixed = (
        dot_t(gat_mine[rows, :], wo[...]) + dot_t(side[rows, :], wot[...])
    ).astype(BF16)
    visible = lower_triangle()
    query_total, key_total = rows_to_columns(totals[...] + totals_over[...], 2)
    query_inner = jnp.zeros((CHUNK, 1), F32)
    key_inner = jnp.zeros((seen, 1), F32)
    for at, tile in enumerate(tiles(width, LANES)):
        grad_query = jnp.zeros((CHUNK, LANES), F32)
        grad_key = [jnp.zeros((CHUNK, LANES), F32) for _ in range(chunk + 1)]
        grad_value = [jnp.zeros((CHUNK, LANES), F32) for _ in range(chunk + 1)]
        for index in range(2):
            mask = head_mask(CHUNK, index)
            query_head = only(mask, q_rot[rows, tile])
            grad_head = only(mask, grad_mixed[:, tile])
            log_column = logs[rows, 2 * at + index : 2 * at + index + 1]
            weights, grads = [], []
            for block in range(chunk + 1):
                span = slice(block * CHUNK, (block + 1) * CHUNK)
                scores = dot_t(query_head, k_rot[span, tile])
                if block == chunk:
                    scores = jnp.where(visible, scores, MASKED)
                weights.append(jnp.exp(scores - log_column))
                grads.append(dot_t(grad_head, values[span, tile]))
            inner = sum(row_sum(w * g) for w, g in zip(weights, grads))
            for block in range(chunk + 1):
                span = slice(block * CHUNK, (block + 1) * CHUNK)
                weight = weights[block]
                grad_scores = (weight * (grads[block] - inner)).astype(BF16)
                grad_value[block] = grad_value[block] + t_dot(weight.astype(BF16), grad_head)
                grad_query = grad_query + dot(grad_scores, only(mask, k_rot[span, tile]))
                grad_key[block] = grad_key[block] + t_dot(grad_scores, query_head)
        back = turn(grad_query * FACTOR, cosine[rows, :], -sine_part[rows, :])
        gqn[:, tile] = back
        query_inner = query_inner + row_sum(back * qgain[:, tile] * queries[rows, tile])
        if chunk == 0:
            gk_sum[:, tile] = grad_key[0]
            gv_sum[:, tile] = grad_value[0]
        else:
            key_all = jnp.concatenate([gk_in[:, tile] + grad_key[0], grad_key[1]], axis=0)
            value_all = jnp.concatenate([gv_in[:, tile] + grad_value[0], grad_value[1]], axis=0)
            gv_low[:, tile] = value_all.astype(BF16)
            back = turn(key_all, cosine[...], -sine_part[...])
            gkn[:, tile] = back
            key_inner = key_inner + row_sum(back * kgain[:, tile] * keys[:, tile])
    if chunk == 0:
        column[...] = jnp.broadcast_to(query_inner, (CHUNK, LANES))
    else:
        query_inner = jnp.concatenate([column_in[:, :1], query_inner], axis=0)
        inner_out[...] = columns_to_rows([query_inner, key_inner])


def query_key_back_kernel(
    gqn_first,
    gqn_second,
    gkn,
    queries,
    keys,
    totals,
    totals_over,
    inner,
    inner_over,
    qgain,
    kgain,
    mlp_part,
    attn_part,
    grads,
    gain_mine,
    gain_give,
):
    width = queries.shape[1]
    half = gain_mine.shape[1]
    for out, columns in ((gain_mine, slice(0, half)), (gain_give, slice(half, 2 * half))):
        out[...] = jnp.zeros(out.shape, F32)
        out[0:1, :] = mlp_part[:, columns]
        out[1:2, :] = attn_part[:, columns]
    query_total, key_total = rows_to_columns(totals[...] + totals_over[...], 2)
    query_inner, key_inner = rows_to_columns(inner[...] + inner_over[...], 2)
    gqn = jnp.concatenate([gqn_first[...], gqn_second[...]], axis=0)
    for at, raw, back, total, sums, gain, low in (
        (2, queries, gqn, query_total, query_inner, qgain, grads.at[:, :width]),
        (3, keys, gkn[...], key_total, key_inner, kgain, grads.at[:, width:]),
    ):
        scale = rms_scale(total)
        value = raw[...]
        low[...] = (
            scale * (back * gain[...]) - value * (scale * scale * scale * sums / D)
        ).astype(BF16)
        gained = jnp.sum(back * value * scale, axis=0, keepdims=True)
        gain_mine[at : at + 1, :] = gained
        gain_give[at : at + 1, :] = gained


GAIN_ROWS = 16


def plain_weight_kernel(products, *refs):
    plain = refs[-1]

    def view(operand):
        index, start, stop = operand
        return refs[index].at[:, start:stop]

    at = 0
    for product in products:
        left, left_far, right, right_far = [view(operand) for operand in product]
        width = product[2][2] - product[2][1]
        for tile in tiles(plain.shape[0]):
            plain[tile, at : at + width] = (
                t_dot(left[:, tile], right[...]) + t_dot(left_far[:, tile], right_far[...])
            ).astype(BF16)
        at += width


def weight_kernel(with_gains, products, *refs):
    keep, give, plain = refs[-3:]
    plain_weight_kernel(products, *refs[:-3], plain)
    half = plain.shape[0] // 2
    mine = pl.multiple_of(own_half() * half, half)
    theirs = pl.multiple_of((1 - own_half()) * half, half)
    keep[:half, :] = plain[pl.ds(mine, half), :]
    give[:half, :] = plain[pl.ds(theirs, half), :]
    if with_gains:
        gains = refs[-5][...] + refs[-4][...]
        width = gains.shape[1]
        rows = jnp.concatenate([gains, jnp.zeros_like(gains)], axis=0)
        rest = jnp.zeros((GAIN_ROWS, plain.shape[1] - width), F32)
        rows = jnp.concatenate([rows, rest], axis=1).astype(BF16)
        keep[half:, :] = rows
        give[half:, :] = rows


def add_kernel(mine, *rest):
    out = rest[-1]
    at = 0
    for piece in rest[:-1]:
        rows = slice(at, at + piece.shape[0])
        out[rows, :] = (mine[rows, :].astype(F32) + piece[...].astype(F32)).astype(BF16)
        at = rows.stop


def inner_kernel(mine, received, out):
    out[...] = jnp.where(is_inner(), mine[...], received[...])


def finish_kernel(mine, received, *outs):
    half = outs[0].shape[0] // 2
    for place, source in enumerate((mine, received)):
        to = pl.multiple_of((own_half() ^ place) * half, half)
        column = 0
        for out in outs:
            width = out.shape[1]
            out[pl.ds(to, half), :] = source[:half, column : column + width].astype(F32)
            column += width


def in_far_kernel(side_far, block, out):
    out[...] = jnp.where(on_own_chip(), side_far[:, side_far.shape[1] - out.shape[1] :], block[...])


def gains_out_kernel(total, *outs):
    rows = total[total.shape[0] - GAIN_ROWS :, :].astype(F32)
    for index, out in enumerate(outs):
        out[...] = rows[index : index + 1, : out.shape[1]]


def finish_rest_kernel(mine, received, query_first, query, key):
    half = query.shape[0] // 2
    split = query_first.shape[1]
    more = query.shape[1] - split
    query[:, :split] = query_first[...]
    for place, source in enumerate((mine, received)):
        to = pl.multiple_of((own_half() ^ place) * half, half)
        query[pl.ds(to, half), split:] = source[:half, :more].astype(F32)
        key[pl.ds(to, half), :] = source[:half, more:].astype(F32)


def grad_input_kernel(stays, moves, across, corner, out):
    own = on_own_chip()
    out[...] = jnp.where(own, stays[...], moves[...]) + jnp.where(
        own, across[...], corner[...]
    ).astype(F32)


def input_back_kernel(
    grads, gv, wq, wqt, wk, wkt, wv, wvt, *rest
):
    width = wq.shape[1]
    gq, gk = grads.at[:, :width], grads.at[:, width:]
    gh_mine, gh_theirs = rest[:2], rest[2:4]
    stays, moves, across, corner = rest[4:]
    for tile in tiles(wq.shape[0]):
        mine = (
            dot_t(gq[...], wq[tile, :]) + dot_t(gk[...], wk[tile, :]) + dot_t(gv[...], wv[tile, :])
        )
        theirs = (
            dot_t(gq[...], wqt[tile, :])
            + dot_t(gk[...], wkt[tile, :])
            + dot_t(gv[...], wvt[tile, :])
        )
        for chunk in range(2):
            rows = slice(chunk * CHUNK, (chunk + 1) * CHUNK)
            stays[rows, tile] = gh_mine[chunk][:, tile] + mine[rows]
            moves[rows, tile] = gh_theirs[chunk][:, tile] + theirs[rows]
        across[:, tile] = mine.astype(BF16)
        corner[:, tile] = theirs.astype(BF16)


def dp_exchange(values, bit):
    size = lax.axis_size("dp")
    return lax.ppermute(values, "dp", [(i, i ^ (1 << bit)) for i in range(size)])


def dp_bits():
    return lax.axis_size("dp").bit_length() - 1


def along_line(values, moves):
    pairs = [(2 * a + half, 2 * b + half) for a, b in moves for half in range(2)]
    return lax.ppermute(values, "dp", pairs)


def in_turn(operands, received):
    return lax.optimization_barrier((operands, received))


class Chain:
    def __init__(self, name, high, widths, keep, give):
        self.name, self.high, self.widths, self.keep, self.give = name, high, widths, keep, give
        self.back = False
        self.received = None

    def kernel(self, body, args, part, after, outs=None):
        out = call(
            body, outs or [shape(self.keep.shape)], args, f"{self.name}_{part}", after=after
        )
        if outs is None:
            (self.keep,) = out
        else:
            self.out = out
        return out[0]

    def combine(self, body, part, after):
        return self.kernel(body, [self.keep, *self.received], part, after)

    def finish(self, after):
        outs = [shape((self.high, w), F32) for w in self.widths]
        return self.kernel(finish_kernel, [self.keep, *self.received], "out", after, outs)


LINE = ((0, 1), (3, 2)), ((1, 2), (2, 1)), ((1, 0), (2, 3))


class Lanes:
    def __init__(self):
        self.line = [None, None, None]
        self.latest = None

    def send_y(self, chain, before=None):
        operands = [chain.keep if chain.back else chain.give]
        if before is not None:
            operands, before.received = in_turn(operands, before.received)
        chain.received = [dp_exchange(piece, 0) for piece in operands]

    def pass_on(self, index, chain):
        before, self.line[index] = self.line[index], chain
        if before is not None and chain is not None:
            chain.keep, before.received = in_turn(chain.keep, before.received)
        if chain is not None:
            chain.received = [along_line(chain.keep, LINE[index])]
        return before

    def advance(self, chain, following=None, after=()):
        current = chain
        late = following is not None and following is self.line[2]
        if following is not None and not late:
            self.send_y(following, chain)
        done = None
        if chain.back:
            done, chain = chain, None
        else:
            self.latest = chain.combine(add_kernel, "y", (self.latest, *after))
            if lax.axis_size("dp") != 8:
                for bit in range(1, dp_bits()):
                    other = dp_exchange(chain.keep, bit).astype(F32)
                    chain.keep = (chain.keep.astype(F32) + other).astype(BF16)
                chain.back = True
                chain = None
        for index, (body, part) in enumerate(
            ((add_kernel, "in"), (add_kernel, "across"), (inner_kernel, "out"))
        ):
            chain = self.pass_on(index, chain)
            if chain is not None:
                self.latest = chain.combine(body, f"z_{part}", (self.latest,))
        if chain is not None:
            chain.back = True
        if late:
            self.send_y(following, current)
        if done is not None:
            self.latest = done.finish((self.latest,))


def on_device(
    block_in,
    w_query,
    w_key,
    w_value,
    w_output,
    w_gate,
    w_up,
    w_down,
    qnorm_gain,
    knorm_gain,
    attn_gain,
    mlp_gain,
    cotangent,
):
    rows, half = block_in.shape
    width = w_query.shape[1]
    ff = w_gate.shape[1]
    pair = ("row", "col")

    to_over = [(0, 1), (3, 2)]
    to_corner = [(1, 2), (2, 1)]
    to_beside = [(2, 0), (1, 3)]
    from_same = [(0, 2), (3, 1)]

    in_over = lax.ppermute(block_in, pair, to_over)
    in_corner = lax.ppermute(block_in, pair, to_corner)
    in_beside = lax.ppermute(block_in, pair, to_beside)
    wq_far, wk_far = swap(w_query, "row"), swap(w_key, "row")
    qgain, kgain = qnorm_gain[None], knorm_gain[None]
    cosine, sine_part = rope_tables(rows)

    near = call(
        copy_kernel,
        [shape((rows, half)), shape((half, width)), shape((half, width))],
        [block_in, w_query, w_key],
        "near",
    )
    (ff_weights,) = call(
        pack_weights_kernel,
        [shape((half, 2 * ff + -(-ff // half) * half))],
        [w_gate, w_up, w_down],
        "ff_weights",
        after=(near[0],),
    )
    (gains,) = call(
        pack_kernel,
        [shape((8, half), F32)],
        [attn_gain[None], mlp_gain[None]],
        "gains",
        after=(ff_weights,),
    )
    (wv_give, wo_give, gains), (in_corner, in_over, ff_weights, *near) = in_turn(
        [w_value, w_output, gains], [in_corner, in_over, ff_weights, *near]
    )
    wv_far, wo_far, gains_far = [swap(value, "row") for value in (wv_give, wo_give, gains)]

    queries, keys, totals, in_mine, in_theirs = call(
        query_key_kernel,
        [shape((rows, width), F32)] * 2 + [shape((8, rows), F32)] + [shape((rows, half))] * 2,
        [*near, in_over, in_beside, in_corner, wq_far, wk_far],
        "query_key",
    )
    totals_over = swap(totals, "col")
    (values,) = call(
        value_kernel,
        [shape((rows, width))],
        [in_mine, in_theirs, w_value, wv_far],
        "value",
    )
    (cotangent, ff_weights), (totals_over, values, wo_far, gains_far) = in_turn(
        [cotangent, ff_weights], [totals_over, values, wo_far, gains_far]
    )
    cot_over = lax.ppermute(cotangent, pair, to_over)
    cot_corner = lax.ppermute(cotangent, pair, to_corner)
    w_far = swap(ff_weights, "row")
    attention_args = [
        queries,
        keys,
        values,
        totals,
        totals_over,
        qgain,
        kgain,
        cosine,
        sine_part,
        w_output,
        wo_far,
    ]
    partial = [shape((CHUNK // PIECES, D))] * PIECES
    attention_outs = [shape((rows, width))] * 3 + [shape((rows, LANES), F32), *partial]

    def send_over(pieces, before=None):
        if before is not None:
            for index in range(PIECES):
                (pieces[index],), (before[index],) = in_turn([pieces[index]], [before[index]])
        return [swap(piece, "col") for piece in pieces]

    *kept, first_a, first_b = call(
        functools.partial(attention_kernel, 0),
        attention_outs,
        attention_args,
        "attention_0",
    )
    first = [first_a, first_b]
    first_over = send_over(first)
    *kept, second_a, second_b = call(
        functools.partial(attention_kernel, 1),
        attention_outs,
        attention_args + kept,
        "attention_1",
    )
    q_rot, k_rot, mixed, logs = kept
    second = [second_a, second_b]
    second_over = send_over(second, first_over)
    parts, parts_over = [first, second], [first_over, second_over]

    (cot_mine,) = call(
        choose_kernel, [shape((rows, half))], [cotangent, cot_over], "cotangent_mine"
    )
    side_width = ff + half + width + half

    def forward(chunk, over, kept, after):
        return call(
            functools.partial(forward_kernel, chunk),
            [shape((rows, half)), shape((rows, side_width)), shape((CHUNK, D), F32)]
            + [shape((CHUNK, ff), F32)] * 2
            + partial,
            [*parts[chunk], *over, in_mine, in_theirs, gains, gains_far]
            + [w_gate, w_up, w_down, w_far]
            + kept,
            f"forward_{chunk}",
            after=after,
        )

    low_mine, side, *saved = forward(0, first_over, [], (cot_mine, cot_corner))
    saved_all, ff_first = [saved[:3]], saved[3:]
    (cotangent,), (low_mine,) = in_turn([cotangent], [low_mine])
    cot_beside = lax.ppermute(cotangent, pair, to_beside)
    (cot_theirs,) = call(
        choose_kernel, [shape((rows, half))], [cot_beside, cot_corner], "cotangent_theirs"
    )
    ff_first_over = send_over(ff_first, second_over)
    low_mine, side, *saved = forward(1, second_over, [mixed, low_mine, side], ())
    saved_all.append(saved[:3])
    ff_second = saved[3:]
    ff_second_over = send_over(ff_second, ff_first_over)

    def weight_grad(name, arrays, products, after, gains=()):
        high = products[0][0][2] - products[0][0][1]
        widths = [right[2] - right[1] for _, _, right, _ in products]
        extra = GAIN_ROWS if gains else 0
        keep, give = call(
            functools.partial(weight_kernel, bool(gains), products),
            [shape((high // 2 + extra, sum(widths)))] * 2,
            [*arrays, *gains],
            name,
            scratch=[pltpu.VMEM((high, sum(widths)), BF16)],
            after=after,
        )
        return Chain(name, high, widths, keep, give)

    def ff_norm_back(chunk, mine, over, more, after):
        return call(
            functools.partial(ff_norm_back_kernel, chunk),
            [shape((rows, half))] * 2 + [shape((rows, half), F32)] * 2 + [shape((1, D), F32)],
            [*mine, *over, saved_all[chunk][0], cot_mine, cot_theirs, gains, gains_far, *more],
            f"ff_norm_back_{chunk}",
            after=after,
        )

    def backward(chunk, more, after):
        return call(
            functools.partial(backward_kernel, chunk),
            [shape((rows, 2 * ff)), *partial],
            [gff_mine, gff_theirs, *saved_all[chunk][1:]]
            + [w_gate, w_up, w_down, w_far]
            + more,
            f"backward_{chunk}",
            after=after,
        )

    *kept, mlp_part = ff_norm_back(0, ff_first, ff_first_over, [], ())
    gff_mine, gff_theirs, _, _ = kept
    grads, *gh_first = backward(0, [], ())
    gh_first_over = send_over(gh_first, ff_second_over)
    *kept, mlp_part = ff_norm_back(
        1, ff_second, ff_second_over, [mlp_part, *kept], ()
    )
    gff_mine, gff_theirs, out_mine, out_theirs = kept
    (side,), (gff_theirs,) = in_turn([side], [gff_theirs])
    side_far = swap(side, "row")
    gff_far = swap(gff_theirs, "row")
    out_beside = lax.ppermute(out_theirs, pair, from_same)
    grads, *gh_second = backward(1, [grads], ())
    lanes = Lanes()
    down = weight_grad(
        "down",
        [side, side_far, gff_mine, gff_far],
        [((0, 0, ff), (1, 0, ff), (2, 0, half), (3, 0, half))],
        (grads,),
    )
    (block_out,) = call(
        choose_kernel,
        [shape((rows, half), F32)],
        [out_mine, out_beside],
        "block_out",
        after=(down.keep,),
    )
    (in_far,) = call(
        in_far_kernel, [shape((rows, half))], [side_far, block_in], "in_far", after=(block_out,)
    )
    lanes.send_y(down)
    (gh_second, grads), (gh_first_over, down.keep, in_far) = in_turn(
        [gh_second, grads], [gh_first_over, down.keep, in_far]
    )
    gh_second_over = send_over(gh_second)
    grads_far = swap(grads, "row")
    grad_parts, grad_over = [gh_first, gh_second], [gh_first_over, gh_second_over]

    def ff_grad(name, start, after):
        span = (start, start + ff)
        return weight_grad(
            name,
            [low_mine, side_far, grads, grads_far],
            [((0, 0, half), (1, ff, ff + half), (2, *span), (3, *span))],
            after,
        )

    latest = down.keep
    gh_mine, gh_theirs, gqn = [], [], []
    for chunk in range(2):
        args = [
            *grad_parts[chunk],
            *grad_over[chunk],
            *parts[chunk],
            *parts_over[chunk],
            cot_mine,
            cot_theirs,
            gains,
            gains_far,
            w_output,
            wo_far,
            q_rot,
            k_rot,
            values,
            logs,
            queries,
            keys,
            totals,
            totals_over,
            qgain,
            kgain,
            cosine,
            sine_part,
        ]
        outs = [shape((rows, half))] * 2
        outs += [shape((CHUNK, half), F32)] * 2 + [shape((CHUNK, width), F32), shape((1, D), F32)]
        if chunk == 0:
            outs += [shape((CHUNK, LANES), F32)] + [shape((CHUNK, width), F32)] * 2
        else:
            outs += [shape((rows, width), F32), shape((rows, width)), shape((8, rows), F32)]
            args += [attn_part, column, gk_sum, gv_sum, gat_mine, gat_theirs]
        gat_mine, gat_theirs, gm, gt, gq_turned, attn_part, *more = call(
            functools.partial(attention_back_kernel, chunk),
            outs,
            args,
            f"attention_back_{chunk}",
            after=(latest,),
            flops=3e10 if chunk else 1,
        )
        gh_mine.append(gm)
        gh_theirs.append(gt)
        gqn.append(gq_turned)
        if chunk == 0:
            column, gk_sum, gv_sum = more
            up = ff_grad("up", ff, (column,))
            gate = ff_grad("gate", 0, (up.keep,))
            lanes.latest = gate.keep
            lanes.advance(down, gate, grad_over[1])
            latest = lanes.latest
        else:
            gkn, gv, inner = more
    inner_over = swap(inner, "col")
    gat_far, gv_far = swap(gat_theirs, "row"), swap(gv, "row")
    grads_back, gain_mine, gain_give = call(
        query_key_back_kernel,
        [shape((rows, 2 * width))] + [shape((8, half), F32)] * 2,
        [
            *gqn,
            gkn,
            queries,
            keys,
            totals,
            totals_over,
            inner,
            inner_over,
            qgain,
            kgain,
            mlp_part,
            attn_part,
        ],
        "query_key_back",
        after=(gv,),
    )
    grads_back_far = swap(grads_back, "row")
    gain_far = swap(gain_give, "row")
    lanes.latest = grads_back
    lanes.advance(gate, up)
    split = width * 3 // 4
    mixing = weight_grad(
        "mixing",
        [mixed, side_far, gat_mine, gat_far, in_mine, in_far, gv, gv_far]
        + [grads_back, grads_back_far],
        [
            ((0, 0, width), (1, ff + half, ff + half + width), (2, 0, half), (3, 0, half)),
            ((4, 0, half), (5, 0, half), (6, 0, width), (7, 0, width)),
            ((4, 0, half), (5, 0, half), (8, 0, split), (9, 0, split)),
        ],
        (lanes.latest,),
    )
    rest = (split, 2 * width)
    matching = weight_grad(
        "matching",
        [in_mine, in_far, grads_back, grads_back_far],
        [((0, 0, half), (1, 0, half), (2, *rest), (3, *rest))],
        (mixing.keep,),
        (gain_mine, gain_far),
    )
    mixing.widths = [half, width, split]
    lanes.latest = matching.keep
    lanes.advance(up, mixing)
    lanes.advance(mixing, matching)
    lanes.advance(matching, down)
    stays, moves, across, corner = call(
        input_back_kernel,
        [shape((rows, half), F32)] * 2 + [shape((rows, half))] * 2,
        [grads_back, gv, w_query, wq_far, w_key, wk_far, w_value, wv_far]
        + [*gh_mine, *gh_theirs],
        "input_back",
        after=(lanes.latest,),
    )
    lanes.latest = across
    moves = lax.ppermute(moves, pair, from_same)
    across = lax.ppermute(across, pair, [(1, 0), (2, 3)])
    lanes.advance(down, gate)
    (corner,), (across,) = in_turn([corner], [across])
    corner = lax.ppermute(corner, pair, to_corner)
    lanes.advance(gate, up)
    (grad_input,) = call(
        grad_input_kernel,
        [shape((rows, half), F32)],
        [stays, moves, across, corner],
        "grad_input",
        after=(lanes.latest,),
    )
    lanes.latest = grad_input
    lanes.advance(up, mixing)
    lanes.advance(mixing, matching)
    gain_out = call(
        gains_out_kernel,
        [shape((1, half), F32)] * 2 + [shape((1, width), F32)] * 2,
        [matching.keep],
        "gains_out",
        after=(lanes.latest,),
    )
    grad_mlpgain, grad_attngain, grad_qgain, grad_kgain = [row[0] for row in gain_out]
    lanes.latest = gain_out[0]
    grad_out, grad_value, query_first = mixing.out
    grad_query, grad_key = call(
        finish_rest_kernel,
        [shape((half, width), F32)] * 2,
        [matching.keep, *matching.received, query_first],
        "matching_out",
        after=(lanes.latest,),
    )
    (grad_down,) = down.out
    (grad_gate,) = gate.out
    (grad_up,) = up.out
    return (
        block_out,
        grad_input,
        grad_query,
        grad_key,
        grad_value,
        grad_out,
        grad_gate,
        grad_up,
        grad_down,
        grad_qgain,
        grad_kgain,
        grad_attngain,
        grad_mlpgain,
    )


def solution(mesh):
    tokens = P(("dp", "col"), "row")
    grid, turned = P("row", "col"), P("col", "row")
    in_specs = (
        tokens,
        grid,
        grid,
        grid,
        turned,
        grid,
        grid,
        turned,
        P("col"),
        P("col"),
        P("row"),
        P("row"),
        tokens,
    )
    out_specs = (
        tokens,
        tokens,
        grid,
        grid,
        grid,
        turned,
        grid,
        grid,
        turned,
        P("col"),
        P("col"),
        P("row"),
        P("row"),
    )
    return jax.shard_map(
        on_device, mesh=mesh, in_specs=in_specs, out_specs=out_specs, check_vma=False
    )
```

```python
import functools
import math

import jax
import jax.numpy as jnp
import numpy as np
from jax import lax
from jax.experimental import pallas as pl
from jax.experimental.pallas import tpu as pltpu
from jax.sharding import PartitionSpec as P

D = 1024
HEAD = 64
SEQ = 512
EPSILON = 1e-06
ROPE_BASE = 500000.0
MASKED = -1e30
CHUNK = 256
PIECES = 2
TILE = 256
LANES = 128
FACTOR = 1.0 / math.sqrt(HEAD)

F32 = jnp.float32
BF16 = jnp.bfloat16


def swap(values, axis):
    return lax.ppermute(values, axis, [(0, 1), (1, 0)])


def dot(left, right):
    return jnp.dot(left, right, preferred_element_type=F32)


def dot_t(left, right):
    return lax.dot_general(left, right, (((1,), (1,)), ((), ())), preferred_element_type=F32)


def t_dot(left, right):
    return lax.dot_general(left, right, (((0,), (0,)), ((), ())), preferred_element_type=F32)


def shape(dims, kind=BF16):
    return jax.ShapeDtypeStruct(dims, kind)


def call(kernel, outs, args, name, scratch=(), after=(), far=(), flops=1):
    count, skip, fetched = len(args), len(after), len(far)
    vmem = pl.BlockSpec(memory_space=pltpu.VMEM)
    anywhere = pl.BlockSpec(memory_space=pl.ANY)
    buffers = [pltpu.VMEM(a.shape, a.dtype) for a in far]
    if fetched:
        buffers.append(pltpu.SemaphoreType.DMA((fetched,)))

    def body(*refs):
        sources, refs = refs[:fetched], refs[fetched:]
        copies = []
        if fetched:
            refs, local = refs[: -fetched - 1], refs[-fetched - 1 :]
            copies = [
                pltpu.make_async_copy(source, local[i], local[-1].at[i])
                for i, source in enumerate(sources)
            ]
            for copy in copies:
                copy.start()
            for copy in copies:
                copy.wait()
            sources = local[:-1]
        kernel(*sources, *refs[:count], *refs[count + skip :])

    return pl.pallas_call(
        body,
        out_shape=tuple(outs),
        in_specs=[pl.BlockSpec(memory_space=pltpu.HBM)] * fetched + [vmem] * count + [anywhere] * skip,
        out_specs=tuple([vmem] * len(outs)),
        scratch_shapes=[*scratch, *buffers],
        compiler_params=pltpu.CompilerParams(
            vmem_limit_bytes=12 << 20, fuse_transposed_lhs_in_matmul=True
        ),
        cost_estimate=pl.CostEstimate(flops=int(flops), bytes_accessed=1, transcendentals=0),
        name=name,
    )(*far, *args, *after)


def tiles(extent, size=TILE):
    return [slice(at, min(at + size, extent)) for at in range(0, extent, size)]


def row_sum(values):
    return jnp.sum(values, axis=1, keepdims=True)


def columns_to_rows(columns):
    count = columns[0].shape[0]
    lane = lax.broadcasted_iota(jnp.int32, (count, LANES), 1)
    packed = jnp.zeros((count, LANES), F32)
    for index, column in enumerate(columns):
        packed = jnp.where(lane == index, column, packed)
    return packed.T[:8]


def rows_to_columns(rows, count):
    turned = jnp.concatenate([rows] * (LANES // 8), axis=0).T
    return [turned[:, i : i + 1] for i in range(count)]


def rms_scale(total):
    return lax.rsqrt(total / D + EPSILON)


def turn(values, cosine, sine_part):
    lane = lax.broadcasted_iota(jnp.int32, cosine.shape, 1)
    first = (lane % HEAD) < HEAD // 2
    out = []
    for tile in tiles(values.shape[1], LANES):
        part = values[:, tile]
        other = jnp.where(
            first, pltpu.roll(part, LANES - HEAD // 2, 1), pltpu.roll(part, HEAD // 2, 1)
        )
        out.append(part * cosine + other * sine_part)
    return jnp.concatenate(out, axis=1)


def rope_tables(count):
    half = HEAD // 2
    frequency = np.exp(np.arange(half, dtype=np.float32) * np.float32(-2.0 * math.log(ROPE_BASE) / HEAD))
    angles = np.arange(count).astype(np.float32)[:, None] * frequency[None, :]
    cosine, sine_part = np.cos(angles), np.sin(angles)
    repeats = LANES // HEAD
    return (
        jnp.asarray(np.concatenate([cosine, cosine] * repeats, axis=1)),
        jnp.asarray(np.concatenate([-sine_part, sine_part] * repeats, axis=1)),
    )


def lower_triangle():
    rows = lax.broadcasted_iota(jnp.int32, (CHUNK, CHUNK), 0)
    cols = lax.broadcasted_iota(jnp.int32, (CHUNK, CHUNK), 1)
    return rows >= cols


def keep_rows(pairs):
    for before, out in pairs:
        out[:CHUNK] = before[:CHUNK]


def head_mask(count, index):
    lane = lax.broadcasted_iota(jnp.int32, (count, LANES), 1)
    return (lane < HEAD) if index == 0 else (lane >= HEAD)


def only(mask, values):
    return jnp.where(mask, values, jnp.zeros_like(values))


def total_of(mine, theirs):
    return jnp.concatenate(
        [a[...].astype(F32) + b[...].astype(F32) for a, b in zip(mine, theirs)], axis=0
    )


def branch_of(mine, theirs):
    branch = total_of(mine, theirs)
    return branch, rms_scale(row_sum(branch * branch))


def store_pieces(pieces, columns, values):
    at = 0
    for piece in pieces:
        high = piece.shape[0]
        piece[:, columns] = values[at : at + high].astype(BF16)
        at += high


def gain_of(mine, theirs, index):
    row = slice(index, index + 1)
    return jnp.concatenate([mine[row, :], theirs[row, :]], axis=1)


def on_own_chip():
    return lax.axis_index("row") == lax.axis_index("col")


def own_half():
    return lax.axis_index("dp") & 1


def is_inner():
    place = lax.axis_index("dp") >> 1
    return (place == 1) | (place == 2)


def norm_back(branch, scale, gain_vec, grad_out):
    weighted = grad_out * gain_vec
    inner = row_sum(weighted * branch)
    grad_branch = scale * weighted - branch * (scale * scale * scale * inner / D)
    grad_gain = jnp.sum(grad_out * branch * scale, axis=0, keepdims=True)
    return grad_branch, grad_gain


def pack_kernel(*refs):
    out = refs[-1]
    out[...] = jnp.zeros(out.shape, F32)
    for index, row in enumerate(refs[:-1]):
        out[index : index + 1, :] = row[...]


def copy_kernel(*refs):
    count = len(refs) // 2
    for source, out in zip(refs[:count], refs[count:]):
        out[...] = source[...]


def pack_weights_kernel(wg, wu, wd, out):
    high, ff = wg.shape
    out[:, :ff] = wg[...]
    out[:, ff : 2 * ff] = wu[...]
    for index, rows in enumerate(tiles(ff, high)):
        at = 2 * ff + index * high
        out[: rows.stop - rows.start, at : at + high] = wd[rows, :]


def packed_weights(packed, ff):
    high = packed.shape[0]
    blocks = []
    for index, rows in enumerate(tiles(ff, high)):
        at = 2 * ff + index * high
        blocks.append((rows, packed.at[: rows.stop - rows.start, at : at + high]))
    return packed.at[:, :ff], packed.at[:, ff : 2 * ff], blocks


def choose_kernel(first, other, out):
    out[...] = jnp.where(on_own_chip(), first[...], other[...])


def choose_two_kernel(first, other, beside, corner, out, out_theirs):
    choose_kernel(first, other, out)
    choose_kernel(beside, corner, out_theirs)


def query_key_kernel(
    block, wq, wk, over, beside, corner, wqt, wkt, q_out, k_out, total_out, mine, theirs
):
    choose_two_kernel(block, over, beside, corner, mine, theirs)
    query_sum = 0.0
    key_sum = 0.0
    for tile in tiles(wq.shape[1]):
        query = dot(mine[...], wq[:, tile]) + dot(theirs[...], wqt[:, tile])
        q_out[:, tile] = query
        query_sum = query_sum + row_sum(query * query)
        key = dot(mine[...], wk[:, tile]) + dot(theirs[...], wkt[:, tile])
        k_out[:, tile] = key
        key_sum = key_sum + row_sum(key * key)
    total_out[...] = columns_to_rows([query_sum, key_sum])


def value_kernel(mine, theirs, wv, wvt, v_out):
    for tile in tiles(wv.shape[1]):
        v_out[:, tile] = (dot(mine[...], wv[:, tile]) + dot(theirs[...], wvt[:, tile])).astype(BF16)


def attention_kernel(
    chunk,
    queries,
    keys,
    values,
    totals,
    totals_over,
    qgain,
    kgain,
    cosine,
    sine_part,
    wo,
    wot,
    *rest,
):
    if chunk == 0:
        q_rot, k_rot, mixed, logs, *partial = rest
    else:
        q_rot, k_rot, mixed, logs, *partial = rest[4:]
        keep_rows(zip(rest[:4], rest[4:]))
    rows = slice(chunk * CHUNK, (chunk + 1) * CHUNK)
    query_total, key_total = rows_to_columns(totals[...] + totals_over[...], 2)
    query = queries[rows, :] * rms_scale(query_total[rows]) * qgain[...]
    key = keys[rows, :] * rms_scale(key_total[rows]) * kgain[...]
    q_rot[rows, :] = (turn(query, cosine[rows, :], sine_part[rows, :]) * FACTOR).astype(BF16)
    k_rot[rows, :] = turn(key, cosine[rows, :], sine_part[rows, :]).astype(BF16)
    visible = lower_triangle()
    lane = lax.broadcasted_iota(jnp.int32, (CHUNK, LANES), 1)
    log_tile = jnp.zeros((CHUNK, LANES), F32)
    for at, tile in enumerate(tiles(queries.shape[1], LANES)):
        total = jnp.zeros((CHUNK, LANES), F32)
        for index in range(2):
            query_head = only(head_mask(CHUNK, index), q_rot[rows, tile])
            scores = []
            for block in range(chunk + 1):
                part = dot_t(query_head, k_rot[block * CHUNK : (block + 1) * CHUNK, tile])
                scores.append(jnp.where(visible, part, MASKED) if block == chunk else part)
            peak = jnp.max(scores[0], axis=1, keepdims=True)
            for part in scores[1:]:
                peak = jnp.maximum(peak, jnp.max(part, axis=1, keepdims=True))
            scores = [jnp.exp(part - peak) for part in scores]
            denominator = sum(row_sum(part) for part in scores)
            inverse = 1.0 / denominator
            for block, part in enumerate(scores):
                value_rows = values[block * CHUNK : (block + 1) * CHUNK, tile]
                total = total + dot(
                    (part * inverse).astype(BF16), only(head_mask(CHUNK, index), value_rows)
                )
            log_tile = jnp.where(lane == 2 * at + index, peak + jnp.log(denominator), log_tile)
        mixed[rows, tile] = total.astype(BF16)
    logs[rows, :] = log_tile
    low = mixed[rows, :]
    half = wo.shape[1]
    store_pieces(partial, slice(0, half), dot(low, wo[...]))
    store_pieces(partial, slice(half, 2 * half), dot(low, wot[...]))


def forward_kernel(
    chunk, *refs
):
    part, part_over = refs[:PIECES], refs[PIECES : 2 * PIECES]
    forward_body(chunk, part, part_over, *refs[2 * PIECES :])


def forward_body(
    chunk, part, part_over, mine, theirs, gains, gains_far, wg, wu, wd, w_far, *rest
):
    if chunk == 0:
        low_mine, side, hidden, gate, up, *partial = rest
    else:
        mixed = rest[0]
        low_mine, side, hidden, gate, up, *partial = rest[3:]
        keep_rows(zip(rest[1:3], rest[3:]))
        at = wg.shape[1] + mine.shape[1]
        side[:, at : at + mixed.shape[1]] = mixed[...]
        side[:, at + mixed.shape[1] :] = theirs[...]
    rows = slice(chunk * CHUNK, (chunk + 1) * CHUNK)
    branch, scale = branch_of(part, part_over)
    half, ff = mine.shape[1], wg.shape[1]
    wgt, wut, wdt = packed_weights(w_far, ff)
    normed = branch * scale * gain_of(gains, gains_far, 0)
    value = mine[rows, :].astype(F32) + normed[:, :half]
    hidden[:, :half] = value
    low_mine[rows, :] = value.astype(BF16)
    value = theirs[rows, :].astype(F32) + normed[:, half:]
    hidden[:, half:] = value
    side[rows, ff : ff + half] = value.astype(BF16)
    for tile in tiles(ff):
        left, right = low_mine[rows, :], side[rows, ff : ff + half]
        gate_act = dot(left, wg[:, tile]) + dot(right, wgt[:, tile])
        up_act = dot(left, wu[:, tile]) + dot(right, wut[:, tile])
        gate[:, tile] = gate_act
        up[:, tile] = up_act
        side[rows, tile] = (gate_act * jax.nn.sigmoid(gate_act) * up_act).astype(BF16)
    low = side[rows, :ff]
    store_pieces(partial, slice(0, half), dot(low, wd[...]))
    theirs_part = sum(dot(side[rows, span], block[...]) for span, block in wdt)
    store_pieces(partial, slice(half, 2 * half), theirs_part)


def ff_norm_back_kernel(
    chunk, *refs
):
    part, part_over = refs[:PIECES], refs[PIECES : 2 * PIECES]
    hidden, cot_mine, cot_theirs, gains, gains_far, *rest = refs[2 * PIECES :]
    if chunk == 0:
        gff_mine, gff_theirs, out_mine, out_theirs, grad_gain = rest
    else:
        gain_before = rest[0]
        gff_mine, gff_theirs, out_mine, out_theirs, grad_gain = rest[5:]
        keep_rows(zip(rest[1:5], rest[5:]))
    rows = slice(chunk * CHUNK, (chunk + 1) * CHUNK)
    branch, scale = branch_of(part, part_over)
    half = cot_mine.shape[1]
    gain = gain_of(gains, gains_far, 1)
    block_out = hidden[...] + branch * scale * gain
    out_mine[rows, :] = block_out[:, :half]
    out_theirs[rows, :] = block_out[:, half:]
    upstream = jnp.concatenate([cot_mine[rows, :], cot_theirs[rows, :]], axis=1).astype(F32)
    grad_branch, gained = norm_back(branch, scale, gain, upstream)
    grad_gain[...] = gained if chunk == 0 else gain_before[...] + gained
    gff_mine[rows, :] = grad_branch[:, :half].astype(BF16)
    gff_theirs[rows, :] = grad_branch[:, half:].astype(BF16)


def backward_kernel(
    chunk, gff_mine, gff_theirs, gate, up, wg, wu, wd, w_far, *rest
):
    if chunk == 0:
        grads, *partial = rest
    else:
        grads, *partial = rest[1:]
        keep_rows([rest[:2]])
    rows = slice(chunk * CHUNK, (chunk + 1) * CHUNK)
    half, ff = wd.shape[1], wg.shape[1]
    wgt, wut, wdt = packed_weights(w_far, ff)
    for tile in tiles(ff):
        span, block = wdt[tile.start // wdt[0][0].stop]
        part = block[tile.start - span.start : tile.stop - span.start, :]
        grad_act = dot_t(gff_mine[rows, :], wd[tile, :]) + dot_t(gff_theirs[rows, :], part)
        gate_act = gate[:, tile]
        sig = jax.nn.sigmoid(gate_act)
        grads[rows, tile] = (
            grad_act * up[:, tile] * sig * (1.0 + gate_act * (1.0 - sig))
        ).astype(BF16)
        there = slice(ff + tile.start, ff + tile.stop)
        grads[rows, there] = (grad_act * gate_act * sig).astype(BF16)
    left, right = grads[rows, :ff], grads[rows, ff:]
    for tile in tiles(half):
        store_pieces(partial, tile, dot_t(left, wg[tile, :]) + dot_t(right, wu[tile, :]))
        there = slice(half + tile.start, half + tile.stop)
        store_pieces(partial, there, dot_t(left, wgt[tile, :]) + dot_t(right, wut[tile, :]))


def attention_back_kernel(chunk, *refs):
    grad_part, grad_over, part, part_over = [
        refs[i * PIECES : (i + 1) * PIECES] for i in range(4)
    ]
    (
        cot_mine,
        cot_theirs,
        gains,
        gains_far,
        wo,
        wot,
        q_rot,
        k_rot,
        values,
        logs,
        queries,
        keys,
        totals,
        totals_over,
        qgain,
        kgain,
        cosine,
        sine_part,
        *rest,
    ) = refs[4 * PIECES :]
    half = wo.shape[1]
    width = queries.shape[1]
    if chunk == 0:
        gat_mine, side, gh_mine, gh_theirs, gqn, grad_gain, column, gk_sum, gv_sum = rest
    else:
        gain_before, column_in, gk_in, gv_in = rest[:4]
        gat_mine, side, gh_mine, gh_theirs, gqn, grad_gain, gkn, gv_low, inner_out = rest[6:]
        keep_rows(zip(rest[4:6], rest[6:]))
    rows = slice(chunk * CHUNK, (chunk + 1) * CHUNK)
    seen = (chunk + 1) * CHUNK
    branch, scale = branch_of(part, part_over)
    grad_hidden = (
        jnp.concatenate([cot_mine[rows, :], cot_theirs[rows, :]], axis=1).astype(F32)
        + total_of(grad_part, grad_over)
    )
    gh_mine[...] = grad_hidden[:, :half]
    gh_theirs[...] = grad_hidden[:, half:]
    grad_branch, gained = norm_back(branch, scale, gain_of(gains, gains_far, 0), grad_hidden)
    grad_gain[...] = gained if chunk == 0 else gain_before[...] + gained
    gat_mine[rows, :] = grad_branch[:, :half].astype(BF16)
    side[rows, :] = grad_branch[:, half:].astype(BF16)
    grad_mixed = (
        dot_t(gat_mine[rows, :], wo[...]) + dot_t(side[rows, :], wot[...])
    ).astype(BF16)
    visible = lower_triangle()
    query_total, key_total = rows_to_columns(totals[...] + totals_over[...], 2)
    query_inner = jnp.zeros((CHUNK, 1), F32)
    key_inner = jnp.zeros((seen, 1), F32)
    for at, tile in enumerate(tiles(width, LANES)):
        grad_query = jnp.zeros((CHUNK, LANES), F32)
        grad_key = [jnp.zeros((CHUNK, LANES), F32) for _ in range(chunk + 1)]
        grad_value = [jnp.zeros((CHUNK, LANES), F32) for _ in range(chunk + 1)]
        for index in range(2):
            mask = head_mask(CHUNK, index)
            query_head = only(mask, q_rot[rows, tile])
            grad_head = only(mask, grad_mixed[:, tile])
            log_column = logs[rows, 2 * at + index : 2 * at + index + 1]
            weights, grads = [], []
            for block in range(chunk + 1):
                span = slice(block * CHUNK, (block + 1) * CHUNK)
                scores = dot_t(query_head, k_rot[span, tile])
                if block == chunk:
                    scores = jnp.where(visible, scores, MASKED)
                weights.append(jnp.exp(scores - log_column))
                grads.append(dot_t(grad_head, values[span, tile]))
            inner = sum(row_sum(w * g) for w, g in zip(weights, grads))
            for block in range(chunk + 1):
                span = slice(block * CHUNK, (block + 1) * CHUNK)
                weight = weights[block]
                grad_scores = (weight * (grads[block] - inner)).astype(BF16)
                grad_value[block] = grad_value[block] + t_dot(weight.astype(BF16), grad_head)
                grad_query = grad_query + dot(grad_scores, only(mask, k_rot[span, tile]))
                grad_key[block] = grad_key[block] + t_dot(grad_scores, query_head)
        back = turn(grad_query * FACTOR, cosine[rows, :], -sine_part[rows, :])
        gqn[:, tile] = back
        query_inner = query_inner + row_sum(back * qgain[:, tile] * queries[rows, tile])
        if chunk == 0:
            gk_sum[:, tile] = grad_key[0]
            gv_sum[:, tile] = grad_value[0]
        else:
            key_all = jnp.concatenate([gk_in[:, tile] + grad_key[0], grad_key[1]], axis=0)
            value_all = jnp.concatenate([gv_in[:, tile] + grad_value[0], grad_value[1]], axis=0)
            gv_low[:, tile] = value_all.astype(BF16)
            back = turn(key_all, cosine[...], -sine_part[...])
            gkn[:, tile] = back
            key_inner = key_inner + row_sum(back * kgain[:, tile] * keys[:, tile])
    if chunk == 0:
        column[...] = jnp.broadcast_to(query_inner, (CHUNK, LANES))
    else:
        query_inner = jnp.concatenate([column_in[:, :1], query_inner], axis=0)
        inner_out[...] = columns_to_rows([query_inner, key_inner])


def query_key_back_kernel(
    gqn_first,
    gqn_second,
    gkn,
    queries,
    keys,
    totals,
    totals_over,
    inner,
    inner_over,
    qgain,
    kgain,
    mlp_part,
    attn_part,
    grads,
    gain_mine,
    gain_give,
):
    width = queries.shape[1]
    half = gain_mine.shape[1]
    for out, columns in ((gain_mine, slice(0, half)), (gain_give, slice(half, 2 * half))):
        out[...] = jnp.zeros(out.shape, F32)
        out[0:1, :] = mlp_part[:, columns]
        out[1:2, :] = attn_part[:, columns]
    query_total, key_total = rows_to_columns(totals[...] + totals_over[...], 2)
    query_inner, key_inner = rows_to_columns(inner[...] + inner_over[...], 2)
    gqn = jnp.concatenate([gqn_first[...], gqn_second[...]], axis=0)
    for at, raw, back, total, sums, gain, low in (
        (2, queries, gqn, query_total, query_inner, qgain, grads.at[:, :width]),
        (3, keys, gkn[...], key_total, key_inner, kgain, grads.at[:, width:]),
    ):
        scale = rms_scale(total)
        value = raw[...]
        low[...] = (
            scale * (back * gain[...]) - value * (scale * scale * scale * sums / D)
        ).astype(BF16)
        gained = jnp.sum(back * value * scale, axis=0, keepdims=True)
        gain_mine[at : at + 1, :] = gained
        gain_give[at : at + 1, :] = gained


GAIN_ROWS = 16


def plain_weight_kernel(products, *refs):
    plain = refs[-1]

    def view(operand):
        index, start, stop = operand
        return refs[index].at[:, start:stop]

    at = 0
    for product in products:
        left, left_far, right, right_far = [view(operand) for operand in product]
        width = product[2][2] - product[2][1]
        for tile in tiles(plain.shape[0]):
            plain[tile, at : at + width] = (
                t_dot(left[:, tile], right[...]) + t_dot(left_far[:, tile], right_far[...])
            ).astype(BF16)
        at += width


def weight_kernel(with_gains, products, *refs):
    keep, give, plain = refs[-3:]
    plain_weight_kernel(products, *refs[:-3], plain)
    half = plain.shape[0] // 2
    mine = pl.multiple_of(own_half() * half, half)
    theirs = pl.multiple_of((1 - own_half()) * half, half)
    keep[:half, :] = plain[pl.ds(mine, half), :]
    give[:half, :] = plain[pl.ds(theirs, half), :]
    if with_gains:
        gains = refs[-5][...] + refs[-4][...]
        width = gains.shape[1]
        rows = jnp.concatenate([gains, jnp.zeros_like(gains)], axis=0)
        rest = jnp.zeros((GAIN_ROWS, plain.shape[1] - width), F32)
        rows = jnp.concatenate([rows, rest], axis=1).astype(BF16)
        keep[half:, :] = rows
        give[half:, :] = rows


def add_kernel(mine, *rest):
    out = rest[-1]
    at = 0
    for piece in rest[:-1]:
        rows = slice(at, at + piece.shape[0])
        out[rows, :] = (mine[rows, :].astype(F32) + piece[...].astype(F32)).astype(BF16)
        at = rows.stop


def inner_kernel(mine, received, out):
    out[...] = jnp.where(is_inner(), mine[...], received[...])


def finish_kernel(mine, received, *outs):
    half = outs[0].shape[0] // 2
    for place, source in enumerate((mine, received)):
        to = pl.multiple_of((own_half() ^ place) * half, half)
        column = 0
        for out in outs:
            width = out.shape[1]
            out[pl.ds(to, half), :] = source[:half, column : column + width].astype(F32)
            column += width


def in_far_kernel(side_far, block, out):
    out[...] = jnp.where(on_own_chip(), side_far[:, side_far.shape[1] - out.shape[1] :], block[...])


def gains_out_kernel(total, *outs):
    rows = total[total.shape[0] - GAIN_ROWS :, :].astype(F32)
    for index, out in enumerate(outs):
        out[...] = rows[index : index + 1, : out.shape[1]]


def finish_rest_kernel(mine, received, query_first, query, key):
    half = query.shape[0] // 2
    split = query_first.shape[1]
    more = query.shape[1] - split
    query[:, :split] = query_first[...]
    for place, source in enumerate((mine, received)):
        to = pl.multiple_of((own_half() ^ place) * half, half)
        query[pl.ds(to, half), split:] = source[:half, :more].astype(F32)
        key[pl.ds(to, half), :] = source[:half, more:].astype(F32)


def grad_input_kernel(stays, moves, across, corner, out):
    own = on_own_chip()
    out[...] = jnp.where(own, stays[...], moves[...]) + jnp.where(
        own, across[...], corner[...]
    ).astype(F32)


def input_back_kernel(
    grads, gv, wq, wqt, wk, wkt, wv, wvt, *rest
):
    width = wq.shape[1]
    gq, gk = grads.at[:, :width], grads.at[:, width:]
    gh_mine, gh_theirs = rest[:2], rest[2:4]
    stays, moves, across, corner = rest[4:]
    for tile in tiles(wq.shape[0]):
        mine = (
            dot_t(gq[...], wq[tile, :]) + dot_t(gk[...], wk[tile, :]) + dot_t(gv[...], wv[tile, :])
        )
        theirs = (
            dot_t(gq[...], wqt[tile, :])
            + dot_t(gk[...], wkt[tile, :])
            + dot_t(gv[...], wvt[tile, :])
        )
        for chunk in range(2):
            rows = slice(chunk * CHUNK, (chunk + 1) * CHUNK)
            stays[rows, tile] = gh_mine[chunk][:, tile] + mine[rows]
            moves[rows, tile] = gh_theirs[chunk][:, tile] + theirs[rows]
        across[:, tile] = mine.astype(BF16)
        corner[:, tile] = theirs.astype(BF16)


def dp_exchange(values, bit):
    size = lax.axis_size("dp")
    return lax.ppermute(values, "dp", [(i, i ^ (1 << bit)) for i in range(size)])


def dp_bits():
    return lax.axis_size("dp").bit_length() - 1


def along_line(values, moves):
    pairs = [(2 * a + half, 2 * b + half) for a, b in moves for half in range(2)]
    return lax.ppermute(values, "dp", pairs)


def in_turn(operands, received):
    return lax.optimization_barrier((operands, received))


class Chain:
    def __init__(self, name, high, widths, keep, give):
        self.name, self.high, self.widths, self.keep, self.give = name, high, widths, keep, give
        self.back = False
        self.received = None

    def kernel(self, body, args, part, after, outs=None):
        out = call(
            body, outs or [shape(self.keep.shape)], args, f"{self.name}_{part}", after=after
        )
        if outs is None:
            (self.keep,) = out
        else:
            self.out = out
        return out[0]

    def combine(self, body, part, after):
        return self.kernel(body, [self.keep, *self.received], part, after)

    def finish(self, after):
        outs = [shape((self.high, w), F32) for w in self.widths]
        return self.kernel(finish_kernel, [self.keep, *self.received], "out", after, outs)


LINE = ((0, 1), (3, 2)), ((1, 2), (2, 1)), ((1, 0), (2, 3))


class Lanes:
    def __init__(self):
        self.line = [None, None, None]
        self.latest = None

    def send_y(self, chain, before=None):
        operands = [chain.keep if chain.back else chain.give]
        if before is not None:
            operands, before.received = in_turn(operands, before.received)
        chain.received = [dp_exchange(piece, 0) for piece in operands]

    def advance(self, chain, following=None, after=()):
        if following is not None:
            self.send_y(following, chain)
        kernels = ((add_kernel, "in"), (add_kernel, "across"), (inner_kernel, "out"))
        for index in (2, 1, 0):
            moved, self.line[index] = self.line[index], None
            if moved is None:
                continue
            body, part = kernels[index]
            self.latest = moved.combine(body, f"z_{part}", (self.latest,))
            self.enter(index + 1, moved)
        if chain.back:
            self.latest = chain.finish((self.latest,))
            return
        self.latest = chain.combine(add_kernel, "y", (self.latest, *after))
        if lax.axis_size("dp") != 8:
            for bit in range(1, dp_bits()):
                other = dp_exchange(chain.keep, bit).astype(F32)
                chain.keep = (chain.keep.astype(F32) + other).astype(BF16)
            chain.back = True
            return
        self.enter(0, chain)

    def enter(self, index, chain):
        if index == len(LINE):
            chain.back = True
            return
        self.line[index] = chain
        chain.received = [along_line(chain.keep, LINE[index])]


def on_device(
    block_in,
    w_query,
    w_key,
    w_value,
    w_output,
    w_gate,
    w_up,
    w_down,
    qnorm_gain,
    knorm_gain,
    attn_gain,
    mlp_gain,
    cotangent,
):
    rows, half = block_in.shape
    width = w_query.shape[1]
    ff = w_gate.shape[1]
    pair = ("row", "col")

    to_over = [(0, 1), (3, 2)]
    to_corner = [(1, 2), (2, 1)]
    to_beside = [(2, 0), (1, 3)]
    from_same = [(0, 2), (3, 1)]

    in_over = lax.ppermute(block_in, pair, to_over)
    in_corner = lax.ppermute(block_in, pair, to_corner)
    in_beside = lax.ppermute(block_in, pair, to_beside)
    wq_far, wk_far = swap(w_query, "row"), swap(w_key, "row")
    qgain, kgain = qnorm_gain[None], knorm_gain[None]
    cosine, sine_part = rope_tables(rows)

    near = call(
        copy_kernel,
        [shape((rows, half)), shape((half, width)), shape((half, width))],
        [block_in, w_query, w_key],
        "near",
    )
    (ff_weights,) = call(
        pack_weights_kernel,
        [shape((half, 2 * ff + -(-ff // half) * half))],
        [w_gate, w_up, w_down],
        "ff_weights",
        after=(near[0],),
    )
    (gains,) = call(
        pack_kernel,
        [shape((8, half), F32)],
        [attn_gain[None], mlp_gain[None]],
        "gains",
        after=(ff_weights,),
    )
    (wv_give, wo_give, gains), (in_corner, in_over, ff_weights, *near) = in_turn(
        [w_value, w_output, gains], [in_corner, in_over, ff_weights, *near]
    )
    wv_far, wo_far, gains_far = [swap(value, "row") for value in (wv_give, wo_give, gains)]

    queries, keys, totals, in_mine, in_theirs = call(
        query_key_kernel,
        [shape((rows, width), F32)] * 2 + [shape((8, rows), F32)] + [shape((rows, half))] * 2,
        [*near, in_over, in_beside, in_corner, wq_far, wk_far],
        "query_key",
    )
    totals_over = swap(totals, "col")
    (values,) = call(
        value_kernel,
        [shape((rows, width))],
        [in_mine, in_theirs, w_value, wv_far],
        "value",
    )
    (cotangent, ff_weights), (totals_over, values, wo_far, gains_far) = in_turn(
        [cotangent, ff_weights], [totals_over, values, wo_far, gains_far]
    )
    cot_over = lax.ppermute(cotangent, pair, to_over)
    cot_corner = lax.ppermute(cotangent, pair, to_corner)
    w_far = swap(ff_weights, "row")
    attention_args = [
        queries,
        keys,
        values,
        totals,
        totals_over,
        qgain,
        kgain,
        cosine,
        sine_part,
        w_output,
        wo_far,
    ]
    partial = [shape((CHUNK // PIECES, D))] * PIECES
    attention_outs = [shape((rows, width))] * 3 + [shape((rows, LANES), F32), *partial]

    def send_over(pieces, before=None):
        if before is not None:
            for index in range(PIECES):
                (pieces[index],), (before[index],) = in_turn([pieces[index]], [before[index]])
        return [swap(piece, "col") for piece in pieces]

    *kept, first_a, first_b = call(
        functools.partial(attention_kernel, 0),
        attention_outs,
        attention_args,
        "attention_0",
    )
    first = [first_a, first_b]
    first_over = send_over(first)
    *kept, second_a, second_b = call(
        functools.partial(attention_kernel, 1),
        attention_outs,
        attention_args + kept,
        "attention_1",
    )
    q_rot, k_rot, mixed, logs = kept
    second = [second_a, second_b]
    second_over = send_over(second, first_over)
    parts, parts_over = [first, second], [first_over, second_over]

    (cot_mine,) = call(
        choose_kernel, [shape((rows, half))], [cotangent, cot_over], "cotangent_mine"
    )
    side_width = ff + half + width + half

    def forward(chunk, over, kept, after):
        return call(
            functools.partial(forward_kernel, chunk),
            [shape((rows, half)), shape((rows, side_width)), shape((CHUNK, D), F32)]
            + [shape((CHUNK, ff), F32)] * 2
            + partial,
            [*parts[chunk], *over, in_mine, in_theirs, gains, gains_far]
            + [w_gate, w_up, w_down, w_far]
            + kept,
            f"forward_{chunk}",
            after=after,
        )

    low_mine, side, *saved = forward(0, first_over, [], (cot_mine, cot_corner))
    saved_all, ff_first = [saved[:3]], saved[3:]
    (cotangent,), (low_mine,) = in_turn([cotangent], [low_mine])
    cot_beside = lax.ppermute(cotangent, pair, to_beside)
    (cot_theirs,) = call(
        choose_kernel, [shape((rows, half))], [cot_beside, cot_corner], "cotangent_theirs"
    )
    ff_first_over = send_over(ff_first, second_over)
    low_mine, side, *saved = forward(1, second_over, [mixed, low_mine, side], ())
    saved_all.append(saved[:3])
    ff_second = saved[3:]
    ff_second_over = send_over(ff_second, ff_first_over)

    def weight_grad(name, arrays, products, after, gains=()):
        high = products[0][0][2] - products[0][0][1]
        widths = [right[2] - right[1] for _, _, right, _ in products]
        extra = GAIN_ROWS if gains else 0
        keep, give = call(
            functools.partial(weight_kernel, bool(gains), products),
            [shape((high // 2 + extra, sum(widths)))] * 2,
            [*arrays, *gains],
            name,
            scratch=[pltpu.VMEM((high, sum(widths)), BF16)],
            after=after,
        )
        return Chain(name, high, widths, keep, give)

    def ff_norm_back(chunk, mine, over, more, after):
        return call(
            functools.partial(ff_norm_back_kernel, chunk),
            [shape((rows, half))] * 2 + [shape((rows, half), F32)] * 2 + [shape((1, D), F32)],
            [*mine, *over, saved_all[chunk][0], cot_mine, cot_theirs, gains, gains_far, *more],
            f"ff_norm_back_{chunk}",
            after=after,
        )

    def backward(chunk, more, after):
        return call(
            functools.partial(backward_kernel, chunk),
            [shape((rows, 2 * ff)), *partial],
            [gff_mine, gff_theirs, *saved_all[chunk][1:]]
            + [w_gate, w_up, w_down, w_far]
            + more,
            f"backward_{chunk}",
            after=after,
        )

    *kept, mlp_part = ff_norm_back(0, ff_first, ff_first_over, [], ())
    gff_mine, gff_theirs, _, _ = kept
    grads, *gh_first = backward(0, [], ())
    gh_first_over = send_over(gh_first, ff_second_over)
    *kept, mlp_part = ff_norm_back(
        1, ff_second, ff_second_over, [mlp_part, *kept], ()
    )
    gff_mine, gff_theirs, out_mine, out_theirs = kept
    (side,), (gff_theirs,) = in_turn([side], [gff_theirs])
    side_far = swap(side, "row")
    gff_far = swap(gff_theirs, "row")
    out_beside = lax.ppermute(out_theirs, pair, from_same)
    grads, *gh_second = backward(1, [grads], ())
    lanes = Lanes()
    down = weight_grad(
        "down",
        [side, side_far, gff_mine, gff_far],
        [((0, 0, ff), (1, 0, ff), (2, 0, half), (3, 0, half))],
        (grads,),
    )
    (block_out,) = call(
        choose_kernel,
        [shape((rows, half), F32)],
        [out_mine, out_beside],
        "block_out",
        after=(down.keep,),
    )
    (in_far,) = call(
        in_far_kernel, [shape((rows, half))], [side_far, block_in], "in_far", after=(block_out,)
    )
    lanes.send_y(down)
    (gh_second, grads), (gh_first_over, down.keep, in_far) = in_turn(
        [gh_second, grads], [gh_first_over, down.keep, in_far]
    )
    gh_second_over = send_over(gh_second)
    grads_far = swap(grads, "row")
    grad_parts, grad_over = [gh_first, gh_second], [gh_first_over, gh_second_over]

    def ff_grad(name, start, after):
        span = (start, start + ff)
        return weight_grad(
            name,
            [low_mine, side_far, grads, grads_far],
            [((0, 0, half), (1, ff, ff + half), (2, *span), (3, *span))],
            after,
        )

    latest = down.keep
    gh_mine, gh_theirs, gqn = [], [], []
    for chunk in range(2):
        args = [
            *grad_parts[chunk],
            *grad_over[chunk],
            *parts[chunk],
            *parts_over[chunk],
            cot_mine,
            cot_theirs,
            gains,
            gains_far,
            w_output,
            wo_far,
            q_rot,
            k_rot,
            values,
            logs,
            queries,
            keys,
            totals,
            totals_over,
            qgain,
            kgain,
            cosine,
            sine_part,
        ]
        outs = [shape((rows, half))] * 2
        outs += [shape((CHUNK, half), F32)] * 2 + [shape((CHUNK, width), F32), shape((1, D), F32)]
        if chunk == 0:
            outs += [shape((CHUNK, LANES), F32)] + [shape((CHUNK, width), F32)] * 2
        else:
            outs += [shape((rows, width), F32), shape((rows, width)), shape((8, rows), F32)]
            args += [attn_part, column, gk_sum, gv_sum, gat_mine, gat_theirs]
        gat_mine, gat_theirs, gm, gt, gq_turned, attn_part, *more = call(
            functools.partial(attention_back_kernel, chunk),
            outs,
            args,
            f"attention_back_{chunk}",
            after=(latest,),
            flops=4e9 if chunk else 1,
        )
        gh_mine.append(gm)
        gh_theirs.append(gt)
        gqn.append(gq_turned)
        if chunk == 0:
            column, gk_sum, gv_sum = more
            up = ff_grad("up", ff, (column,))
            gate = ff_grad("gate", 0, (up.keep,))
            lanes.latest = gate.keep
            lanes.advance(down, gate, grad_over[1])
            latest = lanes.latest
        else:
            gkn, gv, inner = more
    inner_over = swap(inner, "col")
    gat_far, gv_far = swap(gat_theirs, "row"), swap(gv, "row")
    grads_back, gain_mine, gain_give = call(
        query_key_back_kernel,
        [shape((rows, 2 * width))] + [shape((8, half), F32)] * 2,
        [
            *gqn,
            gkn,
            queries,
            keys,
            totals,
            totals_over,
            inner,
            inner_over,
            qgain,
            kgain,
            mlp_part,
            attn_part,
        ],
        "query_key_back",
        after=(gv,),
    )
    grads_back_far = swap(grads_back, "row")
    gain_far = swap(gain_give, "row")
    lanes.latest = grads_back
    lanes.advance(gate, up)
    split = width * 3 // 4
    mixing = weight_grad(
        "mixing",
        [mixed, side_far, gat_mine, gat_far, in_mine, in_far, gv, gv_far]
        + [grads_back, grads_back_far],
        [
            ((0, 0, width), (1, ff + half, ff + half + width), (2, 0, half), (3, 0, half)),
            ((4, 0, half), (5, 0, half), (6, 0, width), (7, 0, width)),
            ((4, 0, half), (5, 0, half), (8, 0, split), (9, 0, split)),
        ],
        (lanes.latest,),
    )
    rest = (split, 2 * width)
    matching = weight_grad(
        "matching",
        [in_mine, in_far, grads_back, grads_back_far],
        [((0, 0, half), (1, 0, half), (2, *rest), (3, *rest))],
        (mixing.keep,),
        (gain_mine, gain_far),
    )
    mixing.widths = [half, width, split]
    lanes.latest = matching.keep
    lanes.advance(up, mixing)
    lanes.advance(mixing, matching)
    lanes.advance(matching, down)
    stays, moves, across, corner = call(
        input_back_kernel,
        [shape((rows, half), F32)] * 2 + [shape((rows, half))] * 2,
        [grads_back, gv, w_query, wq_far, w_key, wk_far, w_value, wv_far]
        + [*gh_mine, *gh_theirs],
        "input_back",
        after=(lanes.latest,),
    )
    lanes.latest = across
    moves = lax.ppermute(moves, pair, from_same)
    across = lax.ppermute(across, pair, [(1, 0), (2, 3)])
    lanes.advance(down, gate)
    (corner,), (across,) = in_turn([corner], [across])
    corner = lax.ppermute(corner, pair, to_corner)
    lanes.advance(gate, up)
    (grad_input,) = call(
        grad_input_kernel,
        [shape((rows, half), F32)],
        [stays, moves, across, corner],
        "grad_input",
        after=(lanes.latest,),
    )
    lanes.latest = grad_input
    lanes.advance(up, mixing)
    lanes.advance(mixing, matching)
    gain_out = call(
        gains_out_kernel,
        [shape((1, half), F32)] * 2 + [shape((1, width), F32)] * 2,
        [matching.keep],
        "gains_out",
        after=(lanes.latest,),
    )
    grad_mlpgain, grad_attngain, grad_qgain, grad_kgain = [row[0] for row in gain_out]
    lanes.latest = gain_out[0]
    grad_out, grad_value, query_first = mixing.out
    grad_query, grad_key = call(
        finish_rest_kernel,
        [shape((half, width), F32)] * 2,
        [matching.keep, *matching.received, query_first],
        "matching_out",
        after=(lanes.latest,),
    )
    (grad_down,) = down.out
    (grad_gate,) = gate.out
    (grad_up,) = up.out
    return (
        block_out,
        grad_input,
        grad_query,
        grad_key,
        grad_value,
        grad_out,
        grad_gate,
        grad_up,
        grad_down,
        grad_qgain,
        grad_kgain,
        grad_attngain,
        grad_mlpgain,
    )


def solution(mesh):
    tokens = P(("dp", "col"), "row")
    grid, turned = P("row", "col"), P("col", "row")
    in_specs = (
        tokens,
        grid,
        grid,
        grid,
        turned,
        grid,
        grid,
        turned,
        P("col"),
        P("col"),
        P("row"),
        P("row"),
        tokens,
    )
    out_specs = (
        tokens,
        tokens,
        grid,
        grid,
        grid,
        turned,
        grid,
        grid,
        turned,
        P("col"),
        P("col"),
        P("row"),
        P("row"),
    )
    return jax.shard_map(
        on_device, mesh=mesh, in_specs=in_specs, out_specs=out_specs, check_vma=False
    )
```

```python
import functools
import math

import jax
import jax.numpy as jnp
import numpy as np
from jax import lax
from jax.experimental import pallas as pl
from jax.experimental.pallas import tpu as pltpu
from jax.sharding import PartitionSpec as P

D = 1024
HEAD = 64
SEQ = 512
EPSILON = 1e-06
ROPE_BASE = 500000.0
MASKED = -1e30
CHUNK = 256
PIECES = 2
TILE = 256
LANES = 128
FACTOR = 1.0 / math.sqrt(HEAD)

F32 = jnp.float32
BF16 = jnp.bfloat16


def swap(values, axis):
    return lax.ppermute(values, axis, [(0, 1), (1, 0)])


def dot(left, right):
    return jnp.dot(left, right, preferred_element_type=F32)


def dot_t(left, right):
    return lax.dot_general(left, right, (((1,), (1,)), ((), ())), preferred_element_type=F32)


def t_dot(left, right):
    return lax.dot_general(left, right, (((0,), (0,)), ((), ())), preferred_element_type=F32)


def shape(dims, kind=BF16):
    return jax.ShapeDtypeStruct(dims, kind)


def call(kernel, outs, args, name, scratch=(), after=(), far=(), flops=1):
    count, skip, fetched = len(args), len(after), len(far)
    vmem = pl.BlockSpec(memory_space=pltpu.VMEM)
    anywhere = pl.BlockSpec(memory_space=pl.ANY)
    buffers = [pltpu.VMEM(a.shape, a.dtype) for a in far]
    if fetched:
        buffers.append(pltpu.SemaphoreType.DMA((fetched,)))

    def body(*refs):
        sources, refs = refs[:fetched], refs[fetched:]
        copies = []
        if fetched:
            refs, local = refs[: -fetched - 1], refs[-fetched - 1 :]
            copies = [
                pltpu.make_async_copy(source, local[i], local[-1].at[i])
                for i, source in enumerate(sources)
            ]
            for copy in copies:
                copy.start()
            for copy in copies:
                copy.wait()
            sources = local[:-1]
        kernel(*sources, *refs[:count], *refs[count + skip :])

    return pl.pallas_call(
        body,
        out_shape=tuple(outs),
        in_specs=[pl.BlockSpec(memory_space=pltpu.HBM)] * fetched + [vmem] * count + [anywhere] * skip,
        out_specs=tuple([vmem] * len(outs)),
        scratch_shapes=[*scratch, *buffers],
        compiler_params=pltpu.CompilerParams(
            vmem_limit_bytes=12 << 20, fuse_transposed_lhs_in_matmul=True
        ),
        cost_estimate=pl.CostEstimate(flops=int(flops), bytes_accessed=1, transcendentals=0),
        name=name,
    )(*far, *args, *after)


def tiles(extent, size=TILE):
    return [slice(at, min(at + size, extent)) for at in range(0, extent, size)]


def row_sum(values):
    return jnp.sum(values, axis=1, keepdims=True)


def columns_to_rows(columns):
    count = columns[0].shape[0]
    lane = lax.broadcasted_iota(jnp.int32, (count, LANES), 1)
    packed = jnp.zeros((count, LANES), F32)
    for index, column in enumerate(columns):
        packed = jnp.where(lane == index, column, packed)
    return packed.T[:8]


def rows_to_columns(rows, count):
    turned = jnp.concatenate([rows] * (LANES // 8), axis=0).T
    return [turned[:, i : i + 1] for i in range(count)]


def rms_scale(total):
    return lax.rsqrt(total / D + EPSILON)


def turn(values, cosine, sine_part):
    lane = lax.broadcasted_iota(jnp.int32, cosine.shape, 1)
    first = (lane % HEAD) < HEAD // 2
    out = []
    for tile in tiles(values.shape[1], LANES):
        part = values[:, tile]
        other = jnp.where(
            first, pltpu.roll(part, LANES - HEAD // 2, 1), pltpu.roll(part, HEAD // 2, 1)
        )
        out.append(part * cosine + other * sine_part)
    return jnp.concatenate(out, axis=1)


def rope_tables(count):
    half = HEAD // 2
    frequency = np.exp(np.arange(half, dtype=np.float32) * np.float32(-2.0 * math.log(ROPE_BASE) / HEAD))
    angles = np.arange(count).astype(np.float32)[:, None] * frequency[None, :]
    cosine, sine_part = np.cos(angles), np.sin(angles)
    repeats = LANES // HEAD
    return (
        jnp.asarray(np.concatenate([cosine, cosine] * repeats, axis=1)),
        jnp.asarray(np.concatenate([-sine_part, sine_part] * repeats, axis=1)),
    )


def lower_triangle():
    rows = lax.broadcasted_iota(jnp.int32, (CHUNK, CHUNK), 0)
    cols = lax.broadcasted_iota(jnp.int32, (CHUNK, CHUNK), 1)
    return rows >= cols


def keep_rows(pairs):
    for before, out in pairs:
        out[:CHUNK] = before[:CHUNK]


def head_mask(count, index):
    lane = lax.broadcasted_iota(jnp.int32, (count, LANES), 1)
    return (lane < HEAD) if index == 0 else (lane >= HEAD)


def only(mask, values):
    return jnp.where(mask, values, jnp.zeros_like(values))


def total_of(mine, theirs):
    return jnp.concatenate(
        [a[...].astype(F32) + b[...].astype(F32) for a, b in zip(mine, theirs)], axis=0
    )


def branch_of(mine, theirs):
    branch = total_of(mine, theirs)
    return branch, rms_scale(row_sum(branch * branch))


def store_pieces(pieces, columns, values):
    at = 0
    for piece in pieces:
        high = piece.shape[0]
        piece[:, columns] = values[at : at + high].astype(BF16)
        at += high


def gain_of(mine, theirs, index):
    row = slice(index, index + 1)
    return jnp.concatenate([mine[row, :], theirs[row, :]], axis=1)


def on_own_chip():
    return lax.axis_index("row") == lax.axis_index("col")


def own_half():
    return lax.axis_index("dp") & 1


def is_inner():
    place = lax.axis_index("dp") >> 1
    return (place == 1) | (place == 2)


def norm_back(branch, scale, gain_vec, grad_out):
    weighted = grad_out * gain_vec
    inner = row_sum(weighted * branch)
    grad_branch = scale * weighted - branch * (scale * scale * scale * inner / D)
    grad_gain = jnp.sum(grad_out * branch * scale, axis=0, keepdims=True)
    return grad_branch, grad_gain


def pack_kernel(*refs):
    out = refs[-1]
    out[...] = jnp.zeros(out.shape, F32)
    for index, row in enumerate(refs[:-1]):
        out[index : index + 1, :] = row[...]


def copy_kernel(*refs):
    count = len(refs) // 2
    for source, out in zip(refs[:count], refs[count:]):
        out[...] = source[...]


def pack_weights_kernel(wg, wu, wd, out):
    high, ff = wg.shape
    out[:, :ff] = wg[...]
    out[:, ff : 2 * ff] = wu[...]
    for index, rows in enumerate(tiles(ff, high)):
        at = 2 * ff + index * high
        out[: rows.stop - rows.start, at : at + high] = wd[rows, :]


def packed_weights(packed, ff):
    high = packed.shape[0]
    blocks = []
    for index, rows in enumerate(tiles(ff, high)):
        at = 2 * ff + index * high
        blocks.append((rows, packed.at[: rows.stop - rows.start, at : at + high]))
    return packed.at[:, :ff], packed.at[:, ff : 2 * ff], blocks


def choose_kernel(first, other, out):
    out[...] = jnp.where(on_own_chip(), first[...], other[...])


def choose_two_kernel(first, other, beside, corner, out, out_theirs):
    choose_kernel(first, other, out)
    choose_kernel(beside, corner, out_theirs)


def query_key_kernel(
    block, wq, wk, over, beside, corner, wqt, wkt, q_out, k_out, total_out, mine, theirs
):
    choose_two_kernel(block, over, beside, corner, mine, theirs)
    query_sum = 0.0
    key_sum = 0.0
    for tile in tiles(wq.shape[1]):
        query = dot(mine[...], wq[:, tile]) + dot(theirs[...], wqt[:, tile])
        q_out[:, tile] = query
        query_sum = query_sum + row_sum(query * query)
        key = dot(mine[...], wk[:, tile]) + dot(theirs[...], wkt[:, tile])
        k_out[:, tile] = key
        key_sum = key_sum + row_sum(key * key)
    total_out[...] = columns_to_rows([query_sum, key_sum])


def value_kernel(mine, theirs, wv, wvt, v_out):
    for tile in tiles(wv.shape[1]):
        v_out[:, tile] = (dot(mine[...], wv[:, tile]) + dot(theirs[...], wvt[:, tile])).astype(BF16)


def attention_kernel(
    chunk,
    queries,
    keys,
    values,
    totals,
    totals_over,
    qgain,
    kgain,
    cosine,
    sine_part,
    wo,
    wot,
    *rest,
):
    if chunk == 0:
        q_rot, k_rot, mixed, logs, *partial = rest
    else:
        q_rot, k_rot, mixed, logs, *partial = rest[4:]
        keep_rows(zip(rest[:4], rest[4:]))
    rows = slice(chunk * CHUNK, (chunk + 1) * CHUNK)
    query_total, key_total = rows_to_columns(totals[...] + totals_over[...], 2)
    query = queries[rows, :] * rms_scale(query_total[rows]) * qgain[...]
    key = keys[rows, :] * rms_scale(key_total[rows]) * kgain[...]
    q_rot[rows, :] = (turn(query, cosine[rows, :], sine_part[rows, :]) * FACTOR).astype(BF16)
    k_rot[rows, :] = turn(key, cosine[rows, :], sine_part[rows, :]).astype(BF16)
    visible = lower_triangle()
    lane = lax.broadcasted_iota(jnp.int32, (CHUNK, LANES), 1)
    log_tile = jnp.zeros((CHUNK, LANES), F32)
    for at, tile in enumerate(tiles(queries.shape[1], LANES)):
        total = jnp.zeros((CHUNK, LANES), F32)
        for index in range(2):
            query_head = only(head_mask(CHUNK, index), q_rot[rows, tile])
            scores = []
            for block in range(chunk + 1):
                part = dot_t(query_head, k_rot[block * CHUNK : (block + 1) * CHUNK, tile])
                scores.append(jnp.where(visible, part, MASKED) if block == chunk else part)
            peak = jnp.max(scores[0], axis=1, keepdims=True)
            for part in scores[1:]:
                peak = jnp.maximum(peak, jnp.max(part, axis=1, keepdims=True))
            scores = [jnp.exp(part - peak) for part in scores]
            denominator = sum(row_sum(part) for part in scores)
            inverse = 1.0 / denominator
            for block, part in enumerate(scores):
                value_rows = values[block * CHUNK : (block + 1) * CHUNK, tile]
                total = total + dot(
                    (part * inverse).astype(BF16), only(head_mask(CHUNK, index), value_rows)
                )
            log_tile = jnp.where(lane == 2 * at + index, peak + jnp.log(denominator), log_tile)
        mixed[rows, tile] = total.astype(BF16)
    logs[rows, :] = log_tile
    low = mixed[rows, :]
    half = wo.shape[1]
    store_pieces(partial, slice(0, half), dot(low, wo[...]))
    store_pieces(partial, slice(half, 2 * half), dot(low, wot[...]))


def forward_kernel(
    chunk, *refs
):
    part, part_over = refs[:PIECES], refs[PIECES : 2 * PIECES]
    forward_body(chunk, part, part_over, *refs[2 * PIECES :])


def forward_body(
    chunk, part, part_over, mine, theirs, gains, gains_far, wg, wu, wd, w_far, *rest
):
    if chunk == 0:
        low_mine, side, hidden, gate, up, *partial = rest
    else:
        mixed = rest[0]
        low_mine, side, hidden, gate, up, *partial = rest[3:]
        keep_rows(zip(rest[1:3], rest[3:]))
        at = wg.shape[1] + mine.shape[1]
        side[:, at : at + mixed.shape[1]] = mixed[...]
        side[:, at + mixed.shape[1] :] = theirs[...]
    rows = slice(chunk * CHUNK, (chunk + 1) * CHUNK)
    branch, scale = branch_of(part, part_over)
    half, ff = mine.shape[1], wg.shape[1]
    wgt, wut, wdt = packed_weights(w_far, ff)
    normed = branch * scale * gain_of(gains, gains_far, 0)
    value = mine[rows, :].astype(F32) + normed[:, :half]
    hidden[:, :half] = value
    low_mine[rows, :] = value.astype(BF16)
    value = theirs[rows, :].astype(F32) + normed[:, half:]
    hidden[:, half:] = value
    side[rows, ff : ff + half] = value.astype(BF16)
    for tile in tiles(ff):
        left, right = low_mine[rows, :], side[rows, ff : ff + half]
        gate_act = dot(left, wg[:, tile]) + dot(right, wgt[:, tile])
        up_act = dot(left, wu[:, tile]) + dot(right, wut[:, tile])
        gate[:, tile] = gate_act
        up[:, tile] = up_act
        side[rows, tile] = (gate_act * jax.nn.sigmoid(gate_act) * up_act).astype(BF16)
    low = side[rows, :ff]
    store_pieces(partial, slice(0, half), dot(low, wd[...]))
    theirs_part = sum(dot(side[rows, span], block[...]) for span, block in wdt)
    store_pieces(partial, slice(half, 2 * half), theirs_part)


def ff_norm_back_kernel(
    chunk, *refs
):
    part, part_over = refs[:PIECES], refs[PIECES : 2 * PIECES]
    hidden, cot_mine, cot_theirs, gains, gains_far, *rest = refs[2 * PIECES :]
    if chunk == 0:
        gff_mine, gff_theirs, out_mine, out_theirs, grad_gain = rest
    else:
        gain_before = rest[0]
        gff_mine, gff_theirs, out_mine, out_theirs, grad_gain = rest[5:]
        keep_rows(zip(rest[1:5], rest[5:]))
    rows = slice(chunk * CHUNK, (chunk + 1) * CHUNK)
    branch, scale = branch_of(part, part_over)
    half = cot_mine.shape[1]
    gain = gain_of(gains, gains_far, 1)
    block_out = hidden[...] + branch * scale * gain
    out_mine[rows, :] = block_out[:, :half]
    out_theirs[rows, :] = block_out[:, half:]
    upstream = jnp.concatenate([cot_mine[rows, :], cot_theirs[rows, :]], axis=1).astype(F32)
    grad_branch, gained = norm_back(branch, scale, gain, upstream)
    grad_gain[...] = gained if chunk == 0 else gain_before[...] + gained
    gff_mine[rows, :] = grad_branch[:, :half].astype(BF16)
    gff_theirs[rows, :] = grad_branch[:, half:].astype(BF16)


def backward_kernel(
    chunk, gff_mine, gff_theirs, gate, up, wg, wu, wd, w_far, *rest
):
    if chunk == 0:
        grads, *partial = rest
    else:
        grads, *partial = rest[1:]
        keep_rows([rest[:2]])
    rows = slice(chunk * CHUNK, (chunk + 1) * CHUNK)
    half, ff = wd.shape[1], wg.shape[1]
    wgt, wut, wdt = packed_weights(w_far, ff)
    for tile in tiles(ff):
        span, block = wdt[tile.start // wdt[0][0].stop]
        part = block[tile.start - span.start : tile.stop - span.start, :]
        grad_act = dot_t(gff_mine[rows, :], wd[tile, :]) + dot_t(gff_theirs[rows, :], part)
        gate_act = gate[:, tile]
        sig = jax.nn.sigmoid(gate_act)
        grads[rows, tile] = (
            grad_act * up[:, tile] * sig * (1.0 + gate_act * (1.0 - sig))
        ).astype(BF16)
        there = slice(ff + tile.start, ff + tile.stop)
        grads[rows, there] = (grad_act * gate_act * sig).astype(BF16)
    left, right = grads[rows, :ff], grads[rows, ff:]
    for tile in tiles(half):
        store_pieces(partial, tile, dot_t(left, wg[tile, :]) + dot_t(right, wu[tile, :]))
        there = slice(half + tile.start, half + tile.stop)
        store_pieces(partial, there, dot_t(left, wgt[tile, :]) + dot_t(right, wut[tile, :]))


def attention_back_kernel(chunk, *refs):
    grad_part, grad_over, part, part_over = [
        refs[i * PIECES : (i + 1) * PIECES] for i in range(4)
    ]
    (
        cot_mine,
        cot_theirs,
        gains,
        gains_far,
        wo,
        wot,
        q_rot,
        k_rot,
        values,
        logs,
        queries,
        keys,
        totals,
        totals_over,
        qgain,
        kgain,
        cosine,
        sine_part,
        *rest,
    ) = refs[4 * PIECES :]
    half = wo.shape[1]
    width = queries.shape[1]
    if chunk == 0:
        gat_mine, side, gh_mine, gh_theirs, gqn, grad_gain, column, gk_sum, gv_sum = rest
    else:
        gain_before, column_in, gk_in, gv_in = rest[:4]
        gat_mine, side, gh_mine, gh_theirs, gqn, grad_gain, gkn, gv_low, inner_out = rest[6:]
        keep_rows(zip(rest[4:6], rest[6:]))
    rows = slice(chunk * CHUNK, (chunk + 1) * CHUNK)
    seen = (chunk + 1) * CHUNK
    branch, scale = branch_of(part, part_over)
    grad_hidden = (
        jnp.concatenate([cot_mine[rows, :], cot_theirs[rows, :]], axis=1).astype(F32)
        + total_of(grad_part, grad_over)
    )
    gh_mine[...] = grad_hidden[:, :half]
    gh_theirs[...] = grad_hidden[:, half:]
    grad_branch, gained = norm_back(branch, scale, gain_of(gains, gains_far, 0), grad_hidden)
    grad_gain[...] = gained if chunk == 0 else gain_before[...] + gained
    gat_mine[rows, :] = grad_branch[:, :half].astype(BF16)
    side[rows, :] = grad_branch[:, half:].astype(BF16)
    grad_mixed = (
        dot_t(gat_mine[rows, :], wo[...]) + dot_t(side[rows, :], wot[...])
    ).astype(BF16)
    visible = lower_triangle()
    query_total, key_total = rows_to_columns(totals[...] + totals_over[...], 2)
    query_inner = jnp.zeros((CHUNK, 1), F32)
    key_inner = jnp.zeros((seen, 1), F32)
    for at, tile in enumerate(tiles(width, LANES)):
        grad_query = jnp.zeros((CHUNK, LANES), F32)
        grad_key = [jnp.zeros((CHUNK, LANES), F32) for _ in range(chunk + 1)]
        grad_value = [jnp.zeros((CHUNK, LANES), F32) for _ in range(chunk + 1)]
        for index in range(2):
            mask = head_mask(CHUNK, index)
            query_head = only(mask, q_rot[rows, tile])
            grad_head = only(mask, grad_mixed[:, tile])
            log_column = logs[rows, 2 * at + index : 2 * at + index + 1]
            weights, grads = [], []
            for block in range(chunk + 1):
                span = slice(block * CHUNK, (block + 1) * CHUNK)
                scores = dot_t(query_head, k_rot[span, tile])
                if block == chunk:
                    scores = jnp.where(visible, scores, MASKED)
                weights.append(jnp.exp(scores - log_column))
                grads.append(dot_t(grad_head, values[span, tile]))
            inner = sum(row_sum(w * g) for w, g in zip(weights, grads))
            for block in range(chunk + 1):
                span = slice(block * CHUNK, (block + 1) * CHUNK)
                weight = weights[block]
                grad_scores = (weight * (grads[block] - inner)).astype(BF16)
                grad_value[block] = grad_value[block] + t_dot(weight.astype(BF16), grad_head)
                grad_query = grad_query + dot(grad_scores, only(mask, k_rot[span, tile]))
                grad_key[block] = grad_key[block] + t_dot(grad_scores, query_head)
        back = turn(grad_query * FACTOR, cosine[rows, :], -sine_part[rows, :])
        gqn[:, tile] = back
        query_inner = query_inner + row_sum(back * qgain[:, tile] * queries[rows, tile])
        if chunk == 0:
            gk_sum[:, tile] = grad_key[0]
            gv_sum[:, tile] = grad_value[0]
        else:
            key_all = jnp.concatenate([gk_in[:, tile] + grad_key[0], grad_key[1]], axis=0)
            value_all = jnp.concatenate([gv_in[:, tile] + grad_value[0], grad_value[1]], axis=0)
            gv_low[:, tile] = value_all.astype(BF16)
            back = turn(key_all, cosine[...], -sine_part[...])
            gkn[:, tile] = back
            key_inner = key_inner + row_sum(back * kgain[:, tile] * keys[:, tile])
    if chunk == 0:
        column[...] = jnp.broadcast_to(query_inner, (CHUNK, LANES))
    else:
        query_inner = jnp.concatenate([column_in[:, :1], query_inner], axis=0)
        inner_out[...] = columns_to_rows([query_inner, key_inner])


def query_key_back_kernel(
    gqn_first,
    gqn_second,
    gkn,
    queries,
    keys,
    totals,
    totals_over,
    inner,
    inner_over,
    qgain,
    kgain,
    mlp_part,
    attn_part,
    grads,
    gain_mine,
    gain_give,
):
    width = queries.shape[1]
    half = gain_mine.shape[1]
    for out, columns in ((gain_mine, slice(0, half)), (gain_give, slice(half, 2 * half))):
        out[...] = jnp.zeros(out.shape, F32)
        out[0:1, :] = mlp_part[:, columns]
        out[1:2, :] = attn_part[:, columns]
    query_total, key_total = rows_to_columns(totals[...] + totals_over[...], 2)
    query_inner, key_inner = rows_to_columns(inner[...] + inner_over[...], 2)
    gqn = jnp.concatenate([gqn_first[...], gqn_second[...]], axis=0)
    for at, raw, back, total, sums, gain, low in (
        (2, queries, gqn, query_total, query_inner, qgain, grads.at[:, :width]),
        (3, keys, gkn[...], key_total, key_inner, kgain, grads.at[:, width:]),
    ):
        scale = rms_scale(total)
        value = raw[...]
        low[...] = (
            scale * (back * gain[...]) - value * (scale * scale * scale * sums / D)
        ).astype(BF16)
        gained = jnp.sum(back * value * scale, axis=0, keepdims=True)
        gain_mine[at : at + 1, :] = gained
        gain_give[at : at + 1, :] = gained


GAIN_ROWS = 16


def plain_weight_kernel(products, *refs):
    plain = refs[-1]

    def view(operand):
        index, start, stop = operand
        return refs[index].at[:, start:stop]

    at = 0
    for product in products:
        left, left_far, right, right_far = [view(operand) for operand in product]
        width = product[2][2] - product[2][1]
        for tile in tiles(plain.shape[0]):
            plain[tile, at : at + width] = (
                t_dot(left[:, tile], right[...]) + t_dot(left_far[:, tile], right_far[...])
            ).astype(BF16)
        at += width


def weight_kernel(with_gains, products, *refs):
    keep, give, plain = refs[-3:]
    plain_weight_kernel(products, *refs[:-3], plain)
    half = plain.shape[0] // 2
    mine = pl.multiple_of(own_half() * half, half)
    theirs = pl.multiple_of((1 - own_half()) * half, half)
    keep[:half, :] = plain[pl.ds(mine, half), :]
    give[:half, :] = plain[pl.ds(theirs, half), :]
    if with_gains:
        gains = refs[-5][...] + refs[-4][...]
        width = gains.shape[1]
        rows = jnp.concatenate([gains, jnp.zeros_like(gains)], axis=0)
        rest = jnp.zeros((GAIN_ROWS, plain.shape[1] - width), F32)
        rows = jnp.concatenate([rows, rest], axis=1).astype(BF16)
        keep[half:, :] = rows
        give[half:, :] = rows


def add_kernel(mine, *rest):
    out = rest[-1]
    at = 0
    for piece in rest[:-1]:
        rows = slice(at, at + piece.shape[0])
        out[rows, :] = (mine[rows, :].astype(F32) + piece[...].astype(F32)).astype(BF16)
        at = rows.stop


def inner_kernel(mine, received, out):
    out[...] = jnp.where(is_inner(), mine[...], received[...])


def finish_kernel(mine, received, *outs):
    half = outs[0].shape[0] // 2
    for place, source in enumerate((mine, received)):
        to = pl.multiple_of((own_half() ^ place) * half, half)
        column = 0
        for out in outs:
            width = out.shape[1]
            out[pl.ds(to, half), :] = source[:half, column : column + width].astype(F32)
            column += width


def in_far_kernel(side_far, block, out):
    out[...] = jnp.where(on_own_chip(), side_far[:, side_far.shape[1] - out.shape[1] :], block[...])


def gains_out_kernel(total, *outs):
    rows = total[total.shape[0] - GAIN_ROWS :, :].astype(F32)
    for index, out in enumerate(outs):
        out[...] = rows[index : index + 1, : out.shape[1]]


def finish_rest_kernel(mine, received, query_first, query, key):
    half = query.shape[0] // 2
    split = query_first.shape[1]
    more = query.shape[1] - split
    query[:, :split] = query_first[...]
    for place, source in enumerate((mine, received)):
        to = pl.multiple_of((own_half() ^ place) * half, half)
        query[pl.ds(to, half), split:] = source[:half, :more].astype(F32)
        key[pl.ds(to, half), :] = source[:half, more:].astype(F32)


def grad_input_kernel(stays, moves, across, corner, out):
    own = on_own_chip()
    out[...] = jnp.where(own, stays[...], moves[...]) + jnp.where(
        own, across[...], corner[...]
    ).astype(F32)


def input_back_kernel(
    grads, gv, wq, wqt, wk, wkt, wv, wvt, *rest
):
    width = wq.shape[1]
    gq, gk = grads.at[:, :width], grads.at[:, width:]
    gh_mine, gh_theirs = rest[:2], rest[2:4]
    stays, moves, across, corner = rest[4:]
    for tile in tiles(wq.shape[0]):
        mine = (
            dot_t(gq[...], wq[tile, :]) + dot_t(gk[...], wk[tile, :]) + dot_t(gv[...], wv[tile, :])
        )
        theirs = (
            dot_t(gq[...], wqt[tile, :])
            + dot_t(gk[...], wkt[tile, :])
            + dot_t(gv[...], wvt[tile, :])
        )
        for chunk in range(2):
            rows = slice(chunk * CHUNK, (chunk + 1) * CHUNK)
            stays[rows, tile] = gh_mine[chunk][:, tile] + mine[rows]
            moves[rows, tile] = gh_theirs[chunk][:, tile] + theirs[rows]
        across[:, tile] = mine.astype(BF16)
        corner[:, tile] = theirs.astype(BF16)


def dp_exchange(values, bit):
    size = lax.axis_size("dp")
    return lax.ppermute(values, "dp", [(i, i ^ (1 << bit)) for i in range(size)])


def dp_bits():
    return lax.axis_size("dp").bit_length() - 1


def along_line(values, moves):
    pairs = [(2 * a + half, 2 * b + half) for a, b in moves for half in range(2)]
    return lax.ppermute(values, "dp", pairs)


def in_turn(operands, received):
    return lax.optimization_barrier((operands, received))


class Chain:
    def __init__(self, name, high, widths, keep, give):
        self.name, self.high, self.widths, self.keep, self.give = name, high, widths, keep, give
        self.back = False
        self.received = None

    def kernel(self, body, args, part, after, outs=None):
        out = call(
            body, outs or [shape(self.keep.shape)], args, f"{self.name}_{part}", after=after
        )
        if outs is None:
            (self.keep,) = out
        else:
            self.out = out
        return out[0]

    def combine(self, body, part, after):
        return self.kernel(body, [self.keep, *self.received], part, after)

    def finish(self, after):
        outs = [shape((self.high, w), F32) for w in self.widths]
        return self.kernel(finish_kernel, [self.keep, *self.received], "out", after, outs)


LINE = ((0, 1), (3, 2)), ((1, 2), (2, 1)), ((1, 0), (2, 3))


class Lanes:
    def __init__(self):
        self.line = [None, None, None]
        self.latest = None

    def send_y(self, chain, before=None):
        operands = [chain.keep if chain.back else chain.give]
        if before is not None:
            operands, before.received = in_turn(operands, before.received)
        chain.received = [dp_exchange(piece, 0) for piece in operands]

    def pass_on(self, index, chain):
        before, self.line[index] = self.line[index], chain
        if before is not None and chain is not None:
            chain.keep, before.received = in_turn(chain.keep, before.received)
        if chain is not None:
            chain.received = [along_line(chain.keep, LINE[index])]
        return before

    def advance(self, chain, following=None, after=()):
        current = chain
        late = following is not None and following is self.line[2]
        if following is not None and not late:
            self.send_y(following, chain)
        done = None
        if chain.back:
            done, chain = chain, None
        else:
            self.latest = chain.combine(add_kernel, "y", (self.latest, *after))
            if lax.axis_size("dp") != 8:
                for bit in range(1, dp_bits()):
                    other = dp_exchange(chain.keep, bit).astype(F32)
                    chain.keep = (chain.keep.astype(F32) + other).astype(BF16)
                chain.back = True
                chain = None
        for index, (body, part) in enumerate(
            ((add_kernel, "in"), (add_kernel, "across"), (inner_kernel, "out"))
        ):
            chain = self.pass_on(index, chain)
            if chain is not None:
                self.latest = chain.combine(body, f"z_{part}", (self.latest,))
        if chain is not None:
            chain.back = True
        if late:
            self.send_y(following, current)
        if done is not None:
            self.latest = done.finish((self.latest,))


def on_device(
    block_in,
    w_query,
    w_key,
    w_value,
    w_output,
    w_gate,
    w_up,
    w_down,
    qnorm_gain,
    knorm_gain,
    attn_gain,
    mlp_gain,
    cotangent,
):
    rows, half = block_in.shape
    width = w_query.shape[1]
    ff = w_gate.shape[1]
    pair = ("row", "col")

    to_over = [(0, 1), (3, 2)]
    to_corner = [(1, 2), (2, 1)]
    to_beside = [(2, 0), (1, 3)]
    from_same = [(0, 2), (3, 1)]

    in_over = lax.ppermute(block_in, pair, to_over)
    in_corner = lax.ppermute(block_in, pair, to_corner)
    in_beside = lax.ppermute(block_in, pair, to_beside)
    wq_far, wk_far = swap(w_query, "row"), swap(w_key, "row")
    qgain, kgain = qnorm_gain[None], knorm_gain[None]
    cosine, sine_part = rope_tables(rows)

    near = call(
        copy_kernel,
        [shape((rows, half)), shape((half, width)), shape((half, width))],
        [block_in, w_query, w_key],
        "near",
    )
    (ff_weights,) = call(
        pack_weights_kernel,
        [shape((half, 2 * ff + -(-ff // half) * half))],
        [w_gate, w_up, w_down],
        "ff_weights",
        after=(near[0],),
    )
    (gains,) = call(
        pack_kernel,
        [shape((8, half), F32)],
        [attn_gain[None], mlp_gain[None]],
        "gains",
        after=(ff_weights,),
    )
    (wv_give, wo_give, gains), (in_corner, in_over, ff_weights, *near) = in_turn(
        [w_value, w_output, gains], [in_corner, in_over, ff_weights, *near]
    )
    wv_far, wo_far, gains_far = [swap(value, "row") for value in (wv_give, wo_give, gains)]

    queries, keys, totals, in_mine, in_theirs = call(
        query_key_kernel,
        [shape((rows, width), F32)] * 2 + [shape((8, rows), F32)] + [shape((rows, half))] * 2,
        [*near, in_over, in_beside, in_corner, wq_far, wk_far],
        "query_key",
    )
    totals_over = swap(totals, "col")
    (values,) = call(
        value_kernel,
        [shape((rows, width))],
        [in_mine, in_theirs, w_value, wv_far],
        "value",
    )
    (cotangent, ff_weights), (totals_over, values, wo_far, gains_far) = in_turn(
        [cotangent, ff_weights], [totals_over, values, wo_far, gains_far]
    )
    cot_over = lax.ppermute(cotangent, pair, to_over)
    cot_corner = lax.ppermute(cotangent, pair, to_corner)
    w_far = swap(ff_weights, "row")
    attention_args = [
        queries,
        keys,
        values,
        totals,
        totals_over,
        qgain,
        kgain,
        cosine,
        sine_part,
        w_output,
        wo_far,
    ]
    partial = [shape((CHUNK // PIECES, D))] * PIECES
    attention_outs = [shape((rows, width))] * 3 + [shape((rows, LANES), F32), *partial]

    def send_over(pieces, before=None):
        if before is not None:
            for index in range(PIECES):
                (pieces[index],), (before[index],) = in_turn([pieces[index]], [before[index]])
        return [swap(piece, "col") for piece in pieces]

    *kept, first_a, first_b = call(
        functools.partial(attention_kernel, 0),
        attention_outs,
        attention_args,
        "attention_0",
    )
    first = [first_a, first_b]
    first_over = send_over(first)
    *kept, second_a, second_b = call(
        functools.partial(attention_kernel, 1),
        attention_outs,
        attention_args + kept,
        "attention_1",
    )
    q_rot, k_rot, mixed, logs = kept
    second = [second_a, second_b]
    second_over = send_over(second, first_over)
    parts, parts_over = [first, second], [first_over, second_over]

    (cot_mine,) = call(
        choose_kernel, [shape((rows, half))], [cotangent, cot_over], "cotangent_mine"
    )
    side_width = ff + half + width + half

    def forward(chunk, over, kept, after):
        return call(
            functools.partial(forward_kernel, chunk),
            [shape((rows, half)), shape((rows, side_width)), shape((CHUNK, D), F32)]
            + [shape((CHUNK, ff), F32)] * 2
            + partial,
            [*parts[chunk], *over, in_mine, in_theirs, gains, gains_far]
            + [w_gate, w_up, w_down, w_far]
            + kept,
            f"forward_{chunk}",
            after=after,
        )

    low_mine, side, *saved = forward(0, first_over, [], (cot_mine, cot_corner))
    saved_all, ff_first = [saved[:3]], saved[3:]
    (cotangent,), (low_mine,) = in_turn([cotangent], [low_mine])
    cot_beside = lax.ppermute(cotangent, pair, to_beside)
    (cot_theirs,) = call(
        choose_kernel, [shape((rows, half))], [cot_beside, cot_corner], "cotangent_theirs"
    )
    ff_first_over = send_over(ff_first, second_over)
    low_mine, side, *saved = forward(1, second_over, [mixed, low_mine, side], ())
    saved_all.append(saved[:3])
    ff_second = saved[3:]
    ff_second_over = send_over(ff_second, ff_first_over)

    def weight_grad(name, arrays, products, after, gains=()):
        high = products[0][0][2] - products[0][0][1]
        widths = [right[2] - right[1] for _, _, right, _ in products]
        extra = GAIN_ROWS if gains else 0
        keep, give = call(
            functools.partial(weight_kernel, bool(gains), products),
            [shape((high // 2 + extra, sum(widths)))] * 2,
            [*arrays, *gains],
            name,
            scratch=[pltpu.VMEM((high, sum(widths)), BF16)],
            after=after,
        )
        return Chain(name, high, widths, keep, give)

    def ff_norm_back(chunk, mine, over, more, after):
        return call(
            functools.partial(ff_norm_back_kernel, chunk),
            [shape((rows, half))] * 2 + [shape((rows, half), F32)] * 2 + [shape((1, D), F32)],
            [*mine, *over, saved_all[chunk][0], cot_mine, cot_theirs, gains, gains_far, *more],
            f"ff_norm_back_{chunk}",
            after=after,
        )

    def backward(chunk, more, after):
        return call(
            functools.partial(backward_kernel, chunk),
            [shape((rows, 2 * ff)), *partial],
            [gff_mine, gff_theirs, *saved_all[chunk][1:]]
            + [w_gate, w_up, w_down, w_far]
            + more,
            f"backward_{chunk}",
            after=after,
        )

    *kept, mlp_part = ff_norm_back(0, ff_first, ff_first_over, [], ())
    gff_mine, gff_theirs, _, _ = kept
    grads, *gh_first = backward(0, [], ())
    gh_first_over = send_over(gh_first, ff_second_over)
    *kept, mlp_part = ff_norm_back(
        1, ff_second, ff_second_over, [mlp_part, *kept], ()
    )
    gff_mine, gff_theirs, out_mine, out_theirs = kept
    (side,), (gff_theirs,) = in_turn([side], [gff_theirs])
    side_far = swap(side, "row")
    gff_far = swap(gff_theirs, "row")
    out_beside = lax.ppermute(out_theirs, pair, from_same)
    grads, *gh_second = backward(1, [grads], ())
    lanes = Lanes()
    down = weight_grad(
        "down",
        [side, side_far, gff_mine, gff_far],
        [((0, 0, ff), (1, 0, ff), (2, 0, half), (3, 0, half))],
        (grads,),
    )
    (block_out,) = call(
        choose_kernel,
        [shape((rows, half), F32)],
        [out_mine, out_beside],
        "block_out",
        after=(down.keep,),
    )
    (in_far,) = call(
        in_far_kernel, [shape((rows, half))], [side_far, block_in], "in_far", after=(block_out,)
    )
    lanes.send_y(down)
    (gh_second, grads), (gh_first_over, down.keep, in_far) = in_turn(
        [gh_second, grads], [gh_first_over, down.keep, in_far]
    )
    gh_second_over = send_over(gh_second)
    grads_far = swap(grads, "row")
    grad_parts, grad_over = [gh_first, gh_second], [gh_first_over, gh_second_over]

    def ff_grad(name, start, after):
        span = (start, start + ff)
        return weight_grad(
            name,
            [low_mine, side_far, grads, grads_far],
            [((0, 0, half), (1, ff, ff + half), (2, *span), (3, *span))],
            after,
        )

    latest = down.keep
    gh_mine, gh_theirs, gqn = [], [], []
    for chunk in range(2):
        args = [
            *grad_parts[chunk],
            *grad_over[chunk],
            *parts[chunk],
            *parts_over[chunk],
            cot_mine,
            cot_theirs,
            gains,
            gains_far,
            w_output,
            wo_far,
            q_rot,
            k_rot,
            values,
            logs,
            queries,
            keys,
            totals,
            totals_over,
            qgain,
            kgain,
            cosine,
            sine_part,
        ]
        outs = [shape((rows, half))] * 2
        outs += [shape((CHUNK, half), F32)] * 2 + [shape((CHUNK, width), F32), shape((1, D), F32)]
        if chunk == 0:
            outs += [shape((CHUNK, LANES), F32)] + [shape((CHUNK, width), F32)] * 2
        else:
            outs += [shape((rows, width), F32), shape((rows, width)), shape((8, rows), F32)]
            args += [attn_part, column, gk_sum, gv_sum, gat_mine, gat_theirs]
        gat_mine, gat_theirs, gm, gt, gq_turned, attn_part, *more = call(
            functools.partial(attention_back_kernel, chunk),
            outs,
            args,
            f"attention_back_{chunk}",
            after=(latest,),
            flops=4e9 if chunk else 1,
        )
        gh_mine.append(gm)
        gh_theirs.append(gt)
        gqn.append(gq_turned)
        if chunk == 0:
            column, gk_sum, gv_sum = more
            up = ff_grad("up", ff, (column,))
            gate = ff_grad("gate", 0, (up.keep,))
            lanes.latest = gate.keep
            lanes.advance(down, gate, grad_over[1])
            latest = lanes.latest
        else:
            gkn, gv, inner = more
    inner_over = swap(inner, "col")
    gat_far, gv_far = swap(gat_theirs, "row"), swap(gv, "row")
    grads_back, gain_mine, gain_give = call(
        query_key_back_kernel,
        [shape((rows, 2 * width))] + [shape((8, half), F32)] * 2,
        [
            *gqn,
            gkn,
            queries,
            keys,
            totals,
            totals_over,
            inner,
            inner_over,
            qgain,
            kgain,
            mlp_part,
            attn_part,
        ],
        "query_key_back",
        after=(gv,),
    )
    grads_back_far = swap(grads_back, "row")
    gain_far = swap(gain_give, "row")
    lanes.latest = grads_back
    lanes.advance(gate, up)
    split = width * 3 // 4
    mixing = weight_grad(
        "mixing",
        [mixed, side_far, gat_mine, gat_far, in_mine, in_far, gv, gv_far]
        + [grads_back, grads_back_far],
        [
            ((0, 0, width), (1, ff + half, ff + half + width), (2, 0, half), (3, 0, half)),
            ((4, 0, half), (5, 0, half), (6, 0, width), (7, 0, width)),
            ((4, 0, half), (5, 0, half), (8, 0, split), (9, 0, split)),
        ],
        (lanes.latest,),
    )
    rest = (split, 2 * width)
    matching = weight_grad(
        "matching",
        [in_mine, in_far, grads_back, grads_back_far],
        [((0, 0, half), (1, 0, half), (2, *rest), (3, *rest))],
        (mixing.keep,),
        (gain_mine, gain_far),
    )
    mixing.widths = [half, width, split]
    lanes.latest = matching.keep
    lanes.advance(up, mixing)
    lanes.advance(mixing, matching)
    lanes.advance(matching, down)
    stays, moves, across, corner = call(
        input_back_kernel,
        [shape((rows, half), F32)] * 2 + [shape((rows, half))] * 2,
        [grads_back, gv, w_query, wq_far, w_key, wk_far, w_value, wv_far]
        + [*gh_mine, *gh_theirs],
        "input_back",
        after=(lanes.latest,),
    )
    lanes.latest = across
    moves = lax.ppermute(moves, pair, from_same)
    across = lax.ppermute(across, pair, [(1, 0), (2, 3)])
    lanes.advance(down, gate)
    (corner,), (across,) = in_turn([corner], [across])
    corner = lax.ppermute(corner, pair, to_corner)
    lanes.advance(gate, up)
    (grad_input,) = call(
        grad_input_kernel,
        [shape((rows, half), F32)],
        [stays, moves, across, corner],
        "grad_input",
        after=(lanes.latest,),
    )
    lanes.latest = grad_input
    lanes.advance(up, mixing)
    lanes.advance(mixing, matching)
    gain_out = call(
        gains_out_kernel,
        [shape((1, half), F32)] * 2 + [shape((1, width), F32)] * 2,
        [matching.keep],
        "gains_out",
        after=(lanes.latest,),
    )
    grad_mlpgain, grad_attngain, grad_qgain, grad_kgain = [row[0] for row in gain_out]
    lanes.latest = gain_out[0]
    grad_out, grad_value, query_first = mixing.out
    grad_query, grad_key = call(
        finish_rest_kernel,
        [shape((half, width), F32)] * 2,
        [matching.keep, *matching.received, query_first],
        "matching_out",
        after=(lanes.latest,),
    )
    (grad_down,) = down.out
    (grad_gate,) = gate.out
    (grad_up,) = up.out
    return (
        block_out,
        grad_input,
        grad_query,
        grad_key,
        grad_value,
        grad_out,
        grad_gate,
        grad_up,
        grad_down,
        grad_qgain,
        grad_kgain,
        grad_attngain,
        grad_mlpgain,
    )


def solution(mesh):
    tokens = P(("dp", "col"), "row")
    grid, turned = P("row", "col"), P("col", "row")
    in_specs = (
        tokens,
        grid,
        grid,
        grid,
        turned,
        grid,
        grid,
        turned,
        P("col"),
        P("col"),
        P("row"),
        P("row"),
        tokens,
    )
    out_specs = (
        tokens,
        tokens,
        grid,
        grid,
        grid,
        turned,
        grid,
        grid,
        turned,
        P("col"),
        P("col"),
        P("row"),
        P("row"),
    )
    return jax.shard_map(
        on_device, mesh=mesh, in_specs=in_specs, out_specs=out_specs, check_vma=False
    )
```

```python
import functools
import math

import jax
import jax.numpy as jnp
import numpy as np
from jax import lax
from jax.experimental import pallas as pl
from jax.experimental.pallas import tpu as pltpu
from jax.sharding import PartitionSpec as P

D = 1024
HEAD = 64
SEQ = 512
EPSILON = 1e-06
ROPE_BASE = 500000.0
MASKED = -1e30
CHUNK = 256
PIECES = 2
TILE = 256
LANES = 128
FACTOR = 1.0 / math.sqrt(HEAD)

F32 = jnp.float32
BF16 = jnp.bfloat16


def swap(values, axis):
    return lax.ppermute(values, axis, [(0, 1), (1, 0)])


def dot(left, right):
    return jnp.dot(left, right, preferred_element_type=F32)


def dot_t(left, right):
    return lax.dot_general(left, right, (((1,), (1,)), ((), ())), preferred_element_type=F32)


def t_dot(left, right):
    return lax.dot_general(left, right, (((0,), (0,)), ((), ())), preferred_element_type=F32)


def shape(dims, kind=BF16):
    return jax.ShapeDtypeStruct(dims, kind)


def call(kernel, outs, args, name, scratch=(), after=(), far=(), flops=1):
    count, skip, fetched = len(args), len(after), len(far)
    vmem = pl.BlockSpec(memory_space=pltpu.VMEM)
    anywhere = pl.BlockSpec(memory_space=pl.ANY)
    buffers = [pltpu.VMEM(a.shape, a.dtype) for a in far]
    if fetched:
        buffers.append(pltpu.SemaphoreType.DMA((fetched,)))

    def body(*refs):
        sources, refs = refs[:fetched], refs[fetched:]
        copies = []
        if fetched:
            refs, local = refs[: -fetched - 1], refs[-fetched - 1 :]
            copies = [
                pltpu.make_async_copy(source, local[i], local[-1].at[i])
                for i, source in enumerate(sources)
            ]
            for copy in copies:
                copy.start()
            for copy in copies:
                copy.wait()
            sources = local[:-1]
        kernel(*sources, *refs[:count], *refs[count + skip :])

    return pl.pallas_call(
        body,
        out_shape=tuple(outs),
        in_specs=[pl.BlockSpec(memory_space=pltpu.HBM)] * fetched + [vmem] * count + [anywhere] * skip,
        out_specs=tuple([vmem] * len(outs)),
        scratch_shapes=[*scratch, *buffers],
        compiler_params=pltpu.CompilerParams(
            vmem_limit_bytes=12 << 20, fuse_transposed_lhs_in_matmul=True
        ),
        cost_estimate=pl.CostEstimate(flops=int(flops), bytes_accessed=1, transcendentals=0),
        name=name,
    )(*far, *args, *after)


def tiles(extent, size=TILE):
    return [slice(at, min(at + size, extent)) for at in range(0, extent, size)]


def row_sum(values):
    return jnp.sum(values, axis=1, keepdims=True)


def columns_to_rows(columns):
    count = columns[0].shape[0]
    lane = lax.broadcasted_iota(jnp.int32, (count, LANES), 1)
    packed = jnp.zeros((count, LANES), F32)
    for index, column in enumerate(columns):
        packed = jnp.where(lane == index, column, packed)
    return packed.T[:8]


def rows_to_columns(rows, count):
    turned = jnp.concatenate([rows] * (LANES // 8), axis=0).T
    return [turned[:, i : i + 1] for i in range(count)]


def rms_scale(total):
    return lax.rsqrt(total / D + EPSILON)


def turn(values, cosine, sine_part):
    lane = lax.broadcasted_iota(jnp.int32, cosine.shape, 1)
    first = (lane % HEAD) < HEAD // 2
    out = []
    for tile in tiles(values.shape[1], LANES):
        part = values[:, tile]
        other = jnp.where(
            first, pltpu.roll(part, LANES - HEAD // 2, 1), pltpu.roll(part, HEAD // 2, 1)
        )
        out.append(part * cosine + other * sine_part)
    return jnp.concatenate(out, axis=1)


def rope_tables(count):
    half = HEAD // 2
    frequency = np.exp(np.arange(half, dtype=np.float32) * np.float32(-2.0 * math.log(ROPE_BASE) / HEAD))
    angles = np.arange(count).astype(np.float32)[:, None] * frequency[None, :]
    cosine, sine_part = np.cos(angles), np.sin(angles)
    repeats = LANES // HEAD
    return (
        jnp.asarray(np.concatenate([cosine, cosine] * repeats, axis=1)),
        jnp.asarray(np.concatenate([-sine_part, sine_part] * repeats, axis=1)),
    )


def lower_triangle():
    rows = lax.broadcasted_iota(jnp.int32, (CHUNK, CHUNK), 0)
    cols = lax.broadcasted_iota(jnp.int32, (CHUNK, CHUNK), 1)
    return rows >= cols


def keep_rows(pairs):
    for before, out in pairs:
        out[:CHUNK] = before[:CHUNK]


def head_mask(count, index):
    lane = lax.broadcasted_iota(jnp.int32, (count, LANES), 1)
    return (lane < HEAD) if index == 0 else (lane >= HEAD)


def only(mask, values):
    return jnp.where(mask, values, jnp.zeros_like(values))


def total_of(mine, theirs):
    return jnp.concatenate(
        [a[...].astype(F32) + b[...].astype(F32) for a, b in zip(mine, theirs)], axis=0
    )


def branch_of(mine, theirs):
    branch = total_of(mine, theirs)
    return branch, rms_scale(row_sum(branch * branch))


def store_pieces(pieces, columns, values):
    at = 0
    for piece in pieces:
        high = piece.shape[0]
        piece[:, columns] = values[at : at + high].astype(BF16)
        at += high


def gain_of(mine, theirs, index):
    row = slice(index, index + 1)
    return jnp.concatenate([mine[row, :], theirs[row, :]], axis=1)


def on_own_chip():
    return lax.axis_index("row") == lax.axis_index("col")


def own_half():
    return lax.axis_index("dp") & 1


def is_inner():
    place = lax.axis_index("dp") >> 1
    return (place == 1) | (place == 2)


def norm_back(branch, scale, gain_vec, grad_out):
    weighted = grad_out * gain_vec
    inner = row_sum(weighted * branch)
    grad_branch = scale * weighted - branch * (scale * scale * scale * inner / D)
    grad_gain = jnp.sum(grad_out * branch * scale, axis=0, keepdims=True)
    return grad_branch, grad_gain


def pack_kernel(*refs):
    out = refs[-1]
    out[...] = jnp.zeros(out.shape, F32)
    for index, row in enumerate(refs[:-1]):
        out[index : index + 1, :] = row[...]


def copy_kernel(*refs):
    count = len(refs) // 2
    for source, out in zip(refs[:count], refs[count:]):
        out[...] = source[...]


def pack_weights_kernel(wg, wu, wd, out):
    high, ff = wg.shape
    out[:, :ff] = wg[...]
    out[:, ff : 2 * ff] = wu[...]
    for index, rows in enumerate(tiles(ff, high)):
        at = 2 * ff + index * high
        out[: rows.stop - rows.start, at : at + high] = wd[rows, :]


def packed_weights(packed, ff):
    high = packed.shape[0]
    blocks = []
    for index, rows in enumerate(tiles(ff, high)):
        at = 2 * ff + index * high
        blocks.append((rows, packed.at[: rows.stop - rows.start, at : at + high]))
    return packed.at[:, :ff], packed.at[:, ff : 2 * ff], blocks


def choose_kernel(first, other, out):
    out[...] = jnp.where(on_own_chip(), first[...], other[...])


def choose_two_kernel(first, other, beside, corner, out, out_theirs):
    choose_kernel(first, other, out)
    choose_kernel(beside, corner, out_theirs)


def query_key_kernel(
    block, wq, wk, over, beside, corner, wqt, wkt, q_out, k_out, total_out, mine, theirs
):
    choose_two_kernel(block, over, beside, corner, mine, theirs)
    query_sum = 0.0
    key_sum = 0.0
    for tile in tiles(wq.shape[1]):
        query = dot(mine[...], wq[:, tile]) + dot(theirs[...], wqt[:, tile])
        q_out[:, tile] = query
        query_sum = query_sum + row_sum(query * query)
        key = dot(mine[...], wk[:, tile]) + dot(theirs[...], wkt[:, tile])
        k_out[:, tile] = key
        key_sum = key_sum + row_sum(key * key)
    total_out[...] = columns_to_rows([query_sum, key_sum])


def value_kernel(mine, theirs, wv, wvt, v_out):
    for tile in tiles(wv.shape[1]):
        v_out[:, tile] = (dot(mine[...], wv[:, tile]) + dot(theirs[...], wvt[:, tile])).astype(BF16)


def attention_kernel(
    chunk,
    queries,
    keys,
    values,
    totals,
    totals_over,
    qgain,
    kgain,
    cosine,
    sine_part,
    wo,
    wot,
    *rest,
):
    if chunk == 0:
        q_rot, k_rot, mixed, logs, *partial = rest
    else:
        q_rot, k_rot, mixed, logs, *partial = rest[4:]
        keep_rows(zip(rest[:4], rest[4:]))
    rows = slice(chunk * CHUNK, (chunk + 1) * CHUNK)
    query_total, key_total = rows_to_columns(totals[...] + totals_over[...], 2)
    query = queries[rows, :] * rms_scale(query_total[rows]) * qgain[...]
    key = keys[rows, :] * rms_scale(key_total[rows]) * kgain[...]
    q_rot[rows, :] = (turn(query, cosine[rows, :], sine_part[rows, :]) * FACTOR).astype(BF16)
    k_rot[rows, :] = turn(key, cosine[rows, :], sine_part[rows, :]).astype(BF16)
    visible = lower_triangle()
    lane = lax.broadcasted_iota(jnp.int32, (CHUNK, LANES), 1)
    log_tile = jnp.zeros((CHUNK, LANES), F32)
    for at, tile in enumerate(tiles(queries.shape[1], LANES)):
        total = jnp.zeros((CHUNK, LANES), F32)
        for index in range(2):
            query_head = only(head_mask(CHUNK, index), q_rot[rows, tile])
            scores = []
            for block in range(chunk + 1):
                part = dot_t(query_head, k_rot[block * CHUNK : (block + 1) * CHUNK, tile])
                scores.append(jnp.where(visible, part, MASKED) if block == chunk else part)
            peak = jnp.max(scores[0], axis=1, keepdims=True)
            for part in scores[1:]:
                peak = jnp.maximum(peak, jnp.max(part, axis=1, keepdims=True))
            scores = [jnp.exp(part - peak) for part in scores]
            denominator = sum(row_sum(part) for part in scores)
            inverse = 1.0 / denominator
            for block, part in enumerate(scores):
                value_rows = values[block * CHUNK : (block + 1) * CHUNK, tile]
                total = total + dot(
                    (part * inverse).astype(BF16), only(head_mask(CHUNK, index), value_rows)
                )
            log_tile = jnp.where(lane == 2 * at + index, peak + jnp.log(denominator), log_tile)
        mixed[rows, tile] = total.astype(BF16)
    logs[rows, :] = log_tile
    low = mixed[rows, :]
    half = wo.shape[1]
    store_pieces(partial, slice(0, half), dot(low, wo[...]))
    store_pieces(partial, slice(half, 2 * half), dot(low, wot[...]))


def forward_kernel(
    chunk, *refs
):
    part, part_over = refs[:PIECES], refs[PIECES : 2 * PIECES]
    forward_body(chunk, part, part_over, *refs[2 * PIECES :])


def forward_body(
    chunk, part, part_over, mine, theirs, gains, gains_far, wg, wu, wd, w_far, *rest
):
    if chunk == 0:
        low_mine, side, hidden, gate, up, *partial = rest
    else:
        mixed = rest[0]
        low_mine, side, hidden, gate, up, *partial = rest[3:]
        keep_rows(zip(rest[1:3], rest[3:]))
        at = wg.shape[1] + mine.shape[1]
        side[:, at : at + mixed.shape[1]] = mixed[...]
        side[:, at + mixed.shape[1] :] = theirs[...]
    rows = slice(chunk * CHUNK, (chunk + 1) * CHUNK)
    branch, scale = branch_of(part, part_over)
    half, ff = mine.shape[1], wg.shape[1]
    wgt, wut, wdt = packed_weights(w_far, ff)
    normed = branch * scale * gain_of(gains, gains_far, 0)
    value = mine[rows, :].astype(F32) + normed[:, :half]
    hidden[:, :half] = value
    low_mine[rows, :] = value.astype(BF16)
    value = theirs[rows, :].astype(F32) + normed[:, half:]
    hidden[:, half:] = value
    side[rows, ff : ff + half] = value.astype(BF16)
    for tile in tiles(ff):
        left, right = low_mine[rows, :], side[rows, ff : ff + half]
        gate_act = dot(left, wg[:, tile]) + dot(right, wgt[:, tile])
        up_act = dot(left, wu[:, tile]) + dot(right, wut[:, tile])
        gate[:, tile] = gate_act
        up[:, tile] = up_act
        side[rows, tile] = (gate_act * jax.nn.sigmoid(gate_act) * up_act).astype(BF16)
    low = side[rows, :ff]
    store_pieces(partial, slice(0, half), dot(low, wd[...]))
    theirs_part = sum(dot(side[rows, span], block[...]) for span, block in wdt)
    store_pieces(partial, slice(half, 2 * half), theirs_part)


def ff_norm_back_kernel(
    chunk, *refs
):
    part, part_over = refs[:PIECES], refs[PIECES : 2 * PIECES]
    hidden, cot_mine, cot_theirs, gains, gains_far, *rest = refs[2 * PIECES :]
    if chunk == 0:
        gff_mine, gff_theirs, out_mine, out_theirs, grad_gain = rest
    else:
        gain_before = rest[0]
        gff_mine, gff_theirs, out_mine, out_theirs, grad_gain = rest[5:]
        keep_rows(zip(rest[1:5], rest[5:]))
    rows = slice(chunk * CHUNK, (chunk + 1) * CHUNK)
    branch, scale = branch_of(part, part_over)
    half = cot_mine.shape[1]
    gain = gain_of(gains, gains_far, 1)
    block_out = hidden[...] + branch * scale * gain
    out_mine[rows, :] = block_out[:, :half]
    out_theirs[rows, :] = block_out[:, half:]
    upstream = jnp.concatenate([cot_mine[rows, :], cot_theirs[rows, :]], axis=1).astype(F32)
    grad_branch, gained = norm_back(branch, scale, gain, upstream)
    grad_gain[...] = gained if chunk == 0 else gain_before[...] + gained
    gff_mine[rows, :] = grad_branch[:, :half].astype(BF16)
    gff_theirs[rows, :] = grad_branch[:, half:].astype(BF16)


def backward_kernel(
    chunk, gff_mine, gff_theirs, gate, up, wg, wu, wd, w_far, *rest
):
    if chunk == 0:
        grads, *partial = rest
    else:
        grads, *partial = rest[1:]
        keep_rows([rest[:2]])
    rows = slice(chunk * CHUNK, (chunk + 1) * CHUNK)
    half, ff = wd.shape[1], wg.shape[1]
    wgt, wut, wdt = packed_weights(w_far, ff)
    for tile in tiles(ff):
        span, block = wdt[tile.start // wdt[0][0].stop]
        part = block[tile.start - span.start : tile.stop - span.start, :]
        grad_act = dot_t(gff_mine[rows, :], wd[tile, :]) + dot_t(gff_theirs[rows, :], part)
        gate_act = gate[:, tile]
        sig = jax.nn.sigmoid(gate_act)
        grads[rows, tile] = (
            grad_act * up[:, tile] * sig * (1.0 + gate_act * (1.0 - sig))
        ).astype(BF16)
        there = slice(ff + tile.start, ff + tile.stop)
        grads[rows, there] = (grad_act * gate_act * sig).astype(BF16)
    left, right = grads[rows, :ff], grads[rows, ff:]
    for tile in tiles(half):
        store_pieces(partial, tile, dot_t(left, wg[tile, :]) + dot_t(right, wu[tile, :]))
        there = slice(half + tile.start, half + tile.stop)
        store_pieces(partial, there, dot_t(left, wgt[tile, :]) + dot_t(right, wut[tile, :]))


def attention_back_kernel(chunk, *refs):
    grad_part, grad_over, part, part_over = [
        refs[i * PIECES : (i + 1) * PIECES] for i in range(4)
    ]
    (
        cot_mine,
        cot_theirs,
        gains,
        gains_far,
        wo,
        wot,
        q_rot,
        k_rot,
        values,
        logs,
        queries,
        keys,
        totals,
        totals_over,
        qgain,
        kgain,
        cosine,
        sine_part,
        *rest,
    ) = refs[4 * PIECES :]
    half = wo.shape[1]
    width = queries.shape[1]
    if chunk == 0:
        gat_mine, side, gh_mine, gh_theirs, gqn, grad_gain, column, gk_sum, gv_sum = rest
    else:
        gain_before, column_in, gk_in, gv_in = rest[:4]
        gat_mine, side, gh_mine, gh_theirs, gqn, grad_gain, gkn, gv_low, inner_out = rest[6:]
        keep_rows(zip(rest[4:6], rest[6:]))
    rows = slice(chunk * CHUNK, (chunk + 1) * CHUNK)
    seen = (chunk + 1) * CHUNK
    branch, scale = branch_of(part, part_over)
    grad_hidden = (
        jnp.concatenate([cot_mine[rows, :], cot_theirs[rows, :]], axis=1).astype(F32)
        + total_of(grad_part, grad_over)
    )
    gh_mine[...] = grad_hidden[:, :half]
    gh_theirs[...] = grad_hidden[:, half:]
    grad_branch, gained = norm_back(branch, scale, gain_of(gains, gains_far, 0), grad_hidden)
    grad_gain[...] = gained if chunk == 0 else gain_before[...] + gained
    gat_mine[rows, :] = grad_branch[:, :half].astype(BF16)
    side[rows, :] = grad_branch[:, half:].astype(BF16)
    grad_mixed = (
        dot_t(gat_mine[rows, :], wo[...]) + dot_t(side[rows, :], wot[...])
    ).astype(BF16)
    visible = lower_triangle()
    query_total, key_total = rows_to_columns(totals[...] + totals_over[...], 2)
    query_inner = jnp.zeros((CHUNK, 1), F32)
    key_inner = jnp.zeros((seen, 1), F32)
    for at, tile in enumerate(tiles(width, LANES)):
        grad_query = jnp.zeros((CHUNK, LANES), F32)
        grad_key = [jnp.zeros((CHUNK, LANES), F32) for _ in range(chunk + 1)]
        grad_value = [jnp.zeros((CHUNK, LANES), F32) for _ in range(chunk + 1)]
        for index in range(2):
            mask = head_mask(CHUNK, index)
            query_head = only(mask, q_rot[rows, tile])
            grad_head = only(mask, grad_mixed[:, tile])
            log_column = logs[rows, 2 * at + index : 2 * at + index + 1]
            weights, grads = [], []
            for block in range(chunk + 1):
                span = slice(block * CHUNK, (block + 1) * CHUNK)
                scores = dot_t(query_head, k_rot[span, tile])
                if block == chunk:
                    scores = jnp.where(visible, scores, MASKED)
                weights.append(jnp.exp(scores - log_column))
                grads.append(dot_t(grad_head, values[span, tile]))
            inner = sum(row_sum(w * g) for w, g in zip(weights, grads))
            for block in range(chunk + 1):
                span = slice(block * CHUNK, (block + 1) * CHUNK)
                weight = weights[block]
                grad_scores = (weight * (grads[block] - inner)).astype(BF16)
                grad_value[block] = grad_value[block] + t_dot(weight.astype(BF16), grad_head)
                grad_query = grad_query + dot(grad_scores, only(mask, k_rot[span, tile]))
                grad_key[block] = grad_key[block] + t_dot(grad_scores, query_head)
        back = turn(grad_query * FACTOR, cosine[rows, :], -sine_part[rows, :])
        gqn[:, tile] = back
        query_inner = query_inner + row_sum(back * qgain[:, tile] * queries[rows, tile])
        if chunk == 0:
            gk_sum[:, tile] = grad_key[0]
            gv_sum[:, tile] = grad_value[0]
        else:
            key_all = jnp.concatenate([gk_in[:, tile] + grad_key[0], grad_key[1]], axis=0)
            value_all = jnp.concatenate([gv_in[:, tile] + grad_value[0], grad_value[1]], axis=0)
            gv_low[:, tile] = value_all.astype(BF16)
            back = turn(key_all, cosine[...], -sine_part[...])
            gkn[:, tile] = back
            key_inner = key_inner + row_sum(back * kgain[:, tile] * keys[:, tile])
    if chunk == 0:
        column[...] = jnp.broadcast_to(query_inner, (CHUNK, LANES))
    else:
        query_inner = jnp.concatenate([column_in[:, :1], query_inner], axis=0)
        inner_out[...] = columns_to_rows([query_inner, key_inner])


def query_key_back_kernel(
    gqn_first,
    gqn_second,
    gkn,
    queries,
    keys,
    totals,
    totals_over,
    inner,
    inner_over,
    qgain,
    kgain,
    mlp_part,
    attn_part,
    grads,
    gain_mine,
    gain_give,
):
    width = queries.shape[1]
    half = gain_mine.shape[1]
    for out, columns in ((gain_mine, slice(0, half)), (gain_give, slice(half, 2 * half))):
        out[...] = jnp.zeros(out.shape, F32)
        out[0:1, :] = mlp_part[:, columns]
        out[1:2, :] = attn_part[:, columns]
    query_total, key_total = rows_to_columns(totals[...] + totals_over[...], 2)
    query_inner, key_inner = rows_to_columns(inner[...] + inner_over[...], 2)
    gqn = jnp.concatenate([gqn_first[...], gqn_second[...]], axis=0)
    for at, raw, back, total, sums, gain, low in (
        (2, queries, gqn, query_total, query_inner, qgain, grads.at[:, :width]),
        (3, keys, gkn[...], key_total, key_inner, kgain, grads.at[:, width:]),
    ):
        scale = rms_scale(total)
        value = raw[...]
        low[...] = (
            scale * (back * gain[...]) - value * (scale * scale * scale * sums / D)
        ).astype(BF16)
        gained = jnp.sum(back * value * scale, axis=0, keepdims=True)
        gain_mine[at : at + 1, :] = gained
        gain_give[at : at + 1, :] = gained


GAIN_ROWS = 16


def plain_weight_kernel(products, *refs):
    plain = refs[-1]

    def view(operand):
        index, start, stop = operand
        return refs[index].at[:, start:stop]

    at = 0
    for product in products:
        left, left_far, right, right_far = [view(operand) for operand in product]
        width = product[2][2] - product[2][1]
        for tile in tiles(plain.shape[0]):
            plain[tile, at : at + width] = (
                t_dot(left[:, tile], right[...]) + t_dot(left_far[:, tile], right_far[...])
            ).astype(BF16)
        at += width


def weight_kernel(with_gains, products, *refs):
    keep, give, plain = refs[-3:]
    plain_weight_kernel(products, *refs[:-3], plain)
    half = plain.shape[0] // 2
    mine = pl.multiple_of(own_half() * half, half)
    theirs = pl.multiple_of((1 - own_half()) * half, half)
    keep[:half, :] = plain[pl.ds(mine, half), :]
    give[:half, :] = plain[pl.ds(theirs, half), :]
    if with_gains:
        gains = refs[-5][...] + refs[-4][...]
        width = gains.shape[1]
        rows = jnp.concatenate([gains, jnp.zeros_like(gains)], axis=0)
        rest = jnp.zeros((GAIN_ROWS, plain.shape[1] - width), F32)
        rows = jnp.concatenate([rows, rest], axis=1).astype(BF16)
        keep[half:, :] = rows
        give[half:, :] = rows


def add_kernel(mine, *rest):
    out = rest[-1]
    at = 0
    for piece in rest[:-1]:
        rows = slice(at, at + piece.shape[0])
        out[rows, :] = (mine[rows, :].astype(F32) + piece[...].astype(F32)).astype(BF16)
        at = rows.stop


def inner_kernel(mine, received, out):
    out[...] = jnp.where(is_inner(), mine[...], received[...])


def finish_kernel(mine, received, *outs):
    half = outs[0].shape[0] // 2
    for place, source in enumerate((mine, received)):
        to = pl.multiple_of((own_half() ^ place) * half, half)
        column = 0
        for out in outs:
            width = out.shape[1]
            out[pl.ds(to, half), :] = source[:half, column : column + width].astype(F32)
            column += width


def in_far_kernel(side_far, block, out):
    out[...] = jnp.where(on_own_chip(), side_far[:, side_far.shape[1] - out.shape[1] :], block[...])


def gains_out_kernel(total, *outs):
    rows = total[total.shape[0] - GAIN_ROWS :, :].astype(F32)
    for index, out in enumerate(outs):
        out[...] = rows[index : index + 1, : out.shape[1]]


def finish_rest_kernel(mine, received, query_first, query, key):
    half = query.shape[0] // 2
    split = query_first.shape[1]
    more = query.shape[1] - split
    query[:, :split] = query_first[...]
    for place, source in enumerate((mine, received)):
        to = pl.multiple_of((own_half() ^ place) * half, half)
        query[pl.ds(to, half), split:] = source[:half, :more].astype(F32)
        key[pl.ds(to, half), :] = source[:half, more:].astype(F32)


def grad_input_kernel(stays, moves, across, corner, out):
    own = on_own_chip()
    out[...] = jnp.where(own, stays[...], moves[...]) + jnp.where(
        own, across[...], corner[...]
    ).astype(F32)


def input_back_kernel(
    grads, gv, wq, wqt, wk, wkt, wv, wvt, *rest
):
    width = wq.shape[1]
    gq, gk = grads.at[:, :width], grads.at[:, width:]
    gh_mine, gh_theirs = rest[:2], rest[2:4]
    stays, moves, across, corner = rest[4:]
    for tile in tiles(wq.shape[0]):
        mine = (
            dot_t(gq[...], wq[tile, :]) + dot_t(gk[...], wk[tile, :]) + dot_t(gv[...], wv[tile, :])
        )
        theirs = (
            dot_t(gq[...], wqt[tile, :])
            + dot_t(gk[...], wkt[tile, :])
            + dot_t(gv[...], wvt[tile, :])
        )
        for chunk in range(2):
            rows = slice(chunk * CHUNK, (chunk + 1) * CHUNK)
            stays[rows, tile] = gh_mine[chunk][:, tile] + mine[rows]
            moves[rows, tile] = gh_theirs[chunk][:, tile] + theirs[rows]
        across[:, tile] = mine.astype(BF16)
        corner[:, tile] = theirs.astype(BF16)


def dp_exchange(values, bit):
    size = lax.axis_size("dp")
    return lax.ppermute(values, "dp", [(i, i ^ (1 << bit)) for i in range(size)])


def dp_bits():
    return lax.axis_size("dp").bit_length() - 1


def along_line(values, moves):
    pairs = [(2 * a + half, 2 * b + half) for a, b in moves for half in range(2)]
    return lax.ppermute(values, "dp", pairs)


def in_turn(operands, received):
    return lax.optimization_barrier((operands, received))


class Chain:
    def __init__(self, name, high, widths, keep, give):
        self.name, self.high, self.widths, self.keep, self.give = name, high, widths, keep, give
        self.back = False
        self.received = None

    def kernel(self, body, args, part, after, outs=None):
        out = call(
            body, outs or [shape(self.keep.shape)], args, f"{self.name}_{part}", after=after
        )
        if outs is None:
            (self.keep,) = out
        else:
            self.out = out
        return out[0]

    def combine(self, body, part, after):
        return self.kernel(body, [self.keep, *self.received], part, after)

    def finish(self, after):
        outs = [shape((self.high, w), F32) for w in self.widths]
        return self.kernel(finish_kernel, [self.keep, *self.received], "out", after, outs)


LINE = ((0, 1), (3, 2)), ((1, 2), (2, 1)), ((1, 0), (2, 3))


class Lanes:
    def __init__(self):
        self.line = [None, None, None]
        self.latest = None

    def send_y(self, chain, before=None):
        operands = [chain.keep if chain.back else chain.give]
        if before is not None:
            operands, before.received = in_turn(operands, before.received)
        chain.received = [dp_exchange(piece, 0) for piece in operands]

    def pass_on(self, index, chain):
        before, self.line[index] = self.line[index], chain
        if before is not None and chain is not None:
            chain.keep, before.received = in_turn(chain.keep, before.received)
        if chain is not None:
            chain.received = [along_line(chain.keep, LINE[index])]
        return before

    def advance(self, chain, following=None, after=()):
        current = chain
        late = following is not None and following is self.line[2]
        if following is not None and not late:
            self.send_y(following, chain)
        done = None
        if chain.back:
            done, chain = chain, None
        else:
            self.latest = chain.combine(add_kernel, "y", (self.latest, *after))
            if lax.axis_size("dp") != 8:
                for bit in range(1, dp_bits()):
                    other = dp_exchange(chain.keep, bit).astype(F32)
                    chain.keep = (chain.keep.astype(F32) + other).astype(BF16)
                chain.back = True
                chain = None
        for index, (body, part) in enumerate(
            ((add_kernel, "in"), (add_kernel, "across"), (inner_kernel, "out"))
        ):
            chain = self.pass_on(index, chain)
            if chain is not None:
                self.latest = chain.combine(body, f"z_{part}", (self.latest,))
        if chain is not None:
            chain.back = True
        if late:
            self.send_y(following, current)
        if done is not None:
            self.latest = done.finish((self.latest,))


def on_device(
    block_in,
    w_query,
    w_key,
    w_value,
    w_output,
    w_gate,
    w_up,
    w_down,
    qnorm_gain,
    knorm_gain,
    attn_gain,
    mlp_gain,
    cotangent,
):
    rows, half = block_in.shape
    width = w_query.shape[1]
    ff = w_gate.shape[1]
    pair = ("row", "col")

    to_over = [(0, 1), (3, 2)]
    to_corner = [(1, 2), (2, 1)]
    to_beside = [(2, 0), (1, 3)]
    from_same = [(0, 2), (3, 1)]

    in_over = lax.ppermute(block_in, pair, to_over)
    in_corner = lax.ppermute(block_in, pair, to_corner)
    in_beside = lax.ppermute(block_in, pair, to_beside)
    wq_far, wk_far = swap(w_query, "row"), swap(w_key, "row")
    qgain, kgain = qnorm_gain[None], knorm_gain[None]
    cosine, sine_part = rope_tables(rows)

    near = call(
        copy_kernel,
        [shape((rows, half)), shape((half, width)), shape((half, width))],
        [block_in, w_query, w_key],
        "near",
    )
    (ff_weights,) = call(
        pack_weights_kernel,
        [shape((half, 2 * ff + -(-ff // half) * half))],
        [w_gate, w_up, w_down],
        "ff_weights",
        after=(near[0],),
    )
    (gains,) = call(
        pack_kernel,
        [shape((8, half), F32)],
        [attn_gain[None], mlp_gain[None]],
        "gains",
        after=(ff_weights,),
    )
    (wv_give, wo_give, gains), (in_corner, in_over, ff_weights, *near) = in_turn(
        [w_value, w_output, gains], [in_corner, in_over, ff_weights, *near]
    )
    wv_far, wo_far, gains_far = [swap(value, "row") for value in (wv_give, wo_give, gains)]

    queries, keys, totals, in_mine, in_theirs = call(
        query_key_kernel,
        [shape((rows, width), F32)] * 2 + [shape((8, rows), F32)] + [shape((rows, half))] * 2,
        [*near, in_over, in_beside, in_corner, wq_far, wk_far],
        "query_key",
    )
    totals_over = swap(totals, "col")
    (values,) = call(
        value_kernel,
        [shape((rows, width))],
        [in_mine, in_theirs, w_value, wv_far],
        "value",
    )
    (cotangent, ff_weights), (totals_over, values, wo_far, gains_far) = in_turn(
        [cotangent, ff_weights], [totals_over, values, wo_far, gains_far]
    )
    cot_corner = lax.ppermute(cotangent, pair, to_corner)
    w_far = swap(ff_weights, "row")
    attention_args = [
        queries,
        keys,
        values,
        totals,
        totals_over,
        qgain,
        kgain,
        cosine,
        sine_part,
        w_output,
        wo_far,
    ]
    partial = [shape((CHUNK // PIECES, D))] * PIECES
    attention_outs = [shape((rows, width))] * 3 + [shape((rows, LANES), F32), *partial]

    def send_over(pieces, before=None):
        if before is not None:
            for index in range(PIECES):
                (pieces[index],), (before[index],) = in_turn([pieces[index]], [before[index]])
        return [swap(piece, "col") for piece in pieces]

    *kept, first_a, first_b = call(
        functools.partial(attention_kernel, 0),
        attention_outs,
        attention_args,
        "attention_0",
    )
    first = [first_a, first_b]
    (cotangent,), (cot_corner, kept[-1]) = in_turn([cotangent], [cot_corner, kept[-1]])
    cot_over = lax.ppermute(cotangent, pair, to_over)
    first_over = send_over(first)
    *kept, second_a, second_b = call(
        functools.partial(attention_kernel, 1),
        attention_outs,
        attention_args + kept,
        "attention_1",
    )
    q_rot, k_rot, mixed, logs = kept
    second = [second_a, second_b]
    second_over = send_over(second, first_over)
    parts, parts_over = [first, second], [first_over, second_over]

    (cot_mine,) = call(
        choose_kernel, [shape((rows, half))], [cotangent, cot_over], "cotangent_mine"
    )
    side_width = ff + half + width + half

    def forward(chunk, over, kept, after):
        return call(
            functools.partial(forward_kernel, chunk),
            [shape((rows, half)), shape((rows, side_width)), shape((CHUNK, D), F32)]
            + [shape((CHUNK, ff), F32)] * 2
            + partial,
            [*parts[chunk], *over, in_mine, in_theirs, gains, gains_far]
            + [w_gate, w_up, w_down, w_far]
            + kept,
            f"forward_{chunk}",
            after=after,
        )

    low_mine, side, *saved = forward(0, first_over, [], (cot_mine, cot_corner))
    saved_all, ff_first = [saved[:3]], saved[3:]
    (cotangent,), (low_mine,) = in_turn([cotangent], [low_mine])
    cot_beside = lax.ppermute(cotangent, pair, to_beside)
    (cot_theirs,) = call(
        choose_kernel, [shape((rows, half))], [cot_beside, cot_corner], "cotangent_theirs"
    )
    ff_first_over = send_over(ff_first, second_over)
    low_mine, side, *saved = forward(1, second_over, [mixed, low_mine, side], ())
    saved_all.append(saved[:3])
    ff_second = saved[3:]
    ff_second_over = send_over(ff_second, ff_first_over)

    def weight_grad(name, arrays, products, after, gains=()):
        high = products[0][0][2] - products[0][0][1]
        widths = [right[2] - right[1] for _, _, right, _ in products]
        extra = GAIN_ROWS if gains else 0
        keep, give = call(
            functools.partial(weight_kernel, bool(gains), products),
            [shape((high // 2 + extra, sum(widths)))] * 2,
            [*arrays, *gains],
            name,
            scratch=[pltpu.VMEM((high, sum(widths)), BF16)],
            after=after,
        )
        return Chain(name, high, widths, keep, give)

    def ff_norm_back(chunk, mine, over, more, after):
        return call(
            functools.partial(ff_norm_back_kernel, chunk),
            [shape((rows, half))] * 2 + [shape((rows, half), F32)] * 2 + [shape((1, D), F32)],
            [*mine, *over, saved_all[chunk][0], cot_mine, cot_theirs, gains, gains_far, *more],
            f"ff_norm_back_{chunk}",
            after=after,
        )

    def backward(chunk, more, after):
        return call(
            functools.partial(backward_kernel, chunk),
            [shape((rows, 2 * ff)), *partial],
            [gff_mine, gff_theirs, *saved_all[chunk][1:]]
            + [w_gate, w_up, w_down, w_far]
            + more,
            f"backward_{chunk}",
            after=after,
        )

    *kept, mlp_part = ff_norm_back(0, ff_first, ff_first_over, [], ())
    gff_mine, gff_theirs, _, _ = kept
    grads, *gh_first = backward(0, [], ())
    gh_first_over = send_over(gh_first, ff_second_over)
    *kept, mlp_part = ff_norm_back(
        1, ff_second, ff_second_over, [mlp_part, *kept], ()
    )
    gff_mine, gff_theirs, out_mine, out_theirs = kept
    (side,), (gff_theirs,) = in_turn([side], [gff_theirs])
    side_far = swap(side, "row")
    gff_far = swap(gff_theirs, "row")
    out_beside = lax.ppermute(out_theirs, pair, from_same)
    grads, *gh_second = backward(1, [grads], ())
    lanes = Lanes()
    down = weight_grad(
        "down",
        [side, side_far, gff_mine, gff_far],
        [((0, 0, ff), (1, 0, ff), (2, 0, half), (3, 0, half))],
        (grads,),
    )
    (block_out,) = call(
        choose_kernel,
        [shape((rows, half), F32)],
        [out_mine, out_beside],
        "block_out",
        after=(down.keep,),
    )
    (in_far,) = call(
        in_far_kernel, [shape((rows, half))], [side_far, block_in], "in_far", after=(block_out,)
    )
    lanes.send_y(down)
    (gh_second, grads), (gh_first_over, down.keep, in_far) = in_turn(
        [gh_second, grads], [gh_first_over, down.keep, in_far]
    )
    gh_second_over = send_over(gh_second)
    grads_far = swap(grads, "row")
    grad_parts, grad_over = [gh_first, gh_second], [gh_first_over, gh_second_over]

    def ff_grad(name, start, after):
        span = (start, start + ff)
        return weight_grad(
            name,
            [low_mine, side_far, grads, grads_far],
            [((0, 0, half), (1, ff, ff + half), (2, *span), (3, *span))],
            after,
        )

    latest = down.keep
    gh_mine, gh_theirs, gqn = [], [], []
    for chunk in range(2):
        args = [
            *grad_parts[chunk],
            *grad_over[chunk],
            *parts[chunk],
            *parts_over[chunk],
            cot_mine,
            cot_theirs,
            gains,
            gains_far,
            w_output,
            wo_far,
            q_rot,
            k_rot,
            values,
            logs,
            queries,
            keys,
            totals,
            totals_over,
            qgain,
            kgain,
            cosine,
            sine_part,
        ]
        outs = [shape((rows, half))] * 2
        outs += [shape((CHUNK, half), F32)] * 2 + [shape((CHUNK, width), F32), shape((1, D), F32)]
        if chunk == 0:
            outs += [shape((CHUNK, LANES), F32)] + [shape((CHUNK, width), F32)] * 2
        else:
            outs += [shape((rows, width), F32), shape((rows, width)), shape((8, rows), F32)]
            args += [attn_part, column, gk_sum, gv_sum, gat_mine, gat_theirs]
        gat_mine, gat_theirs, gm, gt, gq_turned, attn_part, *more = call(
            functools.partial(attention_back_kernel, chunk),
            outs,
            args,
            f"attention_back_{chunk}",
            after=(latest,),
            flops=4e9 if chunk else 1,
        )
        gh_mine.append(gm)
        gh_theirs.append(gt)
        gqn.append(gq_turned)
        if chunk == 0:
            column, gk_sum, gv_sum = more
            up = ff_grad("up", ff, (column,))
            gate = ff_grad("gate", 0, (up.keep,))
            lanes.latest = gate.keep
            lanes.advance(down, gate, grad_over[1])
            latest = lanes.latest
        else:
            gkn, gv, inner = more
    inner_over = swap(inner, "col")
    gat_far, gv_far = swap(gat_theirs, "row"), swap(gv, "row")
    grads_back, gain_mine, gain_give = call(
        query_key_back_kernel,
        [shape((rows, 2 * width))] + [shape((8, half), F32)] * 2,
        [
            *gqn,
            gkn,
            queries,
            keys,
            totals,
            totals_over,
            inner,
            inner_over,
            qgain,
            kgain,
            mlp_part,
            attn_part,
        ],
        "query_key_back",
        after=(gv,),
    )
    grads_back_far = swap(grads_back, "row")
    gain_far = swap(gain_give, "row")
    lanes.latest = grads_back
    lanes.advance(gate, up)
    split = width * 3 // 4
    mixing = weight_grad(
        "mixing",
        [mixed, side_far, gat_mine, gat_far, in_mine, in_far, gv, gv_far]
        + [grads_back, grads_back_far],
        [
            ((0, 0, width), (1, ff + half, ff + half + width), (2, 0, half), (3, 0, half)),
            ((4, 0, half), (5, 0, half), (6, 0, width), (7, 0, width)),
            ((4, 0, half), (5, 0, half), (8, 0, split), (9, 0, split)),
        ],
        (lanes.latest,),
    )
    rest = (split, 2 * width)
    matching = weight_grad(
        "matching",
        [in_mine, in_far, grads_back, grads_back_far],
        [((0, 0, half), (1, 0, half), (2, *rest), (3, *rest))],
        (mixing.keep,),
        (gain_mine, gain_far),
    )
    mixing.widths = [half, width, split]
    lanes.latest = matching.keep
    lanes.advance(up, mixing)
    lanes.advance(mixing, matching)
    lanes.advance(matching, down)
    stays, moves, across, corner = call(
        input_back_kernel,
        [shape((rows, half), F32)] * 2 + [shape((rows, half))] * 2,
        [grads_back, gv, w_query, wq_far, w_key, wk_far, w_value, wv_far]
        + [*gh_mine, *gh_theirs],
        "input_back",
        after=(lanes.latest,),
    )
    lanes.latest = across
    moves = lax.ppermute(moves, pair, from_same)
    across = lax.ppermute(across, pair, [(1, 0), (2, 3)])
    lanes.advance(down, gate)
    (corner,), (across,) = in_turn([corner], [across])
    corner = lax.ppermute(corner, pair, to_corner)
    lanes.advance(gate, up)
    (grad_input,) = call(
        grad_input_kernel,
        [shape((rows, half), F32)],
        [stays, moves, across, corner],
        "grad_input",
        after=(lanes.latest,),
    )
    lanes.latest = grad_input
    lanes.advance(up, mixing)
    lanes.advance(mixing, matching)
    gain_out = call(
        gains_out_kernel,
        [shape((1, half), F32)] * 2 + [shape((1, width), F32)] * 2,
        [matching.keep],
        "gains_out",
        after=(lanes.latest,),
    )
    grad_mlpgain, grad_attngain, grad_qgain, grad_kgain = [row[0] for row in gain_out]
    lanes.latest = gain_out[0]
    grad_out, grad_value, query_first = mixing.out
    grad_query, grad_key = call(
        finish_rest_kernel,
        [shape((half, width), F32)] * 2,
        [matching.keep, *matching.received, query_first],
        "matching_out",
        after=(lanes.latest,),
    )
    (grad_down,) = down.out
    (grad_gate,) = gate.out
    (grad_up,) = up.out
    return (
        block_out,
        grad_input,
        grad_query,
        grad_key,
        grad_value,
        grad_out,
        grad_gate,
        grad_up,
        grad_down,
        grad_qgain,
        grad_kgain,
        grad_attngain,
        grad_mlpgain,
    )


def solution(mesh):
    tokens = P(("dp", "col"), "row")
    grid, turned = P("row", "col"), P("col", "row")
    in_specs = (
        tokens,
        grid,
        grid,
        grid,
        turned,
        grid,
        grid,
        turned,
        P("col"),
        P("col"),
        P("row"),
        P("row"),
        tokens,
    )
    out_specs = (
        tokens,
        tokens,
        grid,
        grid,
        grid,
        turned,
        grid,
        grid,
        turned,
        P("col"),
        P("col"),
        P("row"),
        P("row"),
    )
    return jax.shard_map(
        on_device, mesh=mesh, in_specs=in_specs, out_specs=out_specs, check_vma=False
    )
```

```python
import functools
import math

import jax
import jax.numpy as jnp
import numpy as np
from jax import lax
from jax.experimental import pallas as pl
from jax.experimental.pallas import tpu as pltpu
from jax.sharding import PartitionSpec as P

D = 1024
HEAD = 64
SEQ = 512
EPSILON = 1e-06
ROPE_BASE = 500000.0
MASKED = -1e30
CHUNK = 256
PIECES = 2
TILE = 256
LANES = 128
FACTOR = 1.0 / math.sqrt(HEAD)

F32 = jnp.float32
BF16 = jnp.bfloat16


def swap(values, axis):
    return lax.ppermute(values, axis, [(0, 1), (1, 0)])


def dot(left, right):
    return jnp.dot(left, right, preferred_element_type=F32)


def dot_t(left, right):
    return lax.dot_general(left, right, (((1,), (1,)), ((), ())), preferred_element_type=F32)


def t_dot(left, right):
    return lax.dot_general(left, right, (((0,), (0,)), ((), ())), preferred_element_type=F32)


def shape(dims, kind=BF16):
    return jax.ShapeDtypeStruct(dims, kind)


def call(kernel, outs, args, name, scratch=(), after=(), far=(), flops=1):
    count, skip, fetched = len(args), len(after), len(far)
    vmem = pl.BlockSpec(memory_space=pltpu.VMEM)
    anywhere = pl.BlockSpec(memory_space=pl.ANY)
    buffers = [pltpu.VMEM(a.shape, a.dtype) for a in far]
    if fetched:
        buffers.append(pltpu.SemaphoreType.DMA((fetched,)))

    def body(*refs):
        sources, refs = refs[:fetched], refs[fetched:]
        copies = []
        if fetched:
            refs, local = refs[: -fetched - 1], refs[-fetched - 1 :]
            copies = [
                pltpu.make_async_copy(source, local[i], local[-1].at[i])
                for i, source in enumerate(sources)
            ]
            for copy in copies:
                copy.start()
            for copy in copies:
                copy.wait()
            sources = local[:-1]
        kernel(*sources, *refs[:count], *refs[count + skip :])

    return pl.pallas_call(
        body,
        out_shape=tuple(outs),
        in_specs=[pl.BlockSpec(memory_space=pltpu.HBM)] * fetched + [vmem] * count + [anywhere] * skip,
        out_specs=tuple([vmem] * len(outs)),
        scratch_shapes=[*scratch, *buffers],
        compiler_params=pltpu.CompilerParams(
            vmem_limit_bytes=12 << 20, fuse_transposed_lhs_in_matmul=True
        ),
        cost_estimate=pl.CostEstimate(flops=int(flops), bytes_accessed=1, transcendentals=0),
        name=name,
    )(*far, *args, *after)


def tiles(extent, size=TILE):
    return [slice(at, min(at + size, extent)) for at in range(0, extent, size)]


def row_sum(values):
    return jnp.sum(values, axis=1, keepdims=True)


def columns_to_rows(columns):
    count = columns[0].shape[0]
    lane = lax.broadcasted_iota(jnp.int32, (count, LANES), 1)
    packed = jnp.zeros((count, LANES), F32)
    for index, column in enumerate(columns):
        packed = jnp.where(lane == index, column, packed)
    return packed.T[:8]


def rows_to_columns(rows, count):
    turned = jnp.concatenate([rows] * (LANES // 8), axis=0).T
    return [turned[:, i : i + 1] for i in range(count)]


def rms_scale(total):
    return lax.rsqrt(total / D + EPSILON)


def turn(values, cosine, sine_part):
    lane = lax.broadcasted_iota(jnp.int32, cosine.shape, 1)
    first = (lane % HEAD) < HEAD // 2
    out = []
    for tile in tiles(values.shape[1], LANES):
        part = values[:, tile]
        other = jnp.where(
            first, pltpu.roll(part, LANES - HEAD // 2, 1), pltpu.roll(part, HEAD // 2, 1)
        )
        out.append(part * cosine + other * sine_part)
    return jnp.concatenate(out, axis=1)


def rope_tables(count):
    half = HEAD // 2
    frequency = np.exp(np.arange(half, dtype=np.float32) * np.float32(-2.0 * math.log(ROPE_BASE) / HEAD))
    angles = np.arange(count).astype(np.float32)[:, None] * frequency[None, :]
    cosine, sine_part = np.cos(angles), np.sin(angles)
    repeats = LANES // HEAD
    return (
        jnp.asarray(np.concatenate([cosine, cosine] * repeats, axis=1)),
        jnp.asarray(np.concatenate([-sine_part, sine_part] * repeats, axis=1)),
    )


def lower_triangle():
    rows = lax.broadcasted_iota(jnp.int32, (CHUNK, CHUNK), 0)
    cols = lax.broadcasted_iota(jnp.int32, (CHUNK, CHUNK), 1)
    return rows >= cols


def keep_rows(pairs):
    for before, out in pairs:
        out[:CHUNK] = before[:CHUNK]


def head_mask(count, index):
    lane = lax.broadcasted_iota(jnp.int32, (count, LANES), 1)
    return (lane < HEAD) if index == 0 else (lane >= HEAD)


def only(mask, values):
    return jnp.where(mask, values, jnp.zeros_like(values))


def total_of(mine, theirs):
    return jnp.concatenate(
        [a[...].astype(F32) + b[...].astype(F32) for a, b in zip(mine, theirs)], axis=0
    )


def branch_of(mine, theirs):
    branch = total_of(mine, theirs)
    return branch, rms_scale(row_sum(branch * branch))


def store_pieces(pieces, columns, values):
    at = 0
    for piece in pieces:
        high = piece.shape[0]
        piece[:, columns] = values[at : at + high].astype(BF16)
        at += high


def gain_of(mine, theirs, index):
    row = slice(index, index + 1)
    return jnp.concatenate([mine[row, :], theirs[row, :]], axis=1)


def on_own_chip():
    return lax.axis_index("row") == lax.axis_index("col")


def own_half():
    return lax.axis_index("dp") & 1


def is_inner():
    place = lax.axis_index("dp") >> 1
    return (place == 1) | (place == 2)


def norm_back(branch, scale, gain_vec, grad_out):
    weighted = grad_out * gain_vec
    inner = row_sum(weighted * branch)
    grad_branch = scale * weighted - branch * (scale * scale * scale * inner / D)
    grad_gain = jnp.sum(grad_out * branch * scale, axis=0, keepdims=True)
    return grad_branch, grad_gain


def pack_kernel(*refs):
    out = refs[-1]
    out[...] = jnp.zeros(out.shape, F32)
    for index, row in enumerate(refs[:-1]):
        out[index : index + 1, :] = row[...]


def copy_kernel(*refs):
    count = len(refs) // 2
    for source, out in zip(refs[:count], refs[count:]):
        out[...] = source[...]


def pack_weights_kernel(wg, wu, wd, out):
    high, ff = wg.shape
    out[:, :ff] = wg[...]
    out[:, ff : 2 * ff] = wu[...]
    for index, rows in enumerate(tiles(ff, high)):
        at = 2 * ff + index * high
        out[: rows.stop - rows.start, at : at + high] = wd[rows, :]


def packed_weights(packed, ff):
    high = packed.shape[0]
    blocks = []
    for index, rows in enumerate(tiles(ff, high)):
        at = 2 * ff + index * high
        blocks.append((rows, packed.at[: rows.stop - rows.start, at : at + high]))
    return packed.at[:, :ff], packed.at[:, ff : 2 * ff], blocks


def choose_kernel(first, other, out):
    out[...] = jnp.where(on_own_chip(), first[...], other[...])


def choose_two_kernel(first, other, beside, corner, out, out_theirs):
    choose_kernel(first, other, out)
    choose_kernel(beside, corner, out_theirs)


def query_key_kernel(
    block, wq, wk, over, beside, corner, wqt, wkt, q_out, k_out, total_out, mine, theirs
):
    choose_two_kernel(block, over, beside, corner, mine, theirs)
    query_sum = 0.0
    key_sum = 0.0
    for tile in tiles(wq.shape[1]):
        query = dot(mine[...], wq[:, tile]) + dot(theirs[...], wqt[:, tile])
        q_out[:, tile] = query
        query_sum = query_sum + row_sum(query * query)
        key = dot(mine[...], wk[:, tile]) + dot(theirs[...], wkt[:, tile])
        k_out[:, tile] = key
        key_sum = key_sum + row_sum(key * key)
    total_out[...] = columns_to_rows([query_sum, key_sum])


def value_kernel(mine, theirs, wv, wvt, v_out):
    for tile in tiles(wv.shape[1]):
        v_out[:, tile] = (dot(mine[...], wv[:, tile]) + dot(theirs[...], wvt[:, tile])).astype(BF16)


def attention_kernel(
    chunk,
    queries,
    keys,
    values,
    totals,
    totals_over,
    qgain,
    kgain,
    cosine,
    sine_part,
    wo,
    wot,
    *rest,
):
    if chunk == 0:
        q_rot, k_rot, mixed, logs, *partial = rest
    else:
        q_rot, k_rot, mixed, logs, *partial = rest[4:]
        keep_rows(zip(rest[:4], rest[4:]))
    rows = slice(chunk * CHUNK, (chunk + 1) * CHUNK)
    query_total, key_total = rows_to_columns(totals[...] + totals_over[...], 2)
    query = queries[rows, :] * rms_scale(query_total[rows]) * qgain[...]
    key = keys[rows, :] * rms_scale(key_total[rows]) * kgain[...]
    q_rot[rows, :] = (turn(query, cosine[rows, :], sine_part[rows, :]) * FACTOR).astype(BF16)
    k_rot[rows, :] = turn(key, cosine[rows, :], sine_part[rows, :]).astype(BF16)
    visible = lower_triangle()
    lane = lax.broadcasted_iota(jnp.int32, (CHUNK, LANES), 1)
    log_tile = jnp.zeros((CHUNK, LANES), F32)
    for at, tile in enumerate(tiles(queries.shape[1], LANES)):
        total = jnp.zeros((CHUNK, LANES), F32)
        for index in range(2):
            query_head = only(head_mask(CHUNK, index), q_rot[rows, tile])
            scores = []
            for block in range(chunk + 1):
                part = dot_t(query_head, k_rot[block * CHUNK : (block + 1) * CHUNK, tile])
                scores.append(jnp.where(visible, part, MASKED) if block == chunk else part)
            peak = jnp.max(scores[0], axis=1, keepdims=True)
            for part in scores[1:]:
                peak = jnp.maximum(peak, jnp.max(part, axis=1, keepdims=True))
            scores = [jnp.exp(part - peak) for part in scores]
            denominator = sum(row_sum(part) for part in scores)
            inverse = 1.0 / denominator
            for block, part in enumerate(scores):
                value_rows = values[block * CHUNK : (block + 1) * CHUNK, tile]
                total = total + dot(
                    (part * inverse).astype(BF16), only(head_mask(CHUNK, index), value_rows)
                )
            log_tile = jnp.where(lane == 2 * at + index, peak + jnp.log(denominator), log_tile)
        mixed[rows, tile] = total.astype(BF16)
    logs[rows, :] = log_tile
    low = mixed[rows, :]
    half = wo.shape[1]
    store_pieces(partial, slice(0, half), dot(low, wo[...]))
    store_pieces(partial, slice(half, 2 * half), dot(low, wot[...]))


def forward_kernel(
    chunk, *refs
):
    part, part_over = refs[:PIECES], refs[PIECES : 2 * PIECES]
    forward_body(chunk, part, part_over, *refs[2 * PIECES :])


def forward_body(
    chunk, part, part_over, mine, theirs, gains, gains_far, wg, wu, wd, w_far, *rest
):
    if chunk == 0:
        low_mine, side, hidden, gate, up, *partial = rest
    else:
        mixed = rest[0]
        low_mine, side, hidden, gate, up, *partial = rest[3:]
        keep_rows(zip(rest[1:3], rest[3:]))
        at = wg.shape[1] + mine.shape[1]
        side[:, at : at + mixed.shape[1]] = mixed[...]
        side[:, at + mixed.shape[1] :] = theirs[...]
    rows = slice(chunk * CHUNK, (chunk + 1) * CHUNK)
    branch, scale = branch_of(part, part_over)
    half, ff = mine.shape[1], wg.shape[1]
    wgt, wut, wdt = packed_weights(w_far, ff)
    normed = branch * scale * gain_of(gains, gains_far, 0)
    value = mine[rows, :].astype(F32) + normed[:, :half]
    hidden[:, :half] = value
    low_mine[rows, :] = value.astype(BF16)
    value = theirs[rows, :].astype(F32) + normed[:, half:]
    hidden[:, half:] = value
    side[rows, ff : ff + half] = value.astype(BF16)
    for tile in tiles(ff):
        left, right = low_mine[rows, :], side[rows, ff : ff + half]
        gate_act = dot(left, wg[:, tile]) + dot(right, wgt[:, tile])
        up_act = dot(left, wu[:, tile]) + dot(right, wut[:, tile])
        gate[:, tile] = gate_act
        up[:, tile] = up_act
        side[rows, tile] = (gate_act * jax.nn.sigmoid(gate_act) * up_act).astype(BF16)
    low = side[rows, :ff]
    store_pieces(partial, slice(0, half), dot(low, wd[...]))
    theirs_part = sum(dot(side[rows, span], block[...]) for span, block in wdt)
    store_pieces(partial, slice(half, 2 * half), theirs_part)


def ff_norm_back_kernel(
    chunk, *refs
):
    part, part_over = refs[:PIECES], refs[PIECES : 2 * PIECES]
    hidden, cot_mine, cot_theirs, gains, gains_far, *rest = refs[2 * PIECES :]
    if chunk == 0:
        gff_mine, gff_theirs, out_mine, out_theirs, grad_gain = rest
    else:
        gain_before = rest[0]
        gff_mine, gff_theirs, out_mine, out_theirs, grad_gain = rest[5:]
        keep_rows(zip(rest[1:5], rest[5:]))
    rows = slice(chunk * CHUNK, (chunk + 1) * CHUNK)
    branch, scale = branch_of(part, part_over)
    half = cot_mine.shape[1]
    gain = gain_of(gains, gains_far, 1)
    block_out = hidden[...] + branch * scale * gain
    out_mine[rows, :] = block_out[:, :half]
    out_theirs[rows, :] = block_out[:, half:]
    upstream = jnp.concatenate([cot_mine[rows, :], cot_theirs[rows, :]], axis=1).astype(F32)
    grad_branch, gained = norm_back(branch, scale, gain, upstream)
    grad_gain[...] = gained if chunk == 0 else gain_before[...] + gained
    gff_mine[rows, :] = grad_branch[:, :half].astype(BF16)
    gff_theirs[rows, :] = grad_branch[:, half:].astype(BF16)


def backward_kernel(
    chunk, gff_mine, gff_theirs, gate, up, wg, wu, wd, w_far, *rest
):
    if chunk == 0:
        grads, *partial = rest
    else:
        grads, *partial = rest[1:]
        keep_rows([rest[:2]])
    rows = slice(chunk * CHUNK, (chunk + 1) * CHUNK)
    half, ff = wd.shape[1], wg.shape[1]
    wgt, wut, wdt = packed_weights(w_far, ff)
    for tile in tiles(ff):
        span, block = wdt[tile.start // wdt[0][0].stop]
        part = block[tile.start - span.start : tile.stop - span.start, :]
        grad_act = dot_t(gff_mine[rows, :], wd[tile, :]) + dot_t(gff_theirs[rows, :], part)
        gate_act = gate[:, tile]
        sig = jax.nn.sigmoid(gate_act)
        grads[rows, tile] = (
            grad_act * up[:, tile] * sig * (1.0 + gate_act * (1.0 - sig))
        ).astype(BF16)
        there = slice(ff + tile.start, ff + tile.stop)
        grads[rows, there] = (grad_act * gate_act * sig).astype(BF16)
    left, right = grads[rows, :ff], grads[rows, ff:]
    for tile in tiles(half):
        store_pieces(partial, tile, dot_t(left, wg[tile, :]) + dot_t(right, wu[tile, :]))
        there = slice(half + tile.start, half + tile.stop)
        store_pieces(partial, there, dot_t(left, wgt[tile, :]) + dot_t(right, wut[tile, :]))


def attention_back_kernel(chunk, *refs):
    grad_part, grad_over, part, part_over = [
        refs[i * PIECES : (i + 1) * PIECES] for i in range(4)
    ]
    (
        cot_mine,
        cot_theirs,
        gains,
        gains_far,
        wo,
        wot,
        q_rot,
        k_rot,
        values,
        logs,
        queries,
        keys,
        totals,
        totals_over,
        qgain,
        kgain,
        cosine,
        sine_part,
        *rest,
    ) = refs[4 * PIECES :]
    half = wo.shape[1]
    width = queries.shape[1]
    if chunk == 0:
        gat_mine, side, gh_mine, gh_theirs, gqn, grad_gain, column, gk_sum, gv_sum = rest
    else:
        gain_before, column_in, gk_in, gv_in = rest[:4]
        gat_mine, side, gh_mine, gh_theirs, gqn, grad_gain, gkn, gv_low, inner_out = rest[6:]
        keep_rows(zip(rest[4:6], rest[6:]))
    rows = slice(chunk * CHUNK, (chunk + 1) * CHUNK)
    seen = (chunk + 1) * CHUNK
    branch, scale = branch_of(part, part_over)
    grad_hidden = (
        jnp.concatenate([cot_mine[rows, :], cot_theirs[rows, :]], axis=1).astype(F32)
        + total_of(grad_part, grad_over)
    )
    gh_mine[...] = grad_hidden[:, :half]
    gh_theirs[...] = grad_hidden[:, half:]
    grad_branch, gained = norm_back(branch, scale, gain_of(gains, gains_far, 0), grad_hidden)
    grad_gain[...] = gained if chunk == 0 else gain_before[...] + gained
    gat_mine[rows, :] = grad_branch[:, :half].astype(BF16)
    side[rows, :] = grad_branch[:, half:].astype(BF16)
    grad_mixed = (
        dot_t(gat_mine[rows, :], wo[...]) + dot_t(side[rows, :], wot[...])
    ).astype(BF16)
    visible = lower_triangle()
    query_total, key_total = rows_to_columns(totals[...] + totals_over[...], 2)
    query_inner = jnp.zeros((CHUNK, 1), F32)
    key_inner = jnp.zeros((seen, 1), F32)
    for at, tile in enumerate(tiles(width, LANES)):
        grad_query = jnp.zeros((CHUNK, LANES), F32)
        grad_key = [jnp.zeros((CHUNK, LANES), F32) for _ in range(chunk + 1)]
        grad_value = [jnp.zeros((CHUNK, LANES), F32) for _ in range(chunk + 1)]
        for index in range(2):
            mask = head_mask(CHUNK, index)
            query_head = only(mask, q_rot[rows, tile])
            grad_head = only(mask, grad_mixed[:, tile])
            log_column = logs[rows, 2 * at + index : 2 * at + index + 1]
            weights, grads = [], []
            for block in range(chunk + 1):
                span = slice(block * CHUNK, (block + 1) * CHUNK)
                scores = dot_t(query_head, k_rot[span, tile])
                if block == chunk:
                    scores = jnp.where(visible, scores, MASKED)
                weights.append(jnp.exp(scores - log_column))
                grads.append(dot_t(grad_head, values[span, tile]))
            inner = sum(row_sum(w * g) for w, g in zip(weights, grads))
            for block in range(chunk + 1):
                span = slice(block * CHUNK, (block + 1) * CHUNK)
                weight = weights[block]
                grad_scores = (weight * (grads[block] - inner)).astype(BF16)
                grad_value[block] = grad_value[block] + t_dot(weight.astype(BF16), grad_head)
                grad_query = grad_query + dot(grad_scores, only(mask, k_rot[span, tile]))
                grad_key[block] = grad_key[block] + t_dot(grad_scores, query_head)
        back = turn(grad_query * FACTOR, cosine[rows, :], -sine_part[rows, :])
        gqn[:, tile] = back
        query_inner = query_inner + row_sum(back * qgain[:, tile] * queries[rows, tile])
        if chunk == 0:
            gk_sum[:, tile] = grad_key[0]
            gv_sum[:, tile] = grad_value[0]
        else:
            key_all = jnp.concatenate([gk_in[:, tile] + grad_key[0], grad_key[1]], axis=0)
            value_all = jnp.concatenate([gv_in[:, tile] + grad_value[0], grad_value[1]], axis=0)
            gv_low[:, tile] = value_all.astype(BF16)
            back = turn(key_all, cosine[...], -sine_part[...])
            gkn[:, tile] = back
            key_inner = key_inner + row_sum(back * kgain[:, tile] * keys[:, tile])
    if chunk == 0:
        column[...] = jnp.broadcast_to(query_inner, (CHUNK, LANES))
    else:
        query_inner = jnp.concatenate([column_in[:, :1], query_inner], axis=0)
        inner_out[...] = columns_to_rows([query_inner, key_inner])


def query_key_back_kernel(
    gqn_first,
    gqn_second,
    gkn,
    queries,
    keys,
    totals,
    totals_over,
    inner,
    inner_over,
    qgain,
    kgain,
    mlp_part,
    attn_part,
    grads,
    gain_mine,
    gain_give,
):
    width = queries.shape[1]
    half = gain_mine.shape[1]
    for out, columns in ((gain_mine, slice(0, half)), (gain_give, slice(half, 2 * half))):
        out[...] = jnp.zeros(out.shape, F32)
        out[0:1, :] = mlp_part[:, columns]
        out[1:2, :] = attn_part[:, columns]
    query_total, key_total = rows_to_columns(totals[...] + totals_over[...], 2)
    query_inner, key_inner = rows_to_columns(inner[...] + inner_over[...], 2)
    gqn = jnp.concatenate([gqn_first[...], gqn_second[...]], axis=0)
    for at, raw, back, total, sums, gain, low in (
        (2, queries, gqn, query_total, query_inner, qgain, grads.at[:, :width]),
        (3, keys, gkn[...], key_total, key_inner, kgain, grads.at[:, width:]),
    ):
        scale = rms_scale(total)
        value = raw[...]
        low[...] = (
            scale * (back * gain[...]) - value * (scale * scale * scale * sums / D)
        ).astype(BF16)
        gained = jnp.sum(back * value * scale, axis=0, keepdims=True)
        gain_mine[at : at + 1, :] = gained
        gain_give[at : at + 1, :] = gained


GAIN_ROWS = 16


def plain_weight_kernel(products, *refs):
    plain = refs[-1]

    def view(operand):
        index, start, stop = operand
        return refs[index].at[:, start:stop]

    at = 0
    for product in products:
        left, left_far, right, right_far = [view(operand) for operand in product]
        width = product[2][2] - product[2][1]
        for tile in tiles(plain.shape[0]):
            plain[tile, at : at + width] = (
                t_dot(left[:, tile], right[...]) + t_dot(left_far[:, tile], right_far[...])
            ).astype(BF16)
        at += width


def weight_kernel(with_gains, products, *refs):
    keep, give, plain = refs[-3:]
    plain_weight_kernel(products, *refs[:-3], plain)
    half = plain.shape[0] // 2
    mine = pl.multiple_of(own_half() * half, half)
    theirs = pl.multiple_of((1 - own_half()) * half, half)
    keep[:half, :] = plain[pl.ds(mine, half), :]
    give[:half, :] = plain[pl.ds(theirs, half), :]
    if with_gains:
        gains = refs[-5][...] + refs[-4][...]
        width = gains.shape[1]
        rows = jnp.concatenate([gains, jnp.zeros_like(gains)], axis=0)
        rest = jnp.zeros((GAIN_ROWS, plain.shape[1] - width), F32)
        rows = jnp.concatenate([rows, rest], axis=1).astype(BF16)
        keep[half:, :] = rows
        give[half:, :] = rows


def add_kernel(mine, *rest):
    out = rest[-1]
    at = 0
    for piece in rest[:-1]:
        rows = slice(at, at + piece.shape[0])
        out[rows, :] = (mine[rows, :].astype(F32) + piece[...].astype(F32)).astype(BF16)
        at = rows.stop


def inner_kernel(mine, received, out):
    out[...] = jnp.where(is_inner(), mine[...], received[...])


def finish_kernel(mine, received, *outs):
    half = outs[0].shape[0] // 2
    for place, source in enumerate((mine, received)):
        to = pl.multiple_of((own_half() ^ place) * half, half)
        column = 0
        for out in outs:
            width = out.shape[1]
            out[pl.ds(to, half), :] = source[:half, column : column + width].astype(F32)
            column += width


def in_far_kernel(side_far, block, out):
    out[...] = jnp.where(on_own_chip(), side_far[:, side_far.shape[1] - out.shape[1] :], block[...])


def gains_out_kernel(total, *outs):
    rows = total[total.shape[0] - GAIN_ROWS :, :].astype(F32)
    for index, out in enumerate(outs):
        out[...] = rows[index : index + 1, : out.shape[1]]


def finish_rest_kernel(mine, received, query_first, query, key):
    half = query.shape[0] // 2
    split = query_first.shape[1]
    more = query.shape[1] - split
    query[:, :split] = query_first[...]
    for place, source in enumerate((mine, received)):
        to = pl.multiple_of((own_half() ^ place) * half, half)
        query[pl.ds(to, half), split:] = source[:half, :more].astype(F32)
        key[pl.ds(to, half), :] = source[:half, more:].astype(F32)


def grad_input_kernel(stays, moves, across, corner, out):
    own = on_own_chip()
    out[...] = jnp.where(own, stays[...], moves[...]) + jnp.where(
        own, across[...], corner[...]
    ).astype(F32)


def input_back_kernel(
    grads, gv, wq, wqt, wk, wkt, wv, wvt, *rest
):
    width = wq.shape[1]
    gq, gk = grads.at[:, :width], grads.at[:, width:]
    gh_mine, gh_theirs = rest[:2], rest[2:4]
    stays, moves, across, corner = rest[4:]
    for tile in tiles(wq.shape[0]):
        mine = (
            dot_t(gq[...], wq[tile, :]) + dot_t(gk[...], wk[tile, :]) + dot_t(gv[...], wv[tile, :])
        )
        theirs = (
            dot_t(gq[...], wqt[tile, :])
            + dot_t(gk[...], wkt[tile, :])
            + dot_t(gv[...], wvt[tile, :])
        )
        for chunk in range(2):
            rows = slice(chunk * CHUNK, (chunk + 1) * CHUNK)
            stays[rows, tile] = gh_mine[chunk][:, tile] + mine[rows]
            moves[rows, tile] = gh_theirs[chunk][:, tile] + theirs[rows]
        across[:, tile] = mine.astype(BF16)
        corner[:, tile] = theirs.astype(BF16)


def dp_exchange(values, bit):
    size = lax.axis_size("dp")
    return lax.ppermute(values, "dp", [(i, i ^ (1 << bit)) for i in range(size)])


def dp_bits():
    return lax.axis_size("dp").bit_length() - 1


def along_line(values, moves):
    pairs = [(2 * a + half, 2 * b + half) for a, b in moves for half in range(2)]
    return lax.ppermute(values, "dp", pairs)


def in_turn(operands, received):
    return lax.optimization_barrier((operands, received))


class Chain:
    def __init__(self, name, high, widths, keep, give):
        self.name, self.high, self.widths, self.keep, self.give = name, high, widths, keep, give
        self.back = False
        self.received = None

    def kernel(self, body, args, part, after, outs=None):
        out = call(
            body, outs or [shape(self.keep.shape)], args, f"{self.name}_{part}", after=after
        )
        if outs is None:
            (self.keep,) = out
        else:
            self.out = out
        return out[0]

    def combine(self, body, part, after):
        return self.kernel(body, [self.keep, *self.received], part, after)

    def finish(self, after):
        outs = [shape((self.high, w), F32) for w in self.widths]
        return self.kernel(finish_kernel, [self.keep, *self.received], "out", after, outs)


LINE = ((0, 1), (3, 2)), ((1, 2), (2, 1)), ((1, 0), (2, 3))


class Lanes:
    def __init__(self):
        self.line = [None, None, None]
        self.latest = None

    def send_y(self, chain, before=None):
        operands = [chain.keep if chain.back else chain.give]
        if before is not None:
            operands, before.received = in_turn(operands, before.received)
        chain.received = [dp_exchange(piece, 0) for piece in operands]

    def pass_on(self, index, chain):
        before, self.line[index] = self.line[index], chain
        if before is not None and chain is not None:
            chain.keep, before.received = in_turn(chain.keep, before.received)
        if chain is not None:
            chain.received = [along_line(chain.keep, LINE[index])]
        return before

    def advance(self, chain, following=None, after=()):
        current = chain
        late = following is not None and following is self.line[2]
        if following is not None and not late:
            self.send_y(following, chain)
        done = None
        if chain.back:
            done, chain = chain, None
        else:
            self.latest = chain.combine(add_kernel, "y", (self.latest, *after))
            if lax.axis_size("dp") != 8:
                for bit in range(1, dp_bits()):
                    other = dp_exchange(chain.keep, bit).astype(F32)
                    chain.keep = (chain.keep.astype(F32) + other).astype(BF16)
                chain.back = True
                chain = None
        for index, (body, part) in enumerate(
            ((add_kernel, "in"), (add_kernel, "across"), (inner_kernel, "out"))
        ):
            chain = self.pass_on(index, chain)
            if chain is not None:
                self.latest = chain.combine(body, f"z_{part}", (self.latest,))
        if chain is not None:
            chain.back = True
        if late:
            self.send_y(following, current)
        if done is not None:
            self.latest = done.finish((self.latest,))


def on_device(
    block_in,
    w_query,
    w_key,
    w_value,
    w_output,
    w_gate,
    w_up,
    w_down,
    qnorm_gain,
    knorm_gain,
    attn_gain,
    mlp_gain,
    cotangent,
):
    rows, half = block_in.shape
    width = w_query.shape[1]
    ff = w_gate.shape[1]
    pair = ("row", "col")

    to_over = [(0, 1), (3, 2)]
    to_corner = [(1, 2), (2, 1)]
    to_beside = [(2, 0), (1, 3)]
    from_same = [(0, 2), (3, 1)]

    in_over = lax.ppermute(block_in, pair, to_over)
    in_corner = lax.ppermute(block_in, pair, to_corner)
    in_beside = lax.ppermute(block_in, pair, to_beside)
    wq_far, wk_far = swap(w_query, "row"), swap(w_key, "row")
    qgain, kgain = qnorm_gain[None], knorm_gain[None]
    cosine, sine_part = rope_tables(rows)

    near = call(
        copy_kernel,
        [shape((rows, half)), shape((half, width)), shape((half, width))],
        [block_in, w_query, w_key],
        "near",
    )
    (ff_weights,) = call(
        pack_weights_kernel,
        [shape((half, 2 * ff + -(-ff // half) * half))],
        [w_gate, w_up, w_down],
        "ff_weights",
        after=(near[0],),
    )
    (gains,) = call(
        pack_kernel,
        [shape((8, half), F32)],
        [attn_gain[None], mlp_gain[None]],
        "gains",
        after=(ff_weights,),
    )
    (wv_give, wo_give, gains), (in_corner, in_over, ff_weights, *near) = in_turn(
        [w_value, w_output, gains], [in_corner, in_over, ff_weights, *near]
    )
    wv_far, wo_far, gains_far = [swap(value, "row") for value in (wv_give, wo_give, gains)]

    queries, keys, totals, in_mine, in_theirs = call(
        query_key_kernel,
        [shape((rows, width), F32)] * 2 + [shape((8, rows), F32)] + [shape((rows, half))] * 2,
        [*near, in_over, in_beside, in_corner, wq_far, wk_far],
        "query_key",
    )
    totals_over = swap(totals, "col")
    (values,) = call(
        value_kernel,
        [shape((rows, width))],
        [in_mine, in_theirs, w_value, wv_far],
        "value",
    )
    (cotangent, ff_weights), (totals_over, values, wo_far, gains_far) = in_turn(
        [cotangent, ff_weights], [totals_over, values, wo_far, gains_far]
    )
    cot_over = lax.ppermute(cotangent, pair, to_over)
    cot_corner = lax.ppermute(cotangent, pair, to_corner)
    w_far = swap(ff_weights, "row")
    attention_args = [
        queries,
        keys,
        values,
        totals,
        totals_over,
        qgain,
        kgain,
        cosine,
        sine_part,
        w_output,
        wo_far,
    ]
    partial = [shape((CHUNK // PIECES, D))] * PIECES
    attention_outs = [shape((rows, width))] * 3 + [shape((rows, LANES), F32), *partial]

    def send_over(pieces, before=None):
        if before is not None:
            for index in range(PIECES):
                (pieces[index],), (before[index],) = in_turn([pieces[index]], [before[index]])
        return [swap(piece, "col") for piece in pieces]

    *kept, first_a, first_b = call(
        functools.partial(attention_kernel, 0),
        attention_outs,
        attention_args,
        "attention_0",
    )
    first = [first_a, first_b]
    first_over = send_over(first)
    *kept, second_a, second_b = call(
        functools.partial(attention_kernel, 1),
        attention_outs,
        attention_args + kept,
        "attention_1",
    )
    q_rot, k_rot, mixed, logs = kept
    second = [second_a, second_b]
    second_over = send_over(second, first_over)
    parts, parts_over = [first, second], [first_over, second_over]

    (cot_mine,) = call(
        choose_kernel, [shape((rows, half))], [cotangent, cot_over], "cotangent_mine"
    )
    side_width = ff + half + width + half

    def forward(chunk, over, kept, after):
        return call(
            functools.partial(forward_kernel, chunk),
            [shape((rows, half)), shape((rows, side_width)), shape((CHUNK, D), F32)]
            + [shape((CHUNK, ff), F32)] * 2
            + partial,
            [*parts[chunk], *over, in_mine, in_theirs, gains, gains_far]
            + [w_gate, w_up, w_down, w_far]
            + kept,
            f"forward_{chunk}",
            after=after,
        )

    low_mine, side, *saved = forward(0, first_over, [], (cot_mine, cot_corner))
    saved_all, ff_first = [saved[:3]], saved[3:]
    (cotangent,), (low_mine,) = in_turn([cotangent], [low_mine])
    cot_beside = lax.ppermute(cotangent, pair, to_beside)
    (cot_theirs,) = call(
        choose_kernel, [shape((rows, half))], [cot_beside, cot_corner], "cotangent_theirs"
    )
    ff_first_over = send_over(ff_first, second_over)
    low_mine, side, *saved = forward(1, second_over, [mixed, low_mine, side], ())
    saved_all.append(saved[:3])
    ff_second = saved[3:]
    ff_second_over = send_over(ff_second, ff_first_over)

    def weight_grad(name, arrays, products, after, gains=()):
        high = products[0][0][2] - products[0][0][1]
        widths = [right[2] - right[1] for _, _, right, _ in products]
        extra = GAIN_ROWS if gains else 0
        keep, give = call(
            functools.partial(weight_kernel, bool(gains), products),
            [shape((high // 2 + extra, sum(widths)))] * 2,
            [*arrays, *gains],
            name,
            scratch=[pltpu.VMEM((high, sum(widths)), BF16)],
            after=after,
        )
        return Chain(name, high, widths, keep, give)

    def ff_norm_back(chunk, mine, over, more, after):
        return call(
            functools.partial(ff_norm_back_kernel, chunk),
            [shape((rows, half))] * 2 + [shape((rows, half), F32)] * 2 + [shape((1, D), F32)],
            [*mine, *over, saved_all[chunk][0], cot_mine, cot_theirs, gains, gains_far, *more],
            f"ff_norm_back_{chunk}",
            after=after,
        )

    def backward(chunk, more, after):
        return call(
            functools.partial(backward_kernel, chunk),
            [shape((rows, 2 * ff)), *partial],
            [gff_mine, gff_theirs, *saved_all[chunk][1:]]
            + [w_gate, w_up, w_down, w_far]
            + more,
            f"backward_{chunk}",
            after=after,
        )

    *kept, mlp_part = ff_norm_back(0, ff_first, ff_first_over, [], ())
    gff_mine, gff_theirs, _, _ = kept
    grads, *gh_first = backward(0, [], ())
    gh_first_over = send_over(gh_first, ff_second_over)
    *kept, mlp_part = ff_norm_back(
        1, ff_second, ff_second_over, [mlp_part, *kept], ()
    )
    gff_mine, gff_theirs, out_mine, out_theirs = kept
    (side,), (gff_theirs,) = in_turn([side], [gff_theirs])
    side_far = swap(side, "row")
    gff_far = swap(gff_theirs, "row")
    out_beside = lax.ppermute(out_theirs, pair, from_same)
    grads, *gh_second = backward(1, [grads], ())
    lanes = Lanes()
    down = weight_grad(
        "down",
        [side, side_far, gff_mine, gff_far],
        [((0, 0, ff), (1, 0, ff), (2, 0, half), (3, 0, half))],
        (grads,),
    )
    (block_out,) = call(
        choose_kernel,
        [shape((rows, half), F32)],
        [out_mine, out_beside],
        "block_out",
        after=(down.keep,),
    )
    (in_far,) = call(
        in_far_kernel, [shape((rows, half))], [side_far, block_in], "in_far", after=(block_out,)
    )
    lanes.send_y(down)
    (gh_second, grads), (gh_first_over, down.keep, in_far) = in_turn(
        [gh_second, grads], [gh_first_over, down.keep, in_far]
    )
    gh_second_over = send_over(gh_second)
    grads_far = swap(grads, "row")
    grad_parts, grad_over = [gh_first, gh_second], [gh_first_over, gh_second_over]

    def ff_grad(name, start, after):
        span = (start, start + ff)
        return weight_grad(
            name,
            [low_mine, side_far, grads, grads_far],
            [((0, 0, half), (1, ff, ff + half), (2, *span), (3, *span))],
            after,
        )

    latest = down.keep
    gh_mine, gh_theirs, gqn = [], [], []
    for chunk in range(2):
        args = [
            *grad_parts[chunk],
            *grad_over[chunk],
            *parts[chunk],
            *parts_over[chunk],
            cot_mine,
            cot_theirs,
            gains,
            gains_far,
            w_output,
            wo_far,
            q_rot,
            k_rot,
            values,
            logs,
            queries,
            keys,
            totals,
            totals_over,
            qgain,
            kgain,
            cosine,
            sine_part,
        ]
        outs = [shape((rows, half))] * 2
        outs += [shape((CHUNK, half), F32)] * 2 + [shape((CHUNK, width), F32), shape((1, D), F32)]
        if chunk == 0:
            outs += [shape((CHUNK, LANES), F32)] + [shape((CHUNK, width), F32)] * 2
        else:
            outs += [shape((rows, width), F32), shape((rows, width)), shape((8, rows), F32)]
            args += [attn_part, column, gk_sum, gv_sum, gat_mine, gat_theirs]
        gat_mine, gat_theirs, gm, gt, gq_turned, attn_part, *more = call(
            functools.partial(attention_back_kernel, chunk),
            outs,
            args,
            f"attention_back_{chunk}",
            after=(latest,),
            flops=4e9 if chunk else 1,
        )
        gh_mine.append(gm)
        gh_theirs.append(gt)
        gqn.append(gq_turned)
        if chunk == 0:
            column, gk_sum, gv_sum = more
            up = ff_grad("up", ff, (column,))
            gate = ff_grad("gate", 0, (up.keep,))
            lanes.latest = gate.keep
            lanes.advance(down, gate, grad_over[1])
            latest = lanes.latest
        else:
            gkn, gv, inner = more
    inner_over = swap(inner, "col")
    gat_far, gv_far = swap(gat_theirs, "row"), swap(gv, "row")
    grads_back, gain_mine, gain_give = call(
        query_key_back_kernel,
        [shape((rows, 2 * width))] + [shape((8, half), F32)] * 2,
        [
            *gqn,
            gkn,
            queries,
            keys,
            totals,
            totals_over,
            inner,
            inner_over,
            qgain,
            kgain,
            mlp_part,
            attn_part,
        ],
        "query_key_back",
        after=(gv,),
    )
    grads_back_far = swap(grads_back, "row")
    gain_far = swap(gain_give, "row")
    lanes.latest = grads_back
    lanes.advance(gate, up)
    split = width * 3 // 4
    mixing = weight_grad(
        "mixing",
        [mixed, side_far, gat_mine, gat_far, in_mine, in_far, gv, gv_far]
        + [grads_back, grads_back_far],
        [
            ((0, 0, width), (1, ff + half, ff + half + width), (2, 0, half), (3, 0, half)),
            ((4, 0, half), (5, 0, half), (6, 0, width), (7, 0, width)),
            ((4, 0, half), (5, 0, half), (8, 0, split), (9, 0, split)),
        ],
        (lanes.latest,),
    )
    rest = (split, 2 * width)
    matching = weight_grad(
        "matching",
        [in_mine, in_far, grads_back, grads_back_far],
        [((0, 0, half), (1, 0, half), (2, *rest), (3, *rest))],
        (mixing.keep,),
        (gain_mine, gain_far),
    )
    mixing.widths = [half, width, split]
    lanes.latest = matching.keep
    lanes.advance(up, mixing)
    lanes.advance(mixing, matching)
    lanes.advance(matching, down)
    stays, moves, across, corner = call(
        input_back_kernel,
        [shape((rows, half), F32)] * 2 + [shape((rows, half))] * 2,
        [grads_back, gv, w_query, wq_far, w_key, wk_far, w_value, wv_far]
        + [*gh_mine, *gh_theirs],
        "input_back",
        after=(lanes.latest,),
    )
    lanes.latest = across
    moves = lax.ppermute(moves, pair, from_same)
    across = lax.ppermute(across, pair, [(1, 0), (2, 3)])
    lanes.advance(down, gate)
    corner = lax.ppermute(corner, pair, to_corner)
    lanes.advance(gate, up)
    (grad_input,) = call(
        grad_input_kernel,
        [shape((rows, half), F32)],
        [stays, moves, across, corner],
        "grad_input",
        after=(lanes.latest,),
    )
    lanes.latest = grad_input
    lanes.advance(up, mixing)
    lanes.advance(mixing, matching)
    gain_out = call(
        gains_out_kernel,
        [shape((1, half), F32)] * 2 + [shape((1, width), F32)] * 2,
        [matching.keep],
        "gains_out",
        after=(lanes.latest,),
    )
    grad_mlpgain, grad_attngain, grad_qgain, grad_kgain = [row[0] for row in gain_out]
    lanes.latest = gain_out[0]
    grad_out, grad_value, query_first = mixing.out
    grad_query, grad_key = call(
        finish_rest_kernel,
        [shape((half, width), F32)] * 2,
        [matching.keep, *matching.received, query_first],
        "matching_out",
        after=(lanes.latest,),
    )
    (grad_down,) = down.out
    (grad_gate,) = gate.out
    (grad_up,) = up.out
    return (
        block_out,
        grad_input,
        grad_query,
        grad_key,
        grad_value,
        grad_out,
        grad_gate,
        grad_up,
        grad_down,
        grad_qgain,
        grad_kgain,
        grad_attngain,
        grad_mlpgain,
    )


def solution(mesh):
    tokens = P(("dp", "col"), "row")
    grid, turned = P("row", "col"), P("col", "row")
    in_specs = (
        tokens,
        grid,
        grid,
        grid,
        turned,
        grid,
        grid,
        turned,
        P("col"),
        P("col"),
        P("row"),
        P("row"),
        tokens,
    )
    out_specs = (
        tokens,
        tokens,
        grid,
        grid,
        grid,
        turned,
        grid,
        grid,
        turned,
        P("col"),
        P("col"),
        P("row"),
        P("row"),
    )
    return jax.shard_map(
        on_device, mesh=mesh, in_specs=in_specs, out_specs=out_specs, check_vma=False
    )
```
